32 devices in a mesh: groups: 2 (over y), recv: 4 (over z), win: 2 (over x), freq: 2 (over core).
Axes of the slice: x: 2, y: 2, z: 4, core: 2. Of those that a mesh axis runs over, the one named last changes fastest.
Arguments:
- spectra: bfloat16 [2, 2, 1024, 4096], P('win', None, ('groups', 'recv'), 'freq'), parts along dimension 2, may hold values from -6 to 6
- window_keep: int32 [4], P(('groups', 'win')), parts along dimension 0, may hold values from 0 to 1, as said below
- owners: int32 [8], P('groups'), parts along dimension 0, may hold values from 0 to 3, as said below
- pair_src: int32 [4, 512], P(None, ('groups', 'recv')), parts along dimension 1, may hold values from 0 to 127
- pair_rec: int32 [4, 512], P(None, ('groups', 'recv')), parts along dimension 1, may hold values from 0 to 127
- pair_count: int32 [4, 8], P(None, ('groups', 'recv')), parts along dimension 1, may hold values from 1 to 64, 128 in all within a row
- observed: float32 [4, 512, 4096], P(None, ('groups', 'recv'), ('win', 'freq')), parts along dimension 1, may hold values from -6 to 6
Outputs:
- normed: float32 [4, 512, 4096], P(None, ('groups', 'recv'), ('win', 'freq')), parts along dimension 1
- adjoint: float32 [1024, 4096], P(('groups', 'recv'), ('win', 'freq')), parts along dimension 0
The draws below stay inside these ranges and needn't reach their ends.
There are 2 independent parts, one for each index of `groups`. The reference program is written for one: setup_inputs(seed, part) draws one part's arguments, and reference() takes and returns one part's arrays. A program takes and returns all parts, laid end to end along the dimension named above; each array names one. Nothing has to cross between parts.
Inputs may be any that keep to these rules, and one draw needn't show every extreme that they name: `owners`: distinct receiver blocks. `pair_count`: within one part, for each source block some receiver block holds exactly 64 used slots, and that source block's counts over all receiver blocks of the part sum to 64 * 4 / 2. `window_keep`: within one part at least one window is kept and at least one is dropped.
All inputs are finite; a program needn't handle non-finite values.
Results may differ from the reference program's by a relative error of at most 0.0037.
Values may be sent and summed in bfloat16 or wider, within the bound.
No kernel may reach another device: no remote copies, remote signals or barrier semaphores. Data moves between devices by JAX's collectives and lax.ppermute only.
A program may use at most 128 MiB of HBM per device.

```python
import math
import jax
import jax.numpy as jnp
import numpy as np
from jax import lax

CH_DEV = 128
NF = 4096
LAGS = 4096
BLOCKS = 4
PAIRS = 64
WINS = 2
CHANNELS = 512
N_RECV = 4


def draw_owners(key, part):
    key = jax.random.fold_in(key, 11)
    return jax.random.permutation(key, N_RECV)[:BLOCKS].astype(jnp.int32)


def draw_window_keep(key, part):
    key = jax.random.fold_in(key, 13)
    bit_key, order_key = jax.random.split(key)
    kept = jax.random.randint(bit_key, (WINS,), 0, 2).astype(jnp.int32)
    order = jax.random.permutation(order_key, WINS)
    kept = kept.at[order[0]].set(0)
    kept = kept.at[order[1]].set(1)
    return kept.astype(jnp.int32)


def set_ends(drawn, key, low, top_value):
    shape = drawn.shape
    index_at = [jax.random.randint(jax.random.fold_in(key, axis), (), 0, shape[axis]) for axis in range(len(shape))]
    drawn = drawn.at[tuple(index_at)].set(low)
    longest = shape.index(max(shape))
    index_at[longest] = (index_at[longest] + 1) % shape[longest]
    return drawn.at[tuple(index_at)].set(top_value)


def level_of(stream_key, shape, cuts, least, largest):
    gain, own = 1.0, jax.random.fold_in(stream_key, 6)
    for dim, blocks in cuts:
        heights = jnp.exp(jax.random.uniform(jax.random.fold_in(own, dim), (blocks,), jnp.float32, least / len(cuts), largest / len(cuts)))
        gain = gain * jnp.repeat(heights, shape[dim] // blocks).reshape([-1 if axis == dim else 1 for axis in range(len(shape))])
    return gain


def length_profile(count, total, most, slope):
    loads = [(1 << 20) // math.isqrt(standing ** slope) + 1 for standing in range(2, count + 1)]
    surplus, holding = total - most - (count - 1), [1] * (count - 1)
    while surplus > 0:
        movable = [i for i in range(count - 1) if holding[i] < most]
        mass, budget = sum([loads[i] for i in movable]), surplus
        for i in movable:
            more = min(most - holding[i], max(1, budget * loads[i] // mass), surplus)
            holding[i] = holding[i] + more
            surplus = surplus - more
    return np.array([most] + holding)


def uneven(stream_key, count, total, reach, lean):
    if count == 2:
        one = jax.random.randint(stream_key, (), max(1, total - reach), min(reach, total - 1) + 1)
        return jnp.stack([one, total - one])
    sizes = jnp.asarray(length_profile(count, total, reach, lean), jnp.int32)
    couples = (count - 1) // 2
    donor, taker = sizes[1:1 + 2 * couples:2], sizes[2:2 + 2 * couples:2]
    room = jnp.minimum(donor - 1, reach - taker)
    moved = jax.random.randint(jax.random.fold_in(stream_key, 1), (couples,), 0, 1 << 20) % (room + 1)
    sizes = sizes.at[1:1 + 2 * couples:2].set(donor - moved).at[2:2 + 2 * couples:2].set(taker + moved)
    return sizes[jax.random.permutation(jax.random.fold_in(stream_key, 2), count)]


def scatter_about(key, dims, scale, bound, cuts=(), held_as=jnp.bfloat16):
    drawn = jax.random.normal(key, dims, jnp.float32) * scale
    if len(cuts) > 0:
        drawn = level_of(key, dims, cuts, -0.22, 0.18) * drawn
    return jnp.clip(drawn, min=-bound, max=bound).astype(held_as)


def setup_inputs(seed: int = 0, part: int = 0) -> dict:
    arg_keys = jax.random.split(jax.random.key(seed), 8)
    own_keys = jax.random.split(jax.random.fold_in(arg_keys[7], part), 8)
    spectra = scatter_about(own_keys[0], (WINS, 2, CHANNELS, NF), 1.0, 6.0, ((0, 2), (2, 4), (3, 2)))
    window_keep = draw_window_keep(jax.random.fold_in(jax.random.fold_in(arg_keys[7], part), 71), part)
    owners = draw_owners(jax.random.fold_in(jax.random.fold_in(arg_keys[7], part), 71), part)
    pair_src = set_ends(jax.random.randint(own_keys[3], (BLOCKS, N_RECV * PAIRS), 0, CH_DEV), jax.random.fold_in(own_keys[3], 1), 0, CH_DEV - 1).astype(jnp.int32)
    pair_rec = set_ends(jax.random.randint(own_keys[4], (BLOCKS, N_RECV * PAIRS), 0, CH_DEV), jax.random.fold_in(own_keys[4], 1), 0, CH_DEV - 1).astype(jnp.int32)
    pair_count = jax.vmap(lambda own: uneven(own, N_RECV, PAIRS * N_RECV // 2, PAIRS, 2))(jax.random.split(own_keys[5], BLOCKS)).reshape((BLOCKS, N_RECV)).astype(jnp.int32)
    observed = scatter_about(own_keys[6], (BLOCKS, N_RECV * PAIRS, LAGS), 1.0, 6.0, ((1, 4), (2, 4)), jnp.float32)
    return dict(spectra=spectra, window_keep=window_keep, owners=owners, pair_src=pair_src, pair_rec=pair_rec, pair_count=pair_count, observed=observed)


EPSILON = 1e-06

def dft_table(first_bin, bin_count, bin_total, lag_total):
    frequency = first_bin + jnp.arange(bin_count, dtype=jnp.int32)
    shifts = jnp.arange(lag_total, dtype=jnp.int32) - lag_total // 2
    period = 2 * bin_total
    phase_index = frequency[:, None] * shifts[None, :] % period
    angles = phase_index.astype(jnp.float32) * (2.0 * math.pi / period)
    return jnp.concatenate([jnp.cos(angles), -jnp.sin(angles)], axis=0).astype(jnp.bfloat16)

def reference(spectra, window_keep, owners, pair_src, pair_rec, pair_count, observed):
    kept_weight = window_keep.astype(jnp.float32)
    cosine_table = dft_table(0, NF, NF, LAGS)
    lag_scale = 1.0 / math.sqrt(NF * WINS)
    slot_index = jnp.arange(N_RECV * PAIRS, dtype=jnp.int32)
    device_index = slot_index // PAIRS
    local_index = slot_index % PAIRS
    channel_ids = jnp.arange(CH_DEV, dtype=jnp.int32)
    adjoint = jnp.zeros((CHANNELS, LAGS), jnp.float32)
    results = []
    for block_index in range(BLOCKS):
        owner_row = owners[block_index]
        src_rows = owner_row * CH_DEV + pair_src[block_index]
        rec_rows = device_index * CH_DEV + pair_rec[block_index]
        valid_slots = (local_index < pair_count[block_index][device_index]).astype(jnp.float32)
        source = jnp.take(spectra, src_rows, axis=2).astype(jnp.float32)
        receiver = jnp.take(spectra, rec_rows, axis=2).astype(jnp.float32)
        real_part = source[:, 0] * receiver[:, 0] + source[:, 1] * receiver[:, 1]
        imag_part = source[:, 1] * receiver[:, 0] - source[:, 0] * receiver[:, 1]
        cross = jnp.concatenate([real_part, imag_part], axis=-1).astype(jnp.bfloat16)
        summed_terms = jnp.zeros((N_RECV * PAIRS, LAGS), jnp.float32)
        for window in range(WINS):
            summed_terms = summed_terms + kept_weight[window] * jnp.dot(cross[window], cosine_table, preferred_element_type=jnp.float32)
        corr = summed_terms * lag_scale * valid_slots[:, None]
        target = observed[block_index]
        square = lax.optimization_barrier(jnp.sum(corr * corr, axis=1))
        product = lax.optimization_barrier(jnp.sum(corr * target, axis=1))
        scale_norm = jnp.sqrt(square / LAGS + EPSILON)
        normed = corr / scale_norm[:, None]
        bending = (square / (scale_norm * scale_norm) - product / scale_norm) / LAGS
        gradient = valid_slots[:, None] * (normed - target - normed * bending[:, None]) / scale_norm[:, None]
        selector = (pair_src[block_index][:, None] == channel_ids[None, :]).astype(jnp.float32)
        returned = jnp.dot(selector.T, gradient, precision=lax.Precision.HIGHEST)
        adjoint = lax.dynamic_update_slice(adjoint, returned, ((owner_row * CH_DEV).astype(jnp.int32), jnp.int32(0)))
        results.append(normed)
    return (jnp.stack(results), adjoint)
```

```python
import functools
import math

import jax
import jax.numpy as jnp
import ml_dtypes
import numpy as np
from jax import lax
from jax.experimental import pallas as pl
from jax.experimental.pallas import tpu as pltpu
from jax.sharding import PartitionSpec as P

EPSILON = 1e-06
MIB = 1 << 20
LANES = 128
BF16 = jnp.bfloat16
F32 = jnp.float32


def shifted(value, axis, size, shift):
    if shift % size == 0:
        return value
    return lax.ppermute(value, axis, [(i, (i + shift) % size) for i in range(size)])


def table_kernel(row_cos, row_sin, base_cos, base_sin, table):
    ca, sa = row_cos[0], row_sin[0]
    cb, sb = base_cos[...], base_sin[...]
    table[0, :LANES] = (ca * cb - sa * sb).astype(BF16)
    table[0, LANES:] = (-(sa * cb + ca * sb)).astype(BF16)


def make_table(first_bin, classes, span, period):
    m = np.arange(LANES, dtype=np.int64)[:, None]
    u = np.arange(span, dtype=np.int64)[None, :]
    base = (classes * m * u % period) * (2.0 * math.pi / period)
    base_cos, base_sin = np.cos(base).astype(np.float32), np.sin(base).astype(np.float32)
    frequency = first_bin + jnp.arange(classes, dtype=jnp.int32)
    turns = frequency[:, None] * jnp.arange(span, dtype=jnp.int32)[None, :] % period
    angles = turns.astype(F32) * (2.0 * math.pi / period)
    row_cos, row_sin = jnp.cos(angles)[:, None, :], jnp.sin(angles)[:, None, :]
    row = pl.BlockSpec((1, 1, span), lambda r: (r, 0, 0))
    whole = pl.BlockSpec((LANES, span), lambda r: (0, 0))
    return pl.pallas_call(
        table_kernel,
        grid=(classes,),
        out_shape=jax.ShapeDtypeStruct((classes, 2 * LANES, span), BF16),
        in_specs=[row, row, whole, whole],
        out_specs=pl.BlockSpec((1, 2 * LANES, span), lambda r: (r, 0, 0)),
        compiler_params=pltpu.CompilerParams(vmem_limit_bytes=16 * MIB),
        cost_estimate=pl.CostEstimate(
            flops=6 * classes * LANES * span, bytes_accessed=6 * MIB, transcendentals=0
        ),
        name="table",
    )(row_cos, row_sin, jnp.asarray(base_cos), jnp.asarray(base_sin))


def rows_kernel(used, shifts, order, *refs):
    held, (perm, pick_src, pick_rec), outs = refs[:shifts], refs[shifts : shifts + 3], refs[shifts + 3 :]
    slots = outs[0].shape[2]
    blocks = outs[-1].shape[0]
    for u in range(used):
        for half in range(2):
            x = held[0][half]
            for s in range(1, shifts):
                x = jnp.where(order[u] == s, held[s][half], x)
            x = jnp.dot(x, perm[...], preferred_element_type=F32).astype(BF16)
            sent = jnp.dot(pick_src[...], x, preferred_element_type=F32).astype(BF16)
            for d, out in enumerate(outs[:-1]):
                out[u, half] = sent[d * slots : (d + 1) * slots]
            own = jnp.dot(pick_rec[...], x, preferred_element_type=F32).astype(BF16)
            for b in range(blocks):
                outs[-1][b, u, half] = own[b * slots : (b + 1) * slots]


def gather_rows(order, held, classes, pick_src, pick_rec, slots):
    shifts, used = len(held), order.shape[0]
    part = held[0].shape[-1]
    source = np.arange(part)
    perm = np.zeros((part, part), ml_dtypes.bfloat16)
    perm[source, source % classes * LANES + source // classes] = 1
    sends, blocks = pick_src.shape[0] // slots, pick_rec.shape[0] // slots
    sent = jax.ShapeDtypeStruct((used, 2, slots, part), BF16)
    own = jax.ShapeDtypeStruct((blocks, used, 2, slots, part), BF16)
    vmem = pl.BlockSpec(memory_space=pltpu.VMEM)
    return pl.pallas_call(
        functools.partial(rows_kernel, used, shifts),
        out_shape=[sent] * sends + [own],
        in_specs=[pl.BlockSpec(memory_space=pltpu.SMEM)] + [vmem] * (shifts + 3),
        out_specs=[vmem] * (sends + 1),
        compiler_params=pltpu.CompilerParams(vmem_limit_bytes=32 * MIB),
        cost_estimate=pl.CostEstimate(
            flops=4 * used * part * (128 * part + 512 * 128), bytes_accessed=8 * MIB, transcendentals=0
        ),
        name="rows",
    )(order, *held, jnp.asarray(perm), pick_src, pick_rec)


def combine(values, classes, outputs, origin, span, period):
    plain, scaled = [None] * outputs, [None] * outputs

    def add(into, k, value, sign):
        if into[k] is None:
            into[k] = value if sign > 0 else -value
        else:
            into[k] = into[k] + value if sign > 0 else into[k] - value

    for r, (real, imag) in enumerate(values):
        both = None
        for k in range(outputs):
            eighths = r * (span * k - origin) * 8 // period % 8
            assert r * (span * k - origin) * 8 % period == 0
            if eighths % 2 == 0:
                value, sign = ((real, 1), (imag, -1), (real, -1), (imag, 1))[eighths // 2]
                add(plain, k, value, sign)
            else:
                if both is None:
                    both = real + imag, real - imag
                value, sign = ((both[1], 1), (both[0], -1), (both[1], -1), (both[0], 1))[eighths // 2]
                add(scaled, k, value, sign)
    root = math.sqrt(0.5)
    return [a if b is None else a + root * b for a, b in zip(plain, scaled)]


def lags_kernel(geometry, place, weight, s_ref, r_ref, table, keep, send, lhs):
    classes, span, outputs, origin, period, chunk = geometry
    used, _, slots, _ = s_ref.shape
    lag_dev = keep.shape[-1]
    cores = 2
    for r in range(classes):
        bins = slice(r * LANES, (r + 1) * LANES)
        real = imag = None
        for u in range(used):
            sr, si = s_ref[u, 0, :, bins].astype(F32), s_ref[u, 1, :, bins].astype(F32)
            rr, ri = r_ref[0, u, 0, :, bins].astype(F32), r_ref[0, u, 1, :, bins].astype(F32)
            re, im = sr * rr + si * ri, si * rr - sr * ri
            if u:
                re, im = real + weight[u] * re, imag + weight[u] * im
            real, imag = re, im
        lhs[r, :slots, :LANES] = real.astype(BF16)
        lhs[r, :slots, LANES:] = imag.astype(BF16)
        lhs[r, slots:, :LANES] = imag.astype(BF16)
        lhs[r, slots:, LANES:] = (-real).astype(BF16)
    first = place[1] == 0
    for start in range(0, span, chunk):
        values = []
        for r in range(classes):
            y = jnp.dot(lhs[r], table[r, :, start : start + chunk], preferred_element_type=F32)
            values.append((y[:slots], y[slots:]))
        pieces = {}
        for k, value in enumerate(combine(values, classes, outputs, origin, span, period)):
            lag = span * k + start
            pieces[lag // (cores * lag_dev), lag // lag_dev % cores, lag % lag_dev] = value
        for (column, core, offset), value in pieces.items():
            lags = slice(offset, offset + chunk)

            @pl.when(place[1] == core)
            def _():
                keep[column, :, lags] = value

            @pl.when(place[1] != core)
            def _():
                send[column, :, lags] = value


def lag_parts(block, core, weight, rows, own, table, geometry, columns, lag_dev):
    classes, span, outputs, origin, period, chunk = geometry
    used, _, slots, part = rows.shape
    out = jax.ShapeDtypeStruct((columns, slots, lag_dev), F32)
    whole = lambda shape: pl.BlockSpec(shape, lambda i, place, weight: (0,) * len(shape))
    grid_spec = pltpu.PrefetchScalarGridSpec(
        num_scalar_prefetch=2,
        grid=(1,),
        in_specs=[
            whole(rows.shape),
            pl.BlockSpec((1,) + own.shape[1:], lambda i, place, weight: (place[0], 0, 0, 0, 0)),
            whole(table.shape),
        ],
        out_specs=[whole(out.shape)] * 2,
        scratch_shapes=[pltpu.VMEM((classes, 2 * slots, 2 * LANES), BF16)],
    )
    return pl.pallas_call(
        functools.partial(lags_kernel, geometry),
        grid_spec=grid_spec,
        out_shape=[out] * 2,
        compiler_params=pltpu.CompilerParams(vmem_limit_bytes=32 * MIB),
        cost_estimate=pl.CostEstimate(
            flops=8 * slots * part * span, bytes_accessed=8 * MIB, transcendentals=0
        ),
        name="lags",
    )(jnp.stack([block, core]).astype(jnp.int32), weight, rows, own, table)


def shards(spectra, window_keep, owners, pair_src, pair_rec, pair_count, observed):
    columns, cores, places = lax.axis_size("win"), lax.axis_size("freq"), lax.axis_size("recv")
    column, core, place = lax.axis_index("win"), lax.axis_index("freq"), lax.axis_index("recv")
    assert spectra.shape[0] == 1 and cores == 2
    channels, bins_dev = spectra.shape[2:]
    blocks, slots, lag_dev = observed.shape
    lag_total = lag_dev * columns * cores
    bin_total = bins_dev * cores
    period = 2 * bin_total
    part = bins_dev // columns
    classes = part // LANES
    span = period // classes
    geometry = (classes, span, lag_total // span, lag_total // 2, period, 256)
    lag_scale = 1.0 / math.sqrt(bin_total * columns)
    peers = columns * cores

    held = [
        shifted(
            lax.dynamic_slice(
                spectra[0], (0, 0, (column + s) % columns * part), (2, channels, part)
            ),
            "win",
            columns,
            s,
        )
        for s in range(columns)
    ]
    kept = window_keep[0]
    if columns == 2:
        order = (1 - kept)[None]
        weight = jnp.ones((1,), F32)
    else:
        keeps = jnp.stack([shifted(kept, "win", columns, s) for s in range(columns)])
        order = jnp.argsort(-keeps)[: columns - 1].astype(jnp.int32)
        weight = keeps[order].astype(F32)

    shifts = range(places)
    owns = [owners == (place - d) % places for d in shifts]
    unit_block = [jnp.argmax(o).astype(jnp.int32) for o in owns]
    wanted = [
        jnp.where(jnp.any(o), lax.dynamic_index_in_dim(pair_src, b, 0, False), -1)
        for o, b in zip(owns, unit_block)
    ]
    wanted = jnp.concatenate([shifted(x, "recv", places, -d) for d, x in zip(shifts, wanted)])
    channel_ids = jnp.arange(channels, dtype=jnp.int32)[None, :]
    pick_src = (wanted[:, None] == channel_ids).astype(BF16)
    pick_rec = (pair_rec.reshape(-1)[:, None] == channel_ids).astype(BF16)

    table = make_table(core * bins_dev + column * part, classes, span, period)
    *sent, own_rows = gather_rows(order, held, classes, pick_src, pick_rec, slots)
    arrived = [shifted(x, "recv", places, d) for d, x in zip(shifts, sent)]
    if places == blocks:
        units = list(zip(unit_block, arrived))
    else:
        stacked = jnp.stack(arrived)
        units = [
            (
                jnp.int32(b),
                lax.dynamic_index_in_dim(stacked, (place - owners[b]) % places, 0, False),
            )
            for b in range(blocks)
        ]

    def summed_lags(block, rows):
        keep, send = lag_parts(
            block, core, weight, rows, own_rows, table, geometry, columns, lag_dev
        )
        half = keep + shifted(send, "freq", cores, 1)
        total = lax.dynamic_index_in_dim(half, column, 0, False)
        for s in range(1, columns):
            out = lax.dynamic_index_in_dim(half, (column + s) % columns, 0, False)
            total = total + shifted(out.astype(BF16), "win", columns, s).astype(F32)
        return total

    normed = jnp.zeros_like(observed)
    gradients = []
    for block, rows in units:
        count = lax.dynamic_index_in_dim(pair_count, block, 0, False)
        valid = (jnp.arange(slots, dtype=jnp.int32) < count).astype(F32)[:, None]
        target = lax.dynamic_index_in_dim(observed, block, 0, False)
        corr = summed_lags(block, rows) * (lag_scale * valid)
        sums = jnp.stack([jnp.sum(corr * corr, axis=1), jnp.sum(corr * target, axis=1)])
        total = sums
        for s in range(1, peers):
            total = total + shifted(sums, ("win", "freq"), peers, s)
        square, product = total[0][:, None], total[1][:, None]
        scale_norm = jnp.sqrt(square / lag_total + EPSILON)
        unit_normed = corr / scale_norm
        bending = (square / (scale_norm * scale_norm) - product / scale_norm) / lag_total
        gradient = valid * (unit_normed - target - unit_normed * bending) / scale_norm
        gradients.append(gradient.astype(BF16))
        normed = lax.dynamic_update_slice(normed, unit_normed[None], (block, 0, 0))
    if places != blocks:
        stacked_gradients = jnp.stack(gradients)
        gradients = [
            lax.dynamic_index_in_dim(stacked_gradients, b, 0, False) for b in unit_block
        ]
    returned = jnp.concatenate([shifted(g, "recv", places, -d) for d, g in zip(shifts, gradients)])
    adjoint = lax.dot_general(
        pick_src, returned, (((0,), (0,)), ((), ())), preferred_element_type=F32
    )
    return (normed, adjoint)


def solution(mesh):
    return jax.shard_map(
        shards,
        mesh=mesh,
        in_specs=(
            P("win", None, ("groups", "recv"), "freq"),
            P(("groups", "win")),
            P("groups"),
            P(None, ("groups", "recv")),
            P(None, ("groups", "recv")),
            P(None, ("groups", "recv")),
            P(None, ("groups", "recv"), ("win", "freq")),
        ),
        out_specs=(
            P(None, ("groups", "recv"), ("win", "freq")),
            P(("groups", "recv"), ("win", "freq")),
        ),
        check_vma=False,
    )
```

```python
import functools
import math

import jax
import jax.numpy as jnp
import ml_dtypes
import numpy as np
from jax import lax
from jax.experimental import pallas as pl
from jax.experimental.pallas import tpu as pltpu
from jax.sharding import PartitionSpec as P

EPSILON = 1e-06
MIB = 1 << 20
LANES = 128
CHUNKS = 2
CORE, COLUMN, ORDER, BLOCK, COUNT = 0, 1, 2, 8, 16
BF16 = jnp.bfloat16
F32 = jnp.float32
VMEM = pl.BlockSpec(memory_space=pltpu.VMEM)
SMEM = pl.BlockSpec(memory_space=pltpu.SMEM)


def shifted(value, axis, size, shift):
    if shift % size == 0:
        return value
    return lax.ppermute(value, axis, [(i, (i + shift) % size) for i in range(size)])


def params(mib):
    return pltpu.CompilerParams(vmem_limit_bytes=mib * MIB)


def cost(flops, mib):
    return pl.CostEstimate(flops=int(flops), bytes_accessed=int(mib * MIB), transcendentals=0)


def table_kernel(row_cos, row_sin, base_cos, base_sin, table):
    ca, sa = row_cos[0], row_sin[0]
    cb, sb = base_cos[...], base_sin[...]
    table[0, :LANES] = (ca * cb - sa * sb).astype(BF16)
    table[0, LANES:] = (-(sa * cb + ca * sb)).astype(BF16)


def make_table(first_bin, classes, span, period):
    m = np.arange(LANES, dtype=np.int64)[:, None]
    u = np.arange(span, dtype=np.int64)[None, :]
    base = (classes * m * u % period) * (2.0 * math.pi / period)
    base_cos, base_sin = np.cos(base).astype(np.float32), np.sin(base).astype(np.float32)
    frequency = first_bin + jnp.arange(classes, dtype=jnp.int32)
    turns = frequency[:, None] * jnp.arange(span, dtype=jnp.int32)[None, :] % period
    angles = turns.astype(F32) * (2.0 * math.pi / period)
    row_cos, row_sin = jnp.cos(angles)[:, None, :], jnp.sin(angles)[:, None, :]
    row = pl.BlockSpec((1, 1, span), lambda r: (r, 0, 0))
    whole = pl.BlockSpec((LANES, span), lambda r: (0, 0))
    return pl.pallas_call(
        table_kernel,
        grid=(classes,),
        out_shape=jax.ShapeDtypeStruct((classes, 2 * LANES, span), BF16),
        in_specs=[row, row, whole, whole],
        out_specs=pl.BlockSpec((1, 2 * LANES, span), lambda r: (r, 0, 0)),
        compiler_params=params(16),
        cost_estimate=cost(6 * classes * LANES * span, 6),
        name="table",
    )(row_cos, row_sin, jnp.asarray(base_cos), jnp.asarray(base_sin))


def picks(ids, channels):
    row = jnp.concatenate([i[...] for i in ids], axis=1)
    return (lax.broadcasted_iota(jnp.int32, (channels, row.shape[1]), 0) == row).astype(BF16)


def rows_kernel(used, sends, scal, *refs):
    shifts = used + 1
    held, refs = refs[:shifts], refs[shifts:]
    perm, src_ids, rec_ids, outs = refs[0], refs[1 : 1 + sends], refs[1 + sends], refs[2 + sends :]
    rows_out, own_out = outs[: sends * CHUNKS], outs[sends * CHUNKS :]
    units, _, _, slots, _ = own_out[0].shape
    channels = held[0].shape[1]
    pick = picks(
        list(src_ids) + [rec_ids.at[d : d + 1] for d in range(units)], channels
    )
    for u in range(used):
        for half in range(2):
            x = held[0][half]
            for s in range(1, shifts):
                x = jnp.where(scal[ORDER + u] == s, held[s][half], x)
            x = jnp.dot(x, perm[...], preferred_element_type=F32).astype(BF16)
            y = lax.dot_general(
                pick, x, (((0,), (0,)), ((), ())), preferred_element_type=F32
            ).astype(BF16)
            for i, out in enumerate(rows_out):
                out[u, half] = y[i * slots : (i + 1) * slots]
            y = y[sends * CHUNKS * slots :]
            for d in range(units):
                for q, out in enumerate(own_out):
                    first = (d * CHUNKS + q) * slots
                    out[d, u, half] = y[first : first + slots]


def gather_rows(scal, held, classes, src_ids, rec_ids, units, slots):
    used, sends = len(held) - 1, len(src_ids)
    part = held[0].shape[-1]
    source = np.arange(part)
    perm = np.zeros((part, part), ml_dtypes.bfloat16)
    perm[source, source % classes * LANES + source // classes] = 1
    sent = jax.ShapeDtypeStruct((used, 2, slots, part), BF16)
    own = jax.ShapeDtypeStruct((units, used, 2, slots, part), BF16)
    outs = pl.pallas_call(
        functools.partial(rows_kernel, used, sends),
        out_shape=[sent] * (sends * CHUNKS) + [own] * CHUNKS,
        in_specs=[SMEM] + [VMEM] * (len(held) + 2 + sends),
        out_specs=[VMEM] * ((sends + 1) * CHUNKS),
        compiler_params=params(32),
        cost_estimate=cost(4 * used * part * (128 * part + 512 * 128), 6),
        name="rows",
    )(scal, *held, jnp.asarray(perm), *src_ids, rec_ids)
    sends_of = [outs[q : sends * CHUNKS : CHUNKS] for q in range(CHUNKS)]
    return sends_of, outs[sends * CHUNKS :]


def combine(values, classes, outputs, origin, span, period):
    plain, scaled = [None] * outputs, [None] * outputs

    def add(into, k, value, sign):
        if into[k] is None:
            into[k] = value if sign > 0 else -value
        else:
            into[k] = into[k] + value if sign > 0 else into[k] - value

    for r, (real, imag) in enumerate(values):
        both = None
        for k in range(outputs):
            eighths = r * (span * k - origin) * 8 // period % 8
            assert r * (span * k - origin) * 8 % period == 0
            if eighths % 2 == 0:
                value, sign = ((real, 1), (imag, -1), (real, -1), (imag, 1))[eighths // 2]
                add(plain, k, value, sign)
            else:
                if both is None:
                    both = real + imag, real - imag
                value, sign = ((both[1], 1), (both[0], -1), (both[1], -1), (both[0], 1))[eighths // 2]
                add(scaled, k, value, sign)
    root = math.sqrt(0.5)
    return [a if b is None else a + root * b for a, b in zip(plain, scaled)]


def lags_kernel(geometry, units, scal, weight, *refs):
    classes, span, outputs, origin, period, chunk = geometry
    s_refs, (r_ref, table, keep, send, lhs) = refs[:units], refs[units:]
    used, _, slots, _ = s_refs[0].shape
    rows = units * slots
    lag_dev = keep.shape[-1]
    cores = 2
    for d in range(units):
        at = slice(d * slots, (d + 1) * slots)
        turned = slice(rows + d * slots, rows + (d + 1) * slots)
        for r in range(classes):
            bins = slice(r * LANES, (r + 1) * LANES)
            real = imag = None
            for u in range(used):
                sr, si = s_refs[d][u, 0, :, bins].astype(F32), s_refs[d][u, 1, :, bins].astype(F32)
                rr, ri = r_ref[d, u, 0, :, bins].astype(F32), r_ref[d, u, 1, :, bins].astype(F32)
                re, im = sr * rr + si * ri, si * rr - sr * ri
                if u:
                    re, im = real + weight[u] * re, imag + weight[u] * im
                real, imag = re, im
            lhs[r, at, :LANES] = real.astype(BF16)
            lhs[r, at, LANES:] = imag.astype(BF16)
            lhs[r, turned, :LANES] = imag.astype(BF16)
            lhs[r, turned, LANES:] = (-real).astype(BF16)
    for start in range(0, span, chunk):
        values = []
        for r in range(classes):
            y = jnp.dot(lhs[r], table[r, :, start : start + chunk], preferred_element_type=F32)
            values.append((y[:rows], y[rows:]))
        for k, value in enumerate(combine(values, classes, outputs, origin, span, period)):
            lag = span * k + start
            column, core, offset = lag // (cores * lag_dev), lag // lag_dev % cores, lag % lag_dev
            lags = slice(offset, offset + chunk)

            @pl.when(scal[CORE] == core)
            def _():
                keep[column, :, lags] = value

            @pl.when(scal[CORE] != core)
            def _():
                send[column, :, lags] = value


def lag_parts(scal, weight, rows, own, table, geometry, columns, lag_dev):
    classes, span = geometry[:2]
    units = len(rows)
    used, _, slots, part = rows[0].shape
    out = jax.ShapeDtypeStruct((columns, units * slots, lag_dev), F32)
    return pl.pallas_call(
        functools.partial(lags_kernel, geometry, units),
        out_shape=[out] * 2,
        in_specs=[SMEM, SMEM] + [VMEM] * (units + 2),
        out_specs=[VMEM] * 2,
        scratch_shapes=[pltpu.VMEM((classes, 2 * units * slots, 2 * LANES), BF16)],
        compiler_params=params(32),
        cost_estimate=cost(8 * units * slots * part * span, 8),
        name="lags",
    )(scal, weight, *rows, own, table)


def stats_kernel(scale, chunk, units, others, scal, *refs):
    own, more, refs = refs[0], refs[1 : 1 + others], refs[1 + others :]
    targets, (corr, sums) = refs[:units], refs[units:]
    slots = targets[0].shape[1]
    columns = []
    for d in range(units):
        at = slice(d * slots, (d + 1) * slots)
        value = own[at]
        for m in more:
            value = value + m[at].astype(F32)
        slot = chunk * slots + lax.broadcasted_iota(jnp.int32, (slots, 1), 0)
        value = value * jnp.where(slot < scal[COUNT + d], scale, 0.0)
        corr[at] = value
        square = jnp.sum(value * value, axis=1, keepdims=True)
        product = jnp.sum(value * targets[d][0], axis=1, keepdims=True)
        lane = lax.broadcasted_iota(jnp.int32, (slots, LANES), 1)
        columns.append(jnp.where(lane == 0, square, jnp.where(lane == 1, product, 0.0)))
    sums[...] = jnp.concatenate(columns, axis=0).T[:8]


def target_specs(chunk, units, slots, lag_dev):
    return [
        pl.BlockSpec((1, slots, lag_dev), lambda i, scal, d=d: (scal[BLOCK + d], chunk, 0))
        for d in range(units)
    ]


def whole(shape):
    return pl.BlockSpec(shape, lambda i, scal: (0,) * len(shape))


def lag_stats(scal, scale, chunk, own, more, observed, units, slots):
    rows, lag_dev = own.shape
    outs = [jax.ShapeDtypeStruct((rows, lag_dev), F32), jax.ShapeDtypeStruct((8, rows), F32)]
    return pl.pallas_call(
        functools.partial(stats_kernel, scale, chunk, units, len(more)),
        grid_spec=pltpu.PrefetchScalarGridSpec(
            num_scalar_prefetch=1,
            grid=(1,),
            in_specs=[whole(own.shape)] * (1 + len(more))
            + target_specs(chunk, units, slots, lag_dev),
            out_specs=[whole(o.shape) for o in outs],
        ),
        out_shape=outs,
        compiler_params=params(16),
        cost_estimate=cost(8 * rows * lag_dev, 2),
        name="stats",
    )(scal, own, *more, *[observed] * units)


def slot_scales(sums, lag_total):
    total = sums[0][...]
    for s in sums[1:]:
        total = total + s[...]
    rows = total.shape[1]
    square, product = total[0:1], total[1:2]
    inverse = 1.0 / jnp.sqrt(square / lag_total + EPSILON)
    bending = (square * inverse * inverse - product * inverse) / lag_total
    sub = lax.broadcasted_iota(jnp.int32, (LANES, rows), 0)
    both = jnp.where(sub == 0, inverse, jnp.where(sub == 1, bending, 0.0)).T
    return both[:, 0:1], both[:, 1:2]


def gradient_kernel(lag_total, chunk, units, parts, scal, *refs):
    sums, corr, refs = refs[:parts], refs[parts], refs[parts + 1 :]
    targets, outs = refs[:units], refs[units:]
    slots = targets[0].shape[1]
    inverse, bending = slot_scales(sums, lag_total)
    for d in range(units):
        at = slice(d * slots, (d + 1) * slots)
        slot = chunk * slots + lax.broadcasted_iota(jnp.int32, (slots, 1), 0)
        valid = jnp.where(slot < scal[COUNT + d], inverse[at], 0.0)
        normed = corr[at] * inverse[at]
        gradient = (normed - targets[d][0] - normed * bending[at]) * valid
        outs[d][...] = gradient.astype(BF16)


def gradients(scal, lag_total, chunk, sums, corr, observed, units, slots):
    rows, lag_dev = corr.shape
    out = jax.ShapeDtypeStruct((slots, lag_dev), BF16)
    return pl.pallas_call(
        functools.partial(gradient_kernel, lag_total, chunk, units, len(sums)),
        grid_spec=pltpu.PrefetchScalarGridSpec(
            num_scalar_prefetch=1,
            grid=(1,),
            in_specs=[whole(sums[0].shape)] * len(sums)
            + [whole(corr.shape)]
            + target_specs(chunk, units, slots, lag_dev),
            out_specs=[whole(out.shape)] * units,
        ),
        out_shape=[out] * units,
        compiler_params=params(16),
        cost_estimate=cost(8 * rows * lag_dev, 1),
        name="gradient",
    )(scal, *sums, corr, *[observed] * units)


def normed_kernel(lag_total, parts, scal, *refs):
    out = refs[-1]
    slots = out.shape[1] // CHUNKS
    d = pl.program_id(0)
    for q in range(CHUNKS):
        sums, corr = refs[q * (parts + 1) : q * (parts + 1) + parts], refs[q * (parts + 1) + parts]
        inverse, _ = slot_scales(sums, lag_total)
        mine = inverse[0:slots]
        for i in range(1, inverse.shape[0] // slots):
            mine = jnp.where(d == i, inverse[i * slots : (i + 1) * slots], mine)
        out[0, q * slots : (q + 1) * slots] = corr[...] * mine


def normed_rows(scal, lag_total, sums, corr, observed, units, slots):
    lag_dev = corr[0].shape[1]
    ins, specs = [], []
    for s, c in zip(sums, corr):
        ins += [*s, c]
        specs += [whole(s[0].shape)] * len(s)
        specs += [pl.BlockSpec((slots, lag_dev), lambda i, scal: (i, 0))]
    return pl.pallas_call(
        functools.partial(normed_kernel, lag_total, len(sums[0])),
        grid_spec=pltpu.PrefetchScalarGridSpec(
            num_scalar_prefetch=1,
            grid=(units,),
            in_specs=specs,
            out_specs=pl.BlockSpec(
                (1, CHUNKS * slots, lag_dev), lambda i, scal: (scal[BLOCK + i], 0, 0)
            ),
        ),
        out_shape=jax.ShapeDtypeStruct(observed.shape, F32),
        compiler_params=params(16),
        cost_estimate=cost(2 * observed.size, 2),
        name="normed",
    )(scal, *ins)


def adjoint_kernel(sends, *refs):
    ids, parts, out = refs[:sends], refs[sends:-1], refs[-1]
    pick = picks(ids, out.shape[0])
    rows = jnp.concatenate([p[...] for p in parts], axis=0)
    out[...] = jnp.dot(pick, rows, preferred_element_type=F32)


def adjoint_rows(src_ids, parts, channels):
    lag_dev = parts[0].shape[1]
    return pl.pallas_call(
        functools.partial(adjoint_kernel, len(src_ids)),
        out_shape=jax.ShapeDtypeStruct((channels, lag_dev), F32),
        in_specs=[VMEM] * (len(src_ids) + len(parts)),
        out_specs=VMEM,
        compiler_params=params(16),
        cost_estimate=cost(2 * channels * lag_dev * 256, 1),
        name="adjoint",
    )(*src_ids, *parts)


def shards(spectra, window_keep, owners, pair_src, pair_rec, pair_count, observed):
    columns, cores, places = lax.axis_size("win"), lax.axis_size("freq"), lax.axis_size("recv")
    column, core, place = lax.axis_index("win"), lax.axis_index("freq"), lax.axis_index("recv")
    assert spectra.shape[0] == 1 and cores == 2
    channels, bins_dev = spectra.shape[2:]
    blocks, slots, lag_dev = observed.shape
    lag_total = lag_dev * columns * cores
    bin_total = bins_dev * cores
    period = 2 * bin_total
    part = bins_dev // columns
    classes = part // LANES
    span = period // classes
    geometry = (classes, span, lag_total // span, lag_total // 2, period, 256)
    lag_scale = 1.0 / math.sqrt(bin_total * columns)
    peers = columns * cores
    some = slots // CHUNKS
    shifts = range(places)

    held = [
        shifted(
            lax.dynamic_slice(
                spectra[0], (0, 0, (column + s) % columns * part), (2, channels, part)
            ),
            "win",
            columns,
            s,
        )
        for s in range(columns)
    ]
    kept = window_keep[0]
    if columns == 2:
        order = [1 - kept]
        weight = jnp.ones((1,), F32)
    else:
        keeps = jnp.stack([shifted(kept, "win", columns, s) for s in range(columns)])
        ranked = jnp.argsort(-keeps)[: columns - 1].astype(jnp.int32)
        order = [ranked[u] for u in range(columns - 1)]
        weight = keeps[ranked].astype(F32)

    direct = places == blocks
    lane = jnp.arange(LANES, dtype=jnp.int32)
    scal = jnp.where(lane == CORE, core, jnp.where(lane == COLUMN, column, 0))
    for u, o in enumerate(order):
        scal = jnp.where(lane == ORDER + u, o, scal)
    for b in range(blocks):
        unit = (place - owners[b]) % places if direct else b
        scal = jnp.where(lane == BLOCK + unit, b, scal)
        scal = jnp.where(lane == COUNT + unit, pair_count[b, 0], scal)

    def rows_of(ids, d):
        chosen = jnp.full((1, slots), -1, jnp.int32)
        for b in range(blocks):
            chosen = jnp.where(owners[b] == (place - d) % places, ids[b : b + 1], chosen)
        return chosen

    src_ids = [shifted(rows_of(pair_src, d), "recv", places, -d) for d in shifts]
    if direct:
        rec_ids = jnp.concatenate([rows_of(pair_rec, d) for d in shifts], axis=0)
    else:
        rec_ids = pair_rec

    table = make_table(core * bins_dev + column * part, classes, span, period)
    sends, own_rows = gather_rows(scal, held, classes, src_ids, rec_ids, blocks, some)
    corrs, all_sums, returned = [], [], [[] for _ in shifts]
    arrived = [[shifted(x, "recv", places, d) for d, x in zip(shifts, sent)] for sent in sends]
    for q in range(CHUNKS):
        rows = arrived[q]
        if not direct:
            stacked = jnp.stack(rows)
            rows = [
                lax.dynamic_index_in_dim(stacked, (place - owners[b]) % places, 0, False)
                for b in range(blocks)
            ]
        keep, send = lag_parts(scal, weight, rows, own_rows[q], table, geometry, columns, lag_dev)
        half = keep + shifted(send, "freq", cores, 1)
        own = lax.dynamic_index_in_dim(half, column, 0, False)
        more = [
            shifted(
                lax.dynamic_index_in_dim(half, (column + s) % columns, 0, False).astype(BF16),
                "win",
                columns,
                s,
            )
            for s in range(1, columns)
        ]
        corr, sums = lag_stats(scal, lag_scale, q, own, more, observed, blocks, some)
        sums = [shifted(sums, ("win", "freq"), peers, s) for s in range(peers)]
        grads = gradients(scal, lag_total, q, sums, corr, observed, blocks, some)
        if not direct:
            stacked = jnp.stack(list(grads) + [jnp.zeros_like(grads[0])])
            grads = []
            for d in shifts:
                block = jnp.int32(blocks)
                for b in range(blocks):
                    block = jnp.where(owners[b] == (place - d) % places, b, block)
                grads.append(lax.dynamic_index_in_dim(stacked, block, 0, False))
        for d, g in zip(shifts, grads):
            returned[d].append(shifted(g, "recv", places, -d))
        corrs.append(corr)
        all_sums.append(sums)
    normed = normed_rows(scal, lag_total, all_sums, corrs, observed, blocks, some)
    adjoint = adjoint_rows(src_ids, [g for unit in returned for g in unit], channels)
    return (normed, adjoint)


def solution(mesh):
    return jax.shard_map(
        shards,
        mesh=mesh,
        in_specs=(
            P("win", None, ("groups", "recv"), "freq"),
            P(("groups", "win")),
            P("groups"),
            P(None, ("groups", "recv")),
            P(None, ("groups", "recv")),
            P(None, ("groups", "recv")),
            P(None, ("groups", "recv"), ("win", "freq")),
        ),
        out_specs=(
            P(None, ("groups", "recv"), ("win", "freq")),
            P(("groups", "recv"), ("win", "freq")),
        ),
        check_vma=False,
    )
```

```python
import functools
import math

import jax
import jax.numpy as jnp
import ml_dtypes
import numpy as np
from jax import lax
from jax.experimental import pallas as pl
from jax.experimental.pallas import tpu as pltpu
from jax.sharding import PartitionSpec as P

EPSILON = 1e-06
MIB = 1 << 20
LANES = 128
CHUNKS = 2
CORE, COLUMN, ORDER, BLOCK, COUNT = 0, 1, 2, 8, 16
BF16 = jnp.bfloat16
F32 = jnp.float32
VMEM = pl.BlockSpec(memory_space=pltpu.VMEM)
SMEM = pl.BlockSpec(memory_space=pltpu.SMEM)


def shifted(value, axis, size, shift):
    if shift % size == 0:
        return value
    return lax.ppermute(value, axis, [(i, (i + shift) % size) for i in range(size)])


def params(mib):
    return pltpu.CompilerParams(vmem_limit_bytes=mib * MIB)


def cost(flops, mib):
    return pl.CostEstimate(flops=int(flops), bytes_accessed=int(mib * MIB), transcendentals=0)


def tables(classes, span, period, bins_dev, columns, cores):
    u = np.arange(span, dtype=np.int64)[None, :]
    first = np.arange(columns * cores, dtype=np.int64)[:, None] * (bins_dev // columns)
    rows = (first + np.arange(classes)).reshape(-1, 1)
    base = classes * np.arange(LANES, dtype=np.int64)[:, None]
    out = []
    for f in (rows, base):
        angle = (f * u % period) * (2.0 * math.pi / period)
        out += [np.cos(angle).astype(np.float32), np.sin(angle).astype(np.float32)]
    return [jnp.asarray(t) for t in out]


def start_kernel(blocks, direct, classes, window_keep, owners, pair_count, src, rec, *refs):
    row_cos, row_sin, base_cos, base_sin = refs[:4]
    scal, wanted, rec_ids, table = refs[4], refs[5:-2], refs[-2], refs[-1]
    place, places = lax.axis_index("recv"), lax.axis_size("recv")
    column, columns = lax.axis_index("win"), lax.axis_size("win")
    core = lax.axis_index("freq")
    scal[CORE] = core
    scal[COLUMN] = column
    scal[ORDER] = 1 - window_keep[0]
    for b in range(blocks):
        unit = lax.rem(place - owners[b] + places, places) if direct else b
        scal[BLOCK + unit] = b
        scal[COUNT + unit] = pair_count[b, 0]
    for d, out in enumerate(wanted):
        owner = lax.rem(place - d + places, places)
        chosen = jnp.full(out.shape, -1, jnp.int32)
        received = jnp.zeros(out.shape, jnp.int32)
        for b in range(blocks):
            mine = jnp.full(out.shape, owners[b], jnp.int32) == owner
            chosen = jnp.where(mine, src[b : b + 1], chosen)
            received = jnp.where(mine, rec[b : b + 1], received)
        out[...] = chosen
        if direct:
            rec_ids[d : d + 1] = received
    if not direct:
        rec_ids[...] = rec[...]
    first = (core * columns + column) * classes
    cb, sb = base_cos[...], base_sin[...]
    for r in range(classes):
        ca, sa = row_cos[pl.ds(first + r, 1)], row_sin[pl.ds(first + r, 1)]
        table[r, :LANES] = (ca * cb - sa * sb).astype(BF16)
        table[r, LANES:] = (-(sa * cb + ca * sb)).astype(BF16)


def start(window_keep, owners, pair_count, pair_src, pair_rec, places, trig, classes, span):
    blocks, slots = pair_src.shape
    ids = jax.ShapeDtypeStruct((1, slots), jnp.int32)
    scal, *wanted, rec_ids, table = pl.pallas_call(
        functools.partial(start_kernel, blocks, places == blocks, classes),
        out_shape=[jax.ShapeDtypeStruct((LANES,), jnp.int32)]
        + [ids] * places
        + [
            jax.ShapeDtypeStruct(pair_rec.shape, jnp.int32),
            jax.ShapeDtypeStruct((classes, 2 * LANES, span), BF16),
        ],
        in_specs=[SMEM] * 3 + [VMEM] * 6,
        out_specs=[SMEM] + [VMEM] * (places + 2),
        compiler_params=params(16),
        cost_estimate=cost(6 * classes * LANES * span, 6),
        name="start",
    )(window_keep, owners, pair_count, pair_src, pair_rec, *trig)
    return scal, wanted, rec_ids, table


def picks(ids, channels):
    row = jnp.concatenate([i[...] for i in ids], axis=1)
    return (lax.broadcasted_iota(jnp.int32, (channels, row.shape[1]), 0) == row).astype(BF16)


def rows_kernel(half, used, sends, scal, spectra, *refs):
    held, refs = refs[:used], refs[used:]
    perm, src_ids, rec_ids, refs = refs[0], refs[1 : 1 + sends], refs[1 + sends], refs[2 + sends :]
    early, refs = (refs[:sends], refs[sends:]) if half else (None, refs)
    first, second, own_out = refs[:sends], refs[sends:-1], refs[-1]
    units, _, slots, part = own_out.shape
    some = first[0].shape[1]
    channels = spectra.shape[2]
    pick = picks(list(src_ids) + [rec_ids.at[d : d + 1] for d in range(units)], channels)
    here = spectra[0, half, :, pl.ds(pl.multiple_of(scal[COLUMN] * part, part), part)]
    for u in range(used):
        x = here
        for s in range(used):
            x = jnp.where(scal[ORDER + u] == s + 1, held[s][...], x)
        x = jnp.dot(x, perm[...], preferred_element_type=F32).astype(BF16)
        y = lax.dot_general(
            pick, x, (((0,), (0,)), ((), ())), preferred_element_type=F32
        ).astype(BF16)
        for d in range(sends):
            at = d * slots
            first[d][u] = y[at : at + some]
            if half:
                second[d][u, 0] = early[d][u]
                second[d][u, 1] = y[at + some : at + slots]
            else:
                second[d][u] = y[at + some : at + slots]
        for d in range(units):
            at = (sends + d) * slots
            own_out[d, u] = y[at : at + slots]


def gather_rows(half, scal, spectra, held, perm, src_ids, rec_ids, early, some):
    used, sends = len(held), len(src_ids)
    part = held[0].shape[-1]
    units, slots = rec_ids.shape
    shape = lambda *dims: jax.ShapeDtypeStruct(dims, BF16)
    rest = slots - some
    late = shape(used, 2, rest, part) if half else shape(used, rest, part)
    outs = pl.pallas_call(
        functools.partial(rows_kernel, half, used, sends),
        out_shape=[shape(used, some, part)] * sends
        + [late] * sends
        + [shape(units, used, slots, part)],
        in_specs=[SMEM] + [VMEM] * (used + 3 + sends + len(early)),
        out_specs=[VMEM] * (2 * sends + 1),
        compiler_params=params(32),
        cost_estimate=cost(2 * used * part * (128 * part + 512 * 128), 4),
        name="rows",
    )(scal, spectra, *held, perm, *src_ids, rec_ids, *early)
    return outs[:sends], outs[sends:-1], outs[-1]


def combine(values, classes, outputs, origin, span, period):
    plain, scaled = [None] * outputs, [None] * outputs

    def add(into, k, value, sign):
        if into[k] is None:
            into[k] = value if sign > 0 else -value
        else:
            into[k] = into[k] + value if sign > 0 else into[k] - value

    for r, (real, imag) in enumerate(values):
        both = None
        for k in range(outputs):
            eighths = r * (span * k - origin) * 8 // period % 8
            assert r * (span * k - origin) * 8 % period == 0
            if eighths % 2 == 0:
                value, sign = ((real, 1), (imag, -1), (real, -1), (imag, 1))[eighths // 2]
                add(plain, k, value, sign)
            else:
                if both is None:
                    both = real + imag, real - imag
                value, sign = ((both[1], 1), (both[0], -1), (both[1], -1), (both[0], 1))[eighths // 2]
                add(scaled, k, value, sign)
    root = math.sqrt(0.5)
    return [a if b is None else a + root * b for a, b in zip(plain, scaled)]


def lags_kernel(geometry, units, first, split, scal, weight, after, *refs):
    classes, span, outputs, origin, period, chunk = geometry
    count = units * (2 if split else 1)
    s_refs, (r_real, r_imag, table, keep, send, lhs) = refs[:count], refs[count:]
    used, slots = s_refs[0].shape[0], s_refs[0].shape[-2]
    rows = units * slots
    lag_dev = keep.shape[-1]
    cores = 2
    mine = slice(first, first + slots)
    for d in range(units):
        at = slice(d * slots, (d + 1) * slots)
        turned = slice(rows + d * slots, rows + (d + 1) * slots)
        for r in range(classes):
            bins = slice(r * LANES, (r + 1) * LANES)
            real = imag = None
            for u in range(used):
                if split:
                    sr, si = s_refs[d][u, :, bins], s_refs[units + d][u, :, bins]
                else:
                    sr, si = s_refs[d][u, 0, :, bins], s_refs[d][u, 1, :, bins]
                sr, si = sr.astype(F32), si.astype(F32)
                rr, ri = r_real[d, u, mine, bins].astype(F32), r_imag[d, u, mine, bins].astype(F32)
                re, im = sr * rr + si * ri, si * rr - sr * ri
                if u:
                    re, im = real + weight[u] * re, imag + weight[u] * im
                real, imag = re, im
            lhs[r, at, :LANES] = real.astype(BF16)
            lhs[r, at, LANES:] = imag.astype(BF16)
            lhs[r, turned, :LANES] = imag.astype(BF16)
            lhs[r, turned, LANES:] = (-real).astype(BF16)
    for start in range(0, span, chunk):
        values = []
        for r in range(classes):
            y = jnp.dot(lhs[r], table[r, :, start : start + chunk], preferred_element_type=F32)
            values.append((y[:rows], y[rows:]))
        for k, value in enumerate(combine(values, classes, outputs, origin, span, period)):
            lag = span * k + start
            column, core, offset = lag // (cores * lag_dev), lag // lag_dev % cores, lag % lag_dev
            lags = slice(offset, offset + chunk)

            @pl.when(scal[CORE] == core)
            def _():
                keep[column, :, lags] = value

            @pl.when(scal[CORE] != core)
            def _():
                send[column, :, lags] = value.astype(BF16)


def lag_parts(scal, weight, after, rows, own, first, table, geometry, columns, lag_dev):
    classes, span = geometry[:2]
    units = own[0].shape[0]
    split = len(rows) > units
    slots, part = rows[0].shape[-2:]
    shape = (columns, units * slots, lag_dev)
    return pl.pallas_call(
        functools.partial(lags_kernel, geometry, units, first, split),
        out_shape=[jax.ShapeDtypeStruct(shape, F32), jax.ShapeDtypeStruct(shape, BF16)],
        in_specs=[SMEM, SMEM, pl.BlockSpec(memory_space=pl.ANY)] + [VMEM] * (len(rows) + 3),
        out_specs=[VMEM] * 2,
        scratch_shapes=[pltpu.VMEM((classes, 2 * units * slots, 2 * LANES), BF16)],
        compiler_params=params(32),
        cost_estimate=cost(8 * units * slots * part * span, 8),
        name="lags",
    )(scal, weight, after, *rows, *own, table)


def cores_kernel(scal, keep, more, own, *sends):
    columns = keep.shape[0]
    for column in range(columns):
        value = keep[column] + more[column].astype(F32)

        @pl.when(scal[COLUMN] == column)
        def _():
            own[...] = value

        for s, out in enumerate(sends):

            @pl.when(lax.rem(scal[COLUMN] + s + 1, columns) == column)
            def _():
                out[...] = value.astype(BF16)


def add_cores(scal, keep, more):
    columns, rows, lag_dev = keep.shape
    return pl.pallas_call(
        cores_kernel,
        out_shape=[jax.ShapeDtypeStruct((rows, lag_dev), F32)]
        + [jax.ShapeDtypeStruct((rows, lag_dev), BF16)] * (columns - 1),
        in_specs=[SMEM, VMEM, VMEM],
        out_specs=[VMEM] * columns,
        compiler_params=params(16),
        cost_estimate=cost(2 * keep.size, 2),
        name="cores",
    )(scal, keep, more)


def stats_kernel(scale, chunk, units, others, scal, *refs):
    own, more, refs = refs[0], refs[1 : 1 + others], refs[1 + others :]
    targets, (corr, sums) = refs[:units], refs[units:]
    slots = targets[0].shape[1]
    columns = []
    for d in range(units):
        at = slice(d * slots, (d + 1) * slots)
        value = own[at]
        for m in more:
            value = value + m[at].astype(F32)
        slot = chunk * slots + lax.broadcasted_iota(jnp.int32, (slots, 1), 0)
        value = value * jnp.where(slot < scal[COUNT + d], scale, 0.0)
        corr[at] = value
        square = jnp.sum(value * value, axis=1, keepdims=True)
        product = jnp.sum(value * targets[d][0], axis=1, keepdims=True)
        lane = lax.broadcasted_iota(jnp.int32, (slots, LANES), 1)
        columns.append(jnp.where(lane == 0, square, jnp.where(lane == 1, product, 0.0)))
    sums[...] = jnp.concatenate(columns, axis=0).T[:8]


def target_specs(chunk, units, slots, lag_dev):
    return [
        pl.BlockSpec((1, slots, lag_dev), lambda i, scal, d=d: (scal[BLOCK + d], chunk, 0))
        for d in range(units)
    ]


def whole(shape):
    return pl.BlockSpec(shape, lambda i, scal: (0,) * len(shape))


def lag_stats(scal, scale, chunk, own, more, observed, units, slots):
    rows, lag_dev = own.shape
    outs = [jax.ShapeDtypeStruct((rows, lag_dev), F32), jax.ShapeDtypeStruct((8, rows), F32)]
    return pl.pallas_call(
        functools.partial(stats_kernel, scale, chunk, units, len(more)),
        grid_spec=pltpu.PrefetchScalarGridSpec(
            num_scalar_prefetch=1,
            grid=(1,),
            in_specs=[whole(own.shape)] * (1 + len(more))
            + target_specs(chunk, units, slots, lag_dev),
            out_specs=[whole(o.shape) for o in outs],
        ),
        out_shape=outs,
        compiler_params=params(16),
        cost_estimate=cost(8 * rows * lag_dev, 2),
        name="stats",
    )(scal, own, *more, *[observed] * units)


def slot_scales(sums, lag_total):
    total = sums[0][...]
    for s in sums[1:]:
        total = total + s[...]
    rows = total.shape[1]
    square, product = total[0:1], total[1:2]
    inverse = 1.0 / jnp.sqrt(square / lag_total + EPSILON)
    bending = (square * inverse * inverse - product * inverse) / lag_total
    sub = lax.broadcasted_iota(jnp.int32, (LANES, rows), 0)
    both = jnp.where(sub == 0, inverse, jnp.where(sub == 1, bending, 0.0)).T
    return both[:, 0:1], both[:, 1:2]


def gradient_kernel(lag_total, chunk, units, parts, scal, *refs):
    sums, corr, refs = refs[:parts], refs[parts], refs[parts + 1 :]
    targets, outs = refs[:units], refs[units:]
    slots = targets[0].shape[1]
    inverse, bending = slot_scales(sums, lag_total)
    for d in range(units):
        at = slice(d * slots, (d + 1) * slots)
        slot = chunk * slots + lax.broadcasted_iota(jnp.int32, (slots, 1), 0)
        valid = jnp.where(slot < scal[COUNT + d], inverse[at], 0.0)
        normed = corr[at] * inverse[at]
        gradient = (normed - targets[d][0] - normed * bending[at]) * valid
        outs[d][...] = gradient.astype(BF16)


def gradients(scal, lag_total, chunk, sums, corr, observed, units, slots):
    rows, lag_dev = corr.shape
    out = jax.ShapeDtypeStruct((slots, lag_dev), BF16)
    return pl.pallas_call(
        functools.partial(gradient_kernel, lag_total, chunk, units, len(sums)),
        grid_spec=pltpu.PrefetchScalarGridSpec(
            num_scalar_prefetch=1,
            grid=(1,),
            in_specs=[whole(sums[0].shape)] * len(sums)
            + [whole(corr.shape)]
            + target_specs(chunk, units, slots, lag_dev),
            out_specs=[whole(out.shape)] * units,
        ),
        out_shape=[out] * units,
        compiler_params=params(16),
        cost_estimate=cost(8 * rows * lag_dev, 1),
        name="gradient",
    )(scal, *sums, corr, *[observed] * units)


def normed_kernel(lag_total, parts, scal, *refs):
    out = refs[-1]
    slots = out.shape[1] // CHUNKS
    d = pl.program_id(0)
    for q in range(CHUNKS):
        sums, corr = refs[q * (parts + 1) : q * (parts + 1) + parts], refs[q * (parts + 1) + parts]
        inverse, _ = slot_scales(sums, lag_total)
        mine = inverse[0:slots]
        for i in range(1, inverse.shape[0] // slots):
            mine = jnp.where(d == i, inverse[i * slots : (i + 1) * slots], mine)
        out[0, q * slots : (q + 1) * slots] = corr[...] * mine


def normed_rows(scal, lag_total, sums, corr, observed, units, slots):
    lag_dev = corr[0].shape[1]
    ins, specs = [], []
    for s, c in zip(sums, corr):
        ins += [*s, c]
        specs += [whole(s[0].shape)] * len(s)
        specs += [pl.BlockSpec((slots, lag_dev), lambda i, scal: (i, 0))]
    return pl.pallas_call(
        functools.partial(normed_kernel, lag_total, len(sums[0])),
        grid_spec=pltpu.PrefetchScalarGridSpec(
            num_scalar_prefetch=1,
            grid=(units,),
            in_specs=specs,
            out_specs=pl.BlockSpec(
                (1, CHUNKS * slots, lag_dev), lambda i, scal: (scal[BLOCK + i], 0, 0)
            ),
        ),
        out_shape=jax.ShapeDtypeStruct(observed.shape, F32),
        compiler_params=params(16),
        cost_estimate=cost(2 * observed.size, 2),
        name="normed",
    )(scal, *ins)


def adjoint_kernel(sends, *refs):
    ids, parts, out = refs[:sends], refs[sends:-1], refs[-1]
    pick = picks(ids, out.shape[0])
    rows = jnp.concatenate([p[...] for p in parts], axis=0)
    out[...] = jnp.dot(pick, rows, preferred_element_type=F32)


def adjoint_rows(src_ids, parts, channels):
    lag_dev = parts[0].shape[1]
    return pl.pallas_call(
        functools.partial(adjoint_kernel, len(src_ids)),
        out_shape=jax.ShapeDtypeStruct((channels, lag_dev), F32),
        in_specs=[VMEM] * (len(src_ids) + len(parts)),
        out_specs=VMEM,
        compiler_params=params(16),
        cost_estimate=cost(2 * channels * lag_dev * 256, 1),
        name="adjoint",
    )(*src_ids, *parts)


def shards(spectra, window_keep, owners, pair_src, pair_rec, pair_count, observed):
    columns, cores, places = lax.axis_size("win"), lax.axis_size("freq"), lax.axis_size("recv")
    column, core, place = lax.axis_index("win"), lax.axis_index("freq"), lax.axis_index("recv")
    assert spectra.shape[0] == 1 and cores == 2
    channels, bins_dev = spectra.shape[2:]
    blocks, slots, lag_dev = observed.shape
    lag_total = lag_dev * columns * cores
    bin_total = bins_dev * cores
    period = 2 * bin_total
    part = bins_dev // columns
    classes = part // LANES
    span = period // classes
    geometry = (classes, span, lag_total // span, lag_total // 2, period, 256)
    lag_scale = 1.0 / math.sqrt(bin_total * columns)
    peers = columns * cores
    some = slots // CHUNKS
    shifts = range(places)

    held = [
        [
            shifted(
                lax.dynamic_slice(
                    spectra[0, half], (0, (column + s) % columns * part), (channels, part)
                ),
                "win",
                columns,
                s,
            )
            for s in range(1, columns)
        ]
        for half in range(2)
    ]
    trig = tables(classes, span, period, bins_dev, columns, cores)
    scal, wanted, rec_ids, table = start(
        window_keep, owners, pair_count, pair_src, pair_rec, places, trig, classes, span
    )
    if columns == 2:
        weight = jnp.ones((1,), F32)
    else:
        keeps = jnp.stack([shifted(window_keep[0], "win", columns, s) for s in range(columns)])
        ranked = jnp.argsort(-keeps)[: columns - 1].astype(jnp.int32)
        weight = keeps[ranked].astype(F32)
        scal = lax.dynamic_update_slice(scal, ranked, (ORDER,))

    direct = places == blocks
    src_ids = [shifted(x, "recv", places, -d) for d, x in zip(shifts, wanted)]
    source = np.arange(part)
    perm = np.zeros((part, part), ml_dtypes.bfloat16)
    perm[source, source % classes * LANES + source // classes] = 1
    perm = jnp.asarray(perm)
    first_real, rest_real, own_real = gather_rows(
        0, scal, spectra, held[0], perm, src_ids, rec_ids, [], some
    )
    first_imag, rest, own_imag = gather_rows(
        1, scal, spectra, held[1], perm, src_ids, rec_ids, rest_real, some
    )
    sent = [[first_real, first_imag], [rest]]
    arrived = [
        [[shifted(x, "recv", places, d) for d, x in zip(shifts, rows)] for rows in group]
        for group in sent
    ]
    corrs, all_sums, returned = [], [], [[] for _ in shifts]
    after = scal
    for q in range(CHUNKS):
        rows = arrived[q]
        if not direct:
            stacked = [jnp.stack(r) for r in rows]
            rows = [
                [
                    lax.dynamic_index_in_dim(x, (place - owners[b]) % places, 0, False)
                    for b in range(blocks)
                ]
                for x in stacked
            ]
        rows = [x for group in rows for x in group]
        keep, send = lag_parts(
            scal, weight, after, rows, (own_real, own_imag), q * some, table, geometry, columns, lag_dev
        )
        own, *sends = add_cores(scal, keep, shifted(send, "freq", cores, 1))
        after = own
        more = [shifted(x, "win", columns, s + 1) for s, x in enumerate(sends)]
        corr, sums = lag_stats(scal, lag_scale, q, own, more, observed, blocks, some)
        sums = [shifted(sums, ("win", "freq"), peers, s) for s in range(peers)]
        grads = gradients(scal, lag_total, q, sums, corr, observed, blocks, some)
        if not direct:
            stacked = jnp.stack(list(grads) + [jnp.zeros_like(grads[0])])
            grads = []
            for d in shifts:
                block = jnp.int32(blocks)
                for b in range(blocks):
                    block = jnp.where(owners[b] == (place - d) % places, b, block)
                grads.append(lax.dynamic_index_in_dim(stacked, block, 0, False))
        for d, g in zip(shifts, grads):
            returned[d].append(shifted(g, "recv", places, -d))
        corrs.append(corr)
        all_sums.append(sums)
    normed = normed_rows(scal, lag_total, all_sums, corrs, observed, blocks, some)
    adjoint = adjoint_rows(src_ids, [g for unit in returned for g in unit], channels)
    return (normed, adjoint)


def solution(mesh):
    return jax.shard_map(
        shards,
        mesh=mesh,
        in_specs=(
            P("win", None, ("groups", "recv"), "freq"),
            P(("groups", "win")),
            P("groups"),
            P(None, ("groups", "recv")),
            P(None, ("groups", "recv")),
            P(None, ("groups", "recv")),
            P(None, ("groups", "recv"), ("win", "freq")),
        ),
        out_specs=(
            P(None, ("groups", "recv"), ("win", "freq")),
            P(("groups", "recv"), ("win", "freq")),
        ),
        check_vma=False,
    )
```

```python
import functools
import math

import jax
import jax.numpy as jnp
import ml_dtypes
import numpy as np
from jax import lax
from jax.experimental import pallas as pl
from jax.experimental.pallas import tpu as pltpu
from jax.sharding import PartitionSpec as P

EPSILON = 1e-06
MIB = 1 << 20
LANES = 128
CHUNKS = 2
CORE, COLUMN, ORDER, BLOCK, COUNT = 0, 1, 2, 8, 16
BF16 = jnp.bfloat16
F32 = jnp.float32
VMEM = pl.BlockSpec(memory_space=pltpu.VMEM)
SMEM = pl.BlockSpec(memory_space=pltpu.SMEM)


def swapped(value, axis, size, step):
    assert size & (size - 1) == 0
    if step == 0:
        return value
    return lax.ppermute(value, axis, [(i, i ^ step) for i in range(size)])


def params(mib):
    return pltpu.CompilerParams(vmem_limit_bytes=mib * MIB)


SMALL = pl.CostEstimate(flops=1, bytes_accessed=1, transcendentals=0)


def tables(classes, span, period, bins_dev, columns, cores):
    u = np.arange(span, dtype=np.int64)[None, :]
    first = np.arange(columns * cores, dtype=np.int64)[:, None] * (bins_dev // columns)
    rows = (first + np.arange(classes)).reshape(-1)
    high = 16 * classes * np.arange(LANES // 16, dtype=np.int64)
    low = classes * np.arange(16, dtype=np.int64)
    angle = (np.concatenate([rows, high, low])[:, None] * u % period) * (2.0 * math.pi / period)
    return np.stack([np.cos(angle), np.sin(angle)]).astype(np.float32)


def start_kernel(blocks, direct, classes, parts, *refs):
    given, refs = refs[:6], refs[6:]
    scal, wanted, rec_ids, table = refs[0], refs[1:-10], refs[-10], refs[-9]
    held, base, sems = refs[-8:-2], refs[-2], refs[-1]
    copies = [pltpu.make_async_copy(g, h, sems.at[i]) for i, (g, h) in enumerate(zip(given, held))]
    for c in copies:
        c.start()
    for c in copies:
        c.wait()
    window_keep, owners, pair_count, src, rec, trig = held
    place = lax.axis_index("recv")
    column, columns = lax.axis_index("win"), lax.axis_size("win")
    core = lax.axis_index("freq")
    scal[CORE] = core
    scal[COLUMN] = column
    scal[ORDER] = 1 - window_keep[0]
    for b in range(blocks):
        unit = place ^ owners[b] if direct else b
        scal[BLOCK + unit] = b
        scal[COUNT + unit] = pair_count[b]
    for d, out in enumerate(wanted):
        chosen = jnp.full(out.shape, -1, jnp.int32)
        received = jnp.zeros(out.shape, jnp.int32)
        for b in range(blocks):
            mine = jnp.full(out.shape, owners[b], jnp.int32) == (place ^ d)
            chosen = jnp.where(mine, src[b : b + 1], chosen)
            received = jnp.where(mine, rec[b : b + 1], received)
        out[...] = chosen
        if direct:
            rec_ids[d : d + 1] = received
    if not direct:
        rec_ids[...] = rec[...]
    rows = parts * classes
    low = slice(rows + LANES // 16, rows + LANES // 16 + 16)
    cl, sl = trig[0, low], trig[1, low]
    for h in range(LANES // 16):
        ch, sh = trig[0, rows + h : rows + h + 1], trig[1, rows + h : rows + h + 1]
        base[0, 16 * h : 16 * h + 16] = ch * cl - sh * sl
        base[1, 16 * h : 16 * h + 16] = sh * cl + ch * sl
    first = (core * columns + column) * classes
    cb, sb = base[0], base[1]
    for r in range(classes):
        ca, sa = trig[0, pl.ds(first + r, 1)], trig[1, pl.ds(first + r, 1)]
        table[r, :LANES] = (ca * cb - sa * sb).astype(BF16)
        table[r, LANES:] = (-(sa * cb + ca * sb)).astype(BF16)


def start(window_keep, owners, pair_count, pair_src, pair_rec, places, trig, classes, span, parts):
    blocks, slots = pair_src.shape
    ids = jax.ShapeDtypeStruct((1, slots), jnp.int32)
    given = [window_keep, owners, pair_count[:, 0], pair_src, pair_rec, jnp.asarray(trig)]
    scal, *wanted, rec_ids, table = pl.pallas_call(
        functools.partial(start_kernel, blocks, places == blocks, classes, parts),
        out_shape=[jax.ShapeDtypeStruct((LANES,), jnp.int32)]
        + [ids] * places
        + [
            jax.ShapeDtypeStruct(pair_rec.shape, jnp.int32),
            jax.ShapeDtypeStruct((classes, 2 * LANES, span), BF16),
        ],
        in_specs=[pl.BlockSpec(memory_space=pl.ANY)] * 6,
        out_specs=[SMEM] + [VMEM] * (places + 2),
        scratch_shapes=[pltpu.SMEM(g.shape, g.dtype) for g in given[:3]]
        + [pltpu.VMEM(g.shape, g.dtype) for g in given[3:]]
        + [pltpu.VMEM((2, LANES, span), F32), pltpu.SemaphoreType.DMA((6,))],
        compiler_params=params(16),
        cost_estimate=SMALL,
        name="start",
    )(*given)
    return scal, wanted, rec_ids, table


def picks(ids, channels):
    row = jnp.concatenate([i[...] for i in ids], axis=1)
    return (lax.broadcasted_iota(jnp.int32, (channels, row.shape[1]), 0) == row).astype(BF16)


def rows_kernel(used, sends, scal, spectra, *refs):
    held, refs = refs[:used], refs[used:]
    perm, src_ids, rec_ids, refs = refs[0], refs[1 : 1 + sends], refs[1 + sends], refs[2 + sends :]
    chunks, own_out = refs[:-1], refs[-1]
    units, _, _, slots, part = own_out.shape
    some = slots // CHUNKS
    channels = spectra.shape[2]
    pick = picks(list(src_ids) + [rec_ids.at[d : d + 1] for d in range(units)], channels)
    bins = pl.ds(pl.multiple_of(scal[COLUMN] * part, part), part)
    for u in range(used):
        for half in range(2):
            x = spectra[0, half, :, bins]
            for s in range(used):
                x = jnp.where(scal[ORDER + u] == s + 1, held[s][0, half], x)
            x = jnp.dot(x, perm[...], preferred_element_type=F32).astype(BF16)
            y = lax.dot_general(
                pick, x, (((0,), (0,)), ((), ())), preferred_element_type=F32
            ).astype(BF16)
            for i, out in enumerate(chunks):
                at = i % sends * slots + i // sends * some
                out[u, half] = y[at : at + some]
            for d in range(units):
                at = (sends + d) * slots
                own_out[d, u, half] = y[at : at + slots]


def gather_rows(scal, spectra, held, perm, src_ids, rec_ids):
    used, sends = len(held), len(src_ids)
    part = held[0].shape[-1]
    units, slots = rec_ids.shape
    sent = jax.ShapeDtypeStruct((used, 2, slots // CHUNKS, part), BF16)
    outs = pl.pallas_call(
        functools.partial(rows_kernel, used, sends),
        out_shape=[sent] * (sends * CHUNKS)
        + [jax.ShapeDtypeStruct((units, used, 2, slots, part), BF16)],
        in_specs=[SMEM] + [VMEM] * (used + 3 + sends),
        out_specs=[VMEM] * (CHUNKS * sends + 1),
        compiler_params=params(32),
        cost_estimate=SMALL,
        name="rows",
    )(scal, spectra, *held, perm, *src_ids, rec_ids)
    return [outs[q * sends : (q + 1) * sends] for q in range(CHUNKS)], outs[-1]


def combine(values, classes, outputs, origin, span, period):
    plain, scaled = [None] * outputs, [None] * outputs

    def add(into, k, value, sign):
        if into[k] is None:
            into[k] = value if sign > 0 else -value
        else:
            into[k] = into[k] + value if sign > 0 else into[k] - value

    for r, (real, imag) in enumerate(values):
        both = None
        for k in range(outputs):
            eighths = r * (span * k - origin) * 8 // period % 8
            assert r * (span * k - origin) * 8 % period == 0
            if eighths % 2 == 0:
                value, sign = ((real, 1), (imag, -1), (real, -1), (imag, 1))[eighths // 2]
                add(plain, k, value, sign)
            else:
                if both is None:
                    both = real + imag, real - imag
                value, sign = ((both[1], 1), (both[0], -1), (both[1], -1), (both[0], 1))[eighths // 2]
                add(scaled, k, value, sign)
    root = math.sqrt(0.5)
    return [a if b is None else a + root * b for a, b in zip(plain, scaled)]


def lags_kernel(geometry, units, first, scal, weight, after, *refs):
    classes, span, outputs, origin, period, chunk = geometry
    s_refs, (own, table, keep, send, lhs) = refs[:units], refs[units:]
    used, slots = s_refs[0].shape[0], s_refs[0].shape[-2]
    rows = units * slots
    lag_dev = keep.shape[-1]
    cores = 2
    mine = slice(first, first + slots)
    for d in range(units):
        at = slice(d * slots, (d + 1) * slots)
        turned = slice(rows + d * slots, rows + (d + 1) * slots)
        for r in range(classes):
            bins = slice(r * LANES, (r + 1) * LANES)
            real = imag = None
            for u in range(used):
                sr, si = s_refs[d][u, 0, :, bins].astype(F32), s_refs[d][u, 1, :, bins].astype(F32)
                rr, ri = own[d, u, 0, mine, bins].astype(F32), own[d, u, 1, mine, bins].astype(F32)
                re, im = sr * rr + si * ri, si * rr - sr * ri
                if u:
                    re, im = real + weight[u] * re, imag + weight[u] * im
                real, imag = re, im
            lhs[r, at, :LANES] = real.astype(BF16)
            lhs[r, at, LANES:] = imag.astype(BF16)
            lhs[r, turned, :LANES] = imag.astype(BF16)
            lhs[r, turned, LANES:] = (-real).astype(BF16)
    for start in range(0, span, chunk):
        values = []
        for r in range(classes):
            y = jnp.dot(lhs[r], table[r, :, start : start + chunk], preferred_element_type=F32)
            values.append((y[:rows], y[rows:]))
        for k, value in enumerate(combine(values, classes, outputs, origin, span, period)):
            lag = span * k + start
            column, core, offset = lag // (cores * lag_dev), lag // lag_dev % cores, lag % lag_dev
            lags = slice(offset, offset + chunk)

            @pl.when(scal[CORE] == core)
            def _():
                keep[column, :, lags] = value

            @pl.when(scal[CORE] != core)
            def _():
                send[column, :, lags] = value.astype(BF16)


def lag_parts(scal, weight, after, rows, own, first, table, geometry, columns, lag_dev):
    classes, span = geometry[:2]
    units = len(rows)
    slots, part = rows[0].shape[-2:]
    shape = (columns, units * slots, lag_dev)
    return pl.pallas_call(
        functools.partial(lags_kernel, geometry, units, first),
        out_shape=[jax.ShapeDtypeStruct(shape, F32), jax.ShapeDtypeStruct(shape, BF16)],
        in_specs=[SMEM, SMEM, pl.BlockSpec(memory_space=pl.ANY)] + [VMEM] * (units + 2),
        out_specs=[VMEM] * 2,
        scratch_shapes=[pltpu.VMEM((classes, 2 * units * slots, 2 * LANES), BF16)],
        compiler_params=params(32),
        cost_estimate=SMALL,
        name="lags",
    )(scal, weight, after, *rows, own, table)


def cores_kernel(scal, keep, more, own, *sends):
    columns = keep.shape[0]
    for column in range(columns):
        value = keep[column] + more[column].astype(F32)

        @pl.when(scal[COLUMN] == column)
        def _():
            own[...] = value

        for s, out in enumerate(sends):

            @pl.when(scal[COLUMN] ^ (s + 1) == column)
            def _():
                out[...] = value.astype(BF16)


def add_cores(scal, keep, more):
    columns, rows, lag_dev = keep.shape
    return pl.pallas_call(
        cores_kernel,
        out_shape=[jax.ShapeDtypeStruct((rows, lag_dev), F32)]
        + [jax.ShapeDtypeStruct((rows, lag_dev), BF16)] * (columns - 1),
        in_specs=[SMEM, VMEM, VMEM],
        out_specs=[VMEM] * columns,
        compiler_params=params(16),
        cost_estimate=SMALL,
        name="cores",
    )(scal, keep, more)


def stats_kernel(scale, chunk, units, others, scal, *refs):
    own, more, refs = refs[0], refs[1 : 1 + others], refs[1 + others :]
    targets, (corr, sums) = refs[:units], refs[units:]
    slots = targets[0].shape[1]
    columns = []
    for d in range(units):
        at = slice(d * slots, (d + 1) * slots)
        value = own[at]
        for m in more:
            value = value + m[at].astype(F32)
        slot = chunk * slots + lax.broadcasted_iota(jnp.int32, (slots, 1), 0)
        value = value * jnp.where(slot < scal[COUNT + d], scale, 0.0)
        corr[at] = value
        square = jnp.sum(value * value, axis=1, keepdims=True)
        product = jnp.sum(value * targets[d][0], axis=1, keepdims=True)
        lane = lax.broadcasted_iota(jnp.int32, (slots, LANES), 1)
        columns.append(jnp.where(lane == 0, square, jnp.where(lane == 1, product, 0.0)))
    sums[...] = jnp.concatenate(columns, axis=0).T[:8]


def target_specs(chunk, units, slots, lag_dev):
    return [
        pl.BlockSpec((1, slots, lag_dev), lambda i, scal, d=d: (scal[BLOCK + d], chunk, 0))
        for d in range(units)
    ]


def whole(shape):
    return pl.BlockSpec(shape, lambda i, scal: (0,) * len(shape))


def lag_stats(scal, scale, chunk, own, more, observed, units, slots):
    rows, lag_dev = own.shape
    outs = [jax.ShapeDtypeStruct((rows, lag_dev), F32), jax.ShapeDtypeStruct((8, rows), F32)]
    return pl.pallas_call(
        functools.partial(stats_kernel, scale, chunk, units, len(more)),
        grid_spec=pltpu.PrefetchScalarGridSpec(
            num_scalar_prefetch=1,
            grid=(1,),
            in_specs=[whole(own.shape)] * (1 + len(more))
            + target_specs(chunk, units, slots, lag_dev),
            out_specs=[whole(o.shape) for o in outs],
        ),
        out_shape=outs,
        compiler_params=params(16),
        cost_estimate=SMALL,
        name="stats",
    )(scal, own, *more, *[observed] * units)


def slot_scales(sums, lag_total):
    total = sums[0][...]
    for s in sums[1:]:
        total = total + s[...]
    rows = total.shape[1]
    square, product = total[0:1], total[1:2]
    inverse = 1.0 / jnp.sqrt(square / lag_total + EPSILON)
    bending = (square * inverse * inverse - product * inverse) / lag_total
    sub = lax.broadcasted_iota(jnp.int32, (LANES, rows), 0)
    both = jnp.where(sub == 0, inverse, jnp.where(sub == 1, bending, 0.0)).T
    return both[:, 0:1], both[:, 1:2]


def gradient_kernel(lag_total, chunk, units, parts, scal, *refs):
    sums, corr, refs = refs[:parts], refs[parts], refs[parts + 1 :]
    targets, outs = refs[:units], refs[units:]
    slots = targets[0].shape[1]
    inverse, bending = slot_scales(sums, lag_total)
    for d in range(units):
        at = slice(d * slots, (d + 1) * slots)
        slot = chunk * slots + lax.broadcasted_iota(jnp.int32, (slots, 1), 0)
        valid = jnp.where(slot < scal[COUNT + d], inverse[at], 0.0)
        normed = corr[at] * inverse[at]
        gradient = (normed - targets[d][0] - normed * bending[at]) * valid
        outs[d][...] = gradient.astype(BF16)


def gradients(scal, lag_total, chunk, sums, corr, observed, units, slots):
    rows, lag_dev = corr.shape
    out = jax.ShapeDtypeStruct((slots, lag_dev), BF16)
    return pl.pallas_call(
        functools.partial(gradient_kernel, lag_total, chunk, units, len(sums)),
        grid_spec=pltpu.PrefetchScalarGridSpec(
            num_scalar_prefetch=1,
            grid=(1,),
            in_specs=[whole(sums[0].shape)] * len(sums)
            + [whole(corr.shape)]
            + target_specs(chunk, units, slots, lag_dev),
            out_specs=[whole(out.shape)] * units,
        ),
        out_shape=[out] * units,
        compiler_params=params(16),
        cost_estimate=SMALL,
        name="gradient",
    )(scal, *sums, corr, *[observed] * units)


def normed_kernel(lag_total, parts, scal, *refs):
    out = refs[-1]
    slots = out.shape[1] // CHUNKS
    d = pl.program_id(0)
    for q in range(CHUNKS):
        sums, corr = refs[q * (parts + 1) : q * (parts + 1) + parts], refs[q * (parts + 1) + parts]
        inverse, _ = slot_scales(sums, lag_total)
        mine = inverse[0:slots]
        for i in range(1, inverse.shape[0] // slots):
            mine = jnp.where(d == i, inverse[i * slots : (i + 1) * slots], mine)
        out[0, q * slots : (q + 1) * slots] = corr[...] * mine


def normed_rows(scal, lag_total, sums, corr, observed, units, slots):
    lag_dev = corr[0].shape[1]
    ins, specs = [], []
    for s, c in zip(sums, corr):
        ins += [*s, c]
        specs += [whole(s[0].shape)] * len(s)
        specs += [pl.BlockSpec((slots, lag_dev), lambda i, scal: (i, 0))]
    return pl.pallas_call(
        functools.partial(normed_kernel, lag_total, len(sums[0])),
        grid_spec=pltpu.PrefetchScalarGridSpec(
            num_scalar_prefetch=1,
            grid=(units,),
            in_specs=specs,
            out_specs=pl.BlockSpec(
                (1, CHUNKS * slots, lag_dev), lambda i, scal: (scal[BLOCK + i], 0, 0)
            ),
        ),
        out_shape=jax.ShapeDtypeStruct(observed.shape, F32),
        compiler_params=params(16),
        cost_estimate=SMALL,
        name="normed",
    )(scal, *ins)


def adjoint_kernel(sends, *refs):
    ids, parts, out = refs[:sends], refs[sends:-1], refs[-1]
    pick = picks(ids, out.shape[0])
    rows = jnp.concatenate([p[...] for p in parts], axis=0)
    out[...] = jnp.dot(pick, rows, preferred_element_type=F32)


def adjoint_rows(src_ids, parts, channels):
    lag_dev = parts[0].shape[1]
    return pl.pallas_call(
        functools.partial(adjoint_kernel, len(src_ids)),
        out_shape=jax.ShapeDtypeStruct((channels, lag_dev), F32),
        in_specs=[VMEM] * (len(src_ids) + len(parts)),
        out_specs=VMEM,
        compiler_params=params(16),
        cost_estimate=SMALL,
        name="adjoint",
    )(*src_ids, *parts)


def shards(spectra, window_keep, owners, pair_src, pair_rec, pair_count, observed):
    columns, cores, places = lax.axis_size("win"), lax.axis_size("freq"), lax.axis_size("recv")
    column, core, place = lax.axis_index("win"), lax.axis_index("freq"), lax.axis_index("recv")
    assert spectra.shape[0] == 1 and cores == 2
    channels, bins_dev = spectra.shape[2:]
    blocks, slots, lag_dev = observed.shape
    lag_total = lag_dev * columns * cores
    bin_total = bins_dev * cores
    period = 2 * bin_total
    part = bins_dev // columns
    classes = part // LANES
    span = period // classes
    geometry = (classes, span, lag_total // span, lag_total // 2, period, 256)
    lag_scale = 1.0 / math.sqrt(bin_total * columns)
    peers = columns * cores
    some = slots // CHUNKS
    shifts = range(places)

    held = [
        swapped(
            lax.dynamic_slice(
                spectra, (0, 0, 0, (column ^ s) * part), (1, 2, channels, part)
            ),
            "win",
            columns,
            s,
        )
        for s in range(1, columns)
    ]
    trig = tables(classes, span, period, bins_dev, columns, cores)
    scal, wanted, rec_ids, table = start(
        window_keep, owners, pair_count, pair_src, pair_rec, places, trig, classes, span, peers
    )
    if columns == 2:
        weight = jnp.ones((1,), F32)
    else:
        keeps = jnp.stack([swapped(window_keep[0], "win", columns, s) for s in range(columns)])
        ranked = jnp.argsort(-keeps)[: columns - 1].astype(jnp.int32)
        weight = keeps[ranked].astype(F32)
        scal = lax.dynamic_update_slice(scal, ranked, (ORDER,))

    direct = places == blocks
    src_ids = [swapped(x, "recv", places, d) for d, x in zip(shifts, wanted)]
    source = np.arange(part)
    perm = np.zeros((part, part), ml_dtypes.bfloat16)
    perm[source, source % classes * LANES + source // classes] = 1
    sent, own_rows = gather_rows(scal, spectra, held, jnp.asarray(perm), src_ids, rec_ids)
    arrived = [[swapped(x, "recv", places, d) for d, x in zip(shifts, rows)] for rows in sent]
    corrs, all_sums, returned = [], [], [[] for _ in shifts]
    after = scal
    for q in range(CHUNKS):
        rows = arrived[q]
        if not direct:
            stacked = jnp.stack(rows)
            rows = [
                lax.dynamic_index_in_dim(stacked, place ^ owners[b], 0, False)
                for b in range(blocks)
            ]
        keep, send = lag_parts(
            scal, weight, after, rows, own_rows, q * some, table, geometry, columns, lag_dev
        )
        own, *sends = add_cores(scal, keep, swapped(send, "freq", cores, 1))
        after = own
        more = [swapped(x, "win", columns, s + 1) for s, x in enumerate(sends)]
        corr, sums = lag_stats(scal, lag_scale, q, own, more, observed, blocks, some)
        sums = [swapped(sums, ("win", "freq"), peers, s) for s in range(peers)]
        grads = gradients(scal, lag_total, q, sums, corr, observed, blocks, some)
        if not direct:
            stacked = jnp.stack(list(grads) + [jnp.zeros_like(grads[0])])
            grads = []
            for d in shifts:
                block = jnp.int32(blocks)
                for b in range(blocks):
                    block = jnp.where(owners[b] == place ^ d, b, block)
                grads.append(lax.dynamic_index_in_dim(stacked, block, 0, False))
        for d, g in zip(shifts, grads):
            returned[d].append(swapped(g, "recv", places, d))
        corrs.append(corr)
        all_sums.append(sums)
    normed = normed_rows(scal, lag_total, all_sums, corrs, observed, blocks, some)
    adjoint = adjoint_rows(src_ids, [g for unit in returned for g in unit], channels)
    return (normed, adjoint)


def solution(mesh):
    return jax.shard_map(
        shards,
        mesh=mesh,
        in_specs=(
            P("win", None, ("groups", "recv"), "freq"),
            P(("groups", "win")),
            P("groups"),
            P(None, ("groups", "recv")),
            P(None, ("groups", "recv")),
            P(None, ("groups", "recv")),
            P(None, ("groups", "recv"), ("win", "freq")),
        ),
        out_specs=(
            P(None, ("groups", "recv"), ("win", "freq")),
            P(("groups", "recv"), ("win", "freq")),
        ),
        check_vma=False,
    )
```

```python
import functools
import math

import jax
import jax.numpy as jnp
import ml_dtypes
import numpy as np
from jax import lax
from jax.experimental import pallas as pl
from jax.experimental.pallas import tpu as pltpu
from jax.sharding import PartitionSpec as P

EPSILON = 1e-06
MIB = 1 << 20
LANES = 128
CORE, COLUMN, ORDER, BLOCK, COUNT = 0, 1, 2, 8, 16
BF16 = jnp.bfloat16
F32 = jnp.float32
VMEM = pl.BlockSpec(memory_space=pltpu.VMEM)
SMEM = pl.BlockSpec(memory_space=pltpu.SMEM)
HBM = pl.BlockSpec(memory_space=pltpu.HBM)


def swapped(value, axis, size, step):
    assert size & (size - 1) == 0
    if step == 0:
        return value
    return lax.ppermute(value, axis, [(i, i ^ step) for i in range(size)])


def params(mib):
    return pltpu.CompilerParams(vmem_limit_bytes=mib * MIB)


SMALL = pl.CostEstimate(flops=1, bytes_accessed=1, transcendentals=0)
LARGE = pl.CostEstimate(flops=10**12, bytes_accessed=64 * MIB, transcendentals=0)


def tables(classes, span, period, bins_dev, columns, cores):
    u = np.arange(span, dtype=np.int64)[None, :]
    piece = np.arange(columns * cores, dtype=np.int64)[:, None]
    first = piece % cores * bins_dev + piece // cores * (bins_dev // columns)
    rows = (first + np.arange(classes)).reshape(-1)
    high = 16 * classes * np.arange(LANES // 16, dtype=np.int64)
    low = classes * np.arange(16, dtype=np.int64)
    angle = (np.concatenate([rows, high, low])[:, None] * u % period) * (2.0 * math.pi / period)
    return np.stack([np.cos(angle), np.sin(angle)]).astype(np.float32)


def fetch(pairs, sems):
    copies = [pltpu.make_async_copy(a, b, sems.at[i]) for i, (a, b) in enumerate(pairs)]
    for c in copies:
        c.start()
    for c in copies:
        c.wait()


def index_kernel(blocks, direct, *refs):
    given, refs = refs[:5], refs[5:]
    scal, wanted, rec_ids, held, sems = refs[0], refs[1:-7], refs[-7], refs[-6:-1], refs[-1]
    fetch(zip(given, held), sems)
    window_keep, owners, pair_count, src, rec = held
    place = lax.axis_index("recv")
    column, columns = lax.axis_index("win"), lax.axis_size("win")
    core = lax.axis_index("freq")
    scal[CORE] = core
    scal[COLUMN] = column
    scal[ORDER] = 1 - window_keep[0]
    for b in range(blocks):
        unit = place ^ owners[b] if direct else b
        scal[BLOCK + unit] = b
        scal[COUNT + unit] = pair_count[b]
    for d, out in enumerate(wanted):
        chosen = jnp.full(out.shape, -1, jnp.int32)
        received = jnp.zeros(out.shape, jnp.int32)
        for b in range(blocks):
            mine = jnp.full(out.shape, owners[b], jnp.int32) == (place ^ d)
            chosen = jnp.where(mine, src[b : b + 1], chosen)
            received = jnp.where(mine, rec[b : b + 1], received)
        out[...] = chosen
        if direct:
            rec_ids[d : d + 1] = received
    if not direct:
        rec_ids[...] = rec[...]


def index(window_keep, owners, pair_count, pair_src, pair_rec, places):
    blocks, slots = pair_src.shape
    ids = jax.ShapeDtypeStruct((1, slots), jnp.int32)
    given = [window_keep, owners, pair_count[:, 0], pair_src, pair_rec]
    scal, *wanted, rec_ids = pl.pallas_call(
        functools.partial(index_kernel, blocks, places == blocks),
        out_shape=[jax.ShapeDtypeStruct((LANES,), jnp.int32)]
        + [ids] * places
        + [jax.ShapeDtypeStruct(pair_rec.shape, jnp.int32)],
        in_specs=[HBM] * 5,
        out_specs=[SMEM] + [VMEM] * (places + 1),
        scratch_shapes=[pltpu.SMEM(g.shape, g.dtype) for g in given[:3]]
        + [pltpu.VMEM(g.shape, g.dtype) for g in given[3:]]
        + [pltpu.SemaphoreType.DMA((5,))],
        compiler_params=params(16),
        cost_estimate=SMALL,
        name="index",
    )(*given)
    return scal, wanted, rec_ids


def table_kernel(classes, parts, scal, given, spectra, table, perm, here, trig, base, sems):
    part = here.shape[-1]
    bins = pl.ds(pl.multiple_of(scal[COLUMN] * part, part), part)
    fetch([(given, trig), (spectra.at[0, :, :, bins], here)], sems)
    rows = parts * classes
    low = slice(rows + LANES // 16, rows + LANES // 16 + 16)
    cl, sl = trig[0, low], trig[1, low]
    for h in range(LANES // 16):
        ch, sh = trig[0, rows + h : rows + h + 1], trig[1, rows + h : rows + h + 1]
        base[0, 16 * h : 16 * h + 16] = ch * cl - sh * sl
        base[1, 16 * h : 16 * h + 16] = sh * cl + ch * sl
    first = (scal[CORE] + 2 * scal[COLUMN]) * classes
    cb, sb = base[0], base[1]
    for r in range(classes):
        ca, sa = trig[0, pl.ds(first + r, 1)], trig[1, pl.ds(first + r, 1)]
        table[r, :LANES] = (ca * cb - sa * sb).astype(BF16)
        table[r, LANES:] = (-(sa * cb + ca * sb)).astype(BF16)
    source = lax.broadcasted_iota(jnp.int32, (part, LANES), 0)
    target = classes * lax.broadcasted_iota(jnp.int32, (part, LANES), 1)
    for r in range(classes):
        perm[:, r * LANES : (r + 1) * LANES] = (source == target + r).astype(BF16)


def make_table(scal, spectra, trig, classes, span, parts, part):
    channels = spectra.shape[2]
    return pl.pallas_call(
        functools.partial(table_kernel, classes, parts),
        out_shape=[
            jax.ShapeDtypeStruct((classes, 2 * LANES, span), BF16),
            jax.ShapeDtypeStruct((part, part), BF16),
            jax.ShapeDtypeStruct((2, channels, part), BF16),
        ],
        in_specs=[SMEM, HBM, HBM],
        out_specs=[VMEM] * 3,
        scratch_shapes=[
            pltpu.VMEM(trig.shape, F32),
            pltpu.VMEM((2, LANES, span), F32),
            pltpu.SemaphoreType.DMA((2,)),
        ],
        compiler_params=params(24),
        cost_estimate=SMALL,
        name="table",
    )(scal, jnp.asarray(trig), spectra)


def picks(ids, channels):
    row = jnp.concatenate([i[...] for i in ids], axis=1)
    return (lax.broadcasted_iota(jnp.int32, (channels, row.shape[1]), 0) == row).astype(BF16)


def rows_kernel(used, sends, messages, scal, here, *refs):
    held, refs = refs[:used], refs[used:]
    perm, src_ids, rec_ids, refs = refs[0], refs[1 : 1 + sends], refs[1 + sends], refs[2 + sends :]
    outs, own_out = refs[:-1], refs[-1]
    units, _, _, slots, part = own_out.shape
    channels = here.shape[1]
    pick = picks(list(src_ids) + [rec_ids.at[d : d + 1] for d in range(units)], channels)
    for u in range(used):
        for half in range(2):
            x = here[half]
            for s in range(used):
                x = jnp.where(scal[ORDER + u] == s + 1, held[s][0, half], x)
            x = jnp.dot(x, perm[...], preferred_element_type=F32).astype(BF16)
            y = lax.dot_general(
                pick, x, (((0,), (0,)), ((), ())), preferred_element_type=F32
            ).astype(BF16)
            for (d, first, count), out in zip(messages, outs):
                at = d * slots + first
                out[u, half] = y[at : at + count]
            for d in range(units):
                at = (sends + d) * slots
                own_out[d, u, half] = y[at : at + slots]


def gather_rows(scal, here, held, perm, src_ids, rec_ids, messages):
    used, sends = len(held), len(src_ids)
    part = held[0].shape[-1]
    units, slots = rec_ids.shape
    *sent, own = pl.pallas_call(
        functools.partial(rows_kernel, used, sends, messages),
        out_shape=[jax.ShapeDtypeStruct((used, 2, m[2], part), BF16) for m in messages]
        + [jax.ShapeDtypeStruct((units, used, 2, slots, part), BF16)],
        in_specs=[SMEM] + [VMEM] * (used + 3 + sends),
        out_specs=[VMEM] * (len(messages) + 1),
        compiler_params=params(32),
        cost_estimate=SMALL,
        name="rows",
    )(scal, here, *held, perm, *src_ids, rec_ids)
    return sent, own


def combine(values, classes, outputs, origin, span, period):
    plain, scaled = [None] * outputs, [None] * outputs

    def add(into, k, value, sign):
        if into[k] is None:
            into[k] = value if sign > 0 else -value
        else:
            into[k] = into[k] + value if sign > 0 else into[k] - value

    for r, (real, imag) in enumerate(values):
        both = None
        for k in range(outputs):
            eighths = r * (span * k - origin) * 8 // period % 8
            assert r * (span * k - origin) * 8 % period == 0
            if eighths % 2 == 0:
                value, sign = ((real, 1), (imag, -1), (real, -1), (imag, 1))[eighths // 2]
                add(plain, k, value, sign)
            else:
                if both is None:
                    both = real + imag, real - imag
                value, sign = ((both[1], 1), (both[0], -1), (both[1], -1), (both[0], 1))[eighths // 2]
                add(scaled, k, value, sign)
    root = math.sqrt(0.5)
    return [a if b is None else a + root * b for a, b in zip(plain, scaled)]


def placed(pieces):
    at = 0
    for unit, first, count in pieces:
        yield unit, first, count, slice(at, at + count)
        at += count


def cross_kernel(pieces, weight, *refs):
    s_refs, own, lhs = refs[:-2], refs[-2], refs[-1]
    used = own.shape[1]
    rows = lhs.shape[1] // 2
    for s_ref, (unit, first, count, at) in zip(s_refs, placed(pieces)):
        turned = slice(rows + at.start, rows + at.stop)
        mine = slice(first, first + count)
        sent = mine if s_ref.shape[2] > count else slice(0, count)
        for r in range(lhs.shape[0]):
            bins = slice(r * LANES, (r + 1) * LANES)
            real = imag = None
            for u in range(used):
                sr, si = (s_ref[u, half, sent, bins].astype(F32) for half in range(2))
                rr, ri = (own[unit, u, half, mine, bins].astype(F32) for half in range(2))
                re, im = sr * rr + si * ri, si * rr - sr * ri
                if u:
                    re, im = real + weight[u] * re, imag + weight[u] * im
                real, imag = re, im
            lhs[r, at, :LANES] = real.astype(BF16)
            lhs[r, at, LANES:] = imag.astype(BF16)
            lhs[r, turned, :LANES] = imag.astype(BF16)
            lhs[r, turned, LANES:] = (-real).astype(BF16)


def cross_rows(weight, rows, own, pieces, classes):
    count = sum(p[2] for p in pieces)
    return pl.pallas_call(
        functools.partial(cross_kernel, pieces),
        out_shape=jax.ShapeDtypeStruct((classes, 2 * count, 2 * LANES), BF16),
        in_specs=[SMEM] + [VMEM] * (len(rows) + 1),
        out_specs=VMEM,
        compiler_params=params(16),
        cost_estimate=LARGE,
        name="cross",
    )(weight, *rows, own)


def lags_kernel(geometry, direct, skip, scal, *refs):
    classes, span, outputs, origin, period, chunk = geometry
    lhs, table, keep, *sends, sums = refs[skip:]
    rows = lhs.shape[1] // 2
    lag_dev = keep.shape[-1]
    cores = 2
    for start in range(0, span, chunk):
        values = []
        for r in range(classes):
            y = jnp.dot(lhs[r], table[r, :, start : start + chunk], preferred_element_type=F32)
            values.append((y[:rows], y[rows:]))
        for k, value in enumerate(combine(values, classes, outputs, origin, span, period)):
            lag = span * k + start
            lags = slice(lag % lag_dev, lag % lag_dev + chunk)
            sums[lag // lag_dev, :, lags] = value
    if direct:
        piece = cores * scal[COLUMN] + scal[CORE]
        keep[...] = sums[piece]
        for d, out in enumerate(sends):
            out[...] = sums[piece ^ (d + 1)].astype(BF16)
    else:
        for column in range(keep.shape[0]):
            keep[column] = sums[cores * column + scal[CORE]]
            sends[0][column] = sums[cores * column + 1 - scal[CORE]].astype(BF16)


def lag_parts(scal, after, lhs, table, geometry, columns, lag_dev, direct):
    shape = (lhs.shape[1] // 2, lag_dev)
    pieces = 2 * columns
    if direct:
        outs = [jax.ShapeDtypeStruct(shape, F32)] + [jax.ShapeDtypeStruct(shape, BF16)] * (pieces - 1)
    else:
        outs = [jax.ShapeDtypeStruct((columns, *shape), t) for t in (F32, BF16)]
    return pl.pallas_call(
        functools.partial(lags_kernel, geometry, direct, len(after)),
        out_shape=outs,
        in_specs=[SMEM] + [pl.BlockSpec(memory_space=pl.ANY)] * len(after) + [VMEM] * 2,
        out_specs=[VMEM] * len(outs),
        scratch_shapes=[pltpu.VMEM((pieces, *shape), F32)],
        compiler_params=params(32),
        cost_estimate=SMALL,
        name="lags",
    )(scal, *after, lhs, table)


def cores_kernel(scal, keep, more, own, *sends):
    columns = keep.shape[0]
    for column in range(columns):
        value = keep[column] + more[column].astype(F32)

        @pl.when(scal[COLUMN] == column)
        def _():
            own[...] = value

        for s, out in enumerate(sends):

            @pl.when(scal[COLUMN] ^ (s + 1) == column)
            def _():
                out[...] = value.astype(BF16)


def add_cores(scal, keep, more):
    columns, rows, lag_dev = keep.shape
    return pl.pallas_call(
        cores_kernel,
        out_shape=[jax.ShapeDtypeStruct((rows, lag_dev), F32)]
        + [jax.ShapeDtypeStruct((rows, lag_dev), BF16)] * (columns - 1),
        in_specs=[SMEM, VMEM, VMEM],
        out_specs=[VMEM] * columns,
        compiler_params=params(16),
        cost_estimate=SMALL,
        name="cores",
    )(scal, keep, more)


def stats_kernel(scale, pieces, others, scal, *refs):
    own, more, refs = refs[0], refs[1 : 1 + others], refs[1 + others :]
    targets, (corr, sums) = refs[: len(pieces)], refs[len(pieces) :]
    columns = []
    for target, (unit, first, count, at) in zip(targets, placed(pieces)):
        value = own[at]
        for m in more:
            value = value + m[at].astype(F32)
        slot = first + lax.broadcasted_iota(jnp.int32, (count, 1), 0)
        value = value * jnp.where(slot < scal[COUNT + unit], scale, 0.0)
        corr[at] = value
        square = jnp.sum(value * value, axis=1, keepdims=True)
        product = jnp.sum(value * target[0], axis=1, keepdims=True)
        lane = lax.broadcasted_iota(jnp.int32, (count, LANES), 1)
        columns.append(jnp.where(lane == 0, square, jnp.where(lane == 1, product, 0.0)))
    sums[...] = jnp.concatenate(columns, axis=0).T[:8]


def target_specs(pieces, lag_dev):
    return [
        pl.BlockSpec(
            (1, count, lag_dev),
            lambda i, scal, unit=unit, block=first // count: (scal[BLOCK + unit], block, 0),
        )
        for unit, first, count in pieces
    ]


def whole(shape):
    return pl.BlockSpec(shape, lambda i, scal: (0,) * len(shape))


def lag_stats(scal, scale, pieces, own, more, observed):
    rows, lag_dev = own.shape
    outs = [jax.ShapeDtypeStruct((rows, lag_dev), F32), jax.ShapeDtypeStruct((8, rows), F32)]
    return pl.pallas_call(
        functools.partial(stats_kernel, scale, pieces, len(more)),
        grid_spec=pltpu.PrefetchScalarGridSpec(
            num_scalar_prefetch=1,
            grid=(1,),
            in_specs=[whole(own.shape)] * (1 + len(more)) + target_specs(pieces, lag_dev),
            out_specs=[whole(o.shape) for o in outs],
        ),
        out_shape=outs,
        compiler_params=params(16),
        cost_estimate=SMALL,
        name="stats",
    )(scal, own, *more, *[observed] * len(pieces))


def slot_scales(sums, lag_total):
    total = sums[0][...]
    for s in sums[1:]:
        total = total + s[...]
    rows = total.shape[1]
    square, product = total[0:1], total[1:2]
    inverse = 1.0 / jnp.sqrt(square / lag_total + EPSILON)
    bending = (square * inverse * inverse - product * inverse) / lag_total
    sub = lax.broadcasted_iota(jnp.int32, (LANES, rows), 0)
    both = jnp.where(sub == 0, inverse, jnp.where(sub == 1, bending, 0.0)).T
    return both[:, 0:1], both[:, 1:2]


def gradient_kernel(lag_total, pieces, parts, scal, *refs):
    sums, corr, refs = refs[:parts], refs[parts], refs[parts + 1 :]
    targets, outs = refs[: len(pieces)], refs[len(pieces) :]
    inverse, bending = slot_scales(sums, lag_total)
    for target, out, (unit, first, count, at) in zip(targets, outs, placed(pieces)):
        slot = first + lax.broadcasted_iota(jnp.int32, (count, 1), 0)
        valid = jnp.where(slot < scal[COUNT + unit], inverse[at], 0.0)
        normed = corr[at] * inverse[at]
        out[...] = ((normed - target[0] - normed * bending[at]) * valid).astype(BF16)


def gradients(scal, lag_total, pieces, sums, corr, observed):
    lag_dev = corr.shape[1]
    outs = [jax.ShapeDtypeStruct((p[2], lag_dev), BF16) for p in pieces]
    return pl.pallas_call(
        functools.partial(gradient_kernel, lag_total, pieces, len(sums)),
        grid_spec=pltpu.PrefetchScalarGridSpec(
            num_scalar_prefetch=1,
            grid=(1,),
            in_specs=[whole(sums[0].shape)] * len(sums)
            + [whole(corr.shape)]
            + target_specs(pieces, lag_dev),
            out_specs=[whole(o.shape) for o in outs],
        ),
        out_shape=outs,
        compiler_params=params(16),
        cost_estimate=SMALL,
        name="gradient",
    )(scal, *sums, corr, *[observed] * len(pieces))


def normed_kernel(lag_total, chunks, parts, scal, *refs):
    out = refs[-1]
    for q, pieces in enumerate(chunks):
        sums, corr = refs[q * (parts + 1) : q * (parts + 1) + parts], refs[q * (parts + 1) + parts]
        inverse, _ = slot_scales(sums, lag_total)
        for unit, first, count, at in placed(pieces):

            @pl.when(pl.program_id(0) == unit)
            def _():
                out[0, first : first + count] = corr[at] * inverse[at]


def normed_rows(scal, lag_total, chunks, sums, corr, observed):
    blocks, slots, lag_dev = observed.shape
    ins = [x for s, c in zip(sums, corr) for x in (*s, c)]
    return pl.pallas_call(
        functools.partial(normed_kernel, lag_total, chunks, len(sums[0])),
        grid_spec=pltpu.PrefetchScalarGridSpec(
            num_scalar_prefetch=1,
            grid=(blocks,),
            in_specs=[whole(x.shape) for x in ins],
            out_specs=pl.BlockSpec((1, slots, lag_dev), lambda i, scal: (scal[BLOCK + i], 0, 0)),
        ),
        out_shape=jax.ShapeDtypeStruct(observed.shape, F32),
        compiler_params=params(16),
        cost_estimate=SMALL,
        name="normed",
    )(scal, *ins)


def adjoint_kernel(pieces, *refs):
    ids, parts, out = refs[: len(pieces)], refs[len(pieces) : -1], refs[-1]
    pick = picks([i.at[:, p[1] : p[1] + p[2]] for i, p in zip(ids, pieces)], out.shape[0])
    rows = jnp.concatenate([p[...] for p in parts], axis=0)
    out[...] = jnp.dot(pick, rows, preferred_element_type=F32)


def adjoint_rows(src_ids, pieces, parts, channels):
    lag_dev = parts[0].shape[1]
    return pl.pallas_call(
        functools.partial(adjoint_kernel, pieces),
        out_shape=jax.ShapeDtypeStruct((channels, lag_dev), F32),
        in_specs=[VMEM] * (2 * len(parts)),
        out_specs=VMEM,
        compiler_params=params(16),
        cost_estimate=SMALL,
        name="adjoint",
    )(*[src_ids[p[0]] for p in pieces], *parts)


def shards(spectra, window_keep, owners, pair_src, pair_rec, pair_count, observed):
    columns, cores, places = lax.axis_size("win"), lax.axis_size("freq"), lax.axis_size("recv")
    column, core, place = lax.axis_index("win"), lax.axis_index("freq"), lax.axis_index("recv")
    assert spectra.shape[0] == 1 and cores == 2
    channels, bins_dev = spectra.shape[2:]
    blocks, slots, lag_dev = observed.shape
    lag_total = lag_dev * columns * cores
    bin_total = bins_dev * cores
    period = 2 * bin_total
    part = bins_dev // columns
    classes = part // LANES
    span = period // classes
    geometry = (classes, span, lag_total // span, lag_total // 2, period, 256)
    lag_scale = 1.0 / math.sqrt(bin_total * columns)
    peers = columns * cores
    some = slots // 2
    shifts = range(places)

    held = [
        swapped(
            lax.dynamic_slice(
                spectra, (0, 0, 0, (column ^ s) * part), (1, 2, channels, part)
            ),
            "win",
            columns,
            s,
        )
        for s in range(1, columns)
    ]
    scal, wanted, rec_ids = index(
        window_keep, owners, pair_count, pair_src, pair_rec, places
    )
    if columns == 2:
        weight = jnp.ones((1,), F32)
    else:
        keeps = jnp.stack([swapped(window_keep[0], "win", columns, s) for s in range(columns)])
        ranked = jnp.argsort(-keeps)[: columns - 1].astype(jnp.int32)
        weight = keeps[ranked].astype(F32)
        scal = lax.dynamic_update_slice(scal, ranked, (ORDER,))

    direct = places == blocks
    src_ids = [swapped(x, "recv", places, d) for d, x in zip(shifts, wanted)]
    trig = tables(classes, span, period, bins_dev, columns, cores)
    table, perm, here = make_table(scal, spectra, trig, classes, span, peers, part)
    if direct and blocks == 4:
        chunks = [
            [(1, 0, slots), (2, 0, some), (3, 0, some)],
            [(0, 0, slots), (2, some, some), (3, some, some)],
        ]
    else:
        chunks = [[(d, first, some) for d in range(blocks)] for first in (0, some)]
    if direct:
        messages = [piece for pieces in chunks for piece in pieces]
    else:
        messages = [(d, 0, slots) for d in shifts]
    sent, own_rows = gather_rows(scal, here, held, perm, src_ids, rec_ids, messages)
    arrived = [swapped(x, "recv", places, m[0]) for m, x in zip(messages, sent)]
    if not direct:
        stacked = jnp.stack(arrived)
        whole_rows = [
            lax.dynamic_index_in_dim(stacked, place ^ owners[b], 0, False) for b in range(blocks)
        ]
        arrived = [whole_rows[piece[0]] for pieces in chunks for piece in pieces]
    corrs, all_sums, returned, returned_pieces = [], [], [], []
    after = []
    for q, pieces in enumerate(chunks):
        rows = arrived[len(pieces) * q : len(pieces) * (q + 1)]
        straight = q < len(chunks) - 1
        lhs = cross_rows(weight, rows, own_rows, pieces, classes)
        own, *sends = lag_parts(scal, after, lhs, table, geometry, columns, lag_dev, straight)
        if straight:
            more = [swapped(x, ("win", "freq"), peers, d + 1) for d, x in enumerate(sends)]
            after = more
        else:
            own, *sends = add_cores(scal, own, swapped(sends[0], "freq", cores, 1))
            more = [swapped(x, "win", columns, s + 1) for s, x in enumerate(sends)]
        corr, sums = lag_stats(scal, lag_scale, pieces, own, more, observed)
        sums = [swapped(sums, ("win", "freq"), peers, s) for s in range(peers)]
        grads = gradients(scal, lag_total, pieces, sums, corr, observed)
        if not direct:
            stacked = jnp.stack(list(grads) + [jnp.zeros_like(grads[0])])
            grads = []
            for d in shifts:
                block = jnp.int32(blocks)
                for b in range(blocks):
                    block = jnp.where(owners[b] == place ^ d, b, block)
                grads.append(lax.dynamic_index_in_dim(stacked, block, 0, False))
            pieces = [(d, pieces[0][1], some) for d in shifts]
        returned += [swapped(g, "recv", places, p[0]) for p, g in zip(pieces, grads)]
        returned_pieces += pieces
        corrs.append(corr)
        all_sums.append(sums)
    normed = normed_rows(scal, lag_total, chunks, all_sums, corrs, observed)
    adjoint = adjoint_rows(src_ids, returned_pieces, returned, channels)
    return (normed, adjoint)


def solution(mesh):
    return jax.shard_map(
        shards,
        mesh=mesh,
        in_specs=(
            P("win", None, ("groups", "recv"), "freq"),
            P(("groups", "win")),
            P("groups"),
            P(None, ("groups", "recv")),
            P(None, ("groups", "recv")),
            P(None, ("groups", "recv")),
            P(None, ("groups", "recv"), ("win", "freq")),
        ),
        out_specs=(
            P(None, ("groups", "recv"), ("win", "freq")),
            P(("groups", "recv"), ("win", "freq")),
        ),
        check_vma=False,
    )
```

```python
import functools
import math

import jax
import jax.numpy as jnp
import ml_dtypes
import numpy as np
from jax import lax
from jax.experimental import pallas as pl
from jax.experimental.pallas import tpu as pltpu
from jax.sharding import PartitionSpec as P

EPSILON = 1e-06
MIB = 1 << 20
LANES = 128
SPLIT = 4
CORE, COLUMN, ORDER, BLOCK, COUNT = 0, 1, 2, 8, 16
BF16 = jnp.bfloat16
F32 = jnp.float32
VMEM = pl.BlockSpec(memory_space=pltpu.VMEM)
SMEM = pl.BlockSpec(memory_space=pltpu.SMEM)
HBM = pl.BlockSpec(memory_space=pltpu.HBM)


def swapped(value, axis, size, step):
    assert size & (size - 1) == 0
    if step == 0:
        return value
    return lax.ppermute(value, axis, [(i, i ^ step) for i in range(size)])


def params(mib):
    return pltpu.CompilerParams(vmem_limit_bytes=mib * MIB)


SMALL = pl.CostEstimate(flops=1, bytes_accessed=1, transcendentals=0)
LARGE = pl.CostEstimate(flops=2 * 10**10, bytes_accessed=MIB, transcendentals=0)


def tables(classes, span, period, bins_dev, columns, cores):
    u = np.arange(span, dtype=np.int64)[None, :]
    piece = np.arange(columns * cores, dtype=np.int64)[:, None]
    first = piece % cores * bins_dev + piece // cores * (bins_dev // columns)
    rows = (first + np.arange(classes)).reshape(-1)
    high = 16 * classes * np.arange(LANES // 16, dtype=np.int64)
    low = classes * np.arange(16, dtype=np.int64)
    angle = (np.concatenate([rows, high, low])[:, None] * u % period) * (2.0 * math.pi / period)
    return np.stack([np.cos(angle), np.sin(angle)]).astype(np.float32)


def fetch(pairs, sems):
    copies = [pltpu.make_async_copy(a, b, sems.at[i]) for i, (a, b) in enumerate(pairs)]
    for c in copies:
        c.start()
    for c in copies:
        c.wait()


def index_kernel(blocks, direct, *refs):
    given, refs = refs[:5], refs[5:]
    scal, wanted, rec_ids, held, sems = refs[0], refs[1:-7], refs[-7], refs[-6:-1], refs[-1]
    fetch(zip(given, held), sems)
    window_keep, owners, pair_count, src, rec = held
    place = lax.axis_index("recv")
    column, columns = lax.axis_index("win"), lax.axis_size("win")
    core = lax.axis_index("freq")
    scal[CORE] = core
    scal[COLUMN] = column
    scal[ORDER] = 1 - window_keep[0]
    for b in range(blocks):
        unit = place ^ owners[b] if direct else b
        scal[BLOCK + unit] = b
        scal[COUNT + unit] = pair_count[b]
    for d, out in enumerate(wanted):
        chosen = jnp.full(out.shape, -1, jnp.int32)
        received = jnp.zeros(out.shape, jnp.int32)
        for b in range(blocks):
            mine = jnp.full(out.shape, owners[b], jnp.int32) == (place ^ d)
            chosen = jnp.where(mine, src[b : b + 1], chosen)
            received = jnp.where(mine, rec[b : b + 1], received)
        out[...] = chosen
        if direct:
            rec_ids[d : d + 1] = received
    if not direct:
        rec_ids[...] = rec[...]


def index(window_keep, owners, pair_count, pair_src, pair_rec, places):
    blocks, slots = pair_src.shape
    ids = jax.ShapeDtypeStruct((1, slots), jnp.int32)
    given = [window_keep, owners, pair_count[:, 0], pair_src, pair_rec]
    scal, *wanted, rec_ids = pl.pallas_call(
        functools.partial(index_kernel, blocks, places == blocks),
        out_shape=[jax.ShapeDtypeStruct((LANES,), jnp.int32)]
        + [ids] * places
        + [jax.ShapeDtypeStruct(pair_rec.shape, jnp.int32)],
        in_specs=[HBM] * 5,
        out_specs=[SMEM] + [VMEM] * (places + 1),
        scratch_shapes=[pltpu.SMEM(g.shape, g.dtype) for g in given[:3]]
        + [pltpu.VMEM(g.shape, g.dtype) for g in given[3:]]
        + [pltpu.SemaphoreType.DMA((5,))],
        compiler_params=params(16),
        cost_estimate=SMALL,
        name="index",
    )(*given)
    return scal, wanted, rec_ids


def table_kernel(classes, parts, scal, trig, table, base):
    rows = parts * classes
    low = slice(rows + LANES // 16, rows + LANES // 16 + 16)
    cl, sl = trig[0, low], trig[1, low]
    for h in range(LANES // 16):
        ch, sh = trig[0, rows + h : rows + h + 1], trig[1, rows + h : rows + h + 1]
        base[0, 16 * h : 16 * h + 16] = ch * cl - sh * sl
        base[1, 16 * h : 16 * h + 16] = sh * cl + ch * sl
    first = (scal[CORE] + 2 * scal[COLUMN]) * classes
    cb, sb = base[0], base[1]
    for r in range(classes):
        ca, sa = trig[0, pl.ds(first + r, 1)], trig[1, pl.ds(first + r, 1)]
        table[r, :LANES] = (ca * cb - sa * sb).astype(BF16)
        table[r, LANES:] = (-(sa * cb + ca * sb)).astype(BF16)


def make_table(scal, trig, classes, span, parts):
    return pl.pallas_call(
        functools.partial(table_kernel, classes, parts),
        out_shape=jax.ShapeDtypeStruct((classes, 2 * LANES, span), BF16),
        in_specs=[SMEM, VMEM],
        out_specs=VMEM,
        scratch_shapes=[pltpu.VMEM((2, LANES, span), F32)],
        compiler_params=params(12),
        cost_estimate=SMALL,
        name="table",
    )(scal, jnp.asarray(trig))


def perm_kernel(perm):
    part = perm.shape[0]
    classes = part // LANES
    source = lax.broadcasted_iota(jnp.int32, (part, LANES), 0)
    target = classes * lax.broadcasted_iota(jnp.int32, (part, LANES), 1)
    for r in range(classes):
        perm[:, r * LANES : (r + 1) * LANES] = (source == target + r).astype(BF16)


def make_perm(part):
    return pl.pallas_call(
        perm_kernel,
        out_shape=jax.ShapeDtypeStruct((part, part), BF16),
        out_specs=VMEM,
        compiler_params=params(8),
        cost_estimate=SMALL,
        name="perm",
    )()


def picks(ids, channels):
    row = jnp.concatenate([i[...] for i in ids], axis=1)
    return (lax.broadcasted_iota(jnp.int32, (channels, row.shape[1]), 0) == row).astype(BF16)


def rows_kernel(used, sends, messages, scal, here, *refs):
    held, refs = refs[:used], refs[used:]
    perm, src_ids, rec_ids, refs = refs[0], refs[1 : 1 + sends], refs[1 + sends], refs[2 + sends :]
    outs, own_out = refs[:-1], refs[-1]
    units, _, _, slots, part = own_out.shape
    channels = here.shape[2]
    pick = picks(list(src_ids) + [rec_ids.at[d : d + 1] for d in range(units)], channels)
    for u in range(used):
        for half in range(2):
            x = here[0, half]
            for s in range(used):
                x = jnp.where(scal[ORDER + u] == s + 1, held[s][0, half], x)
            x = jnp.dot(x, perm[...], preferred_element_type=F32).astype(BF16)
            y = lax.dot_general(
                pick, x, (((0,), (0,)), ((), ())), preferred_element_type=F32
            ).astype(BF16)
            for (d, first, count), out in zip(messages, outs):
                at = d * slots + first
                out[u, half] = y[at : at + count]
            for d in range(units):
                at = (sends + d) * slots
                own_out[d, u, half] = y[at : at + slots]


def gather_rows(scal, here, held, perm, src_ids, rec_ids, messages):
    used, sends = len(held), len(src_ids)
    part = held[0].shape[-1]
    units, slots = rec_ids.shape
    *sent, own = pl.pallas_call(
        functools.partial(rows_kernel, used, sends, messages),
        out_shape=[jax.ShapeDtypeStruct((used, 2, m[2], part), BF16) for m in messages]
        + [jax.ShapeDtypeStruct((units, used, 2, slots, part), BF16)],
        in_specs=[SMEM] + [VMEM] * (used + 3 + sends),
        out_specs=[VMEM] * (len(messages) + 1),
        compiler_params=params(16),
        cost_estimate=SMALL,
        name="rows",
    )(scal, here, *held, perm, *src_ids, rec_ids)
    return sent, own


def combine(values, classes, outputs, origin, span, period):
    plain, scaled = [None] * outputs, [None] * outputs

    def add(into, k, value, sign):
        if into[k] is None:
            into[k] = value if sign > 0 else -value
        else:
            into[k] = into[k] + value if sign > 0 else into[k] - value

    for r, (real, imag) in enumerate(values):
        both = None
        for k in range(outputs):
            eighths = r * (span * k - origin) * 8 // period % 8
            assert r * (span * k - origin) * 8 % period == 0
            if eighths % 2 == 0:
                value, sign = ((real, 1), (imag, -1), (real, -1), (imag, 1))[eighths // 2]
                add(plain, k, value, sign)
            else:
                if both is None:
                    both = real + imag, real - imag
                value, sign = ((both[1], 1), (both[0], -1), (both[1], -1), (both[0], 1))[eighths // 2]
                add(scaled, k, value, sign)
    root = math.sqrt(0.5)
    return [a if b is None else a + root * b for a, b in zip(plain, scaled)]


def placed(pieces):
    at = 0
    for unit, first, count in pieces:
        yield unit, first, count, slice(at, at + count)
        at += count


def cross_kernel(pieces, weight, *refs):
    s_refs, own, lhs = refs[:-2], refs[-2], refs[-1]
    used = own.shape[1]
    rows = lhs.shape[1] // 2
    for s_ref, (unit, first, count, at) in zip(s_refs, placed(pieces)):
        turned = slice(rows + at.start, rows + at.stop)
        mine = slice(first, first + count)
        sent = mine if s_ref.shape[2] > count else slice(0, count)
        for r in range(lhs.shape[0]):
            bins = slice(r * LANES, (r + 1) * LANES)
            real = imag = None
            for u in range(used):
                sr, si = (s_ref[u, half, sent, bins].astype(F32) for half in range(2))
                rr, ri = (own[unit, u, half, mine, bins].astype(F32) for half in range(2))
                re, im = sr * rr + si * ri, si * rr - sr * ri
                if u:
                    re, im = real + weight[u] * re, imag + weight[u] * im
                real, imag = re, im
            lhs[r, at, :LANES] = real.astype(BF16)
            lhs[r, at, LANES:] = imag.astype(BF16)
            lhs[r, turned, :LANES] = imag.astype(BF16)
            lhs[r, turned, LANES:] = (-real).astype(BF16)


def cross_rows(weight, rows, own, pieces, classes):
    count = sum(p[2] for p in pieces)
    return pl.pallas_call(
        functools.partial(cross_kernel, pieces),
        out_shape=jax.ShapeDtypeStruct((classes, 2 * count, 2 * LANES), BF16),
        in_specs=[SMEM] + [VMEM] * (len(rows) + 1),
        out_specs=VMEM,
        compiler_params=params(8),
        cost_estimate=LARGE,
        name="cross",
    )(weight, *rows, own)


def lags_kernel(geometry, skip, scal, *refs):
    classes, span, outputs, origin, period, chunk = geometry
    lhs, table, keep, *sends, sums = refs[skip:]
    rows = lhs.shape[1] // 2
    lag_dev = keep.shape[-1]
    cores = 2
    for start in range(0, span, chunk):
        values = []
        for r in range(classes):
            y = jnp.dot(lhs[r], table[r, :, start : start + chunk], preferred_element_type=F32)
            values.append((y[:rows], y[rows:]))
        for k, value in enumerate(combine(values, classes, outputs, origin, span, period)):
            lag = span * k + start
            lags = slice(lag % lag_dev, lag % lag_dev + chunk)
            sums[lag // lag_dev, :, lags] = value
    for column in range(keep.shape[0]):
        keep[column] = sums[cores * column + scal[CORE]]
        for i, out in enumerate(sends):
            at = slice(i * out.shape[1], (i + 1) * out.shape[1])
            out[column] = sums[cores * column + 1 - scal[CORE], at].astype(BF16)


def lag_parts(scal, after, lhs, table, geometry, columns, lag_dev, split):
    rows = lhs.shape[1] // 2
    shape = lambda count: (columns, count, lag_dev)
    return pl.pallas_call(
        functools.partial(lags_kernel, geometry, len(after)),
        out_shape=[jax.ShapeDtypeStruct(shape(rows), F32)]
        + [jax.ShapeDtypeStruct(shape(rows // split), BF16)] * split,
        in_specs=[SMEM] + [pl.BlockSpec(memory_space=pl.ANY)] * len(after) + [VMEM] * 2,
        out_specs=[VMEM] * (split + 1),
        scratch_shapes=[pltpu.VMEM((2 * columns, rows, lag_dev), F32)],
        compiler_params=params(16),
        cost_estimate=LARGE,
        name="lags",
    )(scal, *after, lhs, table)


def cores_kernel(skip, split, scal, *refs):
    keep, *refs = refs[skip:]
    more, own, sends = refs[:split], refs[split], refs[split + 1 :]
    columns = keep.shape[0]
    for i, m in enumerate(more):
        at = slice(i * m.shape[1], (i + 1) * m.shape[1])
        for column in range(columns):
            value = keep[column, at] + m[column].astype(F32)

            @pl.when(scal[COLUMN] == column)
            def _():
                own[at] = value

            for s, out in enumerate(sends):

                @pl.when(scal[COLUMN] ^ (s + 1) == column)
                def _():
                    out[at] = value.astype(BF16)


def add_cores(scal, after, keep, more):
    columns, rows, lag_dev = keep.shape
    return pl.pallas_call(
        functools.partial(cores_kernel, len(after), len(more)),
        out_shape=[jax.ShapeDtypeStruct((rows, lag_dev), F32)]
        + [jax.ShapeDtypeStruct((rows, lag_dev), BF16)] * (columns - 1),
        in_specs=[SMEM] + [pl.BlockSpec(memory_space=pl.ANY)] * len(after) + [VMEM] * (1 + len(more)),
        out_specs=[VMEM] * columns,
        compiler_params=params(8),
        cost_estimate=SMALL,
        name="cores",
    )(scal, *after, keep, *more)


def stats_kernel(scale, pieces, others, scal, *refs):
    own, more, refs = refs[0], refs[1 : 1 + others], refs[1 + others :]
    targets, (corr, sums) = refs[: len(pieces)], refs[len(pieces) :]
    columns = []
    for target, (unit, first, count, at) in zip(targets, placed(pieces)):
        value = own[at]
        for m in more:
            value = value + m[at].astype(F32)
        slot = first + lax.broadcasted_iota(jnp.int32, (count, 1), 0)
        value = value * jnp.where(slot < scal[COUNT + unit], scale, 0.0)
        corr[at] = value
        square = jnp.sum(value * value, axis=1, keepdims=True)
        product = jnp.sum(value * target[0], axis=1, keepdims=True)
        lane = lax.broadcasted_iota(jnp.int32, (count, LANES), 1)
        columns.append(jnp.where(lane == 0, square, jnp.where(lane == 1, product, 0.0)))
    sums[...] = jnp.concatenate(columns, axis=0).T[:8]


def target_specs(pieces, lag_dev):
    return [
        pl.BlockSpec(
            (1, count, lag_dev),
            lambda i, scal, unit=unit, block=first // count: (scal[BLOCK + unit], block, 0),
        )
        for unit, first, count in pieces
    ]


def whole(shape):
    return pl.BlockSpec(shape, lambda i, scal: (0,) * len(shape))


def lag_stats(scal, scale, pieces, own, more, observed):
    rows, lag_dev = own.shape
    outs = [jax.ShapeDtypeStruct((rows, lag_dev), F32), jax.ShapeDtypeStruct((8, rows), F32)]
    return pl.pallas_call(
        functools.partial(stats_kernel, scale, pieces, len(more)),
        grid_spec=pltpu.PrefetchScalarGridSpec(
            num_scalar_prefetch=1,
            grid=(1,),
            in_specs=[whole(own.shape)] * (1 + len(more)) + target_specs(pieces, lag_dev),
            out_specs=[whole(o.shape) for o in outs],
        ),
        out_shape=outs,
        compiler_params=params(16),
        cost_estimate=SMALL,
        name="stats",
    )(scal, own, *more, *[observed] * len(pieces))


def slot_scales(sums, lag_total):
    total = sums[0][...]
    for s in sums[1:]:
        total = total + s[...]
    rows = total.shape[1]
    square, product = total[0:1], total[1:2]
    inverse = 1.0 / jnp.sqrt(square / lag_total + EPSILON)
    bending = (square * inverse * inverse - product * inverse) / lag_total
    sub = lax.broadcasted_iota(jnp.int32, (LANES, rows), 0)
    both = jnp.where(sub == 0, inverse, jnp.where(sub == 1, bending, 0.0)).T
    return both[:, 0:1], both[:, 1:2]


def gradient_kernel(lag_total, pieces, parts, scal, *refs):
    sums, corr, refs = refs[:parts], refs[parts], refs[parts + 1 :]
    targets, outs = refs[: len(pieces)], refs[len(pieces) :]
    inverse, bending = slot_scales(sums, lag_total)
    for target, out, (unit, first, count, at) in zip(targets, outs, placed(pieces)):
        slot = first + lax.broadcasted_iota(jnp.int32, (count, 1), 0)
        valid = jnp.where(slot < scal[COUNT + unit], inverse[at], 0.0)
        normed = corr[at] * inverse[at]
        out[...] = ((normed - target[0] - normed * bending[at]) * valid).astype(BF16)


def gradients(scal, lag_total, pieces, sums, corr, observed):
    lag_dev = corr.shape[1]
    outs = [jax.ShapeDtypeStruct((p[2], lag_dev), BF16) for p in pieces]
    return pl.pallas_call(
        functools.partial(gradient_kernel, lag_total, pieces, len(sums)),
        grid_spec=pltpu.PrefetchScalarGridSpec(
            num_scalar_prefetch=1,
            grid=(1,),
            in_specs=[whole(sums[0].shape)] * len(sums)
            + [whole(corr.shape)]
            + target_specs(pieces, lag_dev),
            out_specs=[whole(o.shape) for o in outs],
        ),
        out_shape=outs,
        compiler_params=params(16),
        cost_estimate=SMALL,
        name="gradient",
    )(scal, *sums, corr, *[observed] * len(pieces))


def normed_kernel(lag_total, chunks, parts, scal, *refs):
    out = refs[-1]
    for q, pieces in enumerate(chunks):
        sums, corr = refs[q * (parts + 1) : q * (parts + 1) + parts], refs[q * (parts + 1) + parts]
        inverse, _ = slot_scales(sums, lag_total)
        for unit, first, count, at in placed(pieces):

            @pl.when(pl.program_id(0) == unit)
            def _():
                out[0, first : first + count] = corr[at] * inverse[at]


def normed_rows(scal, lag_total, chunks, sums, corr, observed):
    blocks, slots, lag_dev = observed.shape
    ins = [x for s, c in zip(sums, corr) for x in (*s, c)]
    return pl.pallas_call(
        functools.partial(normed_kernel, lag_total, chunks, len(sums[0])),
        grid_spec=pltpu.PrefetchScalarGridSpec(
            num_scalar_prefetch=1,
            grid=(blocks,),
            in_specs=[whole(x.shape) for x in ins],
            out_specs=pl.BlockSpec((1, slots, lag_dev), lambda i, scal: (scal[BLOCK + i], 0, 0)),
        ),
        out_shape=jax.ShapeDtypeStruct(observed.shape, F32),
        compiler_params=params(16),
        cost_estimate=SMALL,
        name="normed",
    )(scal, *ins)


def adjoint_kernel(pieces, *refs):
    ids, parts, out = refs[: len(pieces)], refs[len(pieces) : -1], refs[-1]
    pick = picks([i.at[:, p[1] : p[1] + p[2]] for i, p in zip(ids, pieces)], out.shape[0])
    rows = jnp.concatenate([p[...] for p in parts], axis=0)
    out[...] = jnp.dot(pick, rows, preferred_element_type=F32)


def adjoint_rows(src_ids, pieces, parts, channels):
    lag_dev = parts[0].shape[1]
    return pl.pallas_call(
        functools.partial(adjoint_kernel, pieces),
        out_shape=jax.ShapeDtypeStruct((channels, lag_dev), F32),
        in_specs=[VMEM] * (2 * len(parts)),
        out_specs=VMEM,
        compiler_params=params(16),
        cost_estimate=SMALL,
        name="adjoint",
    )(*[src_ids[p[0]] for p in pieces], *parts)


def shards(spectra, window_keep, owners, pair_src, pair_rec, pair_count, observed):
    columns, cores, places = lax.axis_size("win"), lax.axis_size("freq"), lax.axis_size("recv")
    column, core, place = lax.axis_index("win"), lax.axis_index("freq"), lax.axis_index("recv")
    assert spectra.shape[0] == 1 and cores == 2
    channels, bins_dev = spectra.shape[2:]
    blocks, slots, lag_dev = observed.shape
    lag_total = lag_dev * columns * cores
    bin_total = bins_dev * cores
    period = 2 * bin_total
    part = bins_dev // columns
    classes = part // LANES
    span = period // classes
    geometry = (classes, span, lag_total // span, lag_total // 2, period, 256)
    lag_scale = 1.0 / math.sqrt(bin_total * columns)
    peers = columns * cores
    some = slots // 2
    shifts = range(places)

    held = [
        swapped(
            lax.dynamic_slice(
                spectra, (0, 0, 0, (column ^ s) * part), (1, 2, channels, part)
            ),
            "win",
            columns,
            s,
        )
        for s in range(columns)
    ]
    scal, wanted, rec_ids = index(
        window_keep, owners, pair_count, pair_src, pair_rec, places
    )
    if columns == 2:
        weight = jnp.ones((1,), F32)
    else:
        keeps = jnp.stack([swapped(window_keep[0], "win", columns, s) for s in range(columns)])
        ranked = jnp.argsort(-keeps)[: columns - 1].astype(jnp.int32)
        weight = keeps[ranked].astype(F32)
        scal = lax.dynamic_update_slice(scal, ranked, (ORDER,))

    direct = places == blocks
    src_ids = [swapped(x, "recv", places, d) for d, x in zip(shifts, wanted)]
    trig = tables(classes, span, period, bins_dev, columns, cores)
    table = make_table(scal, trig, classes, span, peers)
    if direct and blocks == 4:
        chunks = [
            [(1, 0, slots), (2, 0, some), (3, 0, some)],
            [(0, 0, slots), (2, some, some), (3, some, some)],
        ]
    else:
        chunks = [[(d, first, some) for d in range(blocks)] for first in (0, some)]
    if direct:
        messages = [piece for pieces in chunks for piece in pieces]
    else:
        messages = [(d, 0, slots) for d in shifts]
    sent, own_rows = gather_rows(
        scal, held[0], held[1:], make_perm(part), src_ids, rec_ids, messages
    )
    arrived = [swapped(x, "recv", places, m[0]) for m, x in zip(messages, sent)]
    if not direct:
        stacked = jnp.stack(arrived)
        whole_rows = [
            lax.dynamic_index_in_dim(stacked, place ^ owners[b], 0, False) for b in range(blocks)
        ]
        arrived = [whole_rows[piece[0]] for pieces in chunks for piece in pieces]
    corrs, all_sums, returned, returned_pieces = [], [], [], []
    after = []
    for q, pieces in enumerate(chunks):
        rows = arrived[len(pieces) * q : len(pieces) * (q + 1)]
        lhs = cross_rows(weight, rows, own_rows, pieces, classes)
        keep, *sends = lag_parts(
            scal, after[:1], lhs, table, geometry, columns, lag_dev, SPLIT if q else 1
        )
        sends = [swapped(x, "freq", cores, 1) for x in sends]
        own, *sends = add_cores(scal, after[1:], keep, sends)
        more = [swapped(x, "win", columns, s + 1) for s, x in enumerate(sends)]
        after = [own, *more]
        corr, sums = lag_stats(scal, lag_scale, pieces, own, more, observed)
        sums = [swapped(sums, ("win", "freq"), peers, s) for s in range(peers)]
        grads = gradients(scal, lag_total, pieces, sums, corr, observed)
        if not direct:
            stacked = jnp.stack(list(grads) + [jnp.zeros_like(grads[0])])
            grads = []
            for d in shifts:
                block = jnp.int32(blocks)
                for b in range(blocks):
                    block = jnp.where(owners[b] == place ^ d, b, block)
                grads.append(lax.dynamic_index_in_dim(stacked, block, 0, False))
            pieces = [(d, pieces[0][1], some) for d in shifts]
        returned += [swapped(g, "recv", places, p[0]) for p, g in zip(pieces, grads)]
        returned_pieces += pieces
        corrs.append(corr)
        all_sums.append(sums)
    normed = normed_rows(scal, lag_total, chunks, all_sums, corrs, observed)
    adjoint = adjoint_rows(src_ids, returned_pieces, returned, channels)
    return (normed, adjoint)


def solution(mesh):
    return jax.shard_map(
        shards,
        mesh=mesh,
        in_specs=(
            P("win", None, ("groups", "recv"), "freq"),
            P(("groups", "win")),
            P("groups"),
            P(None, ("groups", "recv")),
            P(None, ("groups", "recv")),
            P(None, ("groups", "recv")),
            P(None, ("groups", "recv"), ("win", "freq")),
        ),
        out_specs=(
            P(None, ("groups", "recv"), ("win", "freq")),
            P(("groups", "recv"), ("win", "freq")),
        ),
        check_vma=False,
    )
```

```python
import functools
import math

import jax
import jax.numpy as jnp
import ml_dtypes
import numpy as np
from jax import lax
from jax.experimental import pallas as pl
from jax.experimental.pallas import tpu as pltpu
from jax.sharding import PartitionSpec as P

EPSILON = 1e-06
MIB = 1 << 20
LANES = 128
SPLIT = 4
CORE, COLUMN, ORDER, BLOCK, COUNT = 0, 1, 2, 8, 16
BF16 = jnp.bfloat16
F32 = jnp.float32
VMEM = pl.BlockSpec(memory_space=pltpu.VMEM)
SMEM = pl.BlockSpec(memory_space=pltpu.SMEM)
HBM = pl.BlockSpec(memory_space=pltpu.HBM)


def swapped(value, axis, size, step):
    assert size & (size - 1) == 0
    if step == 0:
        return value
    return lax.ppermute(value, axis, [(i, i ^ step) for i in range(size)])


def params(mib):
    return pltpu.CompilerParams(vmem_limit_bytes=mib * MIB)


SMALL = pl.CostEstimate(flops=1, bytes_accessed=1, transcendentals=0)
LARGE = pl.CostEstimate(flops=2 * 10**10, bytes_accessed=MIB, transcendentals=0)


def tables(classes, span, period, bins_dev, columns, cores):
    u = np.arange(span, dtype=np.int64)[None, :]
    piece = np.arange(columns * cores, dtype=np.int64)[:, None]
    first = piece % cores * bins_dev + piece // cores * (bins_dev // columns)
    rows = (first + np.arange(classes)).reshape(-1)
    high = 16 * classes * np.arange(LANES // 16, dtype=np.int64)
    low = classes * np.arange(16, dtype=np.int64)
    angle = (np.concatenate([rows, high, low])[:, None] * u % period) * (2.0 * math.pi / period)
    return np.stack([np.cos(angle), np.sin(angle)]).astype(np.float32)


def fetch(pairs, sems):
    copies = [pltpu.make_async_copy(a, b, sems.at[i]) for i, (a, b) in enumerate(pairs)]
    for c in copies:
        c.start()
    for c in copies:
        c.wait()


def index_kernel(blocks, direct, *refs):
    given, refs = refs[:5], refs[5:]
    scal, wanted, rec_ids, held, sems = refs[0], refs[1:-7], refs[-7], refs[-6:-1], refs[-1]
    fetch(zip(given, held), sems)
    window_keep, owners, pair_count, src, rec = held
    place = lax.axis_index("recv")
    column, columns = lax.axis_index("win"), lax.axis_size("win")
    core = lax.axis_index("freq")
    scal[CORE] = core
    scal[COLUMN] = column
    scal[ORDER] = 1 - window_keep[0]
    for b in range(blocks):
        unit = place ^ owners[b] if direct else b
        scal[BLOCK + unit] = b
        scal[COUNT + unit] = pair_count[b]
    for d, out in enumerate(wanted):
        chosen = jnp.full(out.shape, -1, jnp.int32)
        received = jnp.zeros(out.shape, jnp.int32)
        for b in range(blocks):
            mine = jnp.full(out.shape, owners[b], jnp.int32) == (place ^ d)
            chosen = jnp.where(mine, src[b : b + 1], chosen)
            received = jnp.where(mine, rec[b : b + 1], received)
        out[...] = chosen
        if direct:
            rec_ids[d : d + 1] = received
    if not direct:
        rec_ids[...] = rec[...]


def index(window_keep, owners, pair_count, pair_src, pair_rec, places):
    blocks, slots = pair_src.shape
    ids = jax.ShapeDtypeStruct((1, slots), jnp.int32)
    given = [window_keep, owners, pair_count[:, 0], pair_src, pair_rec]
    scal, *wanted, rec_ids = pl.pallas_call(
        functools.partial(index_kernel, blocks, places == blocks),
        out_shape=[jax.ShapeDtypeStruct((LANES,), jnp.int32)]
        + [ids] * places
        + [jax.ShapeDtypeStruct(pair_rec.shape, jnp.int32)],
        in_specs=[HBM] * 5,
        out_specs=[SMEM] + [VMEM] * (places + 1),
        scratch_shapes=[pltpu.SMEM(g.shape, g.dtype) for g in given[:3]]
        + [pltpu.VMEM(g.shape, g.dtype) for g in given[3:]]
        + [pltpu.SemaphoreType.DMA((5,))],
        compiler_params=params(16),
        cost_estimate=SMALL,
        name="index",
    )(*given)
    return scal, wanted, rec_ids


def table_kernel(classes, parts, scal, trig, table, base):
    rows = parts * classes
    low = slice(rows + LANES // 16, rows + LANES // 16 + 16)
    cl, sl = trig[0, low], trig[1, low]
    for h in range(LANES // 16):
        ch, sh = trig[0, rows + h : rows + h + 1], trig[1, rows + h : rows + h + 1]
        base[0, 16 * h : 16 * h + 16] = ch * cl - sh * sl
        base[1, 16 * h : 16 * h + 16] = sh * cl + ch * sl
    first = (scal[CORE] + 2 * scal[COLUMN]) * classes
    cb, sb = base[0], base[1]
    for r in range(classes):
        ca, sa = trig[0, pl.ds(first + r, 1)], trig[1, pl.ds(first + r, 1)]
        table[r, :LANES] = (ca * cb - sa * sb).astype(BF16)
        table[r, LANES:] = (-(sa * cb + ca * sb)).astype(BF16)


def make_table(scal, trig, classes, span, parts):
    return pl.pallas_call(
        functools.partial(table_kernel, classes, parts),
        out_shape=jax.ShapeDtypeStruct((classes, 2 * LANES, span), BF16),
        in_specs=[SMEM, VMEM],
        out_specs=VMEM,
        scratch_shapes=[pltpu.VMEM((2, LANES, span), F32)],
        compiler_params=params(12),
        cost_estimate=SMALL,
        name="table",
    )(scal, jnp.asarray(trig))


def perm_kernel(perm):
    part = perm.shape[0]
    classes = part // LANES
    source = lax.broadcasted_iota(jnp.int32, (part, LANES), 0)
    target = classes * lax.broadcasted_iota(jnp.int32, (part, LANES), 1)
    for r in range(classes):
        perm[:, r * LANES : (r + 1) * LANES] = (source == target + r).astype(BF16)


def make_perm(part):
    return pl.pallas_call(
        perm_kernel,
        out_shape=jax.ShapeDtypeStruct((part, part), BF16),
        out_specs=VMEM,
        compiler_params=params(8),
        cost_estimate=SMALL,
        name="perm",
    )()


def picks(ids, channels):
    row = jnp.concatenate([i[...] for i in ids], axis=1)
    return (lax.broadcasted_iota(jnp.int32, (channels, row.shape[1]), 0) == row).astype(BF16)


def rows_kernel(used, sends, messages, scal, after, here, *refs):
    held, refs = refs[:used], refs[used:]
    perm, src_ids, rec_ids, refs = refs[0], refs[1 : 1 + sends], refs[1 + sends], refs[2 + sends :]
    outs, own_out = refs[:-1], refs[-1]
    units, _, _, slots, part = own_out.shape
    channels = here.shape[2]
    pick = picks(list(src_ids) + [rec_ids.at[d : d + 1] for d in range(units)], channels)
    for u in range(used):
        for half in range(2):
            x = here[0, half]
            for s in range(used):
                x = jnp.where(scal[ORDER + u] == s + 1, held[s][0, half], x)
            x = jnp.dot(x, perm[...], preferred_element_type=F32).astype(BF16)
            y = lax.dot_general(
                pick, x, (((0,), (0,)), ((), ())), preferred_element_type=F32
            ).astype(BF16)
            for (d, first, count), out in zip(messages, outs):
                at = d * slots + first
                out[u, half] = y[at : at + count]
            for d in range(units):
                at = (sends + d) * slots
                own_out[d, u, half] = y[at : at + slots]


def gather_rows(scal, after, here, held, perm, src_ids, rec_ids, messages):
    used, sends = len(held), len(src_ids)
    part = held[0].shape[-1]
    units, slots = rec_ids.shape
    *sent, own = pl.pallas_call(
        functools.partial(rows_kernel, used, sends, messages),
        out_shape=[jax.ShapeDtypeStruct((used, 2, m[2], part), BF16) for m in messages]
        + [jax.ShapeDtypeStruct((units, used, 2, slots, part), BF16)],
        in_specs=[SMEM, pl.BlockSpec(memory_space=pl.ANY)] + [VMEM] * (used + 3 + sends),
        out_specs=[VMEM] * (len(messages) + 1),
        compiler_params=params(16),
        cost_estimate=SMALL,
        name="rows",
    )(scal, after, here, *held, perm, *src_ids, rec_ids)
    return sent, own


def combine(values, classes, outputs, origin, span, period):
    plain, scaled = [None] * outputs, [None] * outputs

    def add(into, k, value, sign):
        if into[k] is None:
            into[k] = value if sign > 0 else -value
        else:
            into[k] = into[k] + value if sign > 0 else into[k] - value

    for r, (real, imag) in enumerate(values):
        both = None
        for k in range(outputs):
            eighths = r * (span * k - origin) * 8 // period % 8
            assert r * (span * k - origin) * 8 % period == 0
            if eighths % 2 == 0:
                value, sign = ((real, 1), (imag, -1), (real, -1), (imag, 1))[eighths // 2]
                add(plain, k, value, sign)
            else:
                if both is None:
                    both = real + imag, real - imag
                value, sign = ((both[1], 1), (both[0], -1), (both[1], -1), (both[0], 1))[eighths // 2]
                add(scaled, k, value, sign)
    root = math.sqrt(0.5)
    return [a if b is None else a + root * b for a, b in zip(plain, scaled)]


def placed(pieces):
    at = 0
    for unit, first, count in pieces:
        yield unit, first, count, slice(at, at + count)
        at += count


def cross_kernel(pieces, skip, weight, *refs):
    refs = refs[skip:]
    s_refs, own, lhs = refs[:-2], refs[-2], refs[-1]
    used = own.shape[1]
    rows = lhs.shape[1] // 2
    for s_ref, (unit, first, count, at) in zip(s_refs, placed(pieces)):
        turned = slice(rows + at.start, rows + at.stop)
        mine = slice(first, first + count)
        sent = mine if s_ref.shape[2] > count else slice(0, count)
        for r in range(lhs.shape[0]):
            bins = slice(r * LANES, (r + 1) * LANES)
            real = imag = None
            for u in range(used):
                sr, si = (s_ref[u, half, sent, bins].astype(F32) for half in range(2))
                rr, ri = (own[unit, u, half, mine, bins].astype(F32) for half in range(2))
                re, im = sr * rr + si * ri, si * rr - sr * ri
                if u:
                    re, im = real + weight[u] * re, imag + weight[u] * im
                real, imag = re, im
            lhs[r, at, :LANES] = real.astype(BF16)
            lhs[r, at, LANES:] = imag.astype(BF16)
            lhs[r, turned, :LANES] = imag.astype(BF16)
            lhs[r, turned, LANES:] = (-real).astype(BF16)


def cross_rows(weight, after, rows, own, pieces, classes):
    count = sum(p[2] for p in pieces)
    return pl.pallas_call(
        functools.partial(cross_kernel, pieces, len(after)),
        out_shape=jax.ShapeDtypeStruct((classes, 2 * count, 2 * LANES), BF16),
        in_specs=[SMEM] + [pl.BlockSpec(memory_space=pl.ANY)] * len(after) + [VMEM] * (len(rows) + 1),
        out_specs=VMEM,
        compiler_params=params(8),
        cost_estimate=LARGE,
        name="cross",
    )(weight, *after, *rows, own)


def lags_kernel(geometry, skip, scal, *refs):
    classes, span, outputs, origin, period, chunk = geometry
    lhs, table, keep, *sends, sums = refs[skip:]
    rows = lhs.shape[1] // 2
    lag_dev = keep.shape[-1]
    cores = 2
    for start in range(0, span, chunk):
        values = []
        for r in range(classes):
            y = jnp.dot(lhs[r], table[r, :, start : start + chunk], preferred_element_type=F32)
            values.append((y[:rows], y[rows:]))
        for k, value in enumerate(combine(values, classes, outputs, origin, span, period)):
            lag = span * k + start
            lags = slice(lag % lag_dev, lag % lag_dev + chunk)
            sums[lag // lag_dev, :, lags] = value
    for column in range(keep.shape[0]):
        keep[column] = sums[cores * column + scal[CORE]]
        for i, out in enumerate(sends):
            at = slice(i * out.shape[1], (i + 1) * out.shape[1])
            out[column] = sums[cores * column + 1 - scal[CORE], at].astype(BF16)


def lag_parts(scal, after, lhs, table, geometry, columns, lag_dev, split, effort):
    rows = lhs.shape[1] // 2
    shape = lambda count: (columns, count, lag_dev)
    return pl.pallas_call(
        functools.partial(lags_kernel, geometry, len(after)),
        out_shape=[jax.ShapeDtypeStruct(shape(rows), F32)]
        + [jax.ShapeDtypeStruct(shape(rows // split), BF16)] * split,
        in_specs=[SMEM] + [pl.BlockSpec(memory_space=pl.ANY)] * len(after) + [VMEM] * 2,
        out_specs=[VMEM] * (split + 1),
        scratch_shapes=[pltpu.VMEM((2 * columns, rows, lag_dev), F32)],
        compiler_params=params(16),
        cost_estimate=effort,
        name="lags",
    )(scal, *after, lhs, table)


def cores_kernel(skip, split, scal, *refs):
    keep, *refs = refs[skip:]
    more, own, sends = refs[:split], refs[split], refs[split + 1 :]
    columns = keep.shape[0]
    for i, m in enumerate(more):
        at = slice(i * m.shape[1], (i + 1) * m.shape[1])
        for column in range(columns):
            value = keep[column, at] + m[column].astype(F32)

            @pl.when(scal[COLUMN] == column)
            def _():
                own[at] = value

            for s, out in enumerate(sends):

                @pl.when(scal[COLUMN] ^ (s + 1) == column)
                def _():
                    out[at] = value.astype(BF16)


def add_cores(scal, after, keep, more):
    columns, rows, lag_dev = keep.shape
    return pl.pallas_call(
        functools.partial(cores_kernel, len(after), len(more)),
        out_shape=[jax.ShapeDtypeStruct((rows, lag_dev), F32)]
        + [jax.ShapeDtypeStruct((rows, lag_dev), BF16)] * (columns - 1),
        in_specs=[SMEM] + [pl.BlockSpec(memory_space=pl.ANY)] * len(after) + [VMEM] * (1 + len(more)),
        out_specs=[VMEM] * columns,
        compiler_params=params(8),
        cost_estimate=SMALL,
        name="cores",
    )(scal, *after, keep, *more)


def stats_kernel(scale, pieces, others, scal, *refs):
    own, more, refs = refs[0], refs[1 : 1 + others], refs[1 + others :]
    targets, (corr, sums) = refs[: len(pieces)], refs[len(pieces) :]
    columns = []
    for target, (unit, first, count, at) in zip(targets, placed(pieces)):
        value = own[at]
        for m in more:
            value = value + m[at].astype(F32)
        slot = first + lax.broadcasted_iota(jnp.int32, (count, 1), 0)
        value = value * jnp.where(slot < scal[COUNT + unit], scale, 0.0)
        corr[at] = value
        square = jnp.sum(value * value, axis=1, keepdims=True)
        product = jnp.sum(value * target[0], axis=1, keepdims=True)
        lane = lax.broadcasted_iota(jnp.int32, (count, LANES), 1)
        columns.append(jnp.where(lane == 0, square, jnp.where(lane == 1, product, 0.0)))
    sums[...] = jnp.concatenate(columns, axis=0).T[:8]


def target_specs(pieces, lag_dev):
    return [
        pl.BlockSpec(
            (1, count, lag_dev),
            lambda i, scal, unit=unit, block=first // count: (scal[BLOCK + unit], block, 0),
        )
        for unit, first, count in pieces
    ]


def whole(shape):
    return pl.BlockSpec(shape, lambda i, scal: (0,) * len(shape))


def lag_stats(scal, scale, pieces, own, more, observed):
    rows, lag_dev = own.shape
    outs = [jax.ShapeDtypeStruct((rows, lag_dev), F32), jax.ShapeDtypeStruct((8, rows), F32)]
    return pl.pallas_call(
        functools.partial(stats_kernel, scale, pieces, len(more)),
        grid_spec=pltpu.PrefetchScalarGridSpec(
            num_scalar_prefetch=1,
            grid=(1,),
            in_specs=[whole(own.shape)] * (1 + len(more)) + target_specs(pieces, lag_dev),
            out_specs=[whole(o.shape) for o in outs],
        ),
        out_shape=outs,
        compiler_params=params(16),
        cost_estimate=SMALL,
        name="stats",
    )(scal, own, *more, *[observed] * len(pieces))


def slot_scales(sums, lag_total):
    total = sums[0][...]
    for s in sums[1:]:
        total = total + s[...]
    rows = total.shape[1]
    square, product = total[0:1], total[1:2]
    inverse = 1.0 / jnp.sqrt(square / lag_total + EPSILON)
    bending = (square * inverse * inverse - product * inverse) / lag_total
    sub = lax.broadcasted_iota(jnp.int32, (LANES, rows), 0)
    both = jnp.where(sub == 0, inverse, jnp.where(sub == 1, bending, 0.0)).T
    return both[:, 0:1], both[:, 1:2]


def gradient_kernel(lag_total, pieces, parts, scal, *refs):
    sums, corr, refs = refs[:parts], refs[parts], refs[parts + 1 :]
    targets, outs = refs[: len(pieces)], refs[len(pieces) :]
    inverse, bending = slot_scales(sums, lag_total)
    for target, out, (unit, first, count, at) in zip(targets, outs, placed(pieces)):
        slot = first + lax.broadcasted_iota(jnp.int32, (count, 1), 0)
        valid = jnp.where(slot < scal[COUNT + unit], inverse[at], 0.0)
        normed = corr[at] * inverse[at]
        out[...] = ((normed - target[0] - normed * bending[at]) * valid).astype(BF16)


def gradients(scal, lag_total, pieces, sums, corr, observed):
    lag_dev = corr.shape[1]
    outs = [jax.ShapeDtypeStruct((p[2], lag_dev), BF16) for p in pieces]
    return pl.pallas_call(
        functools.partial(gradient_kernel, lag_total, pieces, len(sums)),
        grid_spec=pltpu.PrefetchScalarGridSpec(
            num_scalar_prefetch=1,
            grid=(1,),
            in_specs=[whole(sums[0].shape)] * len(sums)
            + [whole(corr.shape)]
            + target_specs(pieces, lag_dev),
            out_specs=[whole(o.shape) for o in outs],
        ),
        out_shape=outs,
        compiler_params=params(16),
        cost_estimate=SMALL,
        name="gradient",
    )(scal, *sums, corr, *[observed] * len(pieces))


def normed_kernel(lag_total, chunks, parts, scal, *refs):
    out = refs[-1]
    for q, pieces in enumerate(chunks):
        sums, corr = refs[q * (parts + 1) : q * (parts + 1) + parts], refs[q * (parts + 1) + parts]
        inverse, _ = slot_scales(sums, lag_total)
        for unit, first, count, at in placed(pieces):

            @pl.when(pl.program_id(0) == unit)
            def _():
                out[0, first : first + count] = corr[at] * inverse[at]


def normed_rows(scal, lag_total, chunks, sums, corr, observed):
    blocks, slots, lag_dev = observed.shape
    ins = [x for s, c in zip(sums, corr) for x in (*s, c)]
    return pl.pallas_call(
        functools.partial(normed_kernel, lag_total, chunks, len(sums[0])),
        grid_spec=pltpu.PrefetchScalarGridSpec(
            num_scalar_prefetch=1,
            grid=(blocks,),
            in_specs=[whole(x.shape) for x in ins],
            out_specs=pl.BlockSpec((1, slots, lag_dev), lambda i, scal: (scal[BLOCK + i], 0, 0)),
        ),
        out_shape=jax.ShapeDtypeStruct(observed.shape, F32),
        compiler_params=params(16),
        cost_estimate=SMALL,
        name="normed",
    )(scal, *ins)


def adjoint_kernel(pieces, *refs):
    ids, parts, out = refs[: len(pieces)], refs[len(pieces) : -1], refs[-1]
    pick = picks([i.at[:, p[1] : p[1] + p[2]] for i, p in zip(ids, pieces)], out.shape[0])
    rows = jnp.concatenate([p[...] for p in parts], axis=0)
    out[...] = jnp.dot(pick, rows, preferred_element_type=F32)


def adjoint_rows(src_ids, pieces, parts, channels):
    lag_dev = parts[0].shape[1]
    return pl.pallas_call(
        functools.partial(adjoint_kernel, pieces),
        out_shape=jax.ShapeDtypeStruct((channels, lag_dev), F32),
        in_specs=[VMEM] * (2 * len(parts)),
        out_specs=VMEM,
        compiler_params=params(16),
        cost_estimate=SMALL,
        name="adjoint",
    )(*[src_ids[p[0]] for p in pieces], *parts)


def shards(spectra, window_keep, owners, pair_src, pair_rec, pair_count, observed):
    columns, cores, places = lax.axis_size("win"), lax.axis_size("freq"), lax.axis_size("recv")
    column, core, place = lax.axis_index("win"), lax.axis_index("freq"), lax.axis_index("recv")
    assert spectra.shape[0] == 1 and cores == 2
    channels, bins_dev = spectra.shape[2:]
    blocks, slots, lag_dev = observed.shape
    lag_total = lag_dev * columns * cores
    bin_total = bins_dev * cores
    period = 2 * bin_total
    part = bins_dev // columns
    classes = part // LANES
    span = period // classes
    geometry = (classes, span, lag_total // span, lag_total // 2, period, 256)
    lag_scale = 1.0 / math.sqrt(bin_total * columns)
    peers = columns * cores
    some = slots // 2
    shifts = range(places)

    held = [
        swapped(
            lax.dynamic_slice(
                spectra, (0, 0, 0, (column ^ s) * part), (1, 2, channels, part)
            ),
            "win",
            columns,
            s,
        )
        for s in range(columns)
    ]
    scal, wanted, rec_ids = index(
        window_keep, owners, pair_count, pair_src, pair_rec, places
    )
    if columns == 2:
        weight = jnp.ones((1,), F32)
    else:
        keeps = jnp.stack([swapped(window_keep[0], "win", columns, s) for s in range(columns)])
        ranked = jnp.argsort(-keeps)[: columns - 1].astype(jnp.int32)
        weight = keeps[ranked].astype(F32)
        scal = lax.dynamic_update_slice(scal, ranked, (ORDER,))

    direct = places == blocks
    src_ids = [swapped(x, "recv", places, d) for d, x in zip(shifts, wanted)]
    trig = tables(classes, span, period, bins_dev, columns, cores)
    table = make_table(scal, trig, classes, span, peers)
    if direct and blocks == 4:
        chunks = [
            [(0, 0, slots), (1, 0, slots)],
            [(2, 0, slots), (3, 0, slots)],
        ]
    else:
        chunks = [[(d, first, some) for d in range(blocks)] for first in (0, some)]
    if direct:
        messages = [piece for pieces in chunks for piece in pieces]
    else:
        messages = [(d, 0, slots) for d in shifts]
    sent, own_rows = gather_rows(
        scal, table, held[0], held[1:], make_perm(part), src_ids, rec_ids, messages
    )
    arrived = [swapped(x, "recv", places, m[0]) for m, x in zip(messages, sent)]
    if not direct:
        stacked = jnp.stack(arrived)
        whole_rows = [
            lax.dynamic_index_in_dim(stacked, place ^ owners[b], 0, False) for b in range(blocks)
        ]
        arrived = [whole_rows[piece[0]] for pieces in chunks for piece in pieces]
    corrs, all_sums, returned, returned_pieces = [], [], [], []
    after = []
    for q, pieces in enumerate(chunks):
        rows = arrived[len(pieces) * q : len(pieces) * (q + 1)]
        lhs = cross_rows(weight, after[:1], rows, own_rows, pieces, classes)
        keep, *sends = lag_parts(
            scal, [], lhs, table, geometry, columns, lag_dev, SPLIT if q else 2 * SPLIT, SMALL if q else LARGE
        )
        sends = [swapped(x, "freq", cores, 1) for x in sends]
        own, *sends = add_cores(scal, after[1:], keep, sends)
        more = [swapped(x, "win", columns, s + 1) for s, x in enumerate(sends)]
        after = [own, *more]
        corr, sums = lag_stats(scal, lag_scale, pieces, own, more, observed)
        sums = [swapped(sums, ("win", "freq"), peers, s) for s in range(peers)]
        grads = gradients(scal, lag_total, pieces, sums, corr, observed)
        if not direct:
            stacked = jnp.stack(list(grads) + [jnp.zeros_like(grads[0])])
            grads = []
            for d in shifts:
                block = jnp.int32(blocks)
                for b in range(blocks):
                    block = jnp.where(owners[b] == place ^ d, b, block)
                grads.append(lax.dynamic_index_in_dim(stacked, block, 0, False))
            pieces = [(d, pieces[0][1], some) for d in shifts]
        returned += [swapped(g, "recv", places, p[0]) for p, g in zip(pieces, grads)]
        returned_pieces += pieces
        corrs.append(corr)
        all_sums.append(sums)
    normed = normed_rows(scal, lag_total, chunks, all_sums, corrs, observed)
    adjoint = adjoint_rows(src_ids, returned_pieces, returned, channels)
    return (normed, adjoint)


def solution(mesh):
    return jax.shard_map(
        shards,
        mesh=mesh,
        in_specs=(
            P("win", None, ("groups", "recv"), "freq"),
            P(("groups", "win")),
            P("groups"),
            P(None, ("groups", "recv")),
            P(None, ("groups", "recv")),
            P(None, ("groups", "recv")),
            P(None, ("groups", "recv"), ("win", "freq")),
        ),
        out_specs=(
            P(None, ("groups", "recv"), ("win", "freq")),
            P(("groups", "recv"), ("win", "freq")),
        ),
        check_vma=False,
    )
```

```python
import functools
import math

import jax
import jax.numpy as jnp
import ml_dtypes
import numpy as np
from jax import lax
from jax.experimental import pallas as pl
from jax.experimental.pallas import tpu as pltpu
from jax.sharding import PartitionSpec as P

EPSILON = 1e-06
MIB = 1 << 20
LANES = 128
GROUP = (16, 32)
CORE, COLUMN, ORDER, BLOCK, COUNT = 0, 1, 2, 8, 16
BF16 = jnp.bfloat16
F32 = jnp.float32
VMEM = pl.BlockSpec(memory_space=pltpu.VMEM)
SMEM = pl.BlockSpec(memory_space=pltpu.SMEM)
HBM = pl.BlockSpec(memory_space=pltpu.HBM)


def swapped(value, axis, size, step):
    assert size & (size - 1) == 0
    if step == 0:
        return value
    return lax.ppermute(value, axis, [(i, i ^ step) for i in range(size)])


def params(mib):
    return pltpu.CompilerParams(vmem_limit_bytes=mib * MIB)


SMALL = pl.CostEstimate(flops=1, bytes_accessed=1, transcendentals=0)
LARGE = pl.CostEstimate(flops=2 * 10**10, bytes_accessed=MIB, transcendentals=0)


def tables(classes, span, period, bins_dev, columns, cores):
    u = np.arange(span, dtype=np.int64)[None, :]
    piece = np.arange(columns * cores, dtype=np.int64)[:, None]
    first = piece % cores * bins_dev + piece // cores * (bins_dev // columns)
    rows = (first + np.arange(classes)).reshape(-1)
    high = 16 * classes * np.arange(LANES // 16, dtype=np.int64)
    low = classes * np.arange(16, dtype=np.int64)
    angle = (np.concatenate([rows, high, low])[:, None] * u % period) * (2.0 * math.pi / period)
    return np.stack([np.cos(angle), np.sin(angle)]).astype(np.float32)


def fetch(pairs, sems):
    copies = [pltpu.make_async_copy(a, b, sems.at[i]) for i, (a, b) in enumerate(pairs)]
    for c in copies:
        c.start()
    for c in copies:
        c.wait()


def index_kernel(blocks, direct, *refs):
    given, refs = refs[:5], refs[5:]
    scal, wanted, rec_ids, held, sems = refs[0], refs[1:-7], refs[-7], refs[-6:-1], refs[-1]
    fetch(zip(given, held), sems)
    window_keep, owners, pair_count, src, rec = held
    place = lax.axis_index("recv")
    column, columns = lax.axis_index("win"), lax.axis_size("win")
    core = lax.axis_index("freq")
    scal[CORE] = core
    scal[COLUMN] = column
    scal[ORDER] = 1 - window_keep[0]
    for b in range(blocks):
        unit = place ^ owners[b] if direct else b
        scal[BLOCK + unit] = b
        scal[COUNT + unit] = pair_count[b]
    for d, out in enumerate(wanted):
        chosen = jnp.full(out.shape, -1, jnp.int32)
        received = jnp.zeros(out.shape, jnp.int32)
        for b in range(blocks):
            mine = jnp.full(out.shape, owners[b], jnp.int32) == (place ^ d)
            chosen = jnp.where(mine, src[b : b + 1], chosen)
            received = jnp.where(mine, rec[b : b + 1], received)
        out[...] = chosen
        if direct:
            rec_ids[d : d + 1] = received
    if not direct:
        rec_ids[...] = rec[...]


def index(window_keep, owners, pair_count, pair_src, pair_rec, places):
    blocks, slots = pair_src.shape
    ids = jax.ShapeDtypeStruct((1, slots), jnp.int32)
    given = [window_keep, owners, pair_count[:, 0], pair_src, pair_rec]
    scal, *wanted, rec_ids = pl.pallas_call(
        functools.partial(index_kernel, blocks, places == blocks),
        out_shape=[jax.ShapeDtypeStruct((LANES,), jnp.int32)]
        + [ids] * places
        + [jax.ShapeDtypeStruct(pair_rec.shape, jnp.int32)],
        in_specs=[HBM] * 5,
        out_specs=[SMEM] + [VMEM] * (places + 1),
        scratch_shapes=[pltpu.SMEM(g.shape, g.dtype) for g in given[:3]]
        + [pltpu.VMEM(g.shape, g.dtype) for g in given[3:]]
        + [pltpu.SemaphoreType.DMA((5,))],
        compiler_params=params(16),
        cost_estimate=SMALL,
        name="index",
    )(*given)
    return scal, wanted, rec_ids


def table_kernel(classes, parts, scal, trig, table, base):
    rows = parts * classes
    low = slice(rows + LANES // 16, rows + LANES // 16 + 16)
    cl, sl = trig[0, low], trig[1, low]
    for h in range(LANES // 16):
        ch, sh = trig[0, rows + h : rows + h + 1], trig[1, rows + h : rows + h + 1]
        base[0, 16 * h : 16 * h + 16] = ch * cl - sh * sl
        base[1, 16 * h : 16 * h + 16] = sh * cl + ch * sl
    first = (scal[CORE] + 2 * scal[COLUMN]) * classes
    cb, sb = base[0], base[1]
    for r in range(classes):
        ca, sa = trig[0, pl.ds(first + r, 1)], trig[1, pl.ds(first + r, 1)]
        table[r, :LANES] = (ca * cb - sa * sb).astype(BF16)
        table[r, LANES:] = (-(sa * cb + ca * sb)).astype(BF16)


def make_table(scal, trig, classes, span, parts):
    return pl.pallas_call(
        functools.partial(table_kernel, classes, parts),
        out_shape=jax.ShapeDtypeStruct((classes, 2 * LANES, span), BF16),
        in_specs=[SMEM, VMEM],
        out_specs=VMEM,
        scratch_shapes=[pltpu.VMEM((2, LANES, span), F32)],
        compiler_params=params(12),
        cost_estimate=SMALL,
        name="table",
    )(scal, jnp.asarray(trig))


def perm_kernel(perm):
    part = perm.shape[0]
    classes = part // LANES
    source = lax.broadcasted_iota(jnp.int32, (part, LANES), 0)
    target = classes * lax.broadcasted_iota(jnp.int32, (part, LANES), 1)
    for r in range(classes):
        perm[:, r * LANES : (r + 1) * LANES] = (source == target + r).astype(BF16)


def make_perm(part):
    return pl.pallas_call(
        perm_kernel,
        out_shape=jax.ShapeDtypeStruct((part, part), BF16),
        out_specs=VMEM,
        compiler_params=params(8),
        cost_estimate=SMALL,
        name="perm",
    )()


def picks(ids, channels):
    row = jnp.concatenate([i[...] for i in ids], axis=1)
    return (lax.broadcasted_iota(jnp.int32, (channels, row.shape[1]), 0) == row).astype(BF16)


def rows_kernel(used, sends, messages, scal, after, here, *refs):
    held, refs = refs[:used], refs[used:]
    perm, src_ids, rec_ids, refs = refs[0], refs[1 : 1 + sends], refs[1 + sends], refs[2 + sends :]
    outs, own_out = refs[:-1], refs[-1]
    units, _, _, slots, part = own_out.shape
    channels = here.shape[2]
    pick = picks(list(src_ids) + [rec_ids.at[d : d + 1] for d in range(units)], channels)
    for u in range(used):
        for half in range(2):
            x = here[0, half]
            for s in range(used):
                x = jnp.where(scal[ORDER + u] == s + 1, held[s][0, half], x)
            x = jnp.dot(x, perm[...], preferred_element_type=F32).astype(BF16)
            y = lax.dot_general(
                pick, x, (((0,), (0,)), ((), ())), preferred_element_type=F32
            ).astype(BF16)
            for (d, first, count), out in zip(messages, outs):
                at = d * slots + first
                out[u, half] = y[at : at + count]
            for d in range(units):
                at = (sends + d) * slots
                own_out[d, u, half] = y[at : at + slots]


def gather_rows(scal, after, here, held, perm, src_ids, rec_ids, messages):
    used, sends = len(held), len(src_ids)
    part = held[0].shape[-1]
    units, slots = rec_ids.shape
    *sent, own = pl.pallas_call(
        functools.partial(rows_kernel, used, sends, messages),
        out_shape=[jax.ShapeDtypeStruct((used, 2, m[2], part), BF16) for m in messages]
        + [jax.ShapeDtypeStruct((units, used, 2, slots, part), BF16)],
        in_specs=[SMEM, pl.BlockSpec(memory_space=pl.ANY)] + [VMEM] * (used + 3 + sends),
        out_specs=[VMEM] * (len(messages) + 1),
        compiler_params=params(16),
        cost_estimate=SMALL,
        name="rows",
    )(scal, after, here, *held, perm, *src_ids, rec_ids)
    return sent, own


def combine(values, classes, outputs, origin, span, period):
    plain, scaled = [None] * outputs, [None] * outputs

    def add(into, k, value, sign):
        if into[k] is None:
            into[k] = value if sign > 0 else -value
        else:
            into[k] = into[k] + value if sign > 0 else into[k] - value

    for r, (real, imag) in enumerate(values):
        both = None
        for k in range(outputs):
            eighths = r * (span * k - origin) * 8 // period % 8
            assert r * (span * k - origin) * 8 % period == 0
            if eighths % 2 == 0:
                value, sign = ((real, 1), (imag, -1), (real, -1), (imag, 1))[eighths // 2]
                add(plain, k, value, sign)
            else:
                if both is None:
                    both = real + imag, real - imag
                value, sign = ((both[1], 1), (both[0], -1), (both[1], -1), (both[0], 1))[eighths // 2]
                add(scaled, k, value, sign)
    root = math.sqrt(0.5)
    return [a if b is None else a + root * b for a, b in zip(plain, scaled)]


def placed(pieces):
    at = 0
    for unit, first, count in pieces:
        yield unit, first, count, slice(at, at + count)
        at += count


def cross_kernel(pieces, skip, weight, *refs):
    refs = refs[skip:]
    s_refs, own, lhs = refs[:-2], refs[-2], refs[-1]
    used = own.shape[1]
    rows = lhs.shape[1] // 2
    for s_ref, (unit, first, count, at) in zip(s_refs, placed(pieces)):
        turned = slice(rows + at.start, rows + at.stop)
        mine = slice(first, first + count)
        sent = mine if s_ref.shape[2] > count else slice(0, count)
        for r in range(lhs.shape[0]):
            bins = slice(r * LANES, (r + 1) * LANES)
            real = imag = None
            for u in range(used):
                sr, si = (s_ref[u, half, sent, bins].astype(F32) for half in range(2))
                rr, ri = (own[unit, u, half, mine, bins].astype(F32) for half in range(2))
                re, im = sr * rr + si * ri, si * rr - sr * ri
                if u:
                    re, im = real + weight[u] * re, imag + weight[u] * im
                real, imag = re, im
            lhs[r, at, :LANES] = real.astype(BF16)
            lhs[r, at, LANES:] = imag.astype(BF16)
            lhs[r, turned, :LANES] = imag.astype(BF16)
            lhs[r, turned, LANES:] = (-real).astype(BF16)


def cross_rows(weight, after, rows, own, pieces, classes):
    count = sum(p[2] for p in pieces)
    return pl.pallas_call(
        functools.partial(cross_kernel, pieces, len(after)),
        out_shape=jax.ShapeDtypeStruct((classes, 2 * count, 2 * LANES), BF16),
        in_specs=[SMEM] + [pl.BlockSpec(memory_space=pl.ANY)] * len(after) + [VMEM] * (len(rows) + 1),
        out_specs=VMEM,
        compiler_params=params(8),
        cost_estimate=LARGE,
        name="cross",
    )(weight, *after, *rows, own)


def lags_kernel(geometry, skip, scal, *refs):
    classes, span, outputs, origin, period, chunk = geometry
    lhs, table, keep, *sends, sums = refs[skip:]
    rows = lhs.shape[1] // 2
    lag_dev = keep.shape[-1]
    cores = 2
    for start in range(0, span, chunk):
        values = []
        for r in range(classes):
            y = jnp.dot(lhs[r], table[r, :, start : start + chunk], preferred_element_type=F32)
            values.append((y[:rows], y[rows:]))
        for k, value in enumerate(combine(values, classes, outputs, origin, span, period)):
            lag = span * k + start
            lags = slice(lag % lag_dev, lag % lag_dev + chunk)
            sums[lag // lag_dev, :, lags] = value
    for column in range(keep.shape[0]):
        keep[column] = sums[cores * column + scal[CORE]]
        for i, out in enumerate(sends):
            at = slice(i * out.shape[1], (i + 1) * out.shape[1])
            out[column] = sums[cores * column + 1 - scal[CORE], at].astype(BF16)


def lag_parts(scal, after, lhs, table, geometry, columns, lag_dev, split, effort):
    rows = lhs.shape[1] // 2
    shape = lambda count: (columns, count, lag_dev)
    return pl.pallas_call(
        functools.partial(lags_kernel, geometry, len(after)),
        out_shape=[jax.ShapeDtypeStruct(shape(rows), F32)]
        + [jax.ShapeDtypeStruct(shape(rows // split), BF16)] * split,
        in_specs=[SMEM] + [pl.BlockSpec(memory_space=pl.ANY)] * len(after) + [VMEM] * 2,
        out_specs=[VMEM] * (split + 1),
        scratch_shapes=[pltpu.VMEM((2 * columns, rows, lag_dev), F32)],
        compiler_params=params(16),
        cost_estimate=effort,
        name="lags",
    )(scal, *after, lhs, table)


def cores_kernel(skip, split, scal, *refs):
    keep, *refs = refs[skip:]
    more, own, sends = refs[:split], refs[split], refs[split + 1 :]
    columns = keep.shape[0]
    for i, m in enumerate(more):
        at = slice(i * m.shape[1], (i + 1) * m.shape[1])
        for column in range(columns):
            value = keep[column, at] + m[column].astype(F32)

            @pl.when(scal[COLUMN] == column)
            def _():
                own[at] = value

            for s, out in enumerate(sends):

                @pl.when(scal[COLUMN] ^ (s + 1) == column)
                def _():
                    out[at] = value.astype(BF16)


def add_cores(scal, after, keep, more):
    columns, rows, lag_dev = keep.shape
    return pl.pallas_call(
        functools.partial(cores_kernel, len(after), len(more)),
        out_shape=[jax.ShapeDtypeStruct((rows, lag_dev), F32)]
        + [jax.ShapeDtypeStruct((rows, lag_dev), BF16)] * (columns - 1),
        in_specs=[SMEM] + [pl.BlockSpec(memory_space=pl.ANY)] * len(after) + [VMEM] * (1 + len(more)),
        out_specs=[VMEM] * columns,
        compiler_params=params(8),
        cost_estimate=SMALL,
        name="cores",
    )(scal, *after, keep, *more)


def stats_kernel(scale, pieces, others, scal, *refs):
    own, more, refs = refs[0], refs[1 : 1 + others], refs[1 + others :]
    targets, (corr, sums) = refs[: len(pieces)], refs[len(pieces) :]
    columns = []
    for target, (unit, first, count, at) in zip(targets, placed(pieces)):
        value = own[at]
        for m in more:
            value = value + m[at].astype(F32)
        slot = first + lax.broadcasted_iota(jnp.int32, (count, 1), 0)
        value = value * jnp.where(slot < scal[COUNT + unit], scale, 0.0)
        corr[at] = value
        square = jnp.sum(value * value, axis=1, keepdims=True)
        product = jnp.sum(value * target[0], axis=1, keepdims=True)
        lane = lax.broadcasted_iota(jnp.int32, (count, LANES), 1)
        columns.append(jnp.where(lane == 0, square, jnp.where(lane == 1, product, 0.0)))
    spare = sums.shape[1] - own.shape[0]
    if spare:
        columns.append(jnp.zeros((spare, LANES), F32))
    sums[...] = jnp.concatenate(columns, axis=0).T[:8]


def target_specs(pieces, lag_dev):
    return [
        pl.BlockSpec(
            (1, count, lag_dev),
            lambda i, scal, unit=unit, block=first // count: (scal[BLOCK + unit], block, 0),
        )
        for unit, first, count in pieces
    ]


def whole(shape):
    return pl.BlockSpec(shape, lambda i, scal: (0,) * len(shape))


def lag_stats(scal, scale, pieces, own, more, observed):
    rows, lag_dev = own.shape
    outs = [jax.ShapeDtypeStruct((rows, lag_dev), F32), jax.ShapeDtypeStruct((8, -(-rows // LANES) * LANES), F32)]
    return pl.pallas_call(
        functools.partial(stats_kernel, scale, pieces, len(more)),
        grid_spec=pltpu.PrefetchScalarGridSpec(
            num_scalar_prefetch=1,
            grid=(1,),
            in_specs=[whole(own.shape)] * (1 + len(more)) + target_specs(pieces, lag_dev),
            out_specs=[whole(o.shape) for o in outs],
        ),
        out_shape=outs,
        compiler_params=params(16),
        cost_estimate=SMALL,
        name="stats",
    )(scal, own, *more, *[observed] * len(pieces))


def slot_scales(sums, lag_total):
    total = sums[0][...]
    for s in sums[1:]:
        total = total + s[...]
    rows = total.shape[1]
    square, product = total[0:1], total[1:2]
    inverse = 1.0 / jnp.sqrt(square / lag_total + EPSILON)
    bending = (square * inverse * inverse - product * inverse) / lag_total
    sub = lax.broadcasted_iota(jnp.int32, (LANES, rows), 0)
    both = jnp.where(sub == 0, inverse, jnp.where(sub == 1, bending, 0.0)).T
    return both[:, 0:1], both[:, 1:2]


def gradient_kernel(lag_total, pieces, parts, scal, *refs):
    sums, corr, refs = refs[:parts], refs[parts], refs[parts + 1 :]
    targets, outs = refs[: len(pieces)], refs[len(pieces) :]
    inverse, bending = slot_scales(sums, lag_total)
    for target, out, (unit, first, count, at) in zip(targets, outs, placed(pieces)):
        slot = first + lax.broadcasted_iota(jnp.int32, (count, 1), 0)
        valid = jnp.where(slot < scal[COUNT + unit], inverse[at], 0.0)
        normed = corr[at] * inverse[at]
        out[...] = ((normed - target[0] - normed * bending[at]) * valid).astype(BF16)


def gradients(scal, lag_total, pieces, sums, corr, observed):
    lag_dev = corr.shape[1]
    outs = [jax.ShapeDtypeStruct((p[2], lag_dev), BF16) for p in pieces]
    return pl.pallas_call(
        functools.partial(gradient_kernel, lag_total, pieces, len(sums)),
        grid_spec=pltpu.PrefetchScalarGridSpec(
            num_scalar_prefetch=1,
            grid=(1,),
            in_specs=[whole(sums[0].shape)] * len(sums)
            + [whole(corr.shape)]
            + target_specs(pieces, lag_dev),
            out_specs=[whole(o.shape) for o in outs],
        ),
        out_shape=outs,
        compiler_params=params(16),
        cost_estimate=SMALL,
        name="gradient",
    )(scal, *sums, corr, *[observed] * len(pieces))


def normed_kernel(lag_total, chunks, parts, scal, *refs):
    out = refs[-1]
    for q, pieces in enumerate(chunks):
        sums, corr = refs[q * (parts + 1) : q * (parts + 1) + parts], refs[q * (parts + 1) + parts]
        inverse, _ = slot_scales(sums, lag_total)
        for unit, first, count, at in placed(pieces):

            @pl.when(pl.program_id(0) == unit)
            def _():
                out[0, first : first + count] = corr[at] * inverse[at]


def normed_rows(scal, lag_total, chunks, sums, corr, observed):
    blocks, slots, lag_dev = observed.shape
    ins = [x for s, c in zip(sums, corr) for x in (*s, c)]
    return pl.pallas_call(
        functools.partial(normed_kernel, lag_total, chunks, len(sums[0])),
        grid_spec=pltpu.PrefetchScalarGridSpec(
            num_scalar_prefetch=1,
            grid=(blocks,),
            in_specs=[whole(x.shape) for x in ins],
            out_specs=pl.BlockSpec((1, slots, lag_dev), lambda i, scal: (scal[BLOCK + i], 0, 0)),
        ),
        out_shape=jax.ShapeDtypeStruct(observed.shape, F32),
        compiler_params=params(16),
        cost_estimate=SMALL,
        name="normed",
    )(scal, *ins)


def adjoint_kernel(pieces, *refs):
    ids, parts, out = refs[: len(pieces)], refs[len(pieces) : -1], refs[-1]
    pick = picks([i.at[:, p[1] : p[1] + p[2]] for i, p in zip(ids, pieces)], out.shape[0])
    rows = jnp.concatenate([p[...] for p in parts], axis=0)
    out[...] = jnp.dot(pick, rows, preferred_element_type=F32)


def adjoint_rows(src_ids, pieces, parts, channels):
    lag_dev = parts[0].shape[1]
    return pl.pallas_call(
        functools.partial(adjoint_kernel, pieces),
        out_shape=jax.ShapeDtypeStruct((channels, lag_dev), F32),
        in_specs=[VMEM] * (2 * len(parts)),
        out_specs=VMEM,
        compiler_params=params(16),
        cost_estimate=SMALL,
        name="adjoint",
    )(*[src_ids[p[0]] for p in pieces], *parts)


def shards(spectra, window_keep, owners, pair_src, pair_rec, pair_count, observed):
    columns, cores, places = lax.axis_size("win"), lax.axis_size("freq"), lax.axis_size("recv")
    column, core, place = lax.axis_index("win"), lax.axis_index("freq"), lax.axis_index("recv")
    assert spectra.shape[0] == 1 and cores == 2
    channels, bins_dev = spectra.shape[2:]
    blocks, slots, lag_dev = observed.shape
    lag_total = lag_dev * columns * cores
    bin_total = bins_dev * cores
    period = 2 * bin_total
    part = bins_dev // columns
    classes = part // LANES
    span = period // classes
    geometry = (classes, span, lag_total // span, lag_total // 2, period, 256)
    lag_scale = 1.0 / math.sqrt(bin_total * columns)
    peers = columns * cores
    some = slots // 2
    shifts = range(places)

    held = [
        swapped(
            lax.dynamic_slice(
                spectra, (0, 0, 0, (column ^ s) * part), (1, 2, channels, part)
            ),
            "win",
            columns,
            s,
        )
        for s in range(columns)
    ]
    scal, wanted, rec_ids = index(
        window_keep, owners, pair_count, pair_src, pair_rec, places
    )
    if columns == 2:
        weight = jnp.ones((1,), F32)
    else:
        keeps = jnp.stack([swapped(window_keep[0], "win", columns, s) for s in range(columns)])
        ranked = jnp.argsort(-keeps)[: columns - 1].astype(jnp.int32)
        weight = keeps[ranked].astype(F32)
        scal = lax.dynamic_update_slice(scal, ranked, (ORDER,))

    direct = places == blocks
    src_ids = [swapped(x, "recv", places, d) for d, x in zip(shifts, wanted)]
    trig = tables(classes, span, period, bins_dev, columns, cores)
    table = make_table(scal, trig, classes, span, peers)
    if direct and blocks == 4:
        chunks = [
            [(3, 0, slots), (1, 0, slots), (0, 0, slots)],
            [(2, 0, slots)],
        ]
    else:
        chunks = [[(d, first, some) for d in range(blocks)] for first in (0, some)]
    if direct:
        messages = [piece for pieces in chunks for piece in pieces]
    else:
        messages = [(d, 0, slots) for d in shifts]
    sent, own_rows = gather_rows(
        scal, table, held[0], held[1:], make_perm(part), src_ids, rec_ids, messages
    )
    arrived = []
    for m, x in zip(messages, sent):
        if direct and m[0] == 2:
            arrived[0], x = lax.optimization_barrier((arrived[0], x))
        arrived.append(swapped(x, "recv", places, m[0]))
    if not direct:
        stacked = jnp.stack(arrived)
        whole_rows = [
            lax.dynamic_index_in_dim(stacked, place ^ owners[b], 0, False) for b in range(blocks)
        ]
        arrived = [whole_rows[piece[0]] for pieces in chunks for piece in pieces]
    corrs, all_sums, returned, returned_pieces = [], [], [], []
    after = []
    for q, pieces in enumerate(chunks):
        rows, arrived = arrived[: len(pieces)], arrived[len(pieces) :]
        lhs = cross_rows(weight, after[:1], rows, own_rows, pieces, classes)
        keep, *sends = lag_parts(
            scal, [], lhs, table, geometry, columns, lag_dev, sum(p[2] for p in pieces) // GROUP[q], SMALL if q else LARGE
        )
        sends = [swapped(x, "freq", cores, 1) for x in sends]
        own, *sends = add_cores(scal, [], keep, sends)
        more = [swapped(x, "win", columns, s + 1) for s, x in enumerate(sends)]
        after = [own, *more]
        corr, sums = lag_stats(scal, lag_scale, pieces, own, more, observed)
        sums = [swapped(sums, ("win", "freq"), peers, s) for s in range(peers)]
        grads = gradients(scal, lag_total, pieces, sums, corr, observed)
        if not direct:
            stacked = jnp.stack(list(grads) + [jnp.zeros_like(grads[0])])
            grads = []
            for d in shifts:
                block = jnp.int32(blocks)
                for b in range(blocks):
                    block = jnp.where(owners[b] == place ^ d, b, block)
                grads.append(lax.dynamic_index_in_dim(stacked, block, 0, False))
            pieces = [(d, pieces[0][1], some) for d in shifts]
        returned += [swapped(g, "recv", places, p[0]) for p, g in zip(pieces, grads)]
        returned_pieces += pieces
        corrs.append(corr)
        all_sums.append(sums)
    normed = normed_rows(scal, lag_total, chunks, all_sums, corrs, observed)
    adjoint = adjoint_rows(src_ids, returned_pieces, returned, channels)
    return (normed, adjoint)


def solution(mesh):
    return jax.shard_map(
        shards,
        mesh=mesh,
        in_specs=(
            P("win", None, ("groups", "recv"), "freq"),
            P(("groups", "win")),
            P("groups"),
            P(None, ("groups", "recv")),
            P(None, ("groups", "recv")),
            P(None, ("groups", "recv")),
            P(None, ("groups", "recv"), ("win", "freq")),
        ),
        out_specs=(
            P(None, ("groups", "recv"), ("win", "freq")),
            P(("groups", "recv"), ("win", "freq")),
        ),
        check_vma=False,
    )
```

```python
import functools
import math

import jax
import jax.numpy as jnp
import ml_dtypes
import numpy as np
from jax import lax
from jax.experimental import pallas as pl
from jax.experimental.pallas import tpu as pltpu
from jax.sharding import PartitionSpec as P

EPSILON = 1e-06
MIB = 1 << 20
LANES = 128
SPLIT = 4
CORE, COLUMN, ORDER, BLOCK, COUNT = 0, 1, 2, 8, 16
BF16 = jnp.bfloat16
F32 = jnp.float32
VMEM = pl.BlockSpec(memory_space=pltpu.VMEM)
SMEM = pl.BlockSpec(memory_space=pltpu.SMEM)
HBM = pl.BlockSpec(memory_space=pltpu.HBM)
ANY = pl.BlockSpec(memory_space=pl.ANY)


def swapped(value, axis, size, step):
    assert size & (size - 1) == 0
    if step == 0:
        return value
    return lax.ppermute(value, axis, [(i, i ^ step) for i in range(size)])


def params(mib):
    return pltpu.CompilerParams(vmem_limit_bytes=mib * MIB)


SMALL = pl.CostEstimate(flops=1, bytes_accessed=1, transcendentals=0)
LARGE = pl.CostEstimate(flops=2 * 10**10, bytes_accessed=MIB, transcendentals=0)


def tables(classes, span, period, bins_dev, columns, cores):
    u = np.arange(span, dtype=np.int64)[None, :]
    piece = np.arange(columns * cores, dtype=np.int64)[:, None]
    first = piece % cores * bins_dev + piece // cores * (bins_dev // columns)
    rows = (first + np.arange(classes)).reshape(-1)
    high = 16 * classes * np.arange(LANES // 16, dtype=np.int64)
    low = classes * np.arange(16, dtype=np.int64)
    angle = (np.concatenate([rows, high, low])[:, None] * u % period) * (2.0 * math.pi / period)
    return np.stack([np.cos(angle), np.sin(angle)]).astype(np.float32)


def fetch(pairs, sems):
    copies = [pltpu.make_async_copy(a, b, sems.at[i]) for i, (a, b) in enumerate(pairs)]
    for c in copies:
        c.start()
    for c in copies:
        c.wait()


def index_kernel(blocks, direct, *refs):
    given, refs = refs[:5], refs[5:]
    scal, wanted, rec_ids, held, sems = refs[0], refs[1:-7], refs[-7], refs[-6:-1], refs[-1]
    fetch(zip(given, held), sems)
    window_keep, owners, pair_count, src, rec = held
    place = lax.axis_index("recv")
    column, columns = lax.axis_index("win"), lax.axis_size("win")
    core = lax.axis_index("freq")
    scal[CORE] = core
    scal[COLUMN] = column
    scal[ORDER] = 1 - window_keep[0]
    for b in range(blocks):
        unit = place ^ owners[b] if direct else b
        scal[BLOCK + unit] = b
        scal[COUNT + unit] = pair_count[b]
    for d, out in enumerate(wanted):
        chosen = jnp.full(out.shape, -1, jnp.int32)
        received = jnp.zeros(out.shape, jnp.int32)
        for b in range(blocks):
            mine = jnp.full(out.shape, owners[b], jnp.int32) == (place ^ d)
            chosen = jnp.where(mine, src[b : b + 1], chosen)
            received = jnp.where(mine, rec[b : b + 1], received)
        out[...] = chosen
        if direct:
            rec_ids[d : d + 1] = received
    if not direct:
        rec_ids[...] = rec[...]


def index(window_keep, owners, pair_count, pair_src, pair_rec, places):
    blocks, slots = pair_src.shape
    ids = jax.ShapeDtypeStruct((1, slots), jnp.int32)
    given = [window_keep, owners, pair_count[:, 0], pair_src, pair_rec]
    scal, *wanted, rec_ids = pl.pallas_call(
        functools.partial(index_kernel, blocks, places == blocks),
        out_shape=[jax.ShapeDtypeStruct((LANES,), jnp.int32)]
        + [ids] * places
        + [jax.ShapeDtypeStruct(pair_rec.shape, jnp.int32)],
        in_specs=[HBM] * 5,
        out_specs=[SMEM] + [VMEM] * (places + 1),
        scratch_shapes=[pltpu.SMEM(g.shape, g.dtype) for g in given[:3]]
        + [pltpu.VMEM(g.shape, g.dtype) for g in given[3:]]
        + [pltpu.SemaphoreType.DMA((5,))],
        compiler_params=params(16),
        cost_estimate=SMALL,
        name="index",
    )(*given)
    return scal, wanted, rec_ids


def table_kernel(classes, parts, scal, trig, table, base):
    rows = parts * classes
    low = slice(rows + LANES // 16, rows + LANES // 16 + 16)
    cl, sl = trig[0, low], trig[1, low]
    for h in range(LANES // 16):
        ch, sh = trig[0, rows + h : rows + h + 1], trig[1, rows + h : rows + h + 1]
        base[0, 16 * h : 16 * h + 16] = ch * cl - sh * sl
        base[1, 16 * h : 16 * h + 16] = sh * cl + ch * sl
    first = (scal[CORE] + 2 * scal[COLUMN]) * classes
    cb, sb = base[0], base[1]
    for r in range(classes):
        ca, sa = trig[0, pl.ds(first + r, 1)], trig[1, pl.ds(first + r, 1)]
        table[r, :LANES] = (ca * cb - sa * sb).astype(BF16)
        table[r, LANES:] = (-(sa * cb + ca * sb)).astype(BF16)


def make_table(scal, trig, classes, span, parts):
    return pl.pallas_call(
        functools.partial(table_kernel, classes, parts),
        out_shape=jax.ShapeDtypeStruct((classes, 2 * LANES, span), BF16),
        in_specs=[SMEM, VMEM],
        out_specs=VMEM,
        scratch_shapes=[pltpu.VMEM((2, LANES, span), F32)],
        compiler_params=params(12),
        cost_estimate=SMALL,
        name="table",
    )(scal, jnp.asarray(trig))


def perm_kernel(perm):
    part = perm.shape[0]
    classes = part // LANES
    source = lax.broadcasted_iota(jnp.int32, (part, LANES), 0)
    target = classes * lax.broadcasted_iota(jnp.int32, (part, LANES), 1)
    for r in range(classes):
        perm[:, r * LANES : (r + 1) * LANES] = (source == target + r).astype(BF16)


def make_perm(part):
    return pl.pallas_call(
        perm_kernel,
        out_shape=jax.ShapeDtypeStruct((part, part), BF16),
        out_specs=VMEM,
        compiler_params=params(8),
        cost_estimate=SMALL,
        name="perm",
    )()


def picks(ids, channels):
    row = jnp.concatenate([i[...] for i in ids], axis=1)
    return (lax.broadcasted_iota(jnp.int32, (channels, row.shape[1]), 0) == row).astype(BF16)


def rows_kernel(half, used, sends, messages, ahead, scal, after, here, *refs):
    held, refs = refs[:used], refs[used:]
    perm, src_ids, rec_ids, refs = refs[0], refs[1 : 1 + sends], refs[1 + sends], refs[2 + sends :]
    if half:
        early, outs, own_out = refs[: len(messages)], refs[len(messages) : -1], refs[-1]
    else:
        first_out, outs, own_out = refs[: sum(h > 0 for h in ahead)], refs[: -1], refs[-1]
        outs = outs[len(first_out) :]
    units, _, slots, part = own_out.shape
    channels = here.shape[2]
    pick = picks(list(src_ids) + [rec_ids.at[d : d + 1] for d in range(units)], channels)
    for u in range(used):
        x = here[0, 0]
        for s in range(used):
            x = jnp.where(scal[ORDER + u] == s + 1, held[s][0, 0], x)
        x = jnp.dot(x, perm[...], preferred_element_type=F32).astype(BF16)
        y = lax.dot_general(
            pick, x, (((0,), (0,)), ((), ())), preferred_element_type=F32
        ).astype(BF16)
        taken = 0
        for i, ((d, first, count), h) in enumerate(zip(messages, ahead)):
            at = d * slots + first
            if half and h:
                outs[i][u, : count - h] = early[i][u]
                outs[i][u, count - h :] = y[at : at + count]
            elif half:
                outs[i][u, 0] = early[i][u]
                outs[i][u, 1] = y[at : at + count]
            else:
                if h:
                    first_out[taken][u] = y[at : at + h]
                    taken += 1
                outs[i][u] = y[at + h : at + count]
        for d in range(units):
            at = (sends + d) * slots
            own_out[d, u] = y[at : at + slots]


def gather_rows(half, scal, after, here, held, perm, src_ids, rec_ids, messages, ahead, early):
    used, sends = len(held), len(src_ids)
    part = held[0].shape[-1]
    units, slots = rec_ids.shape
    if half:
        shapes = [
            (used, 2 * m[2] - h, part) if h else (used, 2, m[2], part)
            for m, h in zip(messages, ahead)
        ]
    else:
        shapes = [(used, h, part) for h in ahead if h]
        shapes += [(used, m[2] - h, part) for m, h in zip(messages, ahead)]
    shapes.append((units, used, slots, part))
    return pl.pallas_call(
        functools.partial(rows_kernel, half, used, sends, messages, ahead),
        out_shape=[jax.ShapeDtypeStruct(x, BF16) for x in shapes],
        in_specs=[SMEM, ANY] + [VMEM] * (used + 3 + sends + len(early)),
        out_specs=[VMEM] * len(shapes),
        compiler_params=params(16),
        cost_estimate=SMALL,
        name="rows",
    )(scal, after, here, *held, perm, *src_ids, rec_ids, *early)


def token_kernel(*refs):
    refs[-1][...] = jnp.zeros(refs[-1].shape, F32)


def token(values):
    return pl.pallas_call(
        token_kernel,
        out_shape=jax.ShapeDtypeStruct((8, LANES), F32),
        in_specs=[ANY] * len(values),
        out_specs=VMEM,
        compiler_params=params(4),
        cost_estimate=LARGE,
        name="token",
    )(*values)


def combine(values, classes, outputs, origin, span, period):
    plain, scaled = [None] * outputs, [None] * outputs

    def add(into, k, value, sign):
        if into[k] is None:
            into[k] = value if sign > 0 else -value
        else:
            into[k] = into[k] + value if sign > 0 else into[k] - value

    for r, (real, imag) in enumerate(values):
        both = None
        for k in range(outputs):
            eighths = r * (span * k - origin) * 8 // period % 8
            assert r * (span * k - origin) * 8 % period == 0
            if eighths % 2 == 0:
                value, sign = ((real, 1), (imag, -1), (real, -1), (imag, 1))[eighths // 2]
                add(plain, k, value, sign)
            else:
                if both is None:
                    both = real + imag, real - imag
                value, sign = ((both[1], 1), (both[0], -1), (both[1], -1), (both[0], 1))[eighths // 2]
                add(scaled, k, value, sign)
    root = math.sqrt(0.5)
    return [a if b is None else a + root * b for a, b in zip(plain, scaled)]


def placed(pieces):
    at = 0
    for unit, first, count in pieces:
        yield unit, first, count, slice(at, at + count)
        at += count


def cross_kernel(pieces, ahead, skip, weight, *refs):
    *refs, own_real, own_imag, lhs = refs[skip:]
    used = own_real.shape[1]
    rows = lhs.shape[1] // 2
    steps = []
    for (unit, first, count, at), h in zip(placed(pieces), ahead):
        ref = refs.pop(0)
        if h:
            more = refs.pop(0)
            steps.append((unit, 0, h, at.start, ref, 0, more, count - h))
            steps.append((unit, h, count - h, at.start + h, more, 0, more, count))
        elif ref.shape[2] > count:
            steps.append((unit, first, count, at.start, ref.at[:, 0], first, ref.at[:, 1], first))
        else:
            steps.append((unit, first, count, at.start, ref.at[:, 0], 0, ref.at[:, 1], 0))
    for unit, first, count, at, real_ref, real_at, imag_ref, imag_at in steps:
        turned = slice(rows + at, rows + at + count)
        at = slice(at, at + count)
        mine = slice(first, first + count)
        for r in range(lhs.shape[0]):
            bins = slice(r * LANES, (r + 1) * LANES)
            real = imag = None
            for u in range(used):
                sr = real_ref[u, real_at : real_at + count, bins].astype(F32)
                si = imag_ref[u, imag_at : imag_at + count, bins].astype(F32)
                rr, ri = (o[unit, u, mine, bins].astype(F32) for o in (own_real, own_imag))
                re, im = sr * rr + si * ri, si * rr - sr * ri
                if u:
                    re, im = real + weight[u] * re, imag + weight[u] * im
                real, imag = re, im
            lhs[r, at, :LANES] = real.astype(BF16)
            lhs[r, at, LANES:] = imag.astype(BF16)
            lhs[r, turned, :LANES] = imag.astype(BF16)
            lhs[r, turned, LANES:] = (-real).astype(BF16)


def cross_rows(weight, after, rows, own, pieces, ahead, classes):
    count = sum(p[2] for p in pieces)
    return pl.pallas_call(
        functools.partial(cross_kernel, pieces, ahead, len(after)),
        out_shape=jax.ShapeDtypeStruct((classes, 2 * count, 2 * LANES), BF16),
        in_specs=[SMEM] + [ANY] * len(after) + [VMEM] * (len(rows) + 2),
        out_specs=VMEM,
        compiler_params=params(16),
        cost_estimate=LARGE,
        name="cross",
    )(weight, *after, *rows, *own)


def lags_kernel(geometry, skip, scal, *refs):
    classes, span, outputs, origin, period, chunk = geometry
    lhs, table, keep, *sends, sums = refs[skip:]
    rows = lhs.shape[1] // 2
    lag_dev = keep.shape[-1]
    cores = 2
    for start in range(0, span, chunk):
        values = []
        for r in range(classes):
            y = jnp.dot(lhs[r], table[r, :, start : start + chunk], preferred_element_type=F32)
            values.append((y[:rows], y[rows:]))
        for k, value in enumerate(combine(values, classes, outputs, origin, span, period)):
            lag = span * k + start
            lags = slice(lag % lag_dev, lag % lag_dev + chunk)
            sums[lag // lag_dev, :, lags] = value
    for column in range(keep.shape[0]):
        keep[column] = sums[cores * column + scal[CORE]]
        for i, out in enumerate(sends):
            at = slice(i * out.shape[1], (i + 1) * out.shape[1])
            out[column] = sums[cores * column + 1 - scal[CORE], at].astype(BF16)


def lag_parts(scal, after, lhs, table, geometry, columns, lag_dev, split, effort):
    rows = lhs.shape[1] // 2
    shape = lambda count: (columns, count, lag_dev)
    return pl.pallas_call(
        functools.partial(lags_kernel, geometry, len(after)),
        out_shape=[jax.ShapeDtypeStruct(shape(rows), F32)]
        + [jax.ShapeDtypeStruct(shape(rows // split), BF16)] * split,
        in_specs=[SMEM] + [ANY] * len(after) + [VMEM] * 2,
        out_specs=[VMEM] * (split + 1),
        scratch_shapes=[pltpu.VMEM((2 * columns, rows, lag_dev), F32)],
        compiler_params=params(16),
        cost_estimate=effort,
        name="lags",
    )(scal, *after, lhs, table)


def cores_kernel(skip, split, scal, *refs):
    keep, *refs = refs[skip:]
    more, own, sends = refs[:split], refs[split], refs[split + 1 :]
    columns = keep.shape[0]
    for i, m in enumerate(more):
        at = slice(i * m.shape[1], (i + 1) * m.shape[1])
        for column in range(columns):
            value = keep[column, at] + m[column].astype(F32)

            @pl.when(scal[COLUMN] == column)
            def _():
                own[at] = value

            for s, out in enumerate(sends):

                @pl.when(scal[COLUMN] ^ (s + 1) == column)
                def _():
                    out[at] = value.astype(BF16)


def add_cores(scal, after, keep, more):
    columns, rows, lag_dev = keep.shape
    return pl.pallas_call(
        functools.partial(cores_kernel, len(after), len(more)),
        out_shape=[jax.ShapeDtypeStruct((rows, lag_dev), F32)]
        + [jax.ShapeDtypeStruct((rows, lag_dev), BF16)] * (columns - 1),
        in_specs=[SMEM] + [ANY] * len(after) + [VMEM] * (1 + len(more)),
        out_specs=[VMEM] * columns,
        compiler_params=params(8),
        cost_estimate=SMALL,
        name="cores",
    )(scal, *after, keep, *more)


def stats_kernel(scale, pieces, others, scal, *refs):
    own, more, refs = refs[0], refs[1 : 1 + others], refs[1 + others :]
    targets, (corr, sums) = refs[: len(pieces)], refs[len(pieces) :]
    columns = []
    for target, (unit, first, count, at) in zip(targets, placed(pieces)):
        value = own[at]
        for m in more:
            value = value + m[at].astype(F32)
        slot = first + lax.broadcasted_iota(jnp.int32, (count, 1), 0)
        value = value * jnp.where(slot < scal[COUNT + unit], scale, 0.0)
        corr[at] = value
        square = jnp.sum(value * value, axis=1, keepdims=True)
        product = jnp.sum(value * target[0], axis=1, keepdims=True)
        lane = lax.broadcasted_iota(jnp.int32, (count, LANES), 1)
        columns.append(jnp.where(lane == 0, square, jnp.where(lane == 1, product, 0.0)))
    sums[...] = jnp.concatenate(columns, axis=0).T[:8]


def target_specs(pieces, lag_dev):
    return [
        pl.BlockSpec(
            (1, count, lag_dev),
            lambda i, scal, unit=unit, block=first // count: (scal[BLOCK + unit], block, 0),
        )
        for unit, first, count in pieces
    ]


def whole(shape):
    return pl.BlockSpec(shape, lambda i, scal: (0,) * len(shape))


def lag_stats(scal, scale, pieces, own, more, observed):
    rows, lag_dev = own.shape
    outs = [jax.ShapeDtypeStruct((rows, lag_dev), F32), jax.ShapeDtypeStruct((8, rows), F32)]
    return pl.pallas_call(
        functools.partial(stats_kernel, scale, pieces, len(more)),
        grid_spec=pltpu.PrefetchScalarGridSpec(
            num_scalar_prefetch=1,
            grid=(1,),
            in_specs=[whole(own.shape)] * (1 + len(more)) + target_specs(pieces, lag_dev),
            out_specs=[whole(o.shape) for o in outs],
        ),
        out_shape=outs,
        compiler_params=params(16),
        cost_estimate=SMALL,
        name="stats",
    )(scal, own, *more, *[observed] * len(pieces))


def slot_scales(sums, lag_total):
    total = sums[0][...]
    for s in sums[1:]:
        total = total + s[...]
    rows = total.shape[1]
    square, product = total[0:1], total[1:2]
    inverse = 1.0 / jnp.sqrt(square / lag_total + EPSILON)
    bending = (square * inverse * inverse - product * inverse) / lag_total
    sub = lax.broadcasted_iota(jnp.int32, (LANES, rows), 0)
    both = jnp.where(sub == 0, inverse, jnp.where(sub == 1, bending, 0.0)).T
    return both[:, 0:1], both[:, 1:2]


def gradient_kernel(lag_total, pieces, parts, scal, *refs):
    sums, corr, refs = refs[:parts], refs[parts], refs[parts + 1 :]
    targets, outs = refs[: len(pieces)], refs[len(pieces) :]
    inverse, bending = slot_scales(sums, lag_total)
    for target, out, (unit, first, count, at) in zip(targets, outs, placed(pieces)):
        slot = first + lax.broadcasted_iota(jnp.int32, (count, 1), 0)
        valid = jnp.where(slot < scal[COUNT + unit], inverse[at], 0.0)
        normed = corr[at] * inverse[at]
        out[...] = ((normed - target[0] - normed * bending[at]) * valid).astype(BF16)


def gradients(scal, lag_total, pieces, sums, corr, observed):
    lag_dev = corr.shape[1]
    outs = [jax.ShapeDtypeStruct((p[2], lag_dev), BF16) for p in pieces]
    return pl.pallas_call(
        functools.partial(gradient_kernel, lag_total, pieces, len(sums)),
        grid_spec=pltpu.PrefetchScalarGridSpec(
            num_scalar_prefetch=1,
            grid=(1,),
            in_specs=[whole(sums[0].shape)] * len(sums)
            + [whole(corr.shape)]
            + target_specs(pieces, lag_dev),
            out_specs=[whole(o.shape) for o in outs],
        ),
        out_shape=outs,
        compiler_params=params(16),
        cost_estimate=SMALL,
        name="gradient",
    )(scal, *sums, corr, *[observed] * len(pieces))


def normed_kernel(lag_total, chunks, parts, scal, *refs):
    out = refs[-1]
    for q, pieces in enumerate(chunks):
        sums, corr = refs[q * (parts + 1) : q * (parts + 1) + parts], refs[q * (parts + 1) + parts]
        inverse, _ = slot_scales(sums, lag_total)
        for unit, first, count, at in placed(pieces):

            @pl.when(pl.program_id(0) == unit)
            def _():
                out[0, first : first + count] = corr[at] * inverse[at]


def normed_rows(scal, lag_total, chunks, sums, corr, observed):
    blocks, slots, lag_dev = observed.shape
    ins = [x for s, c in zip(sums, corr) for x in (*s, c)]
    return pl.pallas_call(
        functools.partial(normed_kernel, lag_total, chunks, len(sums[0])),
        grid_spec=pltpu.PrefetchScalarGridSpec(
            num_scalar_prefetch=1,
            grid=(blocks,),
            in_specs=[whole(x.shape) for x in ins],
            out_specs=pl.BlockSpec((1, slots, lag_dev), lambda i, scal: (scal[BLOCK + i], 0, 0)),
        ),
        out_shape=jax.ShapeDtypeStruct(observed.shape, F32),
        compiler_params=params(16),
        cost_estimate=SMALL,
        name="normed",
    )(scal, *ins)


def adjoint_kernel(pieces, *refs):
    ids, parts, out = refs[: len(pieces)], refs[len(pieces) : -1], refs[-1]
    pick = picks([i.at[:, p[1] : p[1] + p[2]] for i, p in zip(ids, pieces)], out.shape[0])
    rows = jnp.concatenate([p[...] for p in parts], axis=0)
    out[...] = jnp.dot(pick, rows, preferred_element_type=F32)


def adjoint_rows(src_ids, pieces, parts, channels):
    lag_dev = parts[0].shape[1]
    return pl.pallas_call(
        functools.partial(adjoint_kernel, pieces),
        out_shape=jax.ShapeDtypeStruct((channels, lag_dev), F32),
        in_specs=[VMEM] * (2 * len(parts)),
        out_specs=VMEM,
        compiler_params=params(16),
        cost_estimate=SMALL,
        name="adjoint",
    )(*[src_ids[p[0]] for p in pieces], *parts)


def shards(spectra, window_keep, owners, pair_src, pair_rec, pair_count, observed):
    columns, cores, places = lax.axis_size("win"), lax.axis_size("freq"), lax.axis_size("recv")
    column, core, place = lax.axis_index("win"), lax.axis_index("freq"), lax.axis_index("recv")
    assert spectra.shape[0] == 1 and cores == 2
    channels, bins_dev = spectra.shape[2:]
    blocks, slots, lag_dev = observed.shape
    lag_total = lag_dev * columns * cores
    bin_total = bins_dev * cores
    period = 2 * bin_total
    part = bins_dev // columns
    classes = part // LANES
    span = period // classes
    geometry = (classes, span, lag_total // span, lag_total // 2, period, 256)
    lag_scale = 1.0 / math.sqrt(bin_total * columns)
    peers = columns * cores
    some = slots // 2
    shifts = range(places)

    here, *held = [
        [
            swapped(
                lax.dynamic_slice(
                    spectra, (0, half, 0, (column ^ s) * part), (1, 1, channels, part)
                ),
                "win",
                columns,
                s,
            )
            for half in range(2)
        ]
        for s in range(columns)
    ]
    scal, wanted, rec_ids = index(
        window_keep, owners, pair_count, pair_src, pair_rec, places
    )
    if columns == 2:
        weight = jnp.ones((1,), F32)
    else:
        keeps = jnp.stack([swapped(window_keep[0], "win", columns, s) for s in range(columns)])
        ranked = jnp.argsort(-keeps)[: columns - 1].astype(jnp.int32)
        weight = keeps[ranked].astype(F32)
        scal = lax.dynamic_update_slice(scal, ranked, (ORDER,))

    direct = places == blocks
    src_ids = [swapped(x, "recv", places, d) for d, x in zip(shifts, wanted)]
    trig = tables(classes, span, period, bins_dev, columns, cores)
    table = make_table(scal, trig, classes, span, peers)
    if direct and blocks == 4:
        chunks = [
            [(0, 0, slots), (1, 0, slots)],
            [(2, 0, slots), (3, 0, slots)],
        ]
    else:
        chunks = [[(d, first, some) for d in range(blocks)] for first in (0, some)]
    if direct:
        messages = [piece for pieces in chunks for piece in pieces]
    else:
        messages = [(d, 0, slots) for d in shifts]
    ahead = [some // 2 if direct and m[0] > 1 else 0 for m in messages]
    perm = make_perm(part)
    *early, own_real = gather_rows(
        0, scal, scal, here[0], [h[0] for h in held], perm, src_ids, rec_ids, messages, ahead, []
    )
    sent_first = early[: -len(messages)]
    sent_first = [
        swapped(x, "recv", places, m[0])
        for x, m in zip(sent_first, [m for m, h in zip(messages, ahead) if h])
    ]
    *sent, own_imag = gather_rows(
        1,
        scal,
        table,
        here[1],
        [h[1] for h in held],
        perm,
        src_ids,
        rec_ids,
        messages,
        ahead,
        early[-len(messages) :],
    )
    arrived = [swapped(x, "recv", places, m[0]) for m, x in zip(messages, sent)]
    after = [token(sent_first)] if sent_first else []
    arrived = [[sent_first.pop(0), x] if h else [x] for x, h in zip(arrived, ahead)]
    if not direct:
        stacked = jnp.stack([x for (x,) in arrived])
        whole_rows = [
            lax.dynamic_index_in_dim(stacked, place ^ owners[b], 0, False) for b in range(blocks)
        ]
        arrived = [[whole_rows[piece[0]]] for pieces in chunks for piece in pieces]
        ahead = [0] * len(arrived)
    corrs, all_sums, returned, returned_pieces = [], [], [], []
    for q, pieces in enumerate(chunks):
        rows, arrived = [x for a in arrived[: len(pieces)] for x in a], arrived[len(pieces) :]
        fore, ahead = ahead[: len(pieces)], ahead[len(pieces) :]
        lhs = cross_rows(weight, after[:1], rows, (own_real, own_imag), pieces, fore, classes)
        keep, *sends = lag_parts(
            scal, [], lhs, table, geometry, columns, lag_dev, SPLIT if q else 2 * SPLIT, SMALL if q else LARGE
        )
        sends = [swapped(x, "freq", cores, 1) for x in sends]
        own, *sends = add_cores(scal, after[1:], keep, sends)
        more = [swapped(x, "win", columns, s + 1) for s, x in enumerate(sends)]
        after = [own, *more]
        corr, sums = lag_stats(scal, lag_scale, pieces, own, more, observed)
        sums = [swapped(sums, ("win", "freq"), peers, s) for s in range(peers)]
        grads = gradients(scal, lag_total, pieces, sums, corr, observed)
        if not direct:
            stacked = jnp.stack(list(grads) + [jnp.zeros_like(grads[0])])
            grads = []
            for d in shifts:
                block = jnp.int32(blocks)
                for b in range(blocks):
                    block = jnp.where(owners[b] == place ^ d, b, block)
                grads.append(lax.dynamic_index_in_dim(stacked, block, 0, False))
            pieces = [(d, pieces[0][1], some) for d in shifts]
        returned += [swapped(g, "recv", places, p[0]) for p, g in zip(pieces, grads)]
        returned_pieces += pieces
        corrs.append(corr)
        all_sums.append(sums)
    normed = normed_rows(scal, lag_total, chunks, all_sums, corrs, observed)
    adjoint = adjoint_rows(src_ids, returned_pieces, returned, channels)
    return (normed, adjoint)


def solution(mesh):
    return jax.shard_map(
        shards,
        mesh=mesh,
        in_specs=(
            P("win", None, ("groups", "recv"), "freq"),
            P(("groups", "win")),
            P("groups"),
            P(None, ("groups", "recv")),
            P(None, ("groups", "recv")),
            P(None, ("groups", "recv")),
            P(None, ("groups", "recv"), ("win", "freq")),
        ),
        out_specs=(
            P(None, ("groups", "recv"), ("win", "freq")),
            P(("groups", "recv"), ("win", "freq")),
        ),
        check_vma=False,
    )
```

```python
import functools
import math

import jax
import jax.numpy as jnp
import ml_dtypes
import numpy as np
from jax import lax
from jax.experimental import pallas as pl
from jax.experimental.pallas import tpu as pltpu
from jax.sharding import PartitionSpec as P

EPSILON = 1e-06
MIB = 1 << 20
LANES = 128
SPLIT = 4
CORE, COLUMN, ORDER, BLOCK, COUNT = 0, 1, 2, 8, 16
BF16 = jnp.bfloat16
F32 = jnp.float32
VMEM = pl.BlockSpec(memory_space=pltpu.VMEM)
SMEM = pl.BlockSpec(memory_space=pltpu.SMEM)
HBM = pl.BlockSpec(memory_space=pltpu.HBM)
ANY = pl.BlockSpec(memory_space=pl.ANY)


def swapped(value, axis, size, step):
    assert size & (size - 1) == 0
    if step == 0:
        return value
    return lax.ppermute(value, axis, [(i, i ^ step) for i in range(size)])


def params(mib):
    return pltpu.CompilerParams(vmem_limit_bytes=mib * MIB)


SMALL = pl.CostEstimate(flops=1, bytes_accessed=1, transcendentals=0)
LARGE = pl.CostEstimate(flops=2 * 10**10, bytes_accessed=MIB, transcendentals=0)


def tables(classes, span, period, bins_dev, columns, cores):
    u = np.arange(span, dtype=np.int64)[None, :]
    piece = np.arange(columns * cores, dtype=np.int64)[:, None]
    first = piece % cores * bins_dev + piece // cores * (bins_dev // columns)
    rows = (first + np.arange(classes)).reshape(-1)
    high = 16 * classes * np.arange(LANES // 16, dtype=np.int64)
    low = classes * np.arange(16, dtype=np.int64)
    angle = (np.concatenate([rows, high, low])[:, None] * u % period) * (2.0 * math.pi / period)
    return np.stack([np.cos(angle), np.sin(angle)]).astype(np.float32)


def fetch(pairs, sems):
    copies = [pltpu.make_async_copy(a, b, sems.at[i]) for i, (a, b) in enumerate(pairs)]
    for c in copies:
        c.start()
    for c in copies:
        c.wait()


def index_kernel(blocks, direct, *refs):
    given, refs = refs[:5], refs[5:]
    scal, wanted, rec_ids, held, sems = refs[0], refs[1:-7], refs[-7], refs[-6:-1], refs[-1]
    fetch(zip(given, held), sems)
    window_keep, owners, pair_count, src, rec = held
    place = lax.axis_index("recv")
    column, columns = lax.axis_index("win"), lax.axis_size("win")
    core = lax.axis_index("freq")
    scal[CORE] = core
    scal[COLUMN] = column
    scal[ORDER] = 1 - window_keep[0]
    for b in range(blocks):
        unit = place ^ owners[b] if direct else b
        scal[BLOCK + unit] = b
        scal[COUNT + unit] = pair_count[b]
    for d, out in enumerate(wanted):
        chosen = jnp.full(out.shape, -1, jnp.int32)
        received = jnp.zeros(out.shape, jnp.int32)
        for b in range(blocks):
            mine = jnp.full(out.shape, owners[b], jnp.int32) == (place ^ d)
            chosen = jnp.where(mine, src[b : b + 1], chosen)
            received = jnp.where(mine, rec[b : b + 1], received)
        out[...] = chosen
        if direct:
            rec_ids[d : d + 1] = received
    if not direct:
        rec_ids[...] = rec[...]


def index(window_keep, owners, pair_count, pair_src, pair_rec, places):
    blocks, slots = pair_src.shape
    ids = jax.ShapeDtypeStruct((1, slots), jnp.int32)
    given = [window_keep, owners, pair_count[:, 0], pair_src, pair_rec]
    scal, *wanted, rec_ids = pl.pallas_call(
        functools.partial(index_kernel, blocks, places == blocks),
        out_shape=[jax.ShapeDtypeStruct((LANES,), jnp.int32)]
        + [ids] * places
        + [jax.ShapeDtypeStruct(pair_rec.shape, jnp.int32)],
        in_specs=[HBM] * 5,
        out_specs=[SMEM] + [VMEM] * (places + 1),
        scratch_shapes=[pltpu.SMEM(g.shape, g.dtype) for g in given[:3]]
        + [pltpu.VMEM(g.shape, g.dtype) for g in given[3:]]
        + [pltpu.SemaphoreType.DMA((5,))],
        compiler_params=params(16),
        cost_estimate=SMALL,
        name="index",
    )(*given)
    return scal, wanted, rec_ids


def table_kernel(classes, parts, scal, trig, table, base):
    rows = parts * classes
    low = slice(rows + LANES // 16, rows + LANES // 16 + 16)
    cl, sl = trig[0, low], trig[1, low]
    for h in range(LANES // 16):
        ch, sh = trig[0, rows + h : rows + h + 1], trig[1, rows + h : rows + h + 1]
        base[0, 16 * h : 16 * h + 16] = ch * cl - sh * sl
        base[1, 16 * h : 16 * h + 16] = sh * cl + ch * sl
    first = (scal[CORE] + 2 * scal[COLUMN]) * classes
    cb, sb = base[0], base[1]
    for r in range(classes):
        ca, sa = trig[0, pl.ds(first + r, 1)], trig[1, pl.ds(first + r, 1)]
        table[r, :LANES] = (ca * cb - sa * sb).astype(BF16)
        table[r, LANES:] = (-(sa * cb + ca * sb)).astype(BF16)


def make_table(scal, trig, classes, span, parts):
    return pl.pallas_call(
        functools.partial(table_kernel, classes, parts),
        out_shape=jax.ShapeDtypeStruct((classes, 2 * LANES, span), BF16),
        in_specs=[SMEM, VMEM],
        out_specs=VMEM,
        scratch_shapes=[pltpu.VMEM((2, LANES, span), F32)],
        compiler_params=params(12),
        cost_estimate=SMALL,
        name="table",
    )(scal, jnp.asarray(trig))


def perm_kernel(perm):
    part = perm.shape[0]
    classes = part // LANES
    source = lax.broadcasted_iota(jnp.int32, (part, LANES), 0)
    target = classes * lax.broadcasted_iota(jnp.int32, (part, LANES), 1)
    for r in range(classes):
        perm[:, r * LANES : (r + 1) * LANES] = (source == target + r).astype(BF16)


def make_perm(part):
    return pl.pallas_call(
        perm_kernel,
        out_shape=jax.ShapeDtypeStruct((part, part), BF16),
        out_specs=VMEM,
        compiler_params=params(8),
        cost_estimate=SMALL,
        name="perm",
    )()


def picks(ids, channels):
    row = jnp.concatenate([i[...] for i in ids], axis=1)
    return (lax.broadcasted_iota(jnp.int32, (channels, row.shape[1]), 0) == row).astype(BF16)


def rows_kernel(used, sends, messages, scal, after, here, *refs):
    held, refs = refs[:used], refs[used:]
    perm, src_ids, rec_ids, refs = refs[0], refs[sends:0:-1], refs[1 + sends], refs[2 + sends :]
    outs, own_out = refs[:-1], refs[-1]
    units, _, _, slots, part = own_out.shape
    channels = here.shape[2]
    pick = picks(list(src_ids) + [rec_ids.at[d : d + 1] for d in range(units)], channels)
    for u in range(used):
        for half in range(2):
            x = here[0, half]
            for s in range(used):
                x = jnp.where(scal[ORDER + u] == s + 1, held[s][0, half], x)
            x = jnp.dot(x, perm[...], preferred_element_type=F32).astype(BF16)
            y = lax.dot_general(
                pick, x, (((0,), (0,)), ((), ())), preferred_element_type=F32
            ).astype(BF16)
            for (d, first, count), out in zip(messages, outs):
                at = d * slots + first
                out[u, half] = y[at : at + count]
            for d in range(units):
                at = (sends + d) * slots
                own_out[d, u, half] = y[at : at + slots]


def gather_rows(scal, after, here, held, perm, src_ids, rec_ids, messages):
    used, sends = len(held), len(src_ids)
    part = held[0].shape[-1]
    units, slots = rec_ids.shape
    *sent, own = pl.pallas_call(
        functools.partial(rows_kernel, used, sends, messages),
        out_shape=[jax.ShapeDtypeStruct((used, 2, m[2], part), BF16) for m in messages]
        + [jax.ShapeDtypeStruct((units, used, 2, slots, part), BF16)],
        in_specs=[SMEM, pl.BlockSpec(memory_space=pl.ANY)] + [VMEM] * (used + 3 + sends),
        out_specs=[VMEM] * (len(messages) + 1),
        compiler_params=params(16),
        cost_estimate=SMALL,
        name="rows",
    )(scal, after, here, *held, perm, *src_ids[::-1], rec_ids)
    return sent, own


def combine(values, classes, outputs, origin, span, period):
    plain, scaled = [None] * outputs, [None] * outputs

    def add(into, k, value, sign):
        if into[k] is None:
            into[k] = value if sign > 0 else -value
        else:
            into[k] = into[k] + value if sign > 0 else into[k] - value

    for r, (real, imag) in enumerate(values):
        both = None
        for k in range(outputs):
            eighths = r * (span * k - origin) * 8 // period % 8
            assert r * (span * k - origin) * 8 % period == 0
            if eighths % 2 == 0:
                value, sign = ((real, 1), (imag, -1), (real, -1), (imag, 1))[eighths // 2]
                add(plain, k, value, sign)
            else:
                if both is None:
                    both = real + imag, real - imag
                value, sign = ((both[1], 1), (both[0], -1), (both[1], -1), (both[0], 1))[eighths // 2]
                add(scaled, k, value, sign)
    root = math.sqrt(0.5)
    return [a if b is None else a + root * b for a, b in zip(plain, scaled)]


def placed(pieces):
    at = 0
    for unit, first, count in pieces:
        yield unit, first, count, slice(at, at + count)
        at += count


def cross_kernel(pieces, skip, weight, *refs):
    refs = refs[skip:]
    s_refs, own, lhs = refs[:-2], refs[-2], refs[-1]
    used = own.shape[1]
    rows = lhs.shape[1] // 2
    for s_ref, (unit, first, count, at) in zip(s_refs, placed(pieces)):
        turned = slice(rows + at.start, rows + at.stop)
        mine = slice(first, first + count)
        sent = mine if s_ref.shape[2] > count else slice(0, count)
        for r in range(lhs.shape[0]):
            bins = slice(r * LANES, (r + 1) * LANES)
            real = imag = None
            for u in range(used):
                sr, si = (s_ref[u, half, sent, bins].astype(F32) for half in range(2))
                rr, ri = (own[unit, u, half, mine, bins].astype(F32) for half in range(2))
                re, im = sr * rr + si * ri, si * rr - sr * ri
                if u:
                    re, im = real + weight[u] * re, imag + weight[u] * im
                real, imag = re, im
            lhs[r, at, :LANES] = real.astype(BF16)
            lhs[r, at, LANES:] = imag.astype(BF16)
            lhs[r, turned, :LANES] = imag.astype(BF16)
            lhs[r, turned, LANES:] = (-real).astype(BF16)


def cross_rows(weight, after, rows, own, pieces, classes):
    count = sum(p[2] for p in pieces)
    return pl.pallas_call(
        functools.partial(cross_kernel, pieces, len(after)),
        out_shape=jax.ShapeDtypeStruct((classes, 2 * count, 2 * LANES), BF16),
        in_specs=[SMEM] + [ANY] * len(after) + [VMEM] * (len(rows) + 1),
        out_specs=VMEM,
        compiler_params=params(8),
        cost_estimate=LARGE,
        name="cross",
    )(weight, *after, *rows, own)


def lags_kernel(geometry, skip, scal, *refs):
    classes, span, outputs, origin, period, chunk = geometry
    lhs, table, keep, *sends, sums = refs[skip:]
    rows = lhs.shape[1] // 2
    lag_dev = keep.shape[-1]
    cores = 2
    for start in range(0, span, chunk):
        values = []
        for r in range(classes):
            y = jnp.dot(lhs[r], table[r, :, start : start + chunk], preferred_element_type=F32)
            values.append((y[:rows], y[rows:]))
        for k, value in enumerate(combine(values, classes, outputs, origin, span, period)):
            lag = span * k + start
            lags = slice(lag % lag_dev, lag % lag_dev + chunk)
            sums[lag // lag_dev, :, lags] = value
    for column in range(keep.shape[0]):
        keep[column] = sums[cores * column + scal[CORE]]
        for i, out in enumerate(sends):
            at = slice(i * out.shape[1], (i + 1) * out.shape[1])
            out[column] = sums[cores * column + 1 - scal[CORE], at].astype(BF16)


def lag_parts(scal, after, lhs, table, geometry, columns, lag_dev, split, effort):
    rows = lhs.shape[1] // 2
    shape = lambda count: (columns, count, lag_dev)
    return pl.pallas_call(
        functools.partial(lags_kernel, geometry, len(after)),
        out_shape=[jax.ShapeDtypeStruct(shape(rows), F32)]
        + [jax.ShapeDtypeStruct(shape(rows // split), BF16)] * split,
        in_specs=[SMEM] + [ANY] * len(after) + [VMEM] * 2,
        out_specs=[VMEM] * (split + 1),
        scratch_shapes=[pltpu.VMEM((2 * columns, rows, lag_dev), F32)],
        compiler_params=params(16),
        cost_estimate=effort,
        name="lags",
    )(scal, *after, lhs, table)


def cores_kernel(skip, split, scal, *refs):
    keep, *refs = refs[skip:]
    more, own, sends = refs[:split], refs[split], refs[split + 1 :]
    columns = keep.shape[0]
    for i, m in enumerate(more):
        at = slice(i * m.shape[1], (i + 1) * m.shape[1])
        for column in range(columns):
            value = keep[column, at] + m[column].astype(F32)

            @pl.when(scal[COLUMN] == column)
            def _():
                own[at] = value

            for s, out in enumerate(sends):

                @pl.when(scal[COLUMN] ^ (s + 1) == column)
                def _():
                    out[at] = value.astype(BF16)


def add_cores(scal, after, keep, more):
    columns, rows, lag_dev = keep.shape
    return pl.pallas_call(
        functools.partial(cores_kernel, len(after), len(more)),
        out_shape=[jax.ShapeDtypeStruct((rows, lag_dev), F32)]
        + [jax.ShapeDtypeStruct((rows, lag_dev), BF16)] * (columns - 1),
        in_specs=[SMEM] + [ANY] * len(after) + [VMEM] * (1 + len(more)),
        out_specs=[VMEM] * columns,
        compiler_params=params(8),
        cost_estimate=SMALL,
        name="cores",
    )(scal, *after, keep, *more)


def stats_kernel(scale, q, pieces, others, scal, *refs):
    earlier, (own, *refs) = refs[:q], refs[q:]
    more, refs = refs[:others], refs[others:]
    targets, (corr, sums) = refs[: len(pieces)], refs[len(pieces) :]
    columns = []
    for target, (unit, first, count, at) in zip(targets, placed(pieces)):
        value = own[at]
        for m in more:
            value = value + m[at].astype(F32)
        slot = first + lax.broadcasted_iota(jnp.int32, (count, 1), 0)
        value = value * jnp.where(slot < scal[COUNT + unit], scale, 0.0)
        corr[at] = value
        square = jnp.sum(value * value, axis=1, keepdims=True)
        product = jnp.sum(value * target[0], axis=1, keepdims=True)
        lane = lax.broadcasted_iota(jnp.int32, (count, LANES), 1)
        columns.append(jnp.where(lane == 2 * q, square, jnp.where(lane == 2 * q + 1, product, 0.0)))
    total = jnp.concatenate(columns, axis=0).T[:8]
    for e in earlier:
        total = total + e[...]
    sums[...] = total


def target_specs(pieces, lag_dev):
    return [
        pl.BlockSpec(
            (1, count, lag_dev),
            lambda i, scal, unit=unit, block=first // count: (scal[BLOCK + unit], block, 0),
        )
        for unit, first, count in pieces
    ]


def whole(shape):
    return pl.BlockSpec(shape, lambda i, scal: (0,) * len(shape))


def lag_stats(scal, scale, q, pieces, earlier, own, more, observed):
    rows, lag_dev = own.shape
    outs = [jax.ShapeDtypeStruct((rows, lag_dev), F32), jax.ShapeDtypeStruct((8, rows), F32)]
    return pl.pallas_call(
        functools.partial(stats_kernel, scale, q, pieces, len(more)),
        grid_spec=pltpu.PrefetchScalarGridSpec(
            num_scalar_prefetch=1,
            grid=(1,),
            in_specs=[whole(e.shape) for e in earlier]
            + [whole(own.shape)] * (1 + len(more))
            + target_specs(pieces, lag_dev),
            out_specs=[whole(o.shape) for o in outs],
        ),
        out_shape=outs,
        compiler_params=params(16),
        cost_estimate=SMALL,
        name="stats",
    )(scal, *earlier, own, *more, *[observed] * len(pieces))


def slot_scales(sums, lag_total, q):
    total = sums[0][...]
    for s in sums[1:]:
        total = total + s[...]
    rows = total.shape[1]
    square, product = total[2 * q : 2 * q + 1], total[2 * q + 1 : 2 * q + 2]
    inverse = 1.0 / jnp.sqrt(square / lag_total + EPSILON)
    bending = (square * inverse * inverse - product * inverse) / lag_total
    sub = lax.broadcasted_iota(jnp.int32, (LANES, rows), 0)
    both = jnp.where(sub == 0, inverse, jnp.where(sub == 1, bending, 0.0)).T
    return both[:, 0:1], both[:, 1:2]


def gradient_kernel(lag_total, q, pieces, parts, skip, scal, *refs):
    refs = refs[skip:]
    sums, corr, refs = refs[:parts], refs[parts], refs[parts + 1 :]
    targets, outs = refs[: len(pieces)], refs[len(pieces) :]
    inverse, bending = slot_scales(sums, lag_total, q)
    for target, out, (unit, first, count, at) in zip(targets, outs, placed(pieces)):
        slot = first + lax.broadcasted_iota(jnp.int32, (count, 1), 0)
        valid = jnp.where(slot < scal[COUNT + unit], inverse[at], 0.0)
        normed = corr[at] * inverse[at]
        out[...] = ((normed - target[0] - normed * bending[at]) * valid).astype(BF16)


def gradients(scal, lag_total, q, pieces, after, sums, corr, observed):
    lag_dev = corr.shape[1]
    outs = [jax.ShapeDtypeStruct((p[2], lag_dev), BF16) for p in pieces]
    return pl.pallas_call(
        functools.partial(gradient_kernel, lag_total, q, pieces, len(sums), len(after)),
        grid_spec=pltpu.PrefetchScalarGridSpec(
            num_scalar_prefetch=1,
            grid=(1,),
            in_specs=[ANY] * len(after)
            + [whole(sums[0].shape)] * len(sums)
            + [whole(corr.shape)]
            + target_specs(pieces, lag_dev),
            out_specs=[whole(o.shape) for o in outs],
        ),
        out_shape=outs,
        compiler_params=params(16),
        cost_estimate=SMALL,
        name="gradient",
    )(scal, *after, *sums, corr, *[observed] * len(pieces))


def normed_kernel(lag_total, chunks, parts, scal, *refs):
    sums, corrs, out = refs[:parts], refs[parts:-1], refs[-1]
    for q, (pieces, corr) in enumerate(zip(chunks, corrs)):
        inverse, _ = slot_scales(sums, lag_total, q)
        for unit, first, count, at in placed(pieces):

            @pl.when(pl.program_id(0) == unit)
            def _():
                out[0, first : first + count] = corr[at] * inverse[at]


def normed_rows(scal, lag_total, chunks, sums, corrs, observed):
    blocks, slots, lag_dev = observed.shape
    ins = [*sums, *corrs]
    return pl.pallas_call(
        functools.partial(normed_kernel, lag_total, chunks, len(sums)),
        grid_spec=pltpu.PrefetchScalarGridSpec(
            num_scalar_prefetch=1,
            grid=(blocks,),
            in_specs=[whole(x.shape) for x in ins],
            out_specs=pl.BlockSpec((1, slots, lag_dev), lambda i, scal: (scal[BLOCK + i], 0, 0)),
        ),
        out_shape=jax.ShapeDtypeStruct(observed.shape, F32),
        compiler_params=params(16),
        cost_estimate=SMALL,
        name="normed",
    )(scal, *ins)


def adjoint_kernel(pieces, *refs):
    ids, parts, out = refs[: len(pieces)], refs[len(pieces) : -1], refs[-1]
    pick = picks([i.at[:, p[1] : p[1] + p[2]] for i, p in zip(ids, pieces)], out.shape[0])
    rows = jnp.concatenate([p[...] for p in parts], axis=0)
    out[...] = jnp.dot(pick, rows, preferred_element_type=F32)


def adjoint_rows(src_ids, pieces, parts, channels):
    lag_dev = parts[0].shape[1]
    return pl.pallas_call(
        functools.partial(adjoint_kernel, pieces),
        out_shape=jax.ShapeDtypeStruct((channels, lag_dev), F32),
        in_specs=[VMEM] * (2 * len(parts)),
        out_specs=VMEM,
        compiler_params=params(16),
        cost_estimate=SMALL,
        name="adjoint",
    )(*[src_ids[p[0]] for p in pieces], *parts)


def shards(spectra, window_keep, owners, pair_src, pair_rec, pair_count, observed):
    columns, cores, places = lax.axis_size("win"), lax.axis_size("freq"), lax.axis_size("recv")
    column, core, place = lax.axis_index("win"), lax.axis_index("freq"), lax.axis_index("recv")
    assert spectra.shape[0] == 1 and cores == 2
    channels, bins_dev = spectra.shape[2:]
    blocks, slots, lag_dev = observed.shape
    lag_total = lag_dev * columns * cores
    bin_total = bins_dev * cores
    period = 2 * bin_total
    part = bins_dev // columns
    classes = part // LANES
    span = period // classes
    geometry = (classes, span, lag_total // span, lag_total // 2, period, 256)
    lag_scale = 1.0 / math.sqrt(bin_total * columns)
    peers = columns * cores
    some = slots // 2
    shifts = range(places)

    held = [
        swapped(
            lax.dynamic_slice(
                spectra, (0, 0, 0, (column ^ s) * part), (1, 2, channels, part)
            ),
            "win",
            columns,
            s,
        )
        for s in range(columns)
    ]
    scal, wanted, rec_ids = index(
        window_keep, owners, pair_count, pair_src, pair_rec, places
    )
    if columns == 2:
        weight = jnp.ones((1,), F32)
    else:
        keeps = jnp.stack([swapped(window_keep[0], "win", columns, s) for s in range(columns)])
        ranked = jnp.argsort(-keeps)[: columns - 1].astype(jnp.int32)
        weight = keeps[ranked].astype(F32)
        scal = lax.dynamic_update_slice(scal, ranked, (ORDER,))

    direct = places == blocks
    src_ids = [swapped(wanted[d], "recv", places, d) for d in reversed(shifts)][::-1]
    trig = tables(classes, span, period, bins_dev, columns, cores)
    table = make_table(scal, trig, classes, span, peers)
    if direct and blocks == 4:
        chunks = [
            [(0, 0, slots), (1, 0, slots)],
            [(2, 0, slots), (3, 0, slots)],
        ]
    else:
        chunks = [[(d, first, some) for d in range(blocks)] for first in (0, some)]
    if direct:
        messages = [piece for pieces in chunks for piece in pieces]
    else:
        messages = [(d, 0, slots) for d in shifts]
    sent, own_rows = gather_rows(
        scal, table, held[0], held[1:], make_perm(part), src_ids, rec_ids, messages
    )
    arrived = [swapped(x, "recv", places, m[0]) for m, x in reversed(list(zip(messages, sent)))][::-1]
    if not direct:
        stacked = jnp.stack(arrived)
        whole_rows = [
            lax.dynamic_index_in_dim(stacked, place ^ owners[b], 0, False) for b in range(blocks)
        ]
        arrived = [whole_rows[piece[0]] for pieces in chunks for piece in pieces]
    corrs, all_sums, returned, returned_pieces = [], [], [], []
    after = []
    for q, pieces in enumerate(chunks):
        rows = arrived[len(pieces) * q : len(pieces) * (q + 1)]
        lhs = cross_rows(weight, after[:1], rows, own_rows, pieces, classes)
        keep, *sends = lag_parts(
            scal, [], lhs, table, geometry, columns, lag_dev, SPLIT if q else 2 * SPLIT, SMALL if q else LARGE
        )
        sends = [swapped(x, "freq", cores, 1) for x in sends]
        own, *sends = add_cores(scal, after[1:], keep, sends)
        more = [swapped(x, "win", columns, s + 1) for s, x in enumerate(sends)]
        after = [own, *more]
        corr, sums = lag_stats(scal, lag_scale, q, pieces, all_sums, own, more, observed)
        corrs.append(corr)
        all_sums = [sums]
    sums = [swapped(sums, ("win", "freq"), peers, s) for s in range(peers)]
    after = []
    for q in reversed(range(len(chunks))):
        pieces = chunks[q]
        grads = gradients(scal, lag_total, q, pieces, after, sums, corrs[q], observed)
        after = [grads[0]]
        if not direct:
            stacked = jnp.stack(list(grads) + [jnp.zeros_like(grads[0])])
            grads = []
            for d in shifts:
                block = jnp.int32(blocks)
                for b in range(blocks):
                    block = jnp.where(owners[b] == place ^ d, b, block)
                grads.append(lax.dynamic_index_in_dim(stacked, block, 0, False))
            pieces = [(d, pieces[0][1], some) for d in shifts]
        sent = [swapped(g, "recv", places, p[0]) for p, g in reversed(list(zip(pieces, grads)))]
        returned += sent[::-1]
        returned_pieces += pieces
    normed = normed_rows(scal, lag_total, chunks, sums, corrs, observed)
    adjoint = adjoint_rows(src_ids, returned_pieces, returned, channels)
    return (normed, adjoint)


def solution(mesh):
    return jax.shard_map(
        shards,
        mesh=mesh,
        in_specs=(
            P("win", None, ("groups", "recv"), "freq"),
            P(("groups", "win")),
            P("groups"),
            P(None, ("groups", "recv")),
            P(None, ("groups", "recv")),
            P(None, ("groups", "recv")),
            P(None, ("groups", "recv"), ("win", "freq")),
        ),
        out_specs=(
            P(None, ("groups", "recv"), ("win", "freq")),
            P(("groups", "recv"), ("win", "freq")),
        ),
        check_vma=False,
    )
```

```python
import functools
import math

import jax
import jax.numpy as jnp
import ml_dtypes
import numpy as np
from jax import lax
from jax.experimental import pallas as pl
from jax.experimental.pallas import tpu as pltpu
from jax.sharding import PartitionSpec as P

EPSILON = 1e-06
MIB = 1 << 20
LANES = 128
SPLIT = 4
CORE, COLUMN, ORDER, BLOCK, COUNT = 0, 1, 2, 8, 16
BF16 = jnp.bfloat16
F32 = jnp.float32
VMEM = pl.BlockSpec(memory_space=pltpu.VMEM)
SMEM = pl.BlockSpec(memory_space=pltpu.SMEM)
HBM = pl.BlockSpec(memory_space=pltpu.HBM)
ANY = pl.BlockSpec(memory_space=pl.ANY)


def swapped(value, axis, size, step):
    assert size & (size - 1) == 0
    if step == 0:
        return value
    return lax.ppermute(value, axis, [(i, i ^ step) for i in range(size)])


def params(mib):
    return pltpu.CompilerParams(vmem_limit_bytes=mib * MIB)


SMALL = pl.CostEstimate(flops=1, bytes_accessed=1, transcendentals=0)
LARGE = pl.CostEstimate(flops=2 * 10**10, bytes_accessed=MIB, transcendentals=0)


def tables(classes, span, period, bins_dev, columns, cores):
    u = np.arange(span, dtype=np.int64)[None, :]
    piece = np.arange(columns * cores, dtype=np.int64)[:, None]
    first = piece % cores * bins_dev + piece // cores * (bins_dev // columns)
    rows = (first + np.arange(classes)).reshape(-1)
    high = 16 * classes * np.arange(LANES // 16, dtype=np.int64)
    low = classes * np.arange(16, dtype=np.int64)
    angle = (np.concatenate([rows, high, low])[:, None] * u % period) * (2.0 * math.pi / period)
    return np.stack([np.cos(angle), np.sin(angle)]).astype(np.float32)


def fetch(pairs, sems):
    copies = [pltpu.make_async_copy(a, b, sems.at[i]) for i, (a, b) in enumerate(pairs)]
    for c in copies:
        c.start()
    for c in copies:
        c.wait()


def index_kernel(blocks, direct, *refs):
    given, refs = refs[:5], refs[5:]
    scal, wanted, rec_ids, held, sems = refs[0], refs[1:-7], refs[-7], refs[-6:-1], refs[-1]
    fetch(zip(given, held), sems)
    window_keep, owners, pair_count, src, rec = held
    place = lax.axis_index("recv")
    column, columns = lax.axis_index("win"), lax.axis_size("win")
    core = lax.axis_index("freq")
    scal[CORE] = core
    scal[COLUMN] = column
    scal[ORDER] = 1 - window_keep[0]
    for b in range(blocks):
        unit = place ^ owners[b] if direct else b
        scal[BLOCK + unit] = b
        scal[COUNT + unit] = pair_count[b]
    for d, out in enumerate(wanted):
        chosen = jnp.full(out.shape, -1, jnp.int32)
        received = jnp.zeros(out.shape, jnp.int32)
        for b in range(blocks):
            mine = jnp.full(out.shape, owners[b], jnp.int32) == (place ^ d)
            chosen = jnp.where(mine, src[b : b + 1], chosen)
            received = jnp.where(mine, rec[b : b + 1], received)
        out[...] = chosen
        if direct:
            rec_ids[d : d + 1] = received
    if not direct:
        rec_ids[...] = rec[...]


def index(window_keep, owners, pair_count, pair_src, pair_rec, places):
    blocks, slots = pair_src.shape
    ids = jax.ShapeDtypeStruct((1, slots), jnp.int32)
    given = [window_keep, owners, pair_count[:, 0], pair_src, pair_rec]
    scal, *wanted, rec_ids = pl.pallas_call(
        functools.partial(index_kernel, blocks, places == blocks),
        out_shape=[jax.ShapeDtypeStruct((LANES,), jnp.int32)]
        + [ids] * places
        + [jax.ShapeDtypeStruct(pair_rec.shape, jnp.int32)],
        in_specs=[HBM] * 5,
        out_specs=[SMEM] + [VMEM] * (places + 1),
        scratch_shapes=[pltpu.SMEM(g.shape, g.dtype) for g in given[:3]]
        + [pltpu.VMEM(g.shape, g.dtype) for g in given[3:]]
        + [pltpu.SemaphoreType.DMA((5,))],
        compiler_params=params(16),
        cost_estimate=SMALL,
        name="index",
    )(*given)
    return scal, wanted, rec_ids


def table_kernel(classes, parts, scal, trig, table, base):
    rows = parts * classes
    low = slice(rows + LANES // 16, rows + LANES // 16 + 16)
    cl, sl = trig[0, low], trig[1, low]
    for h in range(LANES // 16):
        ch, sh = trig[0, rows + h : rows + h + 1], trig[1, rows + h : rows + h + 1]
        base[0, 16 * h : 16 * h + 16] = ch * cl - sh * sl
        base[1, 16 * h : 16 * h + 16] = sh * cl + ch * sl
    first = (scal[CORE] + 2 * scal[COLUMN]) * classes
    cb, sb = base[0], base[1]
    for r in range(classes):
        ca, sa = trig[0, pl.ds(first + r, 1)], trig[1, pl.ds(first + r, 1)]
        table[r, :LANES] = (ca * cb - sa * sb).astype(BF16)
        table[r, LANES:] = (-(sa * cb + ca * sb)).astype(BF16)


def make_table(scal, trig, classes, span, parts):
    return pl.pallas_call(
        functools.partial(table_kernel, classes, parts),
        out_shape=jax.ShapeDtypeStruct((classes, 2 * LANES, span), BF16),
        in_specs=[SMEM, VMEM],
        out_specs=VMEM,
        scratch_shapes=[pltpu.VMEM((2, LANES, span), F32)],
        compiler_params=params(12),
        cost_estimate=SMALL,
        name="table",
    )(scal, jnp.asarray(trig))


def perm_kernel(perm):
    part = perm.shape[0]
    classes = part // LANES
    source = lax.broadcasted_iota(jnp.int32, (part, LANES), 0)
    target = classes * lax.broadcasted_iota(jnp.int32, (part, LANES), 1)
    for r in range(classes):
        perm[:, r * LANES : (r + 1) * LANES] = (source == target + r).astype(BF16)


def make_perm(part):
    return pl.pallas_call(
        perm_kernel,
        out_shape=jax.ShapeDtypeStruct((part, part), BF16),
        out_specs=VMEM,
        compiler_params=params(8),
        cost_estimate=SMALL,
        name="perm",
    )()


def picks(ids, channels):
    row = jnp.concatenate([i[...] for i in ids], axis=1)
    return (lax.broadcasted_iota(jnp.int32, (channels, row.shape[1]), 0) == row).astype(BF16)


def rows_kernel(used, sends, messages, scal, after, here, *refs):
    held, refs = refs[:used], refs[used:]
    perm, src_ids, rec_ids, refs = refs[0], refs[sends:0:-1], refs[1 + sends], refs[2 + sends :]
    outs, own_out = refs[:-1], refs[-1]
    units, _, _, slots, part = own_out.shape
    channels = here.shape[2]
    pick = picks(list(src_ids) + [rec_ids.at[d : d + 1] for d in range(units)], channels)
    for u in range(used):
        for half in range(2):
            x = here[0, half]
            for s in range(used):
                x = jnp.where(scal[ORDER + u] == s + 1, held[s][0, half], x)
            x = jnp.dot(x, perm[...], preferred_element_type=F32).astype(BF16)
            y = lax.dot_general(
                pick, x, (((0,), (0,)), ((), ())), preferred_element_type=F32
            ).astype(BF16)
            for (d, first, count), out in zip(messages, outs):
                at = d * slots + first
                out[u, half] = y[at : at + count]
            for d in range(units):
                at = (sends + d) * slots
                own_out[d, u, half] = y[at : at + slots]


def gather_rows(scal, after, here, held, perm, src_ids, rec_ids, messages):
    used, sends = len(held), len(src_ids)
    part = held[0].shape[-1]
    units, slots = rec_ids.shape
    *sent, own = pl.pallas_call(
        functools.partial(rows_kernel, used, sends, messages),
        out_shape=[jax.ShapeDtypeStruct((used, 2, m[2], part), BF16) for m in messages]
        + [jax.ShapeDtypeStruct((units, used, 2, slots, part), BF16)],
        in_specs=[SMEM, pl.BlockSpec(memory_space=pl.ANY)] + [VMEM] * (used + 3 + sends),
        out_specs=[VMEM] * (len(messages) + 1),
        compiler_params=params(16),
        cost_estimate=SMALL,
        name="rows",
    )(scal, after, here, *held, perm, *src_ids[::-1], rec_ids)
    return sent, own


def combine(values, classes, outputs, origin, span, period):
    plain, scaled = [None] * outputs, [None] * outputs

    def add(into, k, value, sign):
        if into[k] is None:
            into[k] = value if sign > 0 else -value
        else:
            into[k] = into[k] + value if sign > 0 else into[k] - value

    for r, (real, imag) in enumerate(values):
        both = None
        for k in range(outputs):
            eighths = r * (span * k - origin) * 8 // period % 8
            assert r * (span * k - origin) * 8 % period == 0
            if eighths % 2 == 0:
                value, sign = ((real, 1), (imag, -1), (real, -1), (imag, 1))[eighths // 2]
                add(plain, k, value, sign)
            else:
                if both is None:
                    both = real + imag, real - imag
                value, sign = ((both[1], 1), (both[0], -1), (both[1], -1), (both[0], 1))[eighths // 2]
                add(scaled, k, value, sign)
    root = math.sqrt(0.5)
    return [a if b is None else a + root * b for a, b in zip(plain, scaled)]


def placed(pieces):
    at = 0
    for unit, first, count in pieces:
        yield unit, first, count, slice(at, at + count)
        at += count


def cross_kernel(pieces, skip, weight, *refs):
    refs = refs[skip:]
    s_refs, own, lhs = refs[:-2], refs[-2], refs[-1]
    used = own.shape[1]
    rows = lhs.shape[1] // 2
    for s_ref, (unit, first, count, at) in zip(s_refs, placed(pieces)):
        turned = slice(rows + at.start, rows + at.stop)
        mine = slice(first, first + count)
        sent = mine if s_ref.shape[2] > count else slice(0, count)
        for r in range(lhs.shape[0]):
            bins = slice(r * LANES, (r + 1) * LANES)
            real = imag = None
            for u in range(used):
                sr, si = (s_ref[u, half, sent, bins].astype(F32) for half in range(2))
                rr, ri = (own[unit, u, half, mine, bins].astype(F32) for half in range(2))
                re, im = sr * rr + si * ri, si * rr - sr * ri
                if u:
                    re, im = real + weight[u] * re, imag + weight[u] * im
                real, imag = re, im
            lhs[r, at, :LANES] = real.astype(BF16)
            lhs[r, at, LANES:] = imag.astype(BF16)
            lhs[r, turned, :LANES] = imag.astype(BF16)
            lhs[r, turned, LANES:] = (-real).astype(BF16)


def cross_rows(weight, after, rows, own, pieces, classes):
    count = sum(p[2] for p in pieces)
    return pl.pallas_call(
        functools.partial(cross_kernel, pieces, len(after)),
        out_shape=jax.ShapeDtypeStruct((classes, 2 * count, 2 * LANES), BF16),
        in_specs=[SMEM] + [ANY] * len(after) + [VMEM] * (len(rows) + 1),
        out_specs=VMEM,
        compiler_params=params(8),
        cost_estimate=LARGE,
        name="cross",
    )(weight, *after, *rows, own)


def lags_kernel(geometry, split, skip, scal, *refs):
    classes, span, outputs, origin, period, chunk = geometry
    lhs, table, keep, *refs = refs[skip:]
    sends, sums = refs[:split], refs[split:]
    rows = lhs.shape[1] // 2
    lag_dev = keep.shape[-1]
    cores = 2
    at_once = span == lag_dev
    first = scal[CORE] == 0
    for start in range(0, span, chunk):
        values = []
        for r in range(classes):
            whole_turns = all(
                r * (span * k - origin) * 2 % period == 0 for k in range(outputs)
            )
            left = lhs[r, :rows] if whole_turns else lhs[r]
            y = jnp.dot(left, table[r, :, start : start + chunk], preferred_element_type=F32)
            values.append((y[:rows], None if whole_turns else y[rows:]))
        corr = combine(values, classes, outputs, origin, span, period)
        lags = slice(start, start + chunk)
        for column in range(keep.shape[0]) if at_once else ():
            even, odd = corr[2 * column], corr[2 * column + 1]
            keep[column, :, lags] = jnp.where(first, even, odd)
            other = jnp.where(first, odd, even).astype(BF16)
            for i, out in enumerate(sends):
                out[column, :, lags] = other[i * out.shape[1] : (i + 1) * out.shape[1]]
        for k, value in enumerate(corr) if not at_once else ():
            lag = span * k + start
            sums[0][lag // lag_dev, :, lag % lag_dev : lag % lag_dev + chunk] = value
    if at_once:
        return
    for column in range(keep.shape[0]):
        keep[column] = sums[0][cores * column + scal[CORE]]
        for i, out in enumerate(sends):
            at = slice(i * out.shape[1], (i + 1) * out.shape[1])
            out[column] = sums[0][cores * column + 1 - scal[CORE], at].astype(BF16)


def lag_parts(scal, after, lhs, table, geometry, columns, lag_dev, split, effort):
    rows = lhs.shape[1] // 2
    shape = lambda count: (columns, count, lag_dev)
    return pl.pallas_call(
        functools.partial(lags_kernel, geometry, split, len(after)),
        out_shape=[jax.ShapeDtypeStruct(shape(rows), F32)]
        + [jax.ShapeDtypeStruct(shape(rows // split), BF16)] * split,
        in_specs=[SMEM] + [ANY] * len(after) + [VMEM] * 2,
        out_specs=[VMEM] * (split + 1),
        scratch_shapes=[pltpu.VMEM((2 * columns, rows, lag_dev), F32)] * (geometry[1] != lag_dev),
        compiler_params=params(16),
        cost_estimate=effort,
        name="lags",
    )(scal, *after, lhs, table)


def cores_kernel(skip, split, scal, *refs):
    keep, *refs = refs[skip:]
    more, own, sends = refs[:split], refs[split], refs[split + 1 :]
    columns = keep.shape[0]
    for i, m in enumerate(more):
        at = slice(i * m.shape[1], (i + 1) * m.shape[1])
        for column in range(columns):
            value = keep[column, at] + m[column].astype(F32)

            @pl.when(scal[COLUMN] == column)
            def _():
                own[at] = value

            for s, out in enumerate(sends):

                @pl.when(scal[COLUMN] ^ (s + 1) == column)
                def _():
                    out[at] = value.astype(BF16)


def add_cores(scal, after, keep, more):
    columns, rows, lag_dev = keep.shape
    return pl.pallas_call(
        functools.partial(cores_kernel, len(after), len(more)),
        out_shape=[jax.ShapeDtypeStruct((rows, lag_dev), F32)]
        + [jax.ShapeDtypeStruct((rows, lag_dev), BF16)] * (columns - 1),
        in_specs=[SMEM] + [ANY] * len(after) + [VMEM] * (1 + len(more)),
        out_specs=[VMEM] * columns,
        compiler_params=params(8),
        cost_estimate=SMALL,
        name="cores",
    )(scal, *after, keep, *more)


def stats_kernel(scale, q, pieces, others, scal, *refs):
    earlier, (own, *refs) = refs[:q], refs[q:]
    more, refs = refs[:others], refs[others:]
    targets, (corr, sums) = refs[: len(pieces)], refs[len(pieces) :]
    columns = []
    for target, (unit, first, count, at) in zip(targets, placed(pieces)):
        value = own[at]
        for m in more:
            value = value + m[at].astype(F32)
        slot = first + lax.broadcasted_iota(jnp.int32, (count, 1), 0)
        value = value * jnp.where(slot < scal[COUNT + unit], scale, 0.0)
        corr[at] = value
        square = jnp.sum(value * value, axis=1, keepdims=True)
        product = jnp.sum(value * target[0], axis=1, keepdims=True)
        lane = lax.broadcasted_iota(jnp.int32, (count, LANES), 1)
        columns.append(jnp.where(lane == 2 * q, square, jnp.where(lane == 2 * q + 1, product, 0.0)))
    total = jnp.concatenate(columns, axis=0).T[:8]
    for e in earlier:
        total = total + e[...]
    sums[...] = total


def target_specs(pieces, lag_dev):
    return [
        pl.BlockSpec(
            (1, count, lag_dev),
            lambda i, scal, unit=unit, block=first // count: (scal[BLOCK + unit], block, 0),
        )
        for unit, first, count in pieces
    ]


def whole(shape):
    return pl.BlockSpec(shape, lambda i, scal: (0,) * len(shape))


def lag_stats(scal, scale, q, pieces, earlier, own, more, observed):
    rows, lag_dev = own.shape
    outs = [jax.ShapeDtypeStruct((rows, lag_dev), F32), jax.ShapeDtypeStruct((8, rows), F32)]
    return pl.pallas_call(
        functools.partial(stats_kernel, scale, q, pieces, len(more)),
        grid_spec=pltpu.PrefetchScalarGridSpec(
            num_scalar_prefetch=1,
            grid=(1,),
            in_specs=[whole(e.shape) for e in earlier]
            + [whole(own.shape)] * (1 + len(more))
            + target_specs(pieces, lag_dev),
            out_specs=[whole(o.shape) for o in outs],
        ),
        out_shape=outs,
        compiler_params=params(16),
        cost_estimate=SMALL,
        name="stats",
    )(scal, *earlier, own, *more, *[observed] * len(pieces))


def slot_scales(sums, lag_total, q):
    total = sums[0][...]
    for s in sums[1:]:
        total = total + s[...]
    rows = total.shape[1]
    square, product = total[2 * q : 2 * q + 1], total[2 * q + 1 : 2 * q + 2]
    inverse = 1.0 / jnp.sqrt(square / lag_total + EPSILON)
    bending = (square * inverse * inverse - product * inverse) / lag_total
    sub = lax.broadcasted_iota(jnp.int32, (LANES, rows), 0)
    both = jnp.where(sub == 0, inverse, jnp.where(sub == 1, bending, 0.0)).T
    return both[:, 0:1], both[:, 1:2]


def gradient_kernel(lag_total, q, pieces, parts, skip, scal, *refs):
    refs = refs[skip:]
    sums, corr, refs = refs[:parts], refs[parts], refs[parts + 1 :]
    targets, outs = refs[: len(pieces)], refs[len(pieces) :]
    inverse, bending = slot_scales(sums, lag_total, q)
    for target, out, (unit, first, count, at) in zip(targets, outs, placed(pieces)):
        slot = first + lax.broadcasted_iota(jnp.int32, (count, 1), 0)
        valid = jnp.where(slot < scal[COUNT + unit], inverse[at], 0.0)
        normed = corr[at] * inverse[at]
        out[...] = ((normed - target[0] - normed * bending[at]) * valid).astype(BF16)


def gradients(scal, lag_total, q, pieces, after, sums, corr, observed):
    lag_dev = corr.shape[1]
    outs = [jax.ShapeDtypeStruct((p[2], lag_dev), BF16) for p in pieces]
    return pl.pallas_call(
        functools.partial(gradient_kernel, lag_total, q, pieces, len(sums), len(after)),
        grid_spec=pltpu.PrefetchScalarGridSpec(
            num_scalar_prefetch=1,
            grid=(1,),
            in_specs=[ANY] * len(after)
            + [whole(sums[0].shape)] * len(sums)
            + [whole(corr.shape)]
            + target_specs(pieces, lag_dev),
            out_specs=[whole(o.shape) for o in outs],
        ),
        out_shape=outs,
        compiler_params=params(16),
        cost_estimate=SMALL,
        name="gradient",
    )(scal, *after, *sums, corr, *[observed] * len(pieces))


def normed_kernel(lag_total, chunks, parts, scal, *refs):
    sums, corrs, out = refs[:parts], refs[parts:-1], refs[-1]
    for q, (pieces, corr) in enumerate(zip(chunks, corrs)):
        inverse, _ = slot_scales(sums, lag_total, q)
        for unit, first, count, at in placed(pieces):

            @pl.when(pl.program_id(0) == unit)
            def _():
                out[0, first : first + count] = corr[at] * inverse[at]


def normed_rows(scal, lag_total, chunks, sums, corrs, observed):
    blocks, slots, lag_dev = observed.shape
    ins = [*sums, *corrs]
    return pl.pallas_call(
        functools.partial(normed_kernel, lag_total, chunks, len(sums)),
        grid_spec=pltpu.PrefetchScalarGridSpec(
            num_scalar_prefetch=1,
            grid=(blocks,),
            in_specs=[whole(x.shape) for x in ins],
            out_specs=pl.BlockSpec((1, slots, lag_dev), lambda i, scal: (scal[BLOCK + i], 0, 0)),
        ),
        out_shape=jax.ShapeDtypeStruct(observed.shape, F32),
        compiler_params=params(16),
        cost_estimate=SMALL,
        name="normed",
    )(scal, *ins)


def adjoint_kernel(pieces, *refs):
    ids, parts, out = refs[: len(pieces)], refs[len(pieces) : -1], refs[-1]
    pick = picks([i.at[:, p[1] : p[1] + p[2]] for i, p in zip(ids, pieces)], out.shape[0])
    rows = jnp.concatenate([p[...] for p in parts], axis=0)
    out[...] = jnp.dot(pick, rows, preferred_element_type=F32)


def adjoint_rows(src_ids, pieces, parts, channels):
    lag_dev = parts[0].shape[1]
    return pl.pallas_call(
        functools.partial(adjoint_kernel, pieces),
        out_shape=jax.ShapeDtypeStruct((channels, lag_dev), F32),
        in_specs=[VMEM] * (2 * len(parts)),
        out_specs=VMEM,
        compiler_params=params(16),
        cost_estimate=SMALL,
        name="adjoint",
    )(*[src_ids[p[0]] for p in pieces], *parts)


def shards(spectra, window_keep, owners, pair_src, pair_rec, pair_count, observed):
    columns, cores, places = lax.axis_size("win"), lax.axis_size("freq"), lax.axis_size("recv")
    column, core, place = lax.axis_index("win"), lax.axis_index("freq"), lax.axis_index("recv")
    assert spectra.shape[0] == 1 and cores == 2
    channels, bins_dev = spectra.shape[2:]
    blocks, slots, lag_dev = observed.shape
    lag_total = lag_dev * columns * cores
    bin_total = bins_dev * cores
    period = 2 * bin_total
    part = bins_dev // columns
    classes = part // LANES
    span = period // classes
    geometry = (classes, span, lag_total // span, lag_total // 2, period, 256)
    lag_scale = 1.0 / math.sqrt(bin_total * columns)
    peers = columns * cores
    some = slots // 2
    shifts = range(places)

    held = [
        swapped(
            lax.dynamic_slice(
                spectra, (0, 0, 0, (column ^ s) * part), (1, 2, channels, part)
            ),
            "win",
            columns,
            s,
        )
        for s in range(columns)
    ]
    scal, wanted, rec_ids = index(
        window_keep, owners, pair_count, pair_src, pair_rec, places
    )
    if columns == 2:
        weight = jnp.ones((1,), F32)
    else:
        keeps = jnp.stack([swapped(window_keep[0], "win", columns, s) for s in range(columns)])
        ranked = jnp.argsort(-keeps)[: columns - 1].astype(jnp.int32)
        weight = keeps[ranked].astype(F32)
        scal = lax.dynamic_update_slice(scal, ranked, (ORDER,))

    direct = places == blocks
    src_ids = [swapped(wanted[d], "recv", places, d) for d in reversed(shifts)][::-1]
    trig = tables(classes, span, period, bins_dev, columns, cores)
    table = make_table(scal, trig, classes, span, peers)
    if direct and blocks == 4:
        chunks = [
            [(0, 0, slots), (1, 0, slots)],
            [(3, 0, slots), (2, 0, slots)],
        ]
    else:
        chunks = [[(d, first, some) for d in range(blocks)] for first in (0, some)]
    if direct:
        messages = [piece for pieces in chunks for piece in pieces]
    else:
        messages = [(d, 0, slots) for d in shifts]
    sent, own_rows = gather_rows(
        scal, table, held[0], held[1:], make_perm(part), src_ids, rec_ids, messages
    )
    arrived = [swapped(x, "recv", places, m[0]) for m, x in reversed(list(zip(messages, sent)))][::-1]
    if not direct:
        stacked = jnp.stack(arrived)
        whole_rows = [
            lax.dynamic_index_in_dim(stacked, place ^ owners[b], 0, False) for b in range(blocks)
        ]
        arrived = [whole_rows[piece[0]] for pieces in chunks for piece in pieces]
    corrs, all_sums, returned, returned_pieces = [], [], [], []
    after = []
    for q, pieces in enumerate(chunks):
        rows = arrived[len(pieces) * q : len(pieces) * (q + 1)]
        lhs = cross_rows(weight, after[:1], rows, own_rows, pieces, classes)
        keep, *sends = lag_parts(
            scal, [], lhs, table, geometry, columns, lag_dev, SPLIT if q else 2 * SPLIT, SMALL if q else LARGE
        )
        sends = [swapped(x, "freq", cores, 1) for x in sends]
        own, *sends = add_cores(scal, after[1:], keep, sends)
        more = [swapped(x, "win", columns, s + 1) for s, x in enumerate(sends)]
        after = [own, *more]
        corr, sums = lag_stats(scal, lag_scale, q, pieces, all_sums, own, more, observed)
        corrs.append(corr)
        all_sums = [sums]
    sums = [swapped(sums, ("win", "freq"), peers, s) for s in range(peers)]
    after = []
    for q in reversed(range(len(chunks))):
        pieces = chunks[q]
        grads = gradients(scal, lag_total, q, pieces, after, sums, corrs[q], observed)
        after = [grads[0]]
        if not direct:
            stacked = jnp.stack(list(grads) + [jnp.zeros_like(grads[0])])
            grads = []
            for d in shifts:
                block = jnp.int32(blocks)
                for b in range(blocks):
                    block = jnp.where(owners[b] == place ^ d, b, block)
                grads.append(lax.dynamic_index_in_dim(stacked, block, 0, False))
            pieces = [(d, pieces[0][1], some) for d in shifts]
        sent = [swapped(g, "recv", places, p[0]) for p, g in reversed(list(zip(pieces, grads)))]
        returned += sent[::-1]
        returned_pieces += pieces
    normed = normed_rows(scal, lag_total, chunks, sums, corrs, observed)
    adjoint = adjoint_rows(src_ids, returned_pieces, returned, channels)
    return (normed, adjoint)


def solution(mesh):
    return jax.shard_map(
        shards,
        mesh=mesh,
        in_specs=(
            P("win", None, ("groups", "recv"), "freq"),
            P(("groups", "win")),
            P("groups"),
            P(None, ("groups", "recv")),
            P(None, ("groups", "recv")),
            P(None, ("groups", "recv")),
            P(None, ("groups", "recv"), ("win", "freq")),
        ),
        out_specs=(
            P(None, ("groups", "recv"), ("win", "freq")),
            P(("groups", "recv"), ("win", "freq")),
        ),
        check_vma=False,
    )
```

```python
import functools
import math

import jax
import jax.numpy as jnp
import ml_dtypes
import numpy as np
from jax import lax
from jax.experimental import pallas as pl
from jax.experimental.pallas import tpu as pltpu
from jax.sharding import PartitionSpec as P

EPSILON = 1e-06
MIB = 1 << 20
LANES = 128
CORE, COLUMN, ORDER, BLOCK, COUNT = 0, 1, 2, 8, 16
BF16 = jnp.bfloat16
F32 = jnp.float32
VMEM = pl.BlockSpec(memory_space=pltpu.VMEM)
SMEM = pl.BlockSpec(memory_space=pltpu.SMEM)
HBM = pl.BlockSpec(memory_space=pltpu.HBM)
ANY = pl.BlockSpec(memory_space=pl.ANY)


def swapped(value, axis, size, step):
    assert size & (size - 1) == 0
    if step == 0:
        return value
    return lax.ppermute(value, axis, [(i, i ^ step) for i in range(size)])


def params(mib):
    return pltpu.CompilerParams(vmem_limit_bytes=mib * MIB)


SMALL = pl.CostEstimate(flops=1, bytes_accessed=1, transcendentals=0)
LARGE = pl.CostEstimate(flops=2 * 10**10, bytes_accessed=MIB, transcendentals=0)


def tables(classes, span, period, bins_dev, columns, cores):
    u = np.arange(span, dtype=np.int64)[None, :]
    piece = np.arange(columns * cores, dtype=np.int64)[:, None]
    first = piece % cores * bins_dev + piece // cores * (bins_dev // columns)
    rows = (first + np.arange(classes)).reshape(-1)
    high = 16 * classes * np.arange(LANES // 16, dtype=np.int64)
    low = classes * np.arange(16, dtype=np.int64)
    angle = (np.concatenate([rows, high, low])[:, None] * u % period) * (2.0 * math.pi / period)
    return np.stack([np.cos(angle), np.sin(angle)]).astype(np.float32)


def fetch(pairs, sems):
    copies = [pltpu.make_async_copy(a, b, sems.at[i]) for i, (a, b) in enumerate(pairs)]
    for c in copies:
        c.start()
    for c in copies:
        c.wait()


def index_kernel(blocks, direct, *refs):
    given, refs = refs[:5], refs[5:]
    scal, wanted, rec_ids, held, sems = refs[0], refs[1:-7], refs[-7], refs[-6:-1], refs[-1]
    fetch(zip(given, held), sems)
    window_keep, owners, pair_count, src, rec = held
    place = lax.axis_index("recv")
    column, columns = lax.axis_index("win"), lax.axis_size("win")
    core = lax.axis_index("freq")
    scal[CORE] = core
    scal[COLUMN] = column
    scal[ORDER] = 1 - window_keep[0]
    for b in range(blocks):
        unit = place ^ owners[b] if direct else b
        scal[BLOCK + unit] = b
        scal[COUNT + unit] = pair_count[b]
    for d, out in enumerate(wanted):
        chosen = jnp.full(out.shape, -1, jnp.int32)
        received = jnp.zeros(out.shape, jnp.int32)
        for b in range(blocks):
            mine = jnp.full(out.shape, owners[b], jnp.int32) == (place ^ d)
            chosen = jnp.where(mine, src[b : b + 1], chosen)
            received = jnp.where(mine, rec[b : b + 1], received)
        out[...] = chosen
        if direct:
            rec_ids[d : d + 1] = received
    if not direct:
        rec_ids[...] = rec[...]


def index(window_keep, owners, pair_count, pair_src, pair_rec, places):
    blocks, slots = pair_src.shape
    ids = jax.ShapeDtypeStruct((1, slots), jnp.int32)
    given = [window_keep, owners, pair_count[:, 0], pair_src, pair_rec]
    scal, *wanted, rec_ids = pl.pallas_call(
        functools.partial(index_kernel, blocks, places == blocks),
        out_shape=[jax.ShapeDtypeStruct((LANES,), jnp.int32)]
        + [ids] * places
        + [jax.ShapeDtypeStruct(pair_rec.shape, jnp.int32)],
        in_specs=[HBM] * 5,
        out_specs=[SMEM] + [VMEM] * (places + 1),
        scratch_shapes=[pltpu.SMEM(g.shape, g.dtype) for g in given[:3]]
        + [pltpu.VMEM(g.shape, g.dtype) for g in given[3:]]
        + [pltpu.SemaphoreType.DMA((5,))],
        compiler_params=params(16),
        cost_estimate=SMALL,
        name="index",
    )(*given)
    return scal, wanted, rec_ids


def table_kernel(classes, parts, scal, trig, table, base):
    rows = parts * classes
    low = slice(rows + LANES // 16, rows + LANES // 16 + 16)
    cl, sl = trig[0, low], trig[1, low]
    for h in range(LANES // 16):
        ch, sh = trig[0, rows + h : rows + h + 1], trig[1, rows + h : rows + h + 1]
        base[0, 16 * h : 16 * h + 16] = ch * cl - sh * sl
        base[1, 16 * h : 16 * h + 16] = sh * cl + ch * sl
    first = (scal[CORE] + 2 * scal[COLUMN]) * classes
    cb, sb = base[0], base[1]
    for r in range(classes):
        ca, sa = trig[0, pl.ds(first + r, 1)], trig[1, pl.ds(first + r, 1)]
        table[r, :LANES] = (ca * cb - sa * sb).astype(BF16)
        table[r, LANES:] = (-(sa * cb + ca * sb)).astype(BF16)


def make_table(scal, trig, classes, span, parts):
    return pl.pallas_call(
        functools.partial(table_kernel, classes, parts),
        out_shape=jax.ShapeDtypeStruct((classes, 2 * LANES, span), BF16),
        in_specs=[SMEM, VMEM],
        out_specs=VMEM,
        scratch_shapes=[pltpu.VMEM((2, LANES, span), F32)],
        compiler_params=params(12),
        cost_estimate=SMALL,
        name="table",
    )(scal, jnp.asarray(trig))


def perm_kernel(perm):
    part = perm.shape[0]
    classes = part // LANES
    source = lax.broadcasted_iota(jnp.int32, (part, LANES), 0)
    target = classes * lax.broadcasted_iota(jnp.int32, (part, LANES), 1)
    for r in range(classes):
        perm[:, r * LANES : (r + 1) * LANES] = (source == target + r).astype(BF16)


def make_perm(part):
    return pl.pallas_call(
        perm_kernel,
        out_shape=jax.ShapeDtypeStruct((part, part), BF16),
        out_specs=VMEM,
        compiler_params=params(8),
        cost_estimate=SMALL,
        name="perm",
    )()


def picks(ids, channels):
    row = jnp.concatenate([i[...] for i in ids], axis=1)
    return (lax.broadcasted_iota(jnp.int32, (channels, row.shape[1]), 0) == row).astype(BF16)


def rows_kernel(used, sends, messages, scal, after, here, *refs):
    held, perm, src_ids, refs = refs[:used], refs[used], refs[used + 1 : used + 1 + sends], refs[used + 1 + sends :]
    outs, kept = refs[:-1], refs[-1]
    _, _, channels, part = kept.shape
    slots = src_ids[0].shape[1]
    pick = picks(src_ids[::-1], channels)
    for u in range(used):
        x = here[0].reshape(2 * channels, part)
        for s in range(used):
            x = jnp.where(scal[ORDER + u] == s + 1, held[s][0].reshape(2 * channels, part), x)
        x = jnp.dot(x, perm[...], preferred_element_type=F32).astype(BF16)
        for half in range(2):
            z = x[half * channels : (half + 1) * channels]
            kept[u, half] = z
            y = lax.dot_general(
                pick, z, (((0,), (0,)), ((), ())), preferred_element_type=F32
            ).astype(BF16)
            for (d, first, count), out in zip(messages, outs):
                at = d * slots + first
                out[u, half] = y[at : at + count]


def gather_rows(scal, after, here, held, perm, src_ids, messages):
    used = len(held)
    channels, part = held[0].shape[-2:]
    *sent, kept = pl.pallas_call(
        functools.partial(rows_kernel, used, len(src_ids), messages),
        out_shape=[jax.ShapeDtypeStruct((used, 2, m[2], part), BF16) for m in messages]
        + [jax.ShapeDtypeStruct((used, 2, channels, part), BF16)],
        in_specs=[SMEM, ANY] + [VMEM] * (used + 2 + len(src_ids)),
        out_specs=[VMEM] * (len(messages) + 1),
        compiler_params=params(16),
        cost_estimate=SMALL,
        name="rows",
    )(scal, after, here, *held, perm, *src_ids[::-1])
    return sent, kept


def own_kernel(kept, rec_ids, own):
    units, used, _, slots, _ = own.shape
    pick = picks([rec_ids.at[d : d + 1] for d in range(units)], kept.shape[2])
    for u in range(used):
        for half in range(2):
            y = lax.dot_general(
                pick, kept[u, half], (((0,), (0,)), ((), ())), preferred_element_type=F32
            ).astype(BF16)
            for d in range(units):
                own[d, u, half] = y[d * slots : (d + 1) * slots]


def gather_own(kept, rec_ids):
    used, _, _, part = kept.shape
    units, slots = rec_ids.shape
    return pl.pallas_call(
        own_kernel,
        out_shape=jax.ShapeDtypeStruct((units, used, 2, slots, part), BF16),
        in_specs=[VMEM] * 2,
        out_specs=VMEM,
        compiler_params=params(16),
        cost_estimate=SMALL,
        name="own",
    )(kept, rec_ids)


def combine(values, classes, outputs, origin, span, period):
    plain, scaled = [None] * outputs, [None] * outputs

    def add(into, k, value, sign):
        if into[k] is None:
            into[k] = value if sign > 0 else -value
        else:
            into[k] = into[k] + value if sign > 0 else into[k] - value

    for r, (real, imag) in enumerate(values):
        both = None
        for k in range(outputs):
            eighths = r * (span * k - origin) * 8 // period % 8
            assert r * (span * k - origin) * 8 % period == 0
            if eighths % 2 == 0:
                value, sign = ((real, 1), (imag, -1), (real, -1), (imag, 1))[eighths // 2]
                add(plain, k, value, sign)
            else:
                if both is None:
                    both = real + imag, real - imag
                value, sign = ((both[1], 1), (both[0], -1), (both[1], -1), (both[0], 1))[eighths // 2]
                add(scaled, k, value, sign)
    root = math.sqrt(0.5)
    return [a if b is None else a + root * b for a, b in zip(plain, scaled)]


def placed(pieces):
    at = 0
    for unit, first, count in pieces:
        yield unit, first, count, slice(at, at + count)
        at += count


def cross_kernel(pieces, skip, weight, *refs):
    refs = refs[skip:]
    s_refs, own, lhs = refs[:-2], refs[-2], refs[-1]
    used = own.shape[1]
    rows = lhs.shape[1] // 2
    for s_ref, (unit, first, count, at) in zip(s_refs, placed(pieces)):
        turned = slice(rows + at.start, rows + at.stop)
        mine = slice(first, first + count)
        sent = mine if s_ref.shape[2] > count else slice(0, count)
        for r in range(lhs.shape[0]):
            bins = slice(r * LANES, (r + 1) * LANES)
            real = imag = None
            for u in range(used):
                sr, si = (s_ref[u, half, sent, bins].astype(F32) for half in range(2))
                rr, ri = (own[unit, u, half, mine, bins].astype(F32) for half in range(2))
                re, im = sr * rr + si * ri, si * rr - sr * ri
                if u:
                    re, im = real + weight[u] * re, imag + weight[u] * im
                real, imag = re, im
            lhs[r, at, :LANES] = real.astype(BF16)
            lhs[r, at, LANES:] = imag.astype(BF16)
            lhs[r, turned, :LANES] = imag.astype(BF16)
            lhs[r, turned, LANES:] = (-real).astype(BF16)


def cross_rows(weight, after, rows, own, pieces, classes, effort):
    count = sum(p[2] for p in pieces)
    return pl.pallas_call(
        functools.partial(cross_kernel, pieces, len(after)),
        out_shape=jax.ShapeDtypeStruct((classes, 2 * count, 2 * LANES), BF16),
        in_specs=[SMEM] + [ANY] * len(after) + [VMEM] * (len(rows) + 1),
        out_specs=VMEM,
        compiler_params=params(8),
        cost_estimate=effort,
        name="cross",
    )(weight, *after, *rows, own)


def lags_kernel(geometry, split, skip, scal, *refs):
    classes, span, outputs, origin, period, chunk = geometry
    lhs, table, keep, *refs = refs[skip:]
    sends, sums = refs[:split], refs[split:]
    rows = lhs.shape[1] // 2
    lag_dev = keep.shape[-1]
    cores = 2
    at_once = span == lag_dev
    first = scal[CORE] == 0
    for start in range(0, span, chunk):
        values = []
        for r in range(classes):
            whole_turns = all(
                r * (span * k - origin) * 2 % period == 0 for k in range(outputs)
            )
            left = lhs[r, :rows] if whole_turns else lhs[r]
            y = jnp.dot(left, table[r, :, start : start + chunk], preferred_element_type=F32)
            values.append((y[:rows], None if whole_turns else y[rows:]))
        corr = combine(values, classes, outputs, origin, span, period)
        lags = slice(start, start + chunk)
        for column in range(keep.shape[0]) if at_once else ():
            even, odd = corr[2 * column], corr[2 * column + 1]
            keep[column, :, lags] = jnp.where(first, even, odd)
            other = jnp.where(first, odd, even).astype(BF16)
            for i, out in enumerate(sends):
                out[column, :, lags] = other[i * out.shape[1] : (i + 1) * out.shape[1]]
        for k, value in enumerate(corr) if not at_once else ():
            lag = span * k + start
            sums[0][lag // lag_dev, :, lag % lag_dev : lag % lag_dev + chunk] = value
    if at_once:
        return
    for column in range(keep.shape[0]):
        keep[column] = sums[0][cores * column + scal[CORE]]
        for i, out in enumerate(sends):
            at = slice(i * out.shape[1], (i + 1) * out.shape[1])
            out[column] = sums[0][cores * column + 1 - scal[CORE], at].astype(BF16)


def lag_parts(scal, after, lhs, table, geometry, columns, lag_dev, split, effort):
    rows = lhs.shape[1] // 2
    shape = lambda count: (columns, count, lag_dev)
    return pl.pallas_call(
        functools.partial(lags_kernel, geometry, split, len(after)),
        out_shape=[jax.ShapeDtypeStruct(shape(rows), F32)]
        + [jax.ShapeDtypeStruct(shape(rows // split), BF16)] * split,
        in_specs=[SMEM] + [ANY] * len(after) + [VMEM] * 2,
        out_specs=[VMEM] * (split + 1),
        scratch_shapes=[pltpu.VMEM((2 * columns, rows, lag_dev), F32)] * (geometry[1] != lag_dev),
        compiler_params=params(16),
        cost_estimate=effort,
        name="lags",
    )(scal, *after, lhs, table)


def cores_kernel(skip, split, scal, *refs):
    keep, *refs = refs[skip:]
    more, own, sends = refs[:split], refs[split], refs[split + 1 :]
    columns = keep.shape[0]
    for i, m in enumerate(more):
        at = slice(i * m.shape[1], (i + 1) * m.shape[1])
        for column in range(columns):
            value = keep[column, at] + m[column].astype(F32)

            @pl.when(scal[COLUMN] == column)
            def _():
                own[at] = value

            for s, out in enumerate(sends):

                @pl.when(scal[COLUMN] ^ (s + 1) == column)
                def _():
                    out[at] = value.astype(BF16)


def add_cores(scal, after, keep, more):
    columns, rows, lag_dev = keep.shape
    return pl.pallas_call(
        functools.partial(cores_kernel, len(after), len(more)),
        out_shape=[jax.ShapeDtypeStruct((rows, lag_dev), F32)]
        + [jax.ShapeDtypeStruct((rows, lag_dev), BF16)] * (columns - 1),
        in_specs=[SMEM] + [ANY] * len(after) + [VMEM] * (1 + len(more)),
        out_specs=[VMEM] * columns,
        compiler_params=params(8),
        cost_estimate=SMALL,
        name="cores",
    )(scal, *after, keep, *more)


def stats_kernel(scale, q, pieces, others, scal, *refs):
    count = min(q, 1)
    earlier, (own, *refs) = refs[:count], refs[count:]
    more, refs = refs[:others], refs[others:]
    targets, (corr, sums) = refs[: len(pieces)], refs[len(pieces) :]
    columns = []
    for target, (unit, first, count, at) in zip(targets, placed(pieces)):
        value = own[at]
        for m in more:
            value = value + m[at].astype(F32)
        slot = first + lax.broadcasted_iota(jnp.int32, (count, 1), 0)
        value = value * jnp.where(slot < scal[COUNT + unit], scale, 0.0)
        corr[at] = value
        square = jnp.sum(value * value, axis=1, keepdims=True)
        product = jnp.sum(value * target[0], axis=1, keepdims=True)
        lane = lax.broadcasted_iota(jnp.int32, (count, LANES), 1)
        columns.append(jnp.where(lane == 2 * q, square, jnp.where(lane == 2 * q + 1, product, 0.0)))
    spare = sums.shape[1] - own.shape[0]
    if spare:
        columns.append(jnp.zeros((spare, LANES), F32))
    total = jnp.concatenate(columns, axis=0).T[:8]
    for e in earlier:
        total = total + e[...]
    sums[...] = total


def target_specs(pieces, lag_dev):
    return [
        pl.BlockSpec(
            (1, count, lag_dev),
            lambda i, scal, unit=unit, block=first // count: (scal[BLOCK + unit], block, 0),
        )
        for unit, first, count in pieces
    ]


def whole(shape):
    return pl.BlockSpec(shape, lambda i, scal: (0,) * len(shape))


def lag_stats(scal, scale, q, pieces, earlier, own, more, observed):
    rows, lag_dev = own.shape
    outs = [jax.ShapeDtypeStruct((rows, lag_dev), F32), jax.ShapeDtypeStruct((8, -(-rows // LANES) * LANES), F32)]
    return pl.pallas_call(
        functools.partial(stats_kernel, scale, q, pieces, len(more)),
        grid_spec=pltpu.PrefetchScalarGridSpec(
            num_scalar_prefetch=1,
            grid=(1,),
            in_specs=[whole(e.shape) for e in earlier]
            + [whole(own.shape)] * (1 + len(more))
            + target_specs(pieces, lag_dev),
            out_specs=[whole(o.shape) for o in outs],
        ),
        out_shape=outs,
        compiler_params=params(16),
        cost_estimate=SMALL,
        name="stats",
    )(scal, *earlier, own, *more, *[observed] * len(pieces))


def slot_scales(sums, lag_total, q):
    total = sums[0][...]
    for s in sums[1:]:
        total = total + s[...]
    rows = total.shape[1]
    square, product = total[2 * q : 2 * q + 1], total[2 * q + 1 : 2 * q + 2]
    inverse = 1.0 / jnp.sqrt(square / lag_total + EPSILON)
    bending = (square * inverse * inverse - product * inverse) / lag_total
    sub = lax.broadcasted_iota(jnp.int32, (LANES, rows), 0)
    both = jnp.where(sub == 0, inverse, jnp.where(sub == 1, bending, 0.0)).T
    return both[:, 0:1], both[:, 1:2]


def gradient_kernel(lag_total, q, pieces, parts, skip, scal, *refs):
    refs = refs[skip:]
    sums, corr, refs = refs[:parts], refs[parts], refs[parts + 1 :]
    targets, outs = refs[: len(pieces)], refs[len(pieces) :]
    inverse, bending = slot_scales(sums, lag_total, q)
    for target, out, (unit, first, count, at) in zip(targets, outs, placed(pieces)):
        slot = first + lax.broadcasted_iota(jnp.int32, (count, 1), 0)
        valid = jnp.where(slot < scal[COUNT + unit], inverse[at], 0.0)
        normed = corr[at] * inverse[at]
        out[...] = ((normed - target[0] - normed * bending[at]) * valid).astype(BF16)


def gradients(scal, lag_total, q, pieces, after, sums, corr, observed):
    lag_dev = corr.shape[1]
    outs = [jax.ShapeDtypeStruct((p[2], lag_dev), BF16) for p in pieces]
    return pl.pallas_call(
        functools.partial(gradient_kernel, lag_total, q, pieces, len(sums), len(after)),
        grid_spec=pltpu.PrefetchScalarGridSpec(
            num_scalar_prefetch=1,
            grid=(1,),
            in_specs=[ANY] * len(after)
            + [whole(sums[0].shape)] * len(sums)
            + [whole(corr.shape)]
            + target_specs(pieces, lag_dev),
            out_specs=[whole(o.shape) for o in outs],
        ),
        out_shape=outs,
        compiler_params=params(16),
        cost_estimate=SMALL,
        name="gradient",
    )(scal, *after, *sums, corr, *[observed] * len(pieces))


def normed_kernel(lag_total, chunks, parts, scal, *refs):
    sums, corrs, out = refs[:parts], refs[parts:-1], refs[-1]
    for q, (pieces, corr) in enumerate(zip(chunks, corrs)):
        inverse, _ = slot_scales(sums, lag_total, q)
        for unit, first, count, at in placed(pieces):

            @pl.when(pl.program_id(0) == unit)
            def _():
                out[0, first : first + count] = corr[at] * inverse[at]


def normed_rows(scal, lag_total, chunks, sums, corrs, observed):
    blocks, slots, lag_dev = observed.shape
    ins = [*sums, *corrs]
    return pl.pallas_call(
        functools.partial(normed_kernel, lag_total, chunks, len(sums)),
        grid_spec=pltpu.PrefetchScalarGridSpec(
            num_scalar_prefetch=1,
            grid=(blocks,),
            in_specs=[whole(x.shape) for x in ins],
            out_specs=pl.BlockSpec((1, slots, lag_dev), lambda i, scal: (scal[BLOCK + i], 0, 0)),
        ),
        out_shape=jax.ShapeDtypeStruct(observed.shape, F32),
        compiler_params=params(16),
        cost_estimate=SMALL,
        name="normed",
    )(scal, *ins)


def adjoint_kernel(pieces, *refs):
    ids, parts, out = refs[: len(pieces)], refs[len(pieces) : -1], refs[-1]
    pick = picks([i.at[:, p[1] : p[1] + p[2]] for i, p in zip(ids, pieces)], out.shape[0])
    rows = jnp.concatenate([p[...] for p in parts], axis=0)
    out[...] = jnp.dot(pick, rows, preferred_element_type=F32)


def adjoint_rows(src_ids, pieces, parts, channels):
    lag_dev = parts[0].shape[1]
    return pl.pallas_call(
        functools.partial(adjoint_kernel, pieces),
        out_shape=jax.ShapeDtypeStruct((channels, lag_dev), F32),
        in_specs=[VMEM] * (2 * len(parts)),
        out_specs=VMEM,
        compiler_params=params(16),
        cost_estimate=SMALL,
        name="adjoint",
    )(*[src_ids[p[0]] for p in pieces], *parts)


def shards(spectra, window_keep, owners, pair_src, pair_rec, pair_count, observed):
    columns, cores, places = lax.axis_size("win"), lax.axis_size("freq"), lax.axis_size("recv")
    column, core, place = lax.axis_index("win"), lax.axis_index("freq"), lax.axis_index("recv")
    assert spectra.shape[0] == 1 and cores == 2
    channels, bins_dev = spectra.shape[2:]
    blocks, slots, lag_dev = observed.shape
    lag_total = lag_dev * columns * cores
    bin_total = bins_dev * cores
    period = 2 * bin_total
    part = bins_dev // columns
    classes = part // LANES
    span = period // classes
    geometry = (classes, span, lag_total // span, lag_total // 2, period, 256)
    lag_scale = 1.0 / math.sqrt(bin_total * columns)
    peers = columns * cores
    some = slots // 2
    shifts = range(places)

    held = [
        swapped(
            lax.dynamic_slice(
                spectra, (0, 0, 0, (column ^ s) * part), (1, 2, channels, part)
            ),
            "win",
            columns,
            s,
        )
        for s in range(columns)
    ]
    scal, wanted, rec_ids = index(
        window_keep, owners, pair_count, pair_src, pair_rec, places
    )
    if columns == 2:
        weight = jnp.ones((1,), F32)
    else:
        keeps = jnp.stack([swapped(window_keep[0], "win", columns, s) for s in range(columns)])
        ranked = jnp.argsort(-keeps)[: columns - 1].astype(jnp.int32)
        weight = keeps[ranked].astype(F32)
        scal = lax.dynamic_update_slice(scal, ranked, (ORDER,))

    direct = places == blocks
    src_ids = [swapped(wanted[d], "recv", places, d) for d in reversed(shifts)][::-1]
    trig = tables(classes, span, period, bins_dev, columns, cores)
    table = make_table(scal, trig, classes, span, peers)
    if direct and blocks == 4:
        chunks = [
            [(0, 0, slots), (1, 0, slots)],
            [(2, 0, slots)],
            [(3, 0, slots)],
        ]
    else:
        chunks = [[(d, first, some) for d in range(blocks)] for first in (0, some)]
    if direct:
        messages = [piece for pieces in chunks for piece in pieces]
    else:
        messages = [(d, 0, slots) for d in shifts]
    sent, kept = gather_rows(scal, table, held[0], held[1:], make_perm(part), src_ids, messages)
    own_rows = gather_own(kept, rec_ids)
    arrived = [swapped(x, "recv", places, m[0]) for m, x in reversed(list(zip(messages, sent)))][::-1]
    if not direct:
        stacked = jnp.stack(arrived)
        whole_rows = [
            lax.dynamic_index_in_dim(stacked, place ^ owners[b], 0, False) for b in range(blocks)
        ]
        arrived = [whole_rows[piece[0]] for pieces in chunks for piece in pieces]
    corrs, all_sums, returned, returned_pieces = [], [], [], []
    after = []
    for q, pieces in enumerate(chunks):
        rows, arrived = arrived[: len(pieces)], arrived[len(pieces) :]
        lhs = cross_rows(
            weight, after[:1] + (arrived if q == 1 else []), rows, own_rows, pieces, classes, LARGE if q < 2 else SMALL
        )
        groups = sum(p[2] for p in pieces) // (32 if q else 16)
        keep, *sends = lag_parts(
            scal, [], lhs, table, geometry, columns, lag_dev, groups, SMALL if q else LARGE
        )
        sends = [swapped(x, "freq", cores, 1) for x in sends]
        own, *sends = add_cores(scal, after[1:], keep, sends)
        more = [swapped(x, "win", columns, s + 1) for s, x in enumerate(sends)]
        after = [own, *more] if q == 0 else []
        corr, sums = lag_stats(scal, lag_scale, q, pieces, all_sums, own, more, observed)
        corrs.append(corr)
        all_sums = [sums]
    sums = [swapped(sums, ("win", "freq"), peers, s) for s in range(peers)]
    after = []
    for q in reversed(range(len(chunks))):
        pieces = chunks[q]
        grads = gradients(scal, lag_total, q, pieces, after, sums, corrs[q], observed)
        after = [grads[0]]
        if not direct:
            stacked = jnp.stack(list(grads) + [jnp.zeros_like(grads[0])])
            grads = []
            for d in shifts:
                block = jnp.int32(blocks)
                for b in range(blocks):
                    block = jnp.where(owners[b] == place ^ d, b, block)
                grads.append(lax.dynamic_index_in_dim(stacked, block, 0, False))
            pieces = [(d, pieces[0][1], some) for d in shifts]
        sent = [swapped(g, "recv", places, p[0]) for p, g in reversed(list(zip(pieces, grads)))]
        returned += sent[::-1]
        returned_pieces += pieces
    normed = normed_rows(scal, lag_total, chunks, sums, corrs, observed)
    adjoint = adjoint_rows(src_ids, returned_pieces, returned, channels)
    return (normed, adjoint)


def solution(mesh):
    return jax.shard_map(
        shards,
        mesh=mesh,
        in_specs=(
            P("win", None, ("groups", "recv"), "freq"),
            P(("groups", "win")),
            P("groups"),
            P(None, ("groups", "recv")),
            P(None, ("groups", "recv")),
            P(None, ("groups", "recv")),
            P(None, ("groups", "recv"), ("win", "freq")),
        ),
        out_specs=(
            P(None, ("groups", "recv"), ("win", "freq")),
            P(("groups", "recv"), ("win", "freq")),
        ),
        check_vma=False,
    )
```

```python
import functools
import math

import jax
import jax.numpy as jnp
import ml_dtypes
import numpy as np
from jax import lax
from jax.experimental import pallas as pl
from jax.experimental.pallas import tpu as pltpu
from jax.sharding import PartitionSpec as P

EPSILON = 1e-06
MIB = 1 << 20
LANES = 128
CORE, COLUMN, ORDER, BLOCK, COUNT = 0, 1, 2, 8, 16
BF16 = jnp.bfloat16
F32 = jnp.float32
VMEM = pl.BlockSpec(memory_space=pltpu.VMEM)
SMEM = pl.BlockSpec(memory_space=pltpu.SMEM)
HBM = pl.BlockSpec(memory_space=pltpu.HBM)
ANY = pl.BlockSpec(memory_space=pl.ANY)


def swapped(value, axis, size, step):
    assert size & (size - 1) == 0
    if step == 0:
        return value
    return lax.ppermute(value, axis, [(i, i ^ step) for i in range(size)])


def params(mib):
    return pltpu.CompilerParams(vmem_limit_bytes=mib * MIB)


SMALL = pl.CostEstimate(flops=1, bytes_accessed=1, transcendentals=0)
LARGE = pl.CostEstimate(flops=2 * 10**10, bytes_accessed=MIB, transcendentals=0)


def tables(classes, span, period, bins_dev, columns, cores):
    u = np.arange(span, dtype=np.int64)[None, :]
    piece = np.arange(columns * cores, dtype=np.int64)[:, None]
    first = piece % cores * bins_dev + piece // cores * (bins_dev // columns)
    rows = (first + np.arange(classes)).reshape(-1)
    high = 16 * classes * np.arange(LANES // 16, dtype=np.int64)
    low = classes * np.arange(16, dtype=np.int64)
    angle = (np.concatenate([rows, high, low])[:, None] * u % period) * (2.0 * math.pi / period)
    return np.stack([np.cos(angle), np.sin(angle)]).astype(np.float32)


def fetch(pairs, sems):
    copies = [pltpu.make_async_copy(a, b, sems.at[i]) for i, (a, b) in enumerate(pairs)]
    for c in copies:
        c.start()
    for c in copies:
        c.wait()


def index_kernel(blocks, direct, *refs):
    given, refs = refs[:5], refs[5:]
    scal, wanted, rec_ids, held, sems = refs[0], refs[1:-7], refs[-7], refs[-6:-1], refs[-1]
    fetch(zip(given, held), sems)
    window_keep, owners, pair_count, src, rec = held
    place = lax.axis_index("recv")
    column, columns = lax.axis_index("win"), lax.axis_size("win")
    core = lax.axis_index("freq")
    scal[CORE] = core
    scal[COLUMN] = column
    scal[ORDER] = 1 - window_keep[0]
    for b in range(blocks):
        unit = place ^ owners[b] if direct else b
        scal[BLOCK + unit] = b
        scal[COUNT + unit] = pair_count[b]
    for d, out in enumerate(wanted):
        chosen = jnp.full(out.shape, -1, jnp.int32)
        received = jnp.zeros(out.shape, jnp.int32)
        for b in range(blocks):
            mine = jnp.full(out.shape, owners[b], jnp.int32) == (place ^ d)
            chosen = jnp.where(mine, src[b : b + 1], chosen)
            received = jnp.where(mine, rec[b : b + 1], received)
        out[...] = chosen
        if direct:
            rec_ids[d : d + 1] = received
    if not direct:
        rec_ids[...] = rec[...]


def index(window_keep, owners, pair_count, pair_src, pair_rec, places):
    blocks, slots = pair_src.shape
    ids = jax.ShapeDtypeStruct((1, slots), jnp.int32)
    given = [window_keep, owners, pair_count[:, 0], pair_src, pair_rec]
    scal, *wanted, rec_ids = pl.pallas_call(
        functools.partial(index_kernel, blocks, places == blocks),
        out_shape=[jax.ShapeDtypeStruct((LANES,), jnp.int32)]
        + [ids] * places
        + [jax.ShapeDtypeStruct(pair_rec.shape, jnp.int32)],
        in_specs=[HBM] * 5,
        out_specs=[SMEM] + [VMEM] * (places + 1),
        scratch_shapes=[pltpu.SMEM(g.shape, g.dtype) for g in given[:3]]
        + [pltpu.VMEM(g.shape, g.dtype) for g in given[3:]]
        + [pltpu.SemaphoreType.DMA((5,))],
        compiler_params=params(16),
        cost_estimate=SMALL,
        name="index",
    )(*given)
    return scal, wanted, rec_ids


def table_kernel(classes, parts, scal, trig, table, base):
    rows = parts * classes
    low = slice(rows + LANES // 16, rows + LANES // 16 + 16)
    cl, sl = trig[0, low], trig[1, low]
    for h in range(LANES // 16):
        ch, sh = trig[0, rows + h : rows + h + 1], trig[1, rows + h : rows + h + 1]
        base[0, 16 * h : 16 * h + 16] = ch * cl - sh * sl
        base[1, 16 * h : 16 * h + 16] = sh * cl + ch * sl
    first = (scal[CORE] + 2 * scal[COLUMN]) * classes
    cb, sb = base[0], base[1]
    for r in range(classes):
        ca, sa = trig[0, pl.ds(first + r, 1)], trig[1, pl.ds(first + r, 1)]
        table[r, :LANES] = (ca * cb - sa * sb).astype(BF16)
        table[r, LANES:] = (-(sa * cb + ca * sb)).astype(BF16)


def perm_kernel(perm):
    part = perm.shape[0]
    classes = part // LANES
    source = lax.broadcasted_iota(jnp.int32, (part, LANES), 0)
    target = classes * lax.broadcasted_iota(jnp.int32, (part, LANES), 1)
    for r in range(classes):
        perm[:, r * LANES : (r + 1) * LANES] = (source == target + r).astype(BF16)


def make_perm(part):
    return pl.pallas_call(
        perm_kernel,
        out_shape=jax.ShapeDtypeStruct((part, part), BF16),
        out_specs=VMEM,
        compiler_params=params(8),
        cost_estimate=SMALL,
        name="perm",
    )()


def picks(ids, channels):
    row = jnp.concatenate([i[...] for i in ids], axis=1)
    return (lax.broadcasted_iota(jnp.int32, (channels, row.shape[1]), 0) == row).astype(BF16)


def rows_kernel(used, sends, messages, scal, here, *refs):
    held, perm, src_ids, refs = refs[:used], refs[used], refs[used + 1 : used + 1 + sends], refs[used + 1 + sends :]
    outs, kept = refs[:-1], refs[-1]
    _, _, channels, part = kept.shape
    slots = src_ids[0].shape[1]
    pick = picks(src_ids[::-1], channels)
    for u in range(used):
        x = here[0].reshape(2 * channels, part)
        for s in range(used):
            x = jnp.where(scal[ORDER + u] == s + 1, held[s][0].reshape(2 * channels, part), x)
        x = jnp.dot(x, perm[...], preferred_element_type=F32).astype(BF16)
        for half in range(2):
            z = x[half * channels : (half + 1) * channels]
            kept[u, half] = z
            y = lax.dot_general(
                pick, z, (((0,), (0,)), ((), ())), preferred_element_type=F32
            ).astype(BF16)
            for (d, first, count), out in zip(messages, outs):
                at = d * slots + first
                out[u, half] = y[at : at + count]


def gather_rows(scal, here, held, perm, src_ids, messages):
    used = len(held)
    channels, part = held[0].shape[-2:]
    *sent, kept = pl.pallas_call(
        functools.partial(rows_kernel, used, len(src_ids), messages),
        out_shape=[jax.ShapeDtypeStruct((used, 2, m[2], part), BF16) for m in messages]
        + [jax.ShapeDtypeStruct((used, 2, channels, part), BF16)],
        in_specs=[SMEM] + [VMEM] * (used + 2 + len(src_ids)),
        out_specs=[VMEM] * (len(messages) + 1),
        compiler_params=params(16),
        cost_estimate=SMALL,
        name="rows",
    )(scal, here, *held, perm, *src_ids[::-1])
    return sent, kept


def own_kernel(classes, parts, scal, kept, rec_ids, trig, own, table, base):
    units, used, _, slots, _ = own.shape
    pick = picks([rec_ids.at[d : d + 1] for d in range(units)], kept.shape[2])
    for u in range(used):
        for half in range(2):
            y = lax.dot_general(
                pick, kept[u, half], (((0,), (0,)), ((), ())), preferred_element_type=F32
            ).astype(BF16)
            for d in range(units):
                own[d, u, half] = y[d * slots : (d + 1) * slots]
    table_kernel(classes, parts, scal, trig, table, base)


def gather_own(scal, kept, rec_ids, trig, classes, span, parts):
    used, _, _, part = kept.shape
    units, slots = rec_ids.shape
    return pl.pallas_call(
        functools.partial(own_kernel, classes, parts),
        out_shape=[
            jax.ShapeDtypeStruct((units, used, 2, slots, part), BF16),
            jax.ShapeDtypeStruct((classes, 2 * LANES, span), BF16),
        ],
        in_specs=[SMEM] + [VMEM] * 3,
        out_specs=[VMEM] * 2,
        scratch_shapes=[pltpu.VMEM((2, LANES, span), F32)],
        compiler_params=params(16),
        cost_estimate=SMALL,
        name="own",
    )(scal, kept, rec_ids, jnp.asarray(trig))


def combine(values, classes, outputs, origin, span, period):
    plain, scaled = [None] * outputs, [None] * outputs

    def add(into, k, value, sign):
        if into[k] is None:
            into[k] = value if sign > 0 else -value
        else:
            into[k] = into[k] + value if sign > 0 else into[k] - value

    for r, (real, imag) in enumerate(values):
        both = None
        for k in range(outputs):
            eighths = r * (span * k - origin) * 8 // period % 8
            assert r * (span * k - origin) * 8 % period == 0
            if eighths % 2 == 0:
                value, sign = ((real, 1), (imag, -1), (real, -1), (imag, 1))[eighths // 2]
                add(plain, k, value, sign)
            else:
                if both is None:
                    both = real + imag, real - imag
                value, sign = ((both[1], 1), (both[0], -1), (both[1], -1), (both[0], 1))[eighths // 2]
                add(scaled, k, value, sign)
    root = math.sqrt(0.5)
    return [a if b is None else a + root * b for a, b in zip(plain, scaled)]


def placed(pieces):
    at = 0
    for unit, first, count in pieces:
        yield unit, first, count, slice(at, at + count)
        at += count


def cross_kernel(pieces, skip, weight, *refs):
    refs = refs[skip:]
    s_refs, own, lhs = refs[:-2], refs[-2], refs[-1]
    used = own.shape[1]
    rows = lhs.shape[1] // 2
    for s_ref, (unit, first, count, at) in zip(s_refs, placed(pieces)):
        turned = slice(rows + at.start, rows + at.stop)
        mine = slice(first, first + count)
        sent = mine if s_ref.shape[2] > count else slice(0, count)
        for r in range(lhs.shape[0]):
            bins = slice(r * LANES, (r + 1) * LANES)
            real = imag = None
            for u in range(used):
                sr, si = (s_ref[u, half, sent, bins].astype(F32) for half in range(2))
                rr, ri = (own[unit, u, half, mine, bins].astype(F32) for half in range(2))
                re, im = sr * rr + si * ri, si * rr - sr * ri
                if u:
                    re, im = real + weight[u] * re, imag + weight[u] * im
                real, imag = re, im
            lhs[r, at, :LANES] = real.astype(BF16)
            lhs[r, at, LANES:] = imag.astype(BF16)
            lhs[r, turned, :LANES] = imag.astype(BF16)
            lhs[r, turned, LANES:] = (-real).astype(BF16)


def cross_rows(weight, after, rows, own, pieces, classes, effort):
    count = sum(p[2] for p in pieces)
    return pl.pallas_call(
        functools.partial(cross_kernel, pieces, len(after)),
        out_shape=jax.ShapeDtypeStruct((classes, 2 * count, 2 * LANES), BF16),
        in_specs=[SMEM] + [ANY] * len(after) + [VMEM] * (len(rows) + 1),
        out_specs=VMEM,
        compiler_params=params(8),
        cost_estimate=effort,
        name="cross",
    )(weight, *after, *rows, own)


def lags_kernel(geometry, split, skip, scal, *refs):
    classes, span, outputs, origin, period, chunk = geometry
    lhs, table, keep, *refs = refs[skip:]
    sends, sums = refs[:split], refs[split:]
    rows = lhs.shape[1] // 2
    lag_dev = keep.shape[-1]
    cores = 2
    at_once = span == lag_dev
    first = scal[CORE] == 0
    for start in range(0, span, chunk):
        values = []
        for r in range(classes):
            whole_turns = all(
                r * (span * k - origin) * 2 % period == 0 for k in range(outputs)
            )
            left = lhs[r, :rows] if whole_turns else lhs[r]
            y = jnp.dot(left, table[r, :, start : start + chunk], preferred_element_type=F32)
            values.append((y[:rows], None if whole_turns else y[rows:]))
        corr = combine(values, classes, outputs, origin, span, period)
        lags = slice(start, start + chunk)
        for column in range(keep.shape[0]) if at_once else ():
            even, odd = corr[2 * column], corr[2 * column + 1]
            keep[column, :, lags] = jnp.where(first, even, odd)
            other = jnp.where(first, odd, even).astype(BF16)
            for i, out in enumerate(sends):
                out[column, :, lags] = other[i * out.shape[1] : (i + 1) * out.shape[1]]
        for k, value in enumerate(corr) if not at_once else ():
            lag = span * k + start
            sums[0][lag // lag_dev, :, lag % lag_dev : lag % lag_dev + chunk] = value
    if at_once:
        return
    for column in range(keep.shape[0]):
        keep[column] = sums[0][cores * column + scal[CORE]]
        for i, out in enumerate(sends):
            at = slice(i * out.shape[1], (i + 1) * out.shape[1])
            out[column] = sums[0][cores * column + 1 - scal[CORE], at].astype(BF16)


def lag_parts(scal, after, lhs, table, geometry, columns, lag_dev, split, effort):
    rows = lhs.shape[1] // 2
    shape = lambda count: (columns, count, lag_dev)
    return pl.pallas_call(
        functools.partial(lags_kernel, geometry, split, len(after)),
        out_shape=[jax.ShapeDtypeStruct(shape(rows), F32)]
        + [jax.ShapeDtypeStruct(shape(rows // split), BF16)] * split,
        in_specs=[SMEM] + [ANY] * len(after) + [VMEM] * 2,
        out_specs=[VMEM] * (split + 1),
        scratch_shapes=[pltpu.VMEM((2 * columns, rows, lag_dev), F32)] * (geometry[1] != lag_dev),
        compiler_params=params(16),
        cost_estimate=effort,
        name="lags",
    )(scal, *after, lhs, table)


def cores_kernel(skip, split, scal, *refs):
    keep, *refs = refs[skip:]
    more, own, sends = refs[:split], refs[split], refs[split + 1 :]
    columns = keep.shape[0]
    for i, m in enumerate(more):
        at = slice(i * m.shape[1], (i + 1) * m.shape[1])
        for column in range(columns):
            value = keep[column, at] + m[column].astype(F32)

            @pl.when(scal[COLUMN] == column)
            def _():
                own[at] = value

            for s, out in enumerate(sends):

                @pl.when(scal[COLUMN] ^ (s + 1) == column)
                def _():
                    out[at] = value.astype(BF16)


def add_cores(scal, after, keep, more):
    columns, rows, lag_dev = keep.shape
    return pl.pallas_call(
        functools.partial(cores_kernel, len(after), len(more)),
        out_shape=[jax.ShapeDtypeStruct((rows, lag_dev), F32)]
        + [jax.ShapeDtypeStruct((rows, lag_dev), BF16)] * (columns - 1),
        in_specs=[SMEM] + [ANY] * len(after) + [VMEM] * (1 + len(more)),
        out_specs=[VMEM] * columns,
        compiler_params=params(8),
        cost_estimate=SMALL,
        name="cores",
    )(scal, *after, keep, *more)


def stats_kernel(scale, q, pieces, others, scal, *refs):
    count = min(q, 1)
    earlier, (own, *refs) = refs[:count], refs[count:]
    more, refs = refs[:others], refs[others:]
    targets, (corr, sums) = refs[: len(pieces)], refs[len(pieces) :]
    columns = []
    for target, (unit, first, count, at) in zip(targets, placed(pieces)):
        value = own[at]
        for m in more:
            value = value + m[at].astype(F32)
        slot = first + lax.broadcasted_iota(jnp.int32, (count, 1), 0)
        value = value * jnp.where(slot < scal[COUNT + unit], scale, 0.0)
        corr[at] = value
        square = jnp.sum(value * value, axis=1, keepdims=True)
        product = jnp.sum(value * target[0], axis=1, keepdims=True)
        lane = lax.broadcasted_iota(jnp.int32, (count, LANES), 1)
        columns.append(jnp.where(lane == 2 * q, square, jnp.where(lane == 2 * q + 1, product, 0.0)))
    spare = sums.shape[1] - own.shape[0]
    if spare:
        columns.append(jnp.zeros((spare, LANES), F32))
    total = jnp.concatenate(columns, axis=0).T[:8]
    for e in earlier:
        total = total + e[...]
    sums[...] = total


def target_specs(pieces, lag_dev):
    return [
        pl.BlockSpec(
            (1, count, lag_dev),
            lambda i, scal, unit=unit, block=first // count: (scal[BLOCK + unit], block, 0),
        )
        for unit, first, count in pieces
    ]


def whole(shape):
    return pl.BlockSpec(shape, lambda i, scal: (0,) * len(shape))


def lag_stats(scal, scale, q, pieces, earlier, own, more, observed):
    rows, lag_dev = own.shape
    outs = [jax.ShapeDtypeStruct((rows, lag_dev), F32), jax.ShapeDtypeStruct((8, -(-rows // LANES) * LANES), F32)]
    return pl.pallas_call(
        functools.partial(stats_kernel, scale, q, pieces, len(more)),
        grid_spec=pltpu.PrefetchScalarGridSpec(
            num_scalar_prefetch=1,
            grid=(1,),
            in_specs=[whole(e.shape) for e in earlier]
            + [whole(own.shape)] * (1 + len(more))
            + target_specs(pieces, lag_dev),
            out_specs=[whole(o.shape) for o in outs],
        ),
        out_shape=outs,
        compiler_params=params(16),
        cost_estimate=SMALL,
        name="stats",
    )(scal, *earlier, own, *more, *[observed] * len(pieces))


def slot_scales(sums, lag_total, q):
    total = sums[0][...]
    for s in sums[1:]:
        total = total + s[...]
    rows = total.shape[1]
    square, product = total[2 * q : 2 * q + 1], total[2 * q + 1 : 2 * q + 2]
    inverse = 1.0 / jnp.sqrt(square / lag_total + EPSILON)
    bending = (square * inverse * inverse - product * inverse) / lag_total
    sub = lax.broadcasted_iota(jnp.int32, (LANES, rows), 0)
    both = jnp.where(sub == 0, inverse, jnp.where(sub == 1, bending, 0.0)).T
    return both[:, 0:1], both[:, 1:2]


def gradient_kernel(lag_total, chunks, parts, skip, scal, *refs):
    sums, refs = refs[skip : skip + parts], refs[skip + parts :]
    corrs, refs = refs[: len(chunks)], refs[len(chunks) :]
    targets, outs = refs[: len(refs) // 2], refs[len(refs) // 2 :]
    i = 0
    for corr, (q, pieces) in zip(corrs, chunks):
        inverse, bending = slot_scales(sums, lag_total, q)
        for unit, first, count, at in placed(pieces):
            slot = first + lax.broadcasted_iota(jnp.int32, (count, 1), 0)
            valid = jnp.where(slot < scal[COUNT + unit], inverse[at], 0.0)
            normed = corr[at] * inverse[at]
            outs[i][...] = ((normed - targets[i][0] - normed * bending[at]) * valid).astype(BF16)
            i += 1


def gradients(scal, lag_total, chunks, after, sums, corrs, observed):
    lag_dev = observed.shape[2]
    pieces = [p for _, some in chunks for p in some]
    outs = [jax.ShapeDtypeStruct((p[2], lag_dev), BF16) for p in pieces]
    return pl.pallas_call(
        functools.partial(gradient_kernel, lag_total, chunks, len(sums), len(after)),
        grid_spec=pltpu.PrefetchScalarGridSpec(
            num_scalar_prefetch=1,
            grid=(1,),
            in_specs=[ANY] * len(after)
            + [whole(x.shape) for x in (*sums, *corrs)]
            + target_specs(pieces, lag_dev),
            out_specs=[whole(o.shape) for o in outs],
        ),
        out_shape=outs,
        compiler_params=params(16),
        cost_estimate=SMALL,
        name="gradient",
    )(scal, *after, *sums, *corrs, *[observed] * len(pieces))


def normed_kernel(lag_total, chunks, parts, scal, *refs):
    sums, corrs, out = refs[:parts], refs[parts:-1], refs[-1]
    for q, (pieces, corr) in enumerate(zip(chunks, corrs)):
        inverse, _ = slot_scales(sums, lag_total, q)
        for unit, first, count, at in placed(pieces):

            @pl.when(pl.program_id(0) == unit)
            def _():
                out[0, first : first + count] = corr[at] * inverse[at]


def normed_rows(scal, lag_total, chunks, sums, corrs, observed):
    blocks, slots, lag_dev = observed.shape
    ins = [*sums, *corrs]
    return pl.pallas_call(
        functools.partial(normed_kernel, lag_total, chunks, len(sums)),
        grid_spec=pltpu.PrefetchScalarGridSpec(
            num_scalar_prefetch=1,
            grid=(blocks,),
            in_specs=[whole(x.shape) for x in ins],
            out_specs=pl.BlockSpec((1, slots, lag_dev), lambda i, scal: (scal[BLOCK + i], 0, 0)),
        ),
        out_shape=jax.ShapeDtypeStruct(observed.shape, F32),
        compiler_params=params(16),
        cost_estimate=SMALL,
        name="normed",
    )(scal, *ins)


def adjoint_kernel(pieces, *refs):
    ids, parts, out = refs[: len(pieces)], refs[len(pieces) : -1], refs[-1]
    pick = picks([i.at[:, p[1] : p[1] + p[2]] for i, p in zip(ids, pieces)], out.shape[0])
    rows = jnp.concatenate([p[...] for p in parts], axis=0)
    out[...] = jnp.dot(pick, rows, preferred_element_type=F32)


def adjoint_rows(src_ids, pieces, parts, channels):
    lag_dev = parts[0].shape[1]
    return pl.pallas_call(
        functools.partial(adjoint_kernel, pieces),
        out_shape=jax.ShapeDtypeStruct((channels, lag_dev), F32),
        in_specs=[VMEM] * (2 * len(parts)),
        out_specs=VMEM,
        compiler_params=params(16),
        cost_estimate=SMALL,
        name="adjoint",
    )(*[src_ids[p[0]] for p in pieces], *parts)


def shards(spectra, window_keep, owners, pair_src, pair_rec, pair_count, observed):
    columns, cores, places = lax.axis_size("win"), lax.axis_size("freq"), lax.axis_size("recv")
    column, core, place = lax.axis_index("win"), lax.axis_index("freq"), lax.axis_index("recv")
    assert spectra.shape[0] == 1 and cores == 2
    channels, bins_dev = spectra.shape[2:]
    blocks, slots, lag_dev = observed.shape
    lag_total = lag_dev * columns * cores
    bin_total = bins_dev * cores
    period = 2 * bin_total
    part = bins_dev // columns
    classes = part // LANES
    span = period // classes
    geometry = (classes, span, lag_total // span, lag_total // 2, period, 256)
    lag_scale = 1.0 / math.sqrt(bin_total * columns)
    peers = columns * cores
    some = slots // 2
    shifts = range(places)

    def cut(values, s):
        return lax.dynamic_slice(values, (0, 0, 0, (column ^ s) * part), (1, 2, channels, part))

    here, *held = [swapped(cut(spectra, s), "win", columns, s) for s in range(columns)]
    scal, wanted, rec_ids = index(
        window_keep, owners, pair_count, pair_src, pair_rec, places
    )
    if columns == 2:
        weight = jnp.ones((1,), F32)
    else:
        keeps = jnp.stack([swapped(window_keep[0], "win", columns, s) for s in range(columns)])
        ranked = jnp.argsort(-keeps)[: columns - 1].astype(jnp.int32)
        weight = keeps[ranked].astype(F32)
        scal = lax.dynamic_update_slice(scal, ranked, (ORDER,))

    direct = places == blocks
    src_ids = [swapped(wanted[d], "recv", places, d) for d in reversed(shifts)][::-1]
    trig = tables(classes, span, period, bins_dev, columns, cores)
    if direct and blocks == 4:
        chunks = [
            [(0, 0, slots), (1, 0, slots)],
            [(2, 0, slots)],
            [(3, 0, slots)],
        ]
    else:
        chunks = [[(d, first, some) for d in range(blocks)] for first in (0, some)]
    if direct:
        messages = [piece for pieces in chunks for piece in pieces]
    else:
        messages = [(d, 0, slots) for d in shifts]
    sent, kept = gather_rows(scal, here, held, make_perm(part), src_ids, messages)
    own_rows, table = gather_own(scal, kept, rec_ids, trig, classes, span, peers)
    arrived = [swapped(x, "recv", places, m[0]) for m, x in reversed(list(zip(messages, sent)))][::-1]
    if not direct:
        stacked = jnp.stack(arrived)
        whole_rows = [
            lax.dynamic_index_in_dim(stacked, place ^ owners[b], 0, False) for b in range(blocks)
        ]
        arrived = [whole_rows[piece[0]] for pieces in chunks for piece in pieces]
    corrs, all_sums, returned, returned_pieces = [], [], [], []
    after = []
    for q, pieces in enumerate(chunks):
        rows, arrived = arrived[: len(pieces)], arrived[len(pieces) :]
        lhs = cross_rows(
            weight, after[:1] + (arrived if q == 1 else []), rows, own_rows, pieces, classes, LARGE if q < 2 else SMALL
        )
        groups = sum(p[2] for p in pieces) // (32 if q else 16)
        keep, *sends = lag_parts(
            scal, [], lhs, table, geometry, columns, lag_dev, groups, SMALL if q else LARGE
        )
        sends = [swapped(x, "freq", cores, 1) for x in sends]
        own, *sends = add_cores(scal, after[1:], keep, sends)
        more = [swapped(x, "win", columns, s + 1) for s, x in enumerate(sends)]
        after = [own, *more] if q == 0 else []
        corr, sums = lag_stats(scal, lag_scale, q, pieces, all_sums, own, more, observed)
        corrs.append(corr)
        all_sums = [sums]
    sums = [swapped(sums, ("win", "freq"), peers, s) for s in range(peers)]
    after = []
    numbered = list(enumerate(chunks))
    for group in (numbered[:0:-1], numbered[:1]):
        grads = gradients(scal, lag_total, group, after, sums, [corrs[q] for q, _ in group], observed)
        pieces = [p for _, some_pieces in group for p in some_pieces]
        after = [grads[0]]
        if not direct:
            stacked = jnp.stack(list(grads) + [jnp.zeros_like(grads[0])])
            grads = []
            for d in shifts:
                block = jnp.int32(blocks)
                for b in range(blocks):
                    block = jnp.where(owners[b] == place ^ d, b, block)
                grads.append(lax.dynamic_index_in_dim(stacked, block, 0, False))
            pieces = [(d, pieces[0][1], some) for d in shifts]
        sent = [swapped(g, "recv", places, p[0]) for p, g in reversed(list(zip(pieces, grads)))]
        returned += sent[::-1]
        returned_pieces += pieces
    normed = normed_rows(scal, lag_total, chunks, sums, corrs, observed)
    adjoint = adjoint_rows(src_ids, returned_pieces, returned, channels)
    return (normed, adjoint)


def solution(mesh):
    return jax.shard_map(
        shards,
        mesh=mesh,
        in_specs=(
            P("win", None, ("groups", "recv"), "freq"),
            P(("groups", "win")),
            P("groups"),
            P(None, ("groups", "recv")),
            P(None, ("groups", "recv")),
            P(None, ("groups", "recv")),
            P(None, ("groups", "recv"), ("win", "freq")),
        ),
        out_specs=(
            P(None, ("groups", "recv"), ("win", "freq")),
            P(("groups", "recv"), ("win", "freq")),
        ),
        check_vma=False,
    )
```

```python
import functools
import math

import jax
import jax.numpy as jnp
import ml_dtypes
import numpy as np
from jax import lax
from jax.experimental import pallas as pl
from jax.experimental.pallas import tpu as pltpu
from jax.sharding import PartitionSpec as P

EPSILON = 1e-06
MIB = 1 << 20
LANES = 128
CORE, COLUMN, ORDER, BLOCK, COUNT = 0, 1, 2, 8, 16
BF16 = jnp.bfloat16
F32 = jnp.float32
VMEM = pl.BlockSpec(memory_space=pltpu.VMEM)
SMEM = pl.BlockSpec(memory_space=pltpu.SMEM)
HBM = pl.BlockSpec(memory_space=pltpu.HBM)
ANY = pl.BlockSpec(memory_space=pl.ANY)


def swapped(value, axis, size, step):
    assert size & (size - 1) == 0
    if step == 0:
        return value
    return lax.ppermute(value, axis, [(i, i ^ step) for i in range(size)])


def params(mib):
    return pltpu.CompilerParams(vmem_limit_bytes=mib * MIB)


SMALL = pl.CostEstimate(flops=1, bytes_accessed=1, transcendentals=0)
LARGE = pl.CostEstimate(flops=2 * 10**10, bytes_accessed=MIB, transcendentals=0)


def tables(classes, span, period, bins_dev, columns, cores):
    u = np.arange(span, dtype=np.int64)[None, :]
    piece = np.arange(columns * cores, dtype=np.int64)[:, None]
    first = piece % cores * bins_dev + piece // cores * (bins_dev // columns)
    rows = (first + np.arange(classes)).reshape(-1)
    high = 16 * classes * np.arange(LANES // 16, dtype=np.int64)
    low = classes * np.arange(16, dtype=np.int64)
    angle = (np.concatenate([rows, high, low])[:, None] * u % period) * (2.0 * math.pi / period)
    return np.stack([np.cos(angle), np.sin(angle)]).astype(np.float32)


def fetch(pairs, sems):
    copies = [pltpu.make_async_copy(a, b, sems.at[i]) for i, (a, b) in enumerate(pairs)]
    for c in copies:
        c.start()
    for c in copies:
        c.wait()


def index_kernel(blocks, direct, *refs):
    given, refs = refs[:5], refs[5:]
    scal, wanted, rec_ids, held, sems = refs[0], refs[1:-7], refs[-7], refs[-6:-1], refs[-1]
    fetch(zip(given, held), sems)
    window_keep, owners, pair_count, src, rec = held
    place = lax.axis_index("recv")
    column, columns = lax.axis_index("win"), lax.axis_size("win")
    core = lax.axis_index("freq")
    scal[CORE] = core
    scal[COLUMN] = column
    scal[ORDER] = 1 - window_keep[0]
    for b in range(blocks):
        unit = place ^ owners[b] if direct else b
        scal[BLOCK + unit] = b
        scal[COUNT + unit] = pair_count[b]
    for d, out in enumerate(wanted):
        chosen = jnp.full(out.shape, -1, jnp.int32)
        received = jnp.zeros(out.shape, jnp.int32)
        for b in range(blocks):
            mine = jnp.full(out.shape, owners[b], jnp.int32) == (place ^ d)
            chosen = jnp.where(mine, src[b : b + 1], chosen)
            received = jnp.where(mine, rec[b : b + 1], received)
        out[...] = chosen
        if direct:
            rec_ids[d : d + 1] = received
    if not direct:
        rec_ids[...] = rec[...]


def index(window_keep, owners, pair_count, pair_src, pair_rec, places):
    blocks, slots = pair_src.shape
    ids = jax.ShapeDtypeStruct((1, slots), jnp.int32)
    given = [window_keep, owners, pair_count[:, 0], pair_src, pair_rec]
    scal, *wanted, rec_ids = pl.pallas_call(
        functools.partial(index_kernel, blocks, places == blocks),
        out_shape=[jax.ShapeDtypeStruct((LANES,), jnp.int32)]
        + [ids] * places
        + [jax.ShapeDtypeStruct(pair_rec.shape, jnp.int32)],
        in_specs=[HBM] * 5,
        out_specs=[SMEM] + [VMEM] * (places + 1),
        scratch_shapes=[pltpu.SMEM(g.shape, g.dtype) for g in given[:3]]
        + [pltpu.VMEM(g.shape, g.dtype) for g in given[3:]]
        + [pltpu.SemaphoreType.DMA((5,))],
        compiler_params=params(16),
        cost_estimate=SMALL,
        name="index",
    )(*given)
    return scal, wanted, rec_ids


def table_kernel(classes, parts, scal, trig, table, base):
    rows = parts * classes
    low = slice(rows + LANES // 16, rows + LANES // 16 + 16)
    cl, sl = trig[0, low], trig[1, low]
    for h in range(LANES // 16):
        ch, sh = trig[0, rows + h : rows + h + 1], trig[1, rows + h : rows + h + 1]
        base[0, 16 * h : 16 * h + 16] = ch * cl - sh * sl
        base[1, 16 * h : 16 * h + 16] = sh * cl + ch * sl
    first = (scal[CORE] + 2 * scal[COLUMN]) * classes
    cb, sb = base[0], base[1]
    for r in range(classes):
        ca, sa = trig[0, pl.ds(first + r, 1)], trig[1, pl.ds(first + r, 1)]
        table[r, :LANES] = (ca * cb - sa * sb).astype(BF16)
        table[r, LANES:] = (-(sa * cb + ca * sb)).astype(BF16)


def perm_kernel(perm):
    part = perm.shape[0]
    classes = part // LANES
    source = lax.broadcasted_iota(jnp.int32, (part, LANES), 0)
    target = classes * lax.broadcasted_iota(jnp.int32, (part, LANES), 1)
    for r in range(classes):
        perm[:, r * LANES : (r + 1) * LANES] = (source == target + r).astype(BF16)


def make_perm(part):
    return pl.pallas_call(
        perm_kernel,
        out_shape=jax.ShapeDtypeStruct((part, part), BF16),
        out_specs=VMEM,
        compiler_params=params(8),
        cost_estimate=SMALL,
        name="perm",
    )()


def picks(ids, channels):
    row = jnp.concatenate([i[...] for i in ids], axis=1)
    return (lax.broadcasted_iota(jnp.int32, (channels, row.shape[1]), 0) == row).astype(BF16)


def rows_kernel(used, sends, messages, scal, here, *refs):
    held, perm, src_ids, refs = refs[:used], refs[used], refs[used + 1 : used + 1 + sends], refs[used + 1 + sends :]
    outs, kept = refs[:-1], refs[-1]
    _, _, channels, part = kept.shape
    slots = src_ids[0].shape[1]
    pick = picks(src_ids[::-1], channels)
    for u in range(used):
        x = here[0].reshape(2 * channels, part)
        for s in range(used):
            x = jnp.where(scal[ORDER + u] == s + 1, held[s][0].reshape(2 * channels, part), x)
        x = jnp.dot(x, perm[...], preferred_element_type=F32).astype(BF16)
        for half in range(2):
            z = x[half * channels : (half + 1) * channels]
            kept[u, half] = z
            y = lax.dot_general(
                pick, z, (((0,), (0,)), ((), ())), preferred_element_type=F32
            ).astype(BF16)
            for (d, first, count), out in zip(messages, outs):
                at = d * slots + first
                out[u, half] = y[at : at + count]


def gather_rows(scal, here, held, perm, src_ids, messages):
    used = len(held)
    channels, part = held[0].shape[-2:]
    *sent, kept = pl.pallas_call(
        functools.partial(rows_kernel, used, len(src_ids), messages),
        out_shape=[jax.ShapeDtypeStruct((used, 2, m[2], part), BF16) for m in messages]
        + [jax.ShapeDtypeStruct((used, 2, channels, part), BF16)],
        in_specs=[SMEM] + [VMEM] * (used + 2 + len(src_ids)),
        out_specs=[VMEM] * (len(messages) + 1),
        compiler_params=params(16),
        cost_estimate=SMALL,
        name="rows",
    )(scal, here, *held, perm, *src_ids[::-1])
    return sent, kept


def own_kernel(classes, parts, scal, kept, rec_ids, trig, own, table, base):
    units, used, _, slots, _ = own.shape
    pick = picks([rec_ids.at[d : d + 1] for d in range(units)], kept.shape[2])
    for u in range(used):
        for half in range(2):
            y = lax.dot_general(
                pick, kept[u, half], (((0,), (0,)), ((), ())), preferred_element_type=F32
            ).astype(BF16)
            for d in range(units):
                own[d, u, half] = y[d * slots : (d + 1) * slots]
    table_kernel(classes, parts, scal, trig, table, base)


def gather_own(scal, kept, rec_ids, trig, classes, span, parts):
    used, _, _, part = kept.shape
    units, slots = rec_ids.shape
    return pl.pallas_call(
        functools.partial(own_kernel, classes, parts),
        out_shape=[
            jax.ShapeDtypeStruct((units, used, 2, slots, part), BF16),
            jax.ShapeDtypeStruct((classes, 2 * LANES, span), BF16),
        ],
        in_specs=[SMEM] + [VMEM] * 3,
        out_specs=[VMEM] * 2,
        scratch_shapes=[pltpu.VMEM((2, LANES, span), F32)],
        compiler_params=params(16),
        cost_estimate=SMALL,
        name="own",
    )(scal, kept, rec_ids, jnp.asarray(trig))


def combine(values, classes, outputs, origin, span, period):
    plain, scaled = [None] * outputs, [None] * outputs

    def add(into, k, value, sign):
        if into[k] is None:
            into[k] = value if sign > 0 else -value
        else:
            into[k] = into[k] + value if sign > 0 else into[k] - value

    for r, (real, imag) in enumerate(values):
        both = None
        for k in range(outputs):
            eighths = r * (span * k - origin) * 8 // period % 8
            assert r * (span * k - origin) * 8 % period == 0
            if eighths % 2 == 0:
                value, sign = ((real, 1), (imag, -1), (real, -1), (imag, 1))[eighths // 2]
                add(plain, k, value, sign)
            else:
                if both is None:
                    both = real + imag, real - imag
                value, sign = ((both[1], 1), (both[0], -1), (both[1], -1), (both[0], 1))[eighths // 2]
                add(scaled, k, value, sign)
    root = math.sqrt(0.5)
    return [a if b is None else a + root * b for a, b in zip(plain, scaled)]


def placed(pieces):
    at = 0
    for unit, first, count in pieces:
        yield unit, first, count, slice(at, at + count)
        at += count


def cross_kernel(pieces, skip, weight, *refs):
    refs = refs[skip:]
    s_refs, own, lhs = refs[:-2], refs[-2], refs[-1]
    used = own.shape[1]
    rows = lhs.shape[1] // 2
    for s_ref, (unit, first, count, at) in zip(s_refs, placed(pieces)):
        turned = slice(rows + at.start, rows + at.stop)
        mine = slice(first, first + count)
        sent = mine if s_ref.shape[2] > count else slice(0, count)
        for r in range(lhs.shape[0]):
            bins = slice(r * LANES, (r + 1) * LANES)
            real = imag = None
            for u in range(used):
                sr, si = (s_ref[u, half, sent, bins].astype(F32) for half in range(2))
                rr, ri = (own[unit, u, half, mine, bins].astype(F32) for half in range(2))
                re, im = sr * rr + si * ri, si * rr - sr * ri
                if u:
                    re, im = real + weight[u] * re, imag + weight[u] * im
                real, imag = re, im
            lhs[r, at, :LANES] = real.astype(BF16)
            lhs[r, at, LANES:] = imag.astype(BF16)
            lhs[r, turned, :LANES] = imag.astype(BF16)
            lhs[r, turned, LANES:] = (-real).astype(BF16)


def cross_rows(weight, after, rows, own, pieces, classes, effort):
    count = sum(p[2] for p in pieces)
    return pl.pallas_call(
        functools.partial(cross_kernel, pieces, len(after)),
        out_shape=jax.ShapeDtypeStruct((classes, 2 * count, 2 * LANES), BF16),
        in_specs=[SMEM] + [ANY] * len(after) + [VMEM] * (len(rows) + 1),
        out_specs=VMEM,
        compiler_params=params(8),
        cost_estimate=effort,
        name="cross",
    )(weight, *after, *rows, own)


def lags_kernel(geometry, split, skip, scal, *refs):
    classes, span, outputs, origin, period, chunk = geometry
    lhs, table, keep, *refs = refs[skip:]
    sends, sums = refs[:split], refs[split:]
    rows = lhs.shape[1] // 2
    lag_dev = keep.shape[-1]
    cores = 2
    at_once = span == lag_dev
    first = scal[CORE] == 0
    for start in range(0, span, chunk):
        values = []
        for r in range(classes):
            whole_turns = all(
                r * (span * k - origin) * 2 % period == 0 for k in range(outputs)
            )
            left = lhs[r, :rows] if whole_turns else lhs[r]
            y = jnp.dot(left, table[r, :, start : start + chunk], preferred_element_type=F32)
            values.append((y[:rows], None if whole_turns else y[rows:]))
        corr = combine(values, classes, outputs, origin, span, period)
        lags = slice(start, start + chunk)
        for column in range(keep.shape[0]) if at_once else ():
            even, odd = corr[2 * column], corr[2 * column + 1]
            keep[column, :, lags] = jnp.where(first, even, odd)
            other = jnp.where(first, odd, even).astype(BF16)
            for i, out in enumerate(sends):
                out[column, :, lags] = other[i * out.shape[1] : (i + 1) * out.shape[1]]
        for k, value in enumerate(corr) if not at_once else ():
            lag = span * k + start
            sums[0][lag // lag_dev, :, lag % lag_dev : lag % lag_dev + chunk] = value
    if at_once:
        return
    for column in range(keep.shape[0]):
        keep[column] = sums[0][cores * column + scal[CORE]]
        for i, out in enumerate(sends):
            at = slice(i * out.shape[1], (i + 1) * out.shape[1])
            out[column] = sums[0][cores * column + 1 - scal[CORE], at].astype(BF16)


def lag_parts(scal, after, lhs, table, geometry, columns, lag_dev, split, effort):
    rows = lhs.shape[1] // 2
    shape = lambda count: (columns, count, lag_dev)
    return pl.pallas_call(
        functools.partial(lags_kernel, geometry, split, len(after)),
        out_shape=[jax.ShapeDtypeStruct(shape(rows), F32)]
        + [jax.ShapeDtypeStruct(shape(rows // split), BF16)] * split,
        in_specs=[SMEM] + [ANY] * len(after) + [VMEM] * 2,
        out_specs=[VMEM] * (split + 1),
        scratch_shapes=[pltpu.VMEM((2 * columns, rows, lag_dev), F32)] * (geometry[1] != lag_dev),
        compiler_params=params(16),
        cost_estimate=effort,
        name="lags",
    )(scal, *after, lhs, table)


def cores_kernel(skip, split, scal, *refs):
    keep, *refs = refs[skip:]
    more, own, sends = refs[:split], refs[split], refs[split + 1 :]
    columns = keep.shape[0]
    for i, m in enumerate(more):
        at = slice(i * m.shape[1], (i + 1) * m.shape[1])
        for column in range(columns):
            value = keep[column, at] + m[column].astype(F32)

            @pl.when(scal[COLUMN] == column)
            def _():
                own[at] = value

            for s, out in enumerate(sends):

                @pl.when(scal[COLUMN] ^ (s + 1) == column)
                def _():
                    out[at] = value.astype(BF16)


def add_cores(scal, after, keep, more):
    columns, rows, lag_dev = keep.shape
    return pl.pallas_call(
        functools.partial(cores_kernel, len(after), len(more)),
        out_shape=[jax.ShapeDtypeStruct((rows, lag_dev), F32)]
        + [jax.ShapeDtypeStruct((rows, lag_dev), BF16)] * (columns - 1),
        in_specs=[SMEM] + [ANY] * len(after) + [VMEM] * (1 + len(more)),
        out_specs=[VMEM] * columns,
        compiler_params=params(8),
        cost_estimate=SMALL,
        name="cores",
    )(scal, *after, keep, *more)


def stats_kernel(scale, q, pieces, others, scal, *refs):
    count = min(q, 1)
    earlier, (own, *refs) = refs[:count], refs[count:]
    more, refs = refs[:others], refs[others:]
    targets, (corr, sums) = refs[: len(pieces)], refs[len(pieces) :]
    columns = []
    for target, (unit, first, count, at) in zip(targets, placed(pieces)):
        value = own[at]
        for m in more:
            value = value + m[at].astype(F32)
        slot = first + lax.broadcasted_iota(jnp.int32, (count, 1), 0)
        value = value * jnp.where(slot < scal[COUNT + unit], scale, 0.0)
        corr[at] = value
        square = jnp.sum(value * value, axis=1, keepdims=True)
        product = jnp.sum(value * target[0], axis=1, keepdims=True)
        lane = lax.broadcasted_iota(jnp.int32, (count, LANES), 1)
        columns.append(jnp.where(lane == 2 * q, square, jnp.where(lane == 2 * q + 1, product, 0.0)))
    spare = sums.shape[1] - own.shape[0]
    if spare:
        columns.append(jnp.zeros((spare, LANES), F32))
    total = jnp.concatenate(columns, axis=0).T[:8]
    for e in earlier:
        total = total + e[...]
    sums[...] = total


def target_specs(pieces, lag_dev):
    return [
        pl.BlockSpec(
            (1, count, lag_dev),
            lambda i, scal, unit=unit, block=first // count: (scal[BLOCK + unit], block, 0),
        )
        for unit, first, count in pieces
    ]


def whole(shape):
    return pl.BlockSpec(shape, lambda i, scal: (0,) * len(shape))


def lag_stats(scal, scale, q, pieces, earlier, own, more, observed):
    rows, lag_dev = own.shape
    outs = [jax.ShapeDtypeStruct((rows, lag_dev), F32), jax.ShapeDtypeStruct((8, -(-rows // LANES) * LANES), F32)]
    return pl.pallas_call(
        functools.partial(stats_kernel, scale, q, pieces, len(more)),
        grid_spec=pltpu.PrefetchScalarGridSpec(
            num_scalar_prefetch=1,
            grid=(1,),
            in_specs=[whole(e.shape) for e in earlier]
            + [whole(own.shape)] * (1 + len(more))
            + target_specs(pieces, lag_dev),
            out_specs=[whole(o.shape) for o in outs],
        ),
        out_shape=outs,
        compiler_params=params(16),
        cost_estimate=SMALL,
        name="stats",
    )(scal, *earlier, own, *more, *[observed] * len(pieces))


def slot_scales(sums, lag_total, q):
    total = sums[0][...]
    for s in sums[1:]:
        total = total + s[...]
    rows = total.shape[1]
    square, product = total[2 * q : 2 * q + 1], total[2 * q + 1 : 2 * q + 2]
    inverse = 1.0 / jnp.sqrt(square / lag_total + EPSILON)
    bending = (square * inverse * inverse - product * inverse) / lag_total
    sub = lax.broadcasted_iota(jnp.int32, (LANES, rows), 0)
    both = jnp.where(sub == 0, inverse, jnp.where(sub == 1, bending, 0.0)).T
    return both[:, 0:1], both[:, 1:2]


def gradient_kernel(lag_total, chunks, parts, skip, scal, *refs):
    sums, refs = refs[skip : skip + parts], refs[skip + parts :]
    corrs, refs = refs[: len(chunks)], refs[len(chunks) :]
    targets, outs = refs[: len(refs) // 2], refs[len(refs) // 2 :]
    i = 0
    for corr, (q, pieces) in zip(corrs, chunks):
        inverse, bending = slot_scales(sums, lag_total, q)
        for unit, first, count, at in placed(pieces):
            slot = first + lax.broadcasted_iota(jnp.int32, (count, 1), 0)
            valid = jnp.where(slot < scal[COUNT + unit], inverse[at], 0.0)
            normed = corr[at] * inverse[at]
            outs[i][...] = ((normed - targets[i][0] - normed * bending[at]) * valid).astype(BF16)
            i += 1


def gradients(scal, lag_total, chunks, after, sums, corrs, observed):
    lag_dev = observed.shape[2]
    pieces = [p for _, some in chunks for p in some]
    outs = [jax.ShapeDtypeStruct((p[2], lag_dev), BF16) for p in pieces]
    return pl.pallas_call(
        functools.partial(gradient_kernel, lag_total, chunks, len(sums), len(after)),
        grid_spec=pltpu.PrefetchScalarGridSpec(
            num_scalar_prefetch=1,
            grid=(1,),
            in_specs=[ANY] * len(after)
            + [whole(x.shape) for x in (*sums, *corrs)]
            + target_specs(pieces, lag_dev),
            out_specs=[whole(o.shape) for o in outs],
        ),
        out_shape=outs,
        compiler_params=params(16),
        cost_estimate=SMALL,
        name="gradient",
    )(scal, *after, *sums, *corrs, *[observed] * len(pieces))


def normed_kernel(lag_total, chunks, parts, scal, *refs):
    sums, corrs, out = refs[:parts], refs[parts:-1], refs[-1]
    for q, (pieces, corr) in enumerate(zip(chunks, corrs)):
        inverse, _ = slot_scales(sums, lag_total, q)
        for unit, first, count, at in placed(pieces):

            @pl.when(pl.program_id(0) == unit)
            def _():
                out[0, first : first + count] = corr[at] * inverse[at]


def normed_rows(scal, lag_total, chunks, sums, corrs, observed):
    blocks, slots, lag_dev = observed.shape
    ins = [*sums, *corrs]
    return pl.pallas_call(
        functools.partial(normed_kernel, lag_total, chunks, len(sums)),
        grid_spec=pltpu.PrefetchScalarGridSpec(
            num_scalar_prefetch=1,
            grid=(blocks,),
            in_specs=[whole(x.shape) for x in ins],
            out_specs=pl.BlockSpec((1, slots, lag_dev), lambda i, scal: (scal[BLOCK + i], 0, 0)),
        ),
        out_shape=jax.ShapeDtypeStruct(observed.shape, F32),
        compiler_params=params(16),
        cost_estimate=SMALL,
        name="normed",
    )(scal, *ins)


def adjoint_kernel(pieces, *refs):
    ids, parts, out = refs[: len(pieces)], refs[len(pieces) : -1], refs[-1]
    pick = picks([i.at[:, p[1] : p[1] + p[2]] for i, p in zip(ids, pieces)], out.shape[0])
    rows = jnp.concatenate([p[...] for p in parts], axis=0)
    out[...] = jnp.dot(pick, rows, preferred_element_type=F32)


def adjoint_rows(src_ids, pieces, parts, channels):
    lag_dev = parts[0].shape[1]
    return pl.pallas_call(
        functools.partial(adjoint_kernel, pieces),
        out_shape=jax.ShapeDtypeStruct((channels, lag_dev), F32),
        in_specs=[VMEM] * (2 * len(parts)),
        out_specs=VMEM,
        compiler_params=params(16),
        cost_estimate=SMALL,
        name="adjoint",
    )(*[src_ids[p[0]] for p in pieces], *parts)


def shards(spectra, window_keep, owners, pair_src, pair_rec, pair_count, observed):
    columns, cores, places = lax.axis_size("win"), lax.axis_size("freq"), lax.axis_size("recv")
    column, core, place = lax.axis_index("win"), lax.axis_index("freq"), lax.axis_index("recv")
    assert spectra.shape[0] == 1 and cores == 2
    channels, bins_dev = spectra.shape[2:]
    blocks, slots, lag_dev = observed.shape
    lag_total = lag_dev * columns * cores
    bin_total = bins_dev * cores
    period = 2 * bin_total
    part = bins_dev // columns
    classes = part // LANES
    span = period // classes
    geometry = (classes, span, lag_total // span, lag_total // 2, period, 256)
    lag_scale = 1.0 / math.sqrt(bin_total * columns)
    peers = columns * cores
    some = slots // 2
    shifts = range(places)

    def cut(values, s):
        return lax.dynamic_slice(values, (0, 0, 0, (column ^ s) * part), (1, 2, channels, part))

    here, *held = [swapped(cut(spectra, s), "win", columns, s) for s in range(columns)]
    scal, wanted, rec_ids = index(
        window_keep, owners, pair_count, pair_src, pair_rec, places
    )
    if columns == 2:
        weight = jnp.ones((1,), F32)
    else:
        keeps = jnp.stack([swapped(window_keep[0], "win", columns, s) for s in range(columns)])
        ranked = jnp.argsort(-keeps)[: columns - 1].astype(jnp.int32)
        weight = keeps[ranked].astype(F32)
        scal = lax.dynamic_update_slice(scal, ranked, (ORDER,))

    direct = places == blocks
    src_ids = [swapped(wanted[d], "recv", places, d) for d in reversed(shifts)][::-1]
    trig = tables(classes, span, period, bins_dev, columns, cores)
    if direct and blocks == 4:
        chunks = [
            [(0, 0, slots), (1, 0, slots)],
            [(3, 0, slots)],
            [(2, 0, slots)],
        ]
    else:
        chunks = [[(d, first, some) for d in range(blocks)] for first in (0, some)]
    if direct:
        messages = [piece for pieces in chunks for piece in pieces]
    else:
        messages = [(d, 0, slots) for d in shifts]
    sent, kept = gather_rows(scal, here, held, make_perm(part), src_ids, messages)
    own_rows, table = gather_own(scal, kept, rec_ids, trig, classes, span, peers)
    arrived = [swapped(x, "recv", places, m[0]) for m, x in reversed(list(zip(messages, sent)))][::-1]
    if not direct:
        stacked = jnp.stack(arrived)
        whole_rows = [
            lax.dynamic_index_in_dim(stacked, place ^ owners[b], 0, False) for b in range(blocks)
        ]
        arrived = [whole_rows[piece[0]] for pieces in chunks for piece in pieces]
    corrs, all_sums, returned, returned_pieces = [], [], [], []
    after = []
    for q, pieces in enumerate(chunks):
        rows, arrived = arrived[: len(pieces)], arrived[len(pieces) :]
        lhs = cross_rows(
            weight, after[:1] + (arrived if q == 1 else []), rows, own_rows, pieces, classes, LARGE if q < 2 else SMALL
        )
        groups = sum(p[2] for p in pieces) // (32 if q else 16)
        keep, *sends = lag_parts(
            scal, [], lhs, table, geometry, columns, lag_dev, groups, SMALL if q else LARGE
        )
        sends = [swapped(x, "freq", cores, 1) for x in sends]
        own, *sends = add_cores(scal, after[1:], keep, sends)
        more = [swapped(x, "win", columns, s + 1) for s, x in enumerate(sends)]
        after = [own, *more] if q == 0 else []
        corr, sums = lag_stats(scal, lag_scale, q, pieces, all_sums, own, more, observed)
        corrs.append(corr)
        all_sums = [sums]
    sums = [swapped(sums, ("win", "freq"), peers, s) for s in reversed(range(peers))]
    after = []
    numbered = list(enumerate(chunks))
    for group in (numbered[1:], numbered[:1]):
        grads = gradients(scal, lag_total, group, after, sums, [corrs[q] for q, _ in group], observed)
        pieces = [p for _, some_pieces in group for p in some_pieces]
        after = [grads[0]]
        if not direct:
            stacked = jnp.stack(list(grads) + [jnp.zeros_like(grads[0])])
            grads = []
            for d in shifts:
                block = jnp.int32(blocks)
                for b in range(blocks):
                    block = jnp.where(owners[b] == place ^ d, b, block)
                grads.append(lax.dynamic_index_in_dim(stacked, block, 0, False))
            pieces = [(d, pieces[0][1], some) for d in shifts]
        sent = [swapped(g, "recv", places, p[0]) for p, g in reversed(list(zip(pieces, grads)))]
        returned += sent[::-1]
        returned_pieces += pieces
    normed = normed_rows(scal, lag_total, chunks, sums, corrs, observed)
    adjoint = adjoint_rows(src_ids, returned_pieces, returned, channels)
    return (normed, adjoint)


def solution(mesh):
    return jax.shard_map(
        shards,
        mesh=mesh,
        in_specs=(
            P("win", None, ("groups", "recv"), "freq"),
            P(("groups", "win")),
            P("groups"),
            P(None, ("groups", "recv")),
            P(None, ("groups", "recv")),
            P(None, ("groups", "recv")),
            P(None, ("groups", "recv"), ("win", "freq")),
        ),
        out_specs=(
            P(None, ("groups", "recv"), ("win", "freq")),
            P(("groups", "recv"), ("win", "freq")),
        ),
        check_vma=False,
    )
```

```python
import functools
import math

import jax
import jax.numpy as jnp
import ml_dtypes
import numpy as np
from jax import lax
from jax.experimental import pallas as pl
from jax.experimental.pallas import tpu as pltpu
from jax.sharding import PartitionSpec as P

EPSILON = 1e-06
MIB = 1 << 20
LANES = 128
CORE, COLUMN, ORDER, BLOCK, COUNT = 0, 1, 2, 8, 16
BF16 = jnp.bfloat16
F32 = jnp.float32
VMEM = pl.BlockSpec(memory_space=pltpu.VMEM)
SMEM = pl.BlockSpec(memory_space=pltpu.SMEM)
HBM = pl.BlockSpec(memory_space=pltpu.HBM)
ANY = pl.BlockSpec(memory_space=pl.ANY)


def swapped(value, axis, size, step):
    assert size & (size - 1) == 0
    if step == 0:
        return value
    return lax.ppermute(value, axis, [(i, i ^ step) for i in range(size)])


def params(mib):
    return pltpu.CompilerParams(vmem_limit_bytes=mib * MIB)


SMALL = pl.CostEstimate(flops=1, bytes_accessed=1, transcendentals=0)
LARGE = pl.CostEstimate(flops=2 * 10**10, bytes_accessed=MIB, transcendentals=0)


def tables(classes, span, period, bins_dev, columns, cores):
    u = np.arange(span, dtype=np.int64)[None, :]
    piece = np.arange(columns * cores, dtype=np.int64)[:, None]
    first = piece % cores * bins_dev + piece // cores * (bins_dev // columns)
    rows = (first + np.arange(classes)).reshape(-1)
    high = 16 * classes * np.arange(LANES // 16, dtype=np.int64)
    low = classes * np.arange(16, dtype=np.int64)
    angle = (np.concatenate([rows, high, low])[:, None] * u % period) * (2.0 * math.pi / period)
    return np.stack([np.cos(angle), np.sin(angle)]).astype(np.float32)


def fetch(pairs, sems):
    copies = [pltpu.make_async_copy(a, b, sems.at[i]) for i, (a, b) in enumerate(pairs)]
    for c in copies:
        c.start()
    for c in copies:
        c.wait()


def index_kernel(blocks, direct, *refs):
    given, refs = refs[:5], refs[5:]
    scal, wanted, rec_ids, held, sems = refs[0], refs[1:-7], refs[-7], refs[-6:-1], refs[-1]
    fetch(zip(given, held), sems)
    window_keep, owners, pair_count, src, rec = held
    place = lax.axis_index("recv")
    column, columns = lax.axis_index("win"), lax.axis_size("win")
    core = lax.axis_index("freq")
    scal[CORE] = core
    scal[COLUMN] = column
    scal[ORDER] = 1 - window_keep[0]
    for b in range(blocks):
        unit = place ^ owners[b] if direct else b
        scal[BLOCK + unit] = b
        scal[COUNT + unit] = pair_count[b]
    for d, out in enumerate(wanted):
        chosen = jnp.full(out.shape, -1, jnp.int32)
        received = jnp.zeros(out.shape, jnp.int32)
        for b in range(blocks):
            mine = jnp.full(out.shape, owners[b], jnp.int32) == (place ^ d)
            chosen = jnp.where(mine, src[b : b + 1], chosen)
            received = jnp.where(mine, rec[b : b + 1], received)
        out[...] = chosen
        if direct:
            rec_ids[d : d + 1] = received
    if not direct:
        rec_ids[...] = rec[...]


def index(window_keep, owners, pair_count, pair_src, pair_rec, places):
    blocks, slots = pair_src.shape
    ids = jax.ShapeDtypeStruct((1, slots), jnp.int32)
    given = [window_keep, owners, pair_count[:, 0], pair_src, pair_rec]
    scal, *wanted, rec_ids = pl.pallas_call(
        functools.partial(index_kernel, blocks, places == blocks),
        out_shape=[jax.ShapeDtypeStruct((LANES,), jnp.int32)]
        + [ids] * places
        + [jax.ShapeDtypeStruct(pair_rec.shape, jnp.int32)],
        in_specs=[HBM] * 5,
        out_specs=[SMEM] + [VMEM] * (places + 1),
        scratch_shapes=[pltpu.SMEM(g.shape, g.dtype) for g in given[:3]]
        + [pltpu.VMEM(g.shape, g.dtype) for g in given[3:]]
        + [pltpu.SemaphoreType.DMA((5,))],
        compiler_params=params(16),
        cost_estimate=SMALL,
        name="index",
    )(*given)
    return scal, wanted, rec_ids


def table_kernel(classes, parts, scal, trig, table, base):
    rows = parts * classes
    low = slice(rows + LANES // 16, rows + LANES // 16 + 16)
    cl, sl = trig[0, low], trig[1, low]
    for h in range(LANES // 16):
        ch, sh = trig[0, rows + h : rows + h + 1], trig[1, rows + h : rows + h + 1]
        base[0, 16 * h : 16 * h + 16] = ch * cl - sh * sl
        base[1, 16 * h : 16 * h + 16] = sh * cl + ch * sl
    first = (scal[CORE] + 2 * scal[COLUMN]) * classes
    cb, sb = base[0], base[1]
    for r in range(classes):
        ca, sa = trig[0, pl.ds(first + r, 1)], trig[1, pl.ds(first + r, 1)]
        table[r, :LANES] = (ca * cb - sa * sb).astype(BF16)
        table[r, LANES:] = (-(sa * cb + ca * sb)).astype(BF16)


def perm_kernel(perm):
    part = perm.shape[0]
    classes = part // LANES
    source = lax.broadcasted_iota(jnp.int32, (part, LANES), 0)
    target = classes * lax.broadcasted_iota(jnp.int32, (part, LANES), 1)
    for r in range(classes):
        perm[:, r * LANES : (r + 1) * LANES] = (source == target + r).astype(BF16)


def make_perm(part):
    return pl.pallas_call(
        perm_kernel,
        out_shape=jax.ShapeDtypeStruct((part, part), BF16),
        out_specs=VMEM,
        compiler_params=params(8),
        cost_estimate=SMALL,
        name="perm",
    )()


def picks(ids, channels):
    row = jnp.concatenate([i[...] for i in ids], axis=1)
    return (lax.broadcasted_iota(jnp.int32, (channels, row.shape[1]), 0) == row).astype(BF16)


def rows_kernel(used, sends, messages, scal, here, *refs):
    held, perm, src_ids, refs = refs[:used], refs[used], refs[used + 1 : used + 1 + sends], refs[used + 1 + sends :]
    outs, kept = refs[:-1], refs[-1]
    _, _, channels, part = kept.shape
    slots = src_ids[0].shape[1]
    pick = picks(src_ids[::-1], channels)
    for u in range(used):
        x = here[0].reshape(2 * channels, part)
        for s in range(used):
            x = jnp.where(scal[ORDER + u] == s + 1, held[s][0].reshape(2 * channels, part), x)
        x = jnp.dot(x, perm[...], preferred_element_type=F32).astype(BF16)
        for half in range(2):
            z = x[half * channels : (half + 1) * channels]
            kept[u, half] = z
            y = lax.dot_general(
                pick, z, (((0,), (0,)), ((), ())), preferred_element_type=F32
            ).astype(BF16)
            for (d, first, count), out in zip(messages, outs):
                at = d * slots + first
                out[u, half] = y[at : at + count]


def gather_rows(scal, here, held, perm, src_ids, messages):
    used = len(held)
    channels, part = held[0].shape[-2:]
    *sent, kept = pl.pallas_call(
        functools.partial(rows_kernel, used, len(src_ids), messages),
        out_shape=[jax.ShapeDtypeStruct((used, 2, m[2], part), BF16) for m in messages]
        + [jax.ShapeDtypeStruct((used, 2, channels, part), BF16)],
        in_specs=[SMEM] + [VMEM] * (used + 2 + len(src_ids)),
        out_specs=[VMEM] * (len(messages) + 1),
        compiler_params=params(16),
        cost_estimate=SMALL,
        name="rows",
    )(scal, here, *held, perm, *src_ids[::-1])
    return sent, kept


def own_kernel(classes, parts, scal, kept, rec_ids, trig, own, table, base):
    units, used, _, slots, _ = own.shape
    pick = picks([rec_ids.at[d : d + 1] for d in range(units)], kept.shape[2])
    for u in range(used):
        for half in range(2):
            y = lax.dot_general(
                pick, kept[u, half], (((0,), (0,)), ((), ())), preferred_element_type=F32
            ).astype(BF16)
            for d in range(units):
                own[d, u, half] = y[d * slots : (d + 1) * slots]
    table_kernel(classes, parts, scal, trig, table, base)


def gather_own(scal, kept, rec_ids, trig, classes, span, parts):
    used, _, _, part = kept.shape
    units, slots = rec_ids.shape
    return pl.pallas_call(
        functools.partial(own_kernel, classes, parts),
        out_shape=[
            jax.ShapeDtypeStruct((units, used, 2, slots, part), BF16),
            jax.ShapeDtypeStruct((classes, 2 * LANES, span), BF16),
        ],
        in_specs=[SMEM] + [VMEM] * 3,
        out_specs=[VMEM] * 2,
        scratch_shapes=[pltpu.VMEM((2, LANES, span), F32)],
        compiler_params=params(16),
        cost_estimate=SMALL,
        name="own",
    )(scal, kept, rec_ids, jnp.asarray(trig))


def combine(values, classes, outputs, origin, span, period):
    plain, scaled = [None] * outputs, [None] * outputs

    def add(into, k, value, sign):
        if into[k] is None:
            into[k] = value if sign > 0 else -value
        else:
            into[k] = into[k] + value if sign > 0 else into[k] - value

    for r, (real, imag) in enumerate(values):
        both = None
        for k in range(outputs):
            eighths = r * (span * k - origin) * 8 // period % 8
            assert r * (span * k - origin) * 8 % period == 0
            if eighths % 2 == 0:
                value, sign = ((real, 1), (imag, -1), (real, -1), (imag, 1))[eighths // 2]
                add(plain, k, value, sign)
            else:
                if both is None:
                    both = real + imag, real - imag
                value, sign = ((both[1], 1), (both[0], -1), (both[1], -1), (both[0], 1))[eighths // 2]
                add(scaled, k, value, sign)
    root = math.sqrt(0.5)
    return [a if b is None else a + root * b for a, b in zip(plain, scaled)]


def placed(pieces):
    at = 0
    for unit, first, count in pieces:
        yield unit, first, count, slice(at, at + count)
        at += count


def cross_kernel(pieces, skip, weight, *refs):
    refs = refs[skip:]
    s_refs, own, lhs = refs[:-2], refs[-2], refs[-1]
    used = own.shape[1]
    rows = lhs.shape[1] // 2
    for s_ref, (unit, first, count, at) in zip(s_refs, placed(pieces)):
        turned = slice(rows + at.start, rows + at.stop)
        mine = slice(first, first + count)
        sent = mine if s_ref.shape[2] > count else slice(0, count)
        for r in range(lhs.shape[0]):
            bins = slice(r * LANES, (r + 1) * LANES)
            real = imag = None
            for u in range(used):
                sr, si = (s_ref[u, half, sent, bins].astype(F32) for half in range(2))
                rr, ri = (own[unit, u, half, mine, bins].astype(F32) for half in range(2))
                re, im = sr * rr + si * ri, si * rr - sr * ri
                if u:
                    re, im = real + weight[u] * re, imag + weight[u] * im
                real, imag = re, im
            lhs[r, at, :LANES] = real.astype(BF16)
            lhs[r, at, LANES:] = imag.astype(BF16)
            lhs[r, turned, :LANES] = imag.astype(BF16)
            lhs[r, turned, LANES:] = (-real).astype(BF16)


def cross_rows(weight, after, rows, own, pieces, classes, effort):
    count = sum(p[2] for p in pieces)
    return pl.pallas_call(
        functools.partial(cross_kernel, pieces, len(after)),
        out_shape=jax.ShapeDtypeStruct((classes, 2 * count, 2 * LANES), BF16),
        in_specs=[SMEM] + [ANY] * len(after) + [VMEM] * (len(rows) + 1),
        out_specs=VMEM,
        compiler_params=params(8),
        cost_estimate=effort,
        name="cross",
    )(weight, *after, *rows, own)


def lags_kernel(geometry, split, skip, scal, *refs):
    classes, span, outputs, origin, period, chunk = geometry
    lhs, table, keep, *refs = refs[skip:]
    sends, sums = refs[:split], refs[split:]
    rows = lhs.shape[1] // 2
    lag_dev = keep.shape[-1]
    cores = 2
    at_once = span == lag_dev
    first = scal[CORE] == 0
    for start in range(0, span, chunk):
        values = []
        for r in range(classes):
            whole_turns = all(
                r * (span * k - origin) * 2 % period == 0 for k in range(outputs)
            )
            left = lhs[r, :rows] if whole_turns else lhs[r]
            y = jnp.dot(left, table[r, :, start : start + chunk], preferred_element_type=F32)
            values.append((y[:rows], None if whole_turns else y[rows:]))
        corr = combine(values, classes, outputs, origin, span, period)
        lags = slice(start, start + chunk)
        for column in range(keep.shape[0]) if at_once else ():
            even, odd = corr[2 * column], corr[2 * column + 1]
            keep[column, :, lags] = jnp.where(first, even, odd)
            other = jnp.where(first, odd, even).astype(BF16)
            for i, out in enumerate(sends):
                out[column, :, lags] = other[i * out.shape[1] : (i + 1) * out.shape[1]]
        for k, value in enumerate(corr) if not at_once else ():
            lag = span * k + start
            sums[0][lag // lag_dev, :, lag % lag_dev : lag % lag_dev + chunk] = value
    if at_once:
        return
    for column in range(keep.shape[0]):
        keep[column] = sums[0][cores * column + scal[CORE]]
        for i, out in enumerate(sends):
            at = slice(i * out.shape[1], (i + 1) * out.shape[1])
            out[column] = sums[0][cores * column + 1 - scal[CORE], at].astype(BF16)


def lag_parts(scal, after, lhs, table, geometry, columns, lag_dev, split, effort):
    rows = lhs.shape[1] // 2
    shape = lambda count: (columns, count, lag_dev)
    return pl.pallas_call(
        functools.partial(lags_kernel, geometry, split, len(after)),
        out_shape=[jax.ShapeDtypeStruct(shape(rows), F32)]
        + [jax.ShapeDtypeStruct(shape(rows // split), BF16)] * split,
        in_specs=[SMEM] + [ANY] * len(after) + [VMEM] * 2,
        out_specs=[VMEM] * (split + 1),
        scratch_shapes=[pltpu.VMEM((2 * columns, rows, lag_dev), F32)] * (geometry[1] != lag_dev),
        compiler_params=params(16),
        cost_estimate=effort,
        name="lags",
    )(scal, *after, lhs, table)


def cores_kernel(skip, split, scal, *refs):
    keep, *refs = refs[skip:]
    more, own, sends = refs[:split], refs[split], refs[split + 1 :]
    columns = keep.shape[0]
    for i, m in enumerate(more):
        at = slice(i * m.shape[1], (i + 1) * m.shape[1])
        for column in range(columns):
            value = keep[column, at] + m[column].astype(F32)

            @pl.when(scal[COLUMN] == column)
            def _():
                own[at] = value

            for s, out in enumerate(sends):

                @pl.when(scal[COLUMN] ^ (s + 1) == column)
                def _():
                    out[at] = value.astype(BF16)


def add_cores(scal, after, keep, more):
    columns, rows, lag_dev = keep.shape
    return pl.pallas_call(
        functools.partial(cores_kernel, len(after), len(more)),
        out_shape=[jax.ShapeDtypeStruct((rows, lag_dev), F32)]
        + [jax.ShapeDtypeStruct((rows, lag_dev), BF16)] * (columns - 1),
        in_specs=[SMEM] + [ANY] * len(after) + [VMEM] * (1 + len(more)),
        out_specs=[VMEM] * columns,
        compiler_params=params(8),
        cost_estimate=SMALL,
        name="cores",
    )(scal, *after, keep, *more)


def stats_kernel(scale, q, pieces, others, count, skip, scal, *refs):
    refs = refs[skip:]
    earlier, (own, *refs) = refs[:count], refs[count:]
    more, refs = refs[:others], refs[others:]
    targets, (corr, sums) = refs[: len(pieces)], refs[len(pieces) :]
    columns = []
    for target, (unit, first, count, at) in zip(targets, placed(pieces)):
        value = own[at]
        for m in more:
            value = value + m[at].astype(F32)
        slot = first + lax.broadcasted_iota(jnp.int32, (count, 1), 0)
        value = value * jnp.where(slot < scal[COUNT + unit], scale, 0.0)
        corr[at] = value
        square = jnp.sum(value * value, axis=1, keepdims=True)
        product = jnp.sum(value * target[0], axis=1, keepdims=True)
        lane = lax.broadcasted_iota(jnp.int32, (count, LANES), 1)
        columns.append(jnp.where(lane == 2 * q, square, jnp.where(lane == 2 * q + 1, product, 0.0)))
    spare = sums.shape[1] - own.shape[0]
    if spare:
        columns.append(jnp.zeros((spare, LANES), F32))
    total = jnp.concatenate(columns, axis=0).T[:8]
    for e in earlier:
        total = total + e[...]
    sums[...] = total


def target_specs(pieces, lag_dev):
    return [
        pl.BlockSpec(
            (1, count, lag_dev),
            lambda i, scal, unit=unit, block=first // count: (scal[BLOCK + unit], block, 0),
        )
        for unit, first, count in pieces
    ]


def whole(shape):
    return pl.BlockSpec(shape, lambda i, scal: (0,) * len(shape))


def lag_stats(scal, scale, q, pieces, after, earlier, own, more, observed):
    rows, lag_dev = own.shape
    outs = [jax.ShapeDtypeStruct((rows, lag_dev), F32), jax.ShapeDtypeStruct((8, -(-rows // LANES) * LANES), F32)]
    return pl.pallas_call(
        functools.partial(
            stats_kernel, scale, q, pieces, len(more), len(earlier), len(after)
        ),
        grid_spec=pltpu.PrefetchScalarGridSpec(
            num_scalar_prefetch=1,
            grid=(1,),
            in_specs=[ANY] * len(after)
            + [whole(e.shape) for e in earlier]
            + [whole(own.shape)] * (1 + len(more))
            + target_specs(pieces, lag_dev),
            out_specs=[whole(o.shape) for o in outs],
        ),
        out_shape=outs,
        compiler_params=params(16),
        cost_estimate=SMALL,
        name="stats",
    )(scal, *after, *earlier, own, *more, *[observed] * len(pieces))


def slot_scales(sums, lag_total, q):
    total = sums[0][...]
    for s in sums[1:]:
        total = total + s[...]
    rows = total.shape[1]
    square, product = total[2 * q : 2 * q + 1], total[2 * q + 1 : 2 * q + 2]
    inverse = 1.0 / jnp.sqrt(square / lag_total + EPSILON)
    bending = (square * inverse * inverse - product * inverse) / lag_total
    sub = lax.broadcasted_iota(jnp.int32, (LANES, rows), 0)
    both = jnp.where(sub == 0, inverse, jnp.where(sub == 1, bending, 0.0)).T
    return both[:, 0:1], both[:, 1:2]


def gradient_kernel(lag_total, chunks, parts, skip, scal, *refs):
    sums, refs = refs[skip : skip + parts], refs[skip + parts :]
    corrs, refs = refs[: len(chunks)], refs[len(chunks) :]
    targets, outs = refs[: len(refs) // 2], refs[len(refs) // 2 :]
    i = 0
    for corr, (q, pieces) in zip(corrs, chunks):
        inverse, bending = slot_scales(sums, lag_total, q)
        for unit, first, count, at in placed(pieces):
            slot = first + lax.broadcasted_iota(jnp.int32, (count, 1), 0)
            valid = jnp.where(slot < scal[COUNT + unit], inverse[at], 0.0)
            normed = corr[at] * inverse[at]
            outs[i][...] = ((normed - targets[i][0] - normed * bending[at]) * valid).astype(BF16)
            i += 1


def gradients(scal, lag_total, chunks, after, sums, corrs, observed):
    lag_dev = observed.shape[2]
    pieces = [p for _, some in chunks for p in some]
    outs = [jax.ShapeDtypeStruct((p[2], lag_dev), BF16) for p in pieces]
    return pl.pallas_call(
        functools.partial(gradient_kernel, lag_total, chunks, len(sums), len(after)),
        grid_spec=pltpu.PrefetchScalarGridSpec(
            num_scalar_prefetch=1,
            grid=(1,),
            in_specs=[ANY] * len(after)
            + [whole(x.shape) for x in (*sums, *corrs)]
            + target_specs(pieces, lag_dev),
            out_specs=[whole(o.shape) for o in outs],
        ),
        out_shape=outs,
        compiler_params=params(16),
        cost_estimate=SMALL,
        name="gradient",
    )(scal, *after, *sums, *corrs, *[observed] * len(pieces))


def normed_kernel(lag_total, chunks, parts, scal, *refs):
    out = refs[-1]
    for q, pieces in enumerate(chunks):
        sums, corr = refs[q * (parts + 1) : q * (parts + 1) + parts], refs[q * (parts + 1) + parts]
        inverse, _ = slot_scales(sums, lag_total, q)
        for unit, first, count, at in placed(pieces):

            @pl.when(pl.program_id(0) == unit)
            def _():
                out[0, first : first + count] = corr[at] * inverse[at]


def normed_rows(scal, lag_total, chunks, sums, corrs, observed):
    blocks, slots, lag_dev = observed.shape
    ins = [x for s, c in zip(sums, corrs) for x in (*s, c)]
    return pl.pallas_call(
        functools.partial(normed_kernel, lag_total, chunks, len(sums[0])),
        grid_spec=pltpu.PrefetchScalarGridSpec(
            num_scalar_prefetch=1,
            grid=(blocks,),
            in_specs=[whole(x.shape) for x in ins],
            out_specs=pl.BlockSpec((1, slots, lag_dev), lambda i, scal: (scal[BLOCK + i], 0, 0)),
        ),
        out_shape=jax.ShapeDtypeStruct(observed.shape, F32),
        compiler_params=params(16),
        cost_estimate=SMALL,
        name="normed",
    )(scal, *ins)


def adjoint_kernel(pieces, *refs):
    ids, parts, out = refs[: len(pieces)], refs[len(pieces) : -1], refs[-1]
    pick = picks([i.at[:, p[1] : p[1] + p[2]] for i, p in zip(ids, pieces)], out.shape[0])
    rows = jnp.concatenate([p[...] for p in parts], axis=0)
    out[...] = jnp.dot(pick, rows, preferred_element_type=F32)


def adjoint_rows(src_ids, pieces, parts, channels):
    lag_dev = parts[0].shape[1]
    return pl.pallas_call(
        functools.partial(adjoint_kernel, pieces),
        out_shape=jax.ShapeDtypeStruct((channels, lag_dev), F32),
        in_specs=[VMEM] * (2 * len(parts)),
        out_specs=VMEM,
        compiler_params=params(16),
        cost_estimate=SMALL,
        name="adjoint",
    )(*[src_ids[p[0]] for p in pieces], *parts)


def shards(spectra, window_keep, owners, pair_src, pair_rec, pair_count, observed):
    columns, cores, places = lax.axis_size("win"), lax.axis_size("freq"), lax.axis_size("recv")
    column, core, place = lax.axis_index("win"), lax.axis_index("freq"), lax.axis_index("recv")
    assert spectra.shape[0] == 1 and cores == 2
    channels, bins_dev = spectra.shape[2:]
    blocks, slots, lag_dev = observed.shape
    lag_total = lag_dev * columns * cores
    bin_total = bins_dev * cores
    period = 2 * bin_total
    part = bins_dev // columns
    classes = part // LANES
    span = period // classes
    geometry = (classes, span, lag_total // span, lag_total // 2, period, 256)
    lag_scale = 1.0 / math.sqrt(bin_total * columns)
    peers = columns * cores
    some = slots // 2
    shifts = range(places)

    def cut(values, s):
        return lax.dynamic_slice(values, (0, 0, 0, (column ^ s) * part), (1, 2, channels, part))

    here, *held = [swapped(cut(spectra, s), "win", columns, s) for s in range(columns)]
    scal, wanted, rec_ids = index(
        window_keep, owners, pair_count, pair_src, pair_rec, places
    )
    if columns == 2:
        weight = jnp.ones((1,), F32)
    else:
        keeps = jnp.stack([swapped(window_keep[0], "win", columns, s) for s in range(columns)])
        ranked = jnp.argsort(-keeps)[: columns - 1].astype(jnp.int32)
        weight = keeps[ranked].astype(F32)
        scal = lax.dynamic_update_slice(scal, ranked, (ORDER,))

    direct = places == blocks
    src_ids = [swapped(wanted[d], "recv", places, d) for d in reversed(shifts)][::-1]
    trig = tables(classes, span, period, bins_dev, columns, cores)
    if direct and blocks == 4:
        chunks = [
            [(0, 0, slots), (3, 0, slots)],
            [(1, 0, slots)],
            [(2, 0, slots)],
        ]
    else:
        chunks = [[(d, first, some) for d in range(blocks)] for first in (0, some)]
    if direct:
        messages = [piece for pieces in chunks for piece in pieces]
    else:
        messages = [(d, 0, slots) for d in shifts]
    sent, kept = gather_rows(scal, here, held, make_perm(part), src_ids, messages)
    own_rows, table = gather_own(scal, kept, rec_ids, trig, classes, span, peers)
    arrived = [swapped(x, "recv", places, m[0]) for m, x in reversed(list(zip(messages, sent)))][::-1]
    if not direct:
        stacked = jnp.stack(arrived)
        whole_rows = [
            lax.dynamic_index_in_dim(stacked, place ^ owners[b], 0, False) for b in range(blocks)
        ]
        arrived = [whole_rows[piece[0]] for pieces in chunks for piece in pieces]
    corrs, all_sums, sums_of, returned, returned_pieces, early = [], [], [], [], [], []
    after = []
    for q, pieces in enumerate(chunks):
        rows, arrived = arrived[: len(pieces)], arrived[len(pieces) :]
        lhs = cross_rows(
            weight, after[:1] + (arrived if q == 1 else []), rows, own_rows, pieces, classes, LARGE if q < 2 else SMALL
        )
        groups = sum(p[2] for p in pieces) // (32 if q else 16)
        keep, *sends = lag_parts(
            scal, [], lhs, table, geometry, columns, lag_dev, groups, SMALL if q else LARGE
        )
        sends = [swapped(x, "freq", cores, 1) for x in sends]
        own, *sends = add_cores(scal, after[1:], keep, sends)
        more = [swapped(x, "win", columns, s + 1) for s, x in enumerate(sends)]
        after = [own, *more] if q == 0 else []
        last = q == len(chunks) - 1
        corr, sums = lag_stats(
            scal, lag_scale, q, pieces, early if last else [], all_sums, own, more, observed
        )
        corrs.append(corr)
        all_sums = [sums]
        if q and not last:
            continue
        sums = [swapped(sums, ("win", "freq"), peers, s) for s in reversed(range(peers))]
        all_sums = []
        group = list(enumerate(chunks))[:1] if q == 0 else list(enumerate(chunks))[:0:-1]
        sums_of += [sums] * len(group)
        grads = gradients(scal, lag_total, group, [], sums, [corrs[i] for i, _ in group], observed)
        early = [grads[0]]
        back = [p for _, these in group for p in these]
        if not direct:
            stacked = jnp.stack(list(grads) + [jnp.zeros_like(grads[0])])
            grads = []
            for d in shifts:
                block = jnp.int32(blocks)
                for b in range(blocks):
                    block = jnp.where(owners[b] == place ^ d, b, block)
                grads.append(lax.dynamic_index_in_dim(stacked, block, 0, False))
            back = [(d, back[0][1], some) for d in shifts]
        returned += [swapped(g, "recv", places, p[0]) for p, g in zip(back, grads)]
        returned_pieces += back
    normed = normed_rows(scal, lag_total, chunks, sums_of, corrs, observed)
    adjoint = adjoint_rows(src_ids, returned_pieces, returned, channels)
    return (normed, adjoint)


def solution(mesh):
    return jax.shard_map(
        shards,
        mesh=mesh,
        in_specs=(
            P("win", None, ("groups", "recv"), "freq"),
            P(("groups", "win")),
            P("groups"),
            P(None, ("groups", "recv")),
            P(None, ("groups", "recv")),
            P(None, ("groups", "recv")),
            P(None, ("groups", "recv"), ("win", "freq")),
        ),
        out_specs=(
            P(None, ("groups", "recv"), ("win", "freq")),
            P(("groups", "recv"), ("win", "freq")),
        ),
        check_vma=False,
    )
```

```python
import functools
import math

import jax
import jax.numpy as jnp
import ml_dtypes
import numpy as np
from jax import lax
from jax.experimental import pallas as pl
from jax.experimental.pallas import tpu as pltpu
from jax.sharding import PartitionSpec as P

EPSILON = 1e-06
MIB = 1 << 20
LANES = 128
CORE, COLUMN, ORDER, BLOCK, COUNT = 0, 1, 2, 8, 16
BF16 = jnp.bfloat16
F32 = jnp.float32
VMEM = pl.BlockSpec(memory_space=pltpu.VMEM)
SMEM = pl.BlockSpec(memory_space=pltpu.SMEM)
HBM = pl.BlockSpec(memory_space=pltpu.HBM)
ANY = pl.BlockSpec(memory_space=pl.ANY)


def swapped(value, axis, size, step):
    assert size & (size - 1) == 0
    if step == 0:
        return value
    return lax.ppermute(value, axis, [(i, i ^ step) for i in range(size)])


def params(mib):
    return pltpu.CompilerParams(vmem_limit_bytes=mib * MIB)


SMALL = pl.CostEstimate(flops=1, bytes_accessed=1, transcendentals=0)
LARGE = pl.CostEstimate(flops=2 * 10**10, bytes_accessed=MIB, transcendentals=0)


def tables(classes, span, period, bins_dev, columns, cores):
    u = np.arange(span, dtype=np.int64)[None, :]
    piece = np.arange(columns * cores, dtype=np.int64)[:, None]
    first = piece % cores * bins_dev + piece // cores * (bins_dev // columns)
    rows = (first + np.arange(classes)).reshape(-1)
    high = 16 * classes * np.arange(LANES // 16, dtype=np.int64)
    low = classes * np.arange(16, dtype=np.int64)
    angle = (np.concatenate([rows, high, low])[:, None] * u % period) * (2.0 * math.pi / period)
    return np.stack([np.cos(angle), np.sin(angle)]).astype(np.float32)


def fetch(pairs, sems):
    copies = [pltpu.make_async_copy(a, b, sems.at[i]) for i, (a, b) in enumerate(pairs)]
    for c in copies:
        c.start()
    for c in copies:
        c.wait()


def index_kernel(blocks, direct, *refs):
    given, refs = refs[:5], refs[5:]
    scal, wanted, rec_ids, held, sems = refs[0], refs[1:-7], refs[-7], refs[-6:-1], refs[-1]
    fetch(zip(given, held), sems)
    window_keep, owners, pair_count, src, rec = held
    place = lax.axis_index("recv")
    column, columns = lax.axis_index("win"), lax.axis_size("win")
    core = lax.axis_index("freq")
    scal[CORE] = core
    scal[COLUMN] = column
    scal[ORDER] = 1 - window_keep[0]
    for b in range(blocks):
        unit = place ^ owners[b] if direct else b
        scal[BLOCK + unit] = b
        scal[COUNT + unit] = pair_count[b]
    for d, out in enumerate(wanted):
        chosen = jnp.full(out.shape, -1, jnp.int32)
        received = jnp.zeros(out.shape, jnp.int32)
        for b in range(blocks):
            mine = jnp.full(out.shape, owners[b], jnp.int32) == (place ^ d)
            chosen = jnp.where(mine, src[b : b + 1], chosen)
            received = jnp.where(mine, rec[b : b + 1], received)
        out[...] = chosen
        if direct:
            rec_ids[d : d + 1] = received
    if not direct:
        rec_ids[...] = rec[...]


def index(window_keep, owners, pair_count, pair_src, pair_rec, places):
    blocks, slots = pair_src.shape
    ids = jax.ShapeDtypeStruct((1, slots), jnp.int32)
    given = [window_keep, owners, pair_count[:, 0], pair_src, pair_rec]
    scal, *wanted, rec_ids = pl.pallas_call(
        functools.partial(index_kernel, blocks, places == blocks),
        out_shape=[jax.ShapeDtypeStruct((LANES,), jnp.int32)]
        + [ids] * places
        + [jax.ShapeDtypeStruct(pair_rec.shape, jnp.int32)],
        in_specs=[HBM] * 5,
        out_specs=[SMEM] + [VMEM] * (places + 1),
        scratch_shapes=[pltpu.SMEM(g.shape, g.dtype) for g in given[:3]]
        + [pltpu.VMEM(g.shape, g.dtype) for g in given[3:]]
        + [pltpu.SemaphoreType.DMA((5,))],
        compiler_params=params(16),
        cost_estimate=SMALL,
        name="index",
    )(*given)
    return scal, wanted, rec_ids


def table_kernel(classes, parts, scal, trig, table, base):
    rows = parts * classes
    low = slice(rows + LANES // 16, rows + LANES // 16 + 16)
    cl, sl = trig[0, low], trig[1, low]
    for h in range(LANES // 16):
        ch, sh = trig[0, rows + h : rows + h + 1], trig[1, rows + h : rows + h + 1]
        base[0, 16 * h : 16 * h + 16] = ch * cl - sh * sl
        base[1, 16 * h : 16 * h + 16] = sh * cl + ch * sl
    first = (scal[CORE] + 2 * scal[COLUMN]) * classes
    cb, sb = base[0], base[1]
    for r in range(classes):
        ca, sa = trig[0, pl.ds(first + r, 1)], trig[1, pl.ds(first + r, 1)]
        table[r, :LANES] = (ca * cb - sa * sb).astype(BF16)
        table[r, LANES:] = (-(sa * cb + ca * sb)).astype(BF16)


def perm_kernel(perm):
    part = perm.shape[0]
    classes = part // LANES
    source = lax.broadcasted_iota(jnp.int32, (part, LANES), 0)
    target = classes * lax.broadcasted_iota(jnp.int32, (part, LANES), 1)
    for r in range(classes):
        perm[:, r * LANES : (r + 1) * LANES] = (source == target + r).astype(BF16)


def make_perm(part):
    return pl.pallas_call(
        perm_kernel,
        out_shape=jax.ShapeDtypeStruct((part, part), BF16),
        out_specs=VMEM,
        compiler_params=params(8),
        cost_estimate=SMALL,
        name="perm",
    )()


def picks(ids, channels):
    row = jnp.concatenate([i[...] for i in ids], axis=1)
    return (lax.broadcasted_iota(jnp.int32, (channels, row.shape[1]), 0) == row).astype(BF16)


def rows_kernel(used, sends, messages, scal, here, *refs):
    held, perm, src_ids, refs = refs[:used], refs[used], refs[used + 1 : used + 1 + sends], refs[used + 1 + sends :]
    outs, kept = refs[:-1], refs[-1]
    _, _, channels, part = kept.shape
    slots = src_ids[0].shape[1]
    pick = picks(src_ids[::-1], channels)
    for u in range(used):
        x = here[0].reshape(2 * channels, part)
        for s in range(used):
            x = jnp.where(scal[ORDER + u] == s + 1, held[s][0].reshape(2 * channels, part), x)
        x = jnp.dot(x, perm[...], preferred_element_type=F32).astype(BF16)
        for half in range(2):
            z = x[half * channels : (half + 1) * channels]
            kept[u, half] = z
            y = lax.dot_general(
                pick, z, (((0,), (0,)), ((), ())), preferred_element_type=F32
            ).astype(BF16)
            for (d, first, count), out in zip(messages, outs):
                at = d * slots + first
                out[u, half] = y[at : at + count]


def gather_rows(scal, here, held, perm, src_ids, messages):
    used = len(held)
    channels, part = held[0].shape[-2:]
    *sent, kept = pl.pallas_call(
        functools.partial(rows_kernel, used, len(src_ids), messages),
        out_shape=[jax.ShapeDtypeStruct((used, 2, m[2], part), BF16) for m in messages]
        + [jax.ShapeDtypeStruct((used, 2, channels, part), BF16)],
        in_specs=[SMEM] + [VMEM] * (used + 2 + len(src_ids)),
        out_specs=[VMEM] * (len(messages) + 1),
        compiler_params=params(16),
        cost_estimate=SMALL,
        name="rows",
    )(scal, here, *held, perm, *src_ids[::-1])
    return sent, kept


def own_kernel(classes, parts, scal, kept, rec_ids, trig, own, table, base):
    units, used, _, slots, _ = own.shape
    pick = picks([rec_ids.at[d : d + 1] for d in range(units)], kept.shape[2])
    for u in range(used):
        for half in range(2):
            y = lax.dot_general(
                pick, kept[u, half], (((0,), (0,)), ((), ())), preferred_element_type=F32
            ).astype(BF16)
            for d in range(units):
                own[d, u, half] = y[d * slots : (d + 1) * slots]
    table_kernel(classes, parts, scal, trig, table, base)


def gather_own(scal, kept, rec_ids, trig, classes, span, parts):
    used, _, _, part = kept.shape
    units, slots = rec_ids.shape
    return pl.pallas_call(
        functools.partial(own_kernel, classes, parts),
        out_shape=[
            jax.ShapeDtypeStruct((units, used, 2, slots, part), BF16),
            jax.ShapeDtypeStruct((classes, 2 * LANES, span), BF16),
        ],
        in_specs=[SMEM] + [VMEM] * 3,
        out_specs=[VMEM] * 2,
        scratch_shapes=[pltpu.VMEM((2, LANES, span), F32)],
        compiler_params=params(16),
        cost_estimate=SMALL,
        name="own",
    )(scal, kept, rec_ids, jnp.asarray(trig))


def combine(values, classes, outputs, origin, span, period):
    plain, scaled = [None] * outputs, [None] * outputs

    def add(into, k, value, sign):
        if into[k] is None:
            into[k] = value if sign > 0 else -value
        else:
            into[k] = into[k] + value if sign > 0 else into[k] - value

    for r, (real, imag) in enumerate(values):
        both = None
        for k in range(outputs):
            eighths = r * (span * k - origin) * 8 // period % 8
            assert r * (span * k - origin) * 8 % period == 0
            if eighths % 2 == 0:
                value, sign = ((real, 1), (imag, -1), (real, -1), (imag, 1))[eighths // 2]
                add(plain, k, value, sign)
            else:
                if both is None:
                    both = real + imag, real - imag
                value, sign = ((both[1], 1), (both[0], -1), (both[1], -1), (both[0], 1))[eighths // 2]
                add(scaled, k, value, sign)
    root = math.sqrt(0.5)
    return [a if b is None else a + root * b for a, b in zip(plain, scaled)]


def placed(pieces):
    at = 0
    for unit, first, count in pieces:
        yield unit, first, count, slice(at, at + count)
        at += count


def cross_kernel(pieces, skip, weight, *refs):
    refs = refs[skip:]
    s_refs, own, lhs = refs[:-2], refs[-2], refs[-1]
    used = own.shape[1]
    rows = lhs.shape[1] // 2
    for s_ref, (unit, first, count, at) in zip(s_refs, placed(pieces)):
        turned = slice(rows + at.start, rows + at.stop)
        mine = slice(first, first + count)
        sent = mine if s_ref.shape[2] > count else slice(0, count)
        for r in range(lhs.shape[0]):
            bins = slice(r * LANES, (r + 1) * LANES)
            real = imag = None
            for u in range(used):
                sr, si = (s_ref[u, half, sent, bins].astype(F32) for half in range(2))
                rr, ri = (own[unit, u, half, mine, bins].astype(F32) for half in range(2))
                re, im = sr * rr + si * ri, si * rr - sr * ri
                if u:
                    re, im = real + weight[u] * re, imag + weight[u] * im
                real, imag = re, im
            lhs[r, at, :LANES] = real.astype(BF16)
            lhs[r, at, LANES:] = imag.astype(BF16)
            lhs[r, turned, :LANES] = imag.astype(BF16)
            lhs[r, turned, LANES:] = (-real).astype(BF16)


def cross_rows(weight, after, rows, own, pieces, classes, effort):
    count = sum(p[2] for p in pieces)
    return pl.pallas_call(
        functools.partial(cross_kernel, pieces, len(after)),
        out_shape=jax.ShapeDtypeStruct((classes, 2 * count, 2 * LANES), BF16),
        in_specs=[SMEM] + [ANY] * len(after) + [VMEM] * (len(rows) + 1),
        out_specs=VMEM,
        compiler_params=params(8),
        cost_estimate=effort,
        name="cross",
    )(weight, *after, *rows, own)


def lags_kernel(geometry, split, skip, scal, *refs):
    classes, span, outputs, origin, period, chunk = geometry
    lhs, table, keep, *refs = refs[skip:]
    sends, sums = refs[:split], refs[split:]
    rows = lhs.shape[1] // 2
    lag_dev = keep.shape[-1]
    cores = 2
    at_once = span == lag_dev
    first = scal[CORE] == 0
    for start in range(0, span, chunk):
        values = []
        for r in range(classes):
            whole_turns = all(
                r * (span * k - origin) * 2 % period == 0 for k in range(outputs)
            )
            left = lhs[r, :rows] if whole_turns else lhs[r]
            y = jnp.dot(left, table[r, :, start : start + chunk], preferred_element_type=F32)
            values.append((y[:rows], None if whole_turns else y[rows:]))
        corr = combine(values, classes, outputs, origin, span, period)
        lags = slice(start, start + chunk)
        for column in range(keep.shape[0]) if at_once else ():
            even, odd = corr[2 * column], corr[2 * column + 1]
            keep[column, :, lags] = jnp.where(first, even, odd)
            other = jnp.where(first, odd, even).astype(BF16)
            for i, out in enumerate(sends):
                out[column, :, lags] = other[i * out.shape[1] : (i + 1) * out.shape[1]]
        for k, value in enumerate(corr) if not at_once else ():
            lag = span * k + start
            sums[0][lag // lag_dev, :, lag % lag_dev : lag % lag_dev + chunk] = value
    if at_once:
        return
    for column in range(keep.shape[0]):
        keep[column] = sums[0][cores * column + scal[CORE]]
        for i, out in enumerate(sends):
            at = slice(i * out.shape[1], (i + 1) * out.shape[1])
            out[column] = sums[0][cores * column + 1 - scal[CORE], at].astype(BF16)


def lag_parts(scal, after, lhs, table, geometry, columns, lag_dev, split, effort):
    rows = lhs.shape[1] // 2
    shape = lambda count: (columns, count, lag_dev)
    return pl.pallas_call(
        functools.partial(lags_kernel, geometry, split, len(after)),
        out_shape=[jax.ShapeDtypeStruct(shape(rows), F32)]
        + [jax.ShapeDtypeStruct(shape(rows // split), BF16)] * split,
        in_specs=[SMEM] + [ANY] * len(after) + [VMEM] * 2,
        out_specs=[VMEM] * (split + 1),
        scratch_shapes=[pltpu.VMEM((2 * columns, rows, lag_dev), F32)] * (geometry[1] != lag_dev),
        compiler_params=params(16),
        cost_estimate=effort,
        name="lags",
    )(scal, *after, lhs, table)


def cores_kernel(skip, split, scal, *refs):
    keep, *refs = refs[skip:]
    more, own, sends = refs[:split], refs[split], refs[split + 1 :]
    columns = keep.shape[0]
    for i, m in enumerate(more):
        at = slice(i * m.shape[1], (i + 1) * m.shape[1])
        for column in range(columns):
            value = keep[column, at] + m[column].astype(F32)

            @pl.when(scal[COLUMN] == column)
            def _():
                own[at] = value

            for s, out in enumerate(sends):

                @pl.when(scal[COLUMN] ^ (s + 1) == column)
                def _():
                    out[at] = value.astype(BF16)


def add_cores(scal, after, keep, more):
    columns, rows, lag_dev = keep.shape
    return pl.pallas_call(
        functools.partial(cores_kernel, len(after), len(more)),
        out_shape=[jax.ShapeDtypeStruct((rows, lag_dev), F32)]
        + [jax.ShapeDtypeStruct((rows, lag_dev), BF16)] * (columns - 1),
        in_specs=[SMEM] + [ANY] * len(after) + [VMEM] * (1 + len(more)),
        out_specs=[VMEM] * columns,
        compiler_params=params(8),
        cost_estimate=SMALL,
        name="cores",
    )(scal, *after, keep, *more)


def stats_kernel(scale, q, pieces, others, scal, *refs):
    count = min(q, 1)
    earlier, (own, *refs) = refs[:count], refs[count:]
    more, refs = refs[:others], refs[others:]
    targets, (corr, sums) = refs[: len(pieces)], refs[len(pieces) :]
    columns = []
    for target, (unit, first, count, at) in zip(targets, placed(pieces)):
        value = own[at]
        for m in more:
            value = value + m[at].astype(F32)
        slot = first + lax.broadcasted_iota(jnp.int32, (count, 1), 0)
        value = value * jnp.where(slot < scal[COUNT + unit], scale, 0.0)
        corr[at] = value
        square = jnp.sum(value * value, axis=1, keepdims=True)
        product = jnp.sum(value * target[0], axis=1, keepdims=True)
        lane = lax.broadcasted_iota(jnp.int32, (count, LANES), 1)
        columns.append(jnp.where(lane == 2 * q, square, jnp.where(lane == 2 * q + 1, product, 0.0)))
    spare = sums.shape[1] - own.shape[0]
    if spare:
        columns.append(jnp.zeros((spare, LANES), F32))
    total = jnp.concatenate(columns, axis=0).T[:8]
    for e in earlier:
        total = total + e[...]
    sums[...] = total


def target_specs(pieces, lag_dev):
    return [
        pl.BlockSpec(
            (1, count, lag_dev),
            lambda i, scal, unit=unit, block=first // count: (scal[BLOCK + unit], block, 0),
        )
        for unit, first, count in pieces
    ]


def whole(shape):
    return pl.BlockSpec(shape, lambda i, scal: (0,) * len(shape))


def lag_stats(scal, scale, q, pieces, earlier, own, more, observed):
    rows, lag_dev = own.shape
    outs = [jax.ShapeDtypeStruct((rows, lag_dev), F32), jax.ShapeDtypeStruct((8, -(-rows // LANES) * LANES), F32)]
    return pl.pallas_call(
        functools.partial(stats_kernel, scale, q, pieces, len(more)),
        grid_spec=pltpu.PrefetchScalarGridSpec(
            num_scalar_prefetch=1,
            grid=(1,),
            in_specs=[whole(e.shape) for e in earlier]
            + [whole(own.shape)] * (1 + len(more))
            + target_specs(pieces, lag_dev),
            out_specs=[whole(o.shape) for o in outs],
        ),
        out_shape=outs,
        compiler_params=params(16),
        cost_estimate=SMALL,
        name="stats",
    )(scal, *earlier, own, *more, *[observed] * len(pieces))


def slot_scales(sums, lag_total, q):
    total = sums[0][...]
    for s in sums[1:]:
        total = total + s[...]
    rows = total.shape[1]
    square, product = total[2 * q : 2 * q + 1], total[2 * q + 1 : 2 * q + 2]
    inverse = 1.0 / jnp.sqrt(square / lag_total + EPSILON)
    bending = (square * inverse * inverse - product * inverse) / lag_total
    sub = lax.broadcasted_iota(jnp.int32, (LANES, rows), 0)
    both = jnp.where(sub == 0, inverse, jnp.where(sub == 1, bending, 0.0)).T
    return both[:, 0:1], both[:, 1:2]


def gradient_kernel(lag_total, chunks, parts, skip, scal, *refs):
    sums, refs = refs[skip : skip + parts], refs[skip + parts :]
    corrs, refs = refs[: len(chunks)], refs[len(chunks) :]
    targets, outs = refs[: len(refs) // 2], refs[len(refs) // 2 :]
    i = 0
    for corr, (q, pieces) in zip(corrs, chunks):
        inverse, bending = slot_scales(sums, lag_total, q)
        for unit, first, count, at in placed(pieces):
            slot = first + lax.broadcasted_iota(jnp.int32, (count, 1), 0)
            valid = jnp.where(slot < scal[COUNT + unit], inverse[at], 0.0)
            normed = corr[at] * inverse[at]
            outs[i][...] = ((normed - targets[i][0] - normed * bending[at]) * valid).astype(BF16)
            i += 1


def gradients(scal, lag_total, chunks, after, sums, corrs, observed):
    lag_dev = observed.shape[2]
    pieces = [p for _, some in chunks for p in some]
    outs = [jax.ShapeDtypeStruct((p[2], lag_dev), BF16) for p in pieces]
    return pl.pallas_call(
        functools.partial(gradient_kernel, lag_total, chunks, len(sums), len(after)),
        grid_spec=pltpu.PrefetchScalarGridSpec(
            num_scalar_prefetch=1,
            grid=(1,),
            in_specs=[ANY] * len(after)
            + [whole(x.shape) for x in (*sums, *corrs)]
            + target_specs(pieces, lag_dev),
            out_specs=[whole(o.shape) for o in outs],
        ),
        out_shape=outs,
        compiler_params=params(16),
        cost_estimate=SMALL,
        name="gradient",
    )(scal, *after, *sums, *corrs, *[observed] * len(pieces))


def normed_kernel(lag_total, chunks, parts, scal, *refs):
    sums, corrs, out = refs[:parts], refs[parts:-1], refs[-1]
    for q, (pieces, corr) in enumerate(zip(chunks, corrs)):
        inverse, _ = slot_scales(sums, lag_total, q)
        for unit, first, count, at in placed(pieces):

            @pl.when(pl.program_id(0) == unit)
            def _():
                out[0, first : first + count] = corr[at] * inverse[at]


def normed_rows(scal, lag_total, chunks, sums, corrs, observed):
    blocks, slots, lag_dev = observed.shape
    ins = [*sums, *corrs]
    return pl.pallas_call(
        functools.partial(normed_kernel, lag_total, chunks, len(sums)),
        grid_spec=pltpu.PrefetchScalarGridSpec(
            num_scalar_prefetch=1,
            grid=(blocks,),
            in_specs=[whole(x.shape) for x in ins],
            out_specs=pl.BlockSpec((1, slots, lag_dev), lambda i, scal: (scal[BLOCK + i], 0, 0)),
        ),
        out_shape=jax.ShapeDtypeStruct(observed.shape, F32),
        compiler_params=params(16),
        cost_estimate=SMALL,
        name="normed",
    )(scal, *ins)


def adjoint_kernel(pieces, *refs):
    ids, parts, out = refs[: len(pieces)], refs[len(pieces) : -1], refs[-1]
    pick = picks([i.at[:, p[1] : p[1] + p[2]] for i, p in zip(ids, pieces)], out.shape[0])
    rows = jnp.concatenate([p[...] for p in parts], axis=0)
    out[...] = jnp.dot(pick, rows, preferred_element_type=F32)


def adjoint_rows(src_ids, pieces, parts, channels):
    lag_dev = parts[0].shape[1]
    return pl.pallas_call(
        functools.partial(adjoint_kernel, pieces),
        out_shape=jax.ShapeDtypeStruct((channels, lag_dev), F32),
        in_specs=[VMEM] * (2 * len(parts)),
        out_specs=VMEM,
        compiler_params=params(16),
        cost_estimate=SMALL,
        name="adjoint",
    )(*[src_ids[p[0]] for p in pieces], *parts)


def shards(spectra, window_keep, owners, pair_src, pair_rec, pair_count, observed):
    columns, cores, places = lax.axis_size("win"), lax.axis_size("freq"), lax.axis_size("recv")
    column, core, place = lax.axis_index("win"), lax.axis_index("freq"), lax.axis_index("recv")
    assert spectra.shape[0] == 1 and cores == 2
    channels, bins_dev = spectra.shape[2:]
    blocks, slots, lag_dev = observed.shape
    lag_total = lag_dev * columns * cores
    bin_total = bins_dev * cores
    period = 2 * bin_total
    part = bins_dev // columns
    classes = part // LANES
    span = period // classes
    geometry = (classes, span, lag_total // span, lag_total // 2, period, 256)
    lag_scale = 1.0 / math.sqrt(bin_total * columns)
    peers = columns * cores
    some = slots // 2
    shifts = range(places)

    def cut(values, s):
        return lax.dynamic_slice(values, (0, 0, 0, (column ^ s) * part), (1, 2, channels, part))

    here, *held = [swapped(cut(spectra, s), "win", columns, s) for s in range(columns)]
    scal, wanted, rec_ids = index(
        window_keep, owners, pair_count, pair_src, pair_rec, places
    )
    if columns == 2:
        weight = jnp.ones((1,), F32)
    else:
        keeps = jnp.stack([swapped(window_keep[0], "win", columns, s) for s in range(columns)])
        ranked = jnp.argsort(-keeps)[: columns - 1].astype(jnp.int32)
        weight = keeps[ranked].astype(F32)
        scal = lax.dynamic_update_slice(scal, ranked, (ORDER,))

    direct = places == blocks
    src_ids = [swapped(wanted[d], "recv", places, d) for d in reversed(shifts)][::-1]
    trig = tables(classes, span, period, bins_dev, columns, cores)
    if direct and blocks == 4:
        chunks = [
            [(0, 0, slots), (1, 0, slots)],
            [(2, 0, slots)],
            [(3, 0, slots)],
        ]
    else:
        chunks = [[(d, first, some) for d in range(blocks)] for first in (0, some)]
    if direct:
        messages = [piece for pieces in chunks for piece in pieces]
    else:
        messages = [(d, 0, slots) for d in shifts]
    sent, kept = gather_rows(scal, here, held, make_perm(part), src_ids, messages)
    own_rows, table = gather_own(scal, kept, rec_ids, trig, classes, span, peers)
    arrived = [swapped(x, "recv", places, m[0]) for m, x in reversed(list(zip(messages, sent)))][::-1]
    if not direct:
        stacked = jnp.stack(arrived)
        whole_rows = [
            lax.dynamic_index_in_dim(stacked, place ^ owners[b], 0, False) for b in range(blocks)
        ]
        arrived = [whole_rows[piece[0]] for pieces in chunks for piece in pieces]
    corrs, all_sums, returned, returned_pieces = [], [], [], []
    after = []
    for q, pieces in enumerate(chunks):
        rows, arrived = arrived[: len(pieces)], arrived[len(pieces) :]
        lhs = cross_rows(
            weight, after[:1], rows, own_rows, pieces, classes, LARGE if q != 1 else SMALL
        )
        groups = sum(p[2] for p in pieces) // (32 if q else 16)
        keep, *sends = lag_parts(
            scal, [], lhs, table, geometry, columns, lag_dev, groups, SMALL if q else LARGE
        )
        sends = [swapped(x, "freq", cores, 1) for x in sends]
        own, *sends = add_cores(scal, after[1:], keep, sends)
        more = [swapped(x, "win", columns, s + 1) for s, x in enumerate(sends)]
        after = [own, *more] if q == 0 else []
        corr, sums = lag_stats(scal, lag_scale, q, pieces, all_sums, own, more, observed)
        corrs.append(corr)
        all_sums = [sums]
    sums = [swapped(sums, ("win", "freq"), peers, s) for s in reversed(range(peers))]
    after = []
    numbered = list(enumerate(chunks))
    for group in (numbered[:0:-1], numbered[:1]):
        grads = gradients(scal, lag_total, group, after, sums, [corrs[q] for q, _ in group], observed)
        pieces = [p for _, some_pieces in group for p in some_pieces]
        after = [grads[0]]
        if not direct:
            stacked = jnp.stack(list(grads) + [jnp.zeros_like(grads[0])])
            grads = []
            for d in shifts:
                block = jnp.int32(blocks)
                for b in range(blocks):
                    block = jnp.where(owners[b] == place ^ d, b, block)
                grads.append(lax.dynamic_index_in_dim(stacked, block, 0, False))
            pieces = [(d, pieces[0][1], some) for d in shifts]
        sent = [swapped(g, "recv", places, p[0]) for p, g in reversed(list(zip(pieces, grads)))]
        returned += sent[::-1]
        returned_pieces += pieces
    normed = normed_rows(scal, lag_total, chunks, sums, corrs, observed)
    adjoint = adjoint_rows(src_ids, returned_pieces, returned, channels)
    return (normed, adjoint)


def solution(mesh):
    return jax.shard_map(
        shards,
        mesh=mesh,
        in_specs=(
            P("win", None, ("groups", "recv"), "freq"),
            P(("groups", "win")),
            P("groups"),
            P(None, ("groups", "recv")),
            P(None, ("groups", "recv")),
            P(None, ("groups", "recv")),
            P(None, ("groups", "recv"), ("win", "freq")),
        ),
        out_specs=(
            P(None, ("groups", "recv"), ("win", "freq")),
            P(("groups", "recv"), ("win", "freq")),
        ),
        check_vma=False,
    )
```

```python
import functools
import math

import jax
import jax.numpy as jnp
import ml_dtypes
import numpy as np
from jax import lax
from jax.experimental import pallas as pl
from jax.experimental.pallas import tpu as pltpu
from jax.sharding import PartitionSpec as P

EPSILON = 1e-06
MIB = 1 << 20
LANES = 128
CORE, COLUMN, ORDER, BLOCK, COUNT = 0, 1, 2, 8, 16
BF16 = jnp.bfloat16
F32 = jnp.float32
VMEM = pl.BlockSpec(memory_space=pltpu.VMEM)
SMEM = pl.BlockSpec(memory_space=pltpu.SMEM)
HBM = pl.BlockSpec(memory_space=pltpu.HBM)
ANY = pl.BlockSpec(memory_space=pl.ANY)


def swapped(value, axis, size, step):
    assert size & (size - 1) == 0
    if step == 0:
        return value
    return lax.ppermute(value, axis, [(i, i ^ step) for i in range(size)])


def params(mib):
    return pltpu.CompilerParams(vmem_limit_bytes=mib * MIB)


SMALL = pl.CostEstimate(flops=1, bytes_accessed=1, transcendentals=0)
LARGE = pl.CostEstimate(flops=2 * 10**10, bytes_accessed=MIB, transcendentals=0)


def tables(classes, span, period, bins_dev, columns, cores):
    u = np.arange(span, dtype=np.int64)[None, :]
    piece = np.arange(columns * cores, dtype=np.int64)[:, None]
    first = piece % cores * bins_dev + piece // cores * (bins_dev // columns)
    rows = (first + np.arange(classes)).reshape(-1)
    high = 16 * classes * np.arange(LANES // 16, dtype=np.int64)
    low = classes * np.arange(16, dtype=np.int64)
    angle = (np.concatenate([rows, high, low])[:, None] * u % period) * (2.0 * math.pi / period)
    return np.stack([np.cos(angle), np.sin(angle)]).astype(np.float32)


def fetch(pairs, sems):
    copies = [pltpu.make_async_copy(a, b, sems.at[i]) for i, (a, b) in enumerate(pairs)]
    for c in copies:
        c.start()
    for c in copies:
        c.wait()


def index_kernel(blocks, direct, *refs):
    given, refs = refs[:5], refs[5:]
    scal, wanted, rec_ids, held, sems = refs[0], refs[1:-7], refs[-7], refs[-6:-1], refs[-1]
    fetch(zip(given, held), sems)
    window_keep, owners, pair_count, src, rec = held
    place = lax.axis_index("recv")
    column, columns = lax.axis_index("win"), lax.axis_size("win")
    core = lax.axis_index("freq")
    scal[CORE] = core
    scal[COLUMN] = column
    scal[ORDER] = 1 - window_keep[0]
    for b in range(blocks):
        unit = place ^ owners[b] if direct else b
        scal[BLOCK + unit] = b
        scal[COUNT + unit] = pair_count[b]
    for d, out in enumerate(wanted):
        chosen = jnp.full(out.shape, -1, jnp.int32)
        received = jnp.zeros(out.shape, jnp.int32)
        for b in range(blocks):
            mine = jnp.full(out.shape, owners[b], jnp.int32) == (place ^ d)
            chosen = jnp.where(mine, src[b : b + 1], chosen)
            received = jnp.where(mine, rec[b : b + 1], received)
        out[...] = chosen
        if direct:
            rec_ids[d : d + 1] = received
    if not direct:
        rec_ids[...] = rec[...]


def index(window_keep, owners, pair_count, pair_src, pair_rec, places):
    blocks, slots = pair_src.shape
    ids = jax.ShapeDtypeStruct((1, slots), jnp.int32)
    given = [window_keep, owners, pair_count[:, 0], pair_src, pair_rec]
    scal, *wanted, rec_ids = pl.pallas_call(
        functools.partial(index_kernel, blocks, places == blocks),
        out_shape=[jax.ShapeDtypeStruct((LANES,), jnp.int32)]
        + [ids] * places
        + [jax.ShapeDtypeStruct(pair_rec.shape, jnp.int32)],
        in_specs=[HBM] * 5,
        out_specs=[SMEM] + [VMEM] * (places + 1),
        scratch_shapes=[pltpu.SMEM(g.shape, g.dtype) for g in given[:3]]
        + [pltpu.VMEM(g.shape, g.dtype) for g in given[3:]]
        + [pltpu.SemaphoreType.DMA((5,))],
        compiler_params=params(16),
        cost_estimate=SMALL,
        name="index",
    )(*given)
    return scal, wanted, rec_ids


def table_kernel(classes, parts, scal, trig, table, base):
    rows = parts * classes
    low = slice(rows + LANES // 16, rows + LANES // 16 + 16)
    cl, sl = trig[0, low], trig[1, low]
    for h in range(LANES // 16):
        ch, sh = trig[0, rows + h : rows + h + 1], trig[1, rows + h : rows + h + 1]
        base[0, 16 * h : 16 * h + 16] = ch * cl - sh * sl
        base[1, 16 * h : 16 * h + 16] = sh * cl + ch * sl
    first = (scal[CORE] + 2 * scal[COLUMN]) * classes
    cb, sb = base[0], base[1]
    for r in range(classes):
        ca, sa = trig[0, pl.ds(first + r, 1)], trig[1, pl.ds(first + r, 1)]
        table[r, :LANES] = (ca * cb - sa * sb).astype(BF16)
        table[r, LANES:] = (-(sa * cb + ca * sb)).astype(BF16)


def perm_kernel(perm):
    part = perm.shape[0]
    classes = part // LANES
    source = lax.broadcasted_iota(jnp.int32, (part, LANES), 0)
    target = classes * lax.broadcasted_iota(jnp.int32, (part, LANES), 1)
    for r in range(classes):
        perm[:, r * LANES : (r + 1) * LANES] = (source == target + r).astype(BF16)


def make_perm(part):
    return pl.pallas_call(
        perm_kernel,
        out_shape=jax.ShapeDtypeStruct((part, part), BF16),
        out_specs=VMEM,
        compiler_params=params(8),
        cost_estimate=SMALL,
        name="perm",
    )()


def picks(ids, channels):
    row = jnp.concatenate([i[...] for i in ids], axis=1)
    return (lax.broadcasted_iota(jnp.int32, (channels, row.shape[1]), 0) == row).astype(BF16)


def rows_kernel(used, sends, messages, scal, here, *refs):
    held, perm, src_ids, refs = refs[:used], refs[used], refs[used + 1 : used + 1 + sends], refs[used + 1 + sends :]
    outs, kept = refs[:-1], refs[-1]
    _, _, channels, part = kept.shape
    slots = src_ids[0].shape[1]
    pick = picks(src_ids[::-1], channels)
    for u in range(used):
        x = here[0].reshape(2 * channels, part)
        for s in range(used):
            x = jnp.where(scal[ORDER + u] == s + 1, held[s][0].reshape(2 * channels, part), x)
        x = jnp.dot(x, perm[...], preferred_element_type=F32).astype(BF16)
        for half in range(2):
            z = x[half * channels : (half + 1) * channels]
            kept[u, half] = z
            y = lax.dot_general(
                pick, z, (((0,), (0,)), ((), ())), preferred_element_type=F32
            ).astype(BF16)
            for (d, first, count), out in zip(messages, outs):
                at = d * slots + first
                out[u, half] = y[at : at + count]


def gather_rows(scal, here, held, perm, src_ids, messages):
    used = len(held)
    channels, part = held[0].shape[-2:]
    *sent, kept = pl.pallas_call(
        functools.partial(rows_kernel, used, len(src_ids), messages),
        out_shape=[jax.ShapeDtypeStruct((used, 2, m[2], part), BF16) for m in messages]
        + [jax.ShapeDtypeStruct((used, 2, channels, part), BF16)],
        in_specs=[SMEM] + [VMEM] * (used + 2 + len(src_ids)),
        out_specs=[VMEM] * (len(messages) + 1),
        compiler_params=params(16),
        cost_estimate=SMALL,
        name="rows",
    )(scal, here, *held, perm, *src_ids[::-1])
    return sent, kept


def own_kernel(classes, parts, scal, kept, rec_ids, trig, own, table, base):
    units, used, _, slots, _ = own.shape
    pick = picks([rec_ids.at[d : d + 1] for d in range(units)], kept.shape[2])
    for u in range(used):
        for half in range(2):
            y = lax.dot_general(
                pick, kept[u, half], (((0,), (0,)), ((), ())), preferred_element_type=F32
            ).astype(BF16)
            for d in range(units):
                own[d, u, half] = y[d * slots : (d + 1) * slots]
    table_kernel(classes, parts, scal, trig, table, base)


def gather_own(scal, kept, rec_ids, trig, classes, span, parts):
    used, _, _, part = kept.shape
    units, slots = rec_ids.shape
    return pl.pallas_call(
        functools.partial(own_kernel, classes, parts),
        out_shape=[
            jax.ShapeDtypeStruct((units, used, 2, slots, part), BF16),
            jax.ShapeDtypeStruct((classes, 2 * LANES, span), BF16),
        ],
        in_specs=[SMEM] + [VMEM] * 3,
        out_specs=[VMEM] * 2,
        scratch_shapes=[pltpu.VMEM((2, LANES, span), F32)],
        compiler_params=params(16),
        cost_estimate=SMALL,
        name="own",
    )(scal, kept, rec_ids, jnp.asarray(trig))


def combine(values, classes, outputs, origin, span, period):
    plain, scaled = [None] * outputs, [None] * outputs

    def add(into, k, value, sign):
        if into[k] is None:
            into[k] = value if sign > 0 else -value
        else:
            into[k] = into[k] + value if sign > 0 else into[k] - value

    for r, (real, imag) in enumerate(values):
        both = None
        for k in range(outputs):
            eighths = r * (span * k - origin) * 8 // period % 8
            assert r * (span * k - origin) * 8 % period == 0
            if eighths % 2 == 0:
                value, sign = ((real, 1), (imag, -1), (real, -1), (imag, 1))[eighths // 2]
                add(plain, k, value, sign)
            else:
                if both is None:
                    both = real + imag, real - imag
                value, sign = ((both[1], 1), (both[0], -1), (both[1], -1), (both[0], 1))[eighths // 2]
                add(scaled, k, value, sign)
    root = math.sqrt(0.5)
    return [a if b is None else a + root * b for a, b in zip(plain, scaled)]


def placed(pieces):
    at = 0
    for unit, first, count in pieces:
        yield unit, first, count, slice(at, at + count)
        at += count


def cross_kernel(pieces, skip, weight, *refs):
    refs = refs[skip:]
    s_refs, own, lhs = refs[:-2], refs[-2], refs[-1]
    used = own.shape[1]
    rows = lhs.shape[1] // 2
    for s_ref, (unit, first, count, at) in zip(s_refs, placed(pieces)):
        turned = slice(rows + at.start, rows + at.stop)
        mine = slice(first, first + count)
        sent = mine if s_ref.shape[2] > count else slice(0, count)
        for r in range(lhs.shape[0]):
            bins = slice(r * LANES, (r + 1) * LANES)
            real = imag = None
            for u in range(used):
                sr, si = (s_ref[u, half, sent, bins].astype(F32) for half in range(2))
                rr, ri = (own[unit, u, half, mine, bins].astype(F32) for half in range(2))
                re, im = sr * rr + si * ri, si * rr - sr * ri
                if u:
                    re, im = real + weight[u] * re, imag + weight[u] * im
                real, imag = re, im
            lhs[r, at, :LANES] = real.astype(BF16)
            lhs[r, at, LANES:] = imag.astype(BF16)
            lhs[r, turned, :LANES] = imag.astype(BF16)
            lhs[r, turned, LANES:] = (-real).astype(BF16)


def cross_rows(weight, after, rows, own, pieces, classes, effort):
    count = sum(p[2] for p in pieces)
    return pl.pallas_call(
        functools.partial(cross_kernel, pieces, len(after)),
        out_shape=jax.ShapeDtypeStruct((classes, 2 * count, 2 * LANES), BF16),
        in_specs=[SMEM] + [ANY] * len(after) + [VMEM] * (len(rows) + 1),
        out_specs=VMEM,
        compiler_params=params(8),
        cost_estimate=effort,
        name="cross",
    )(weight, *after, *rows, own)


def lags_kernel(geometry, split, skip, scal, *refs):
    classes, span, outputs, origin, period, chunk = geometry
    lhs, table, keep, *refs = refs[skip:]
    sends, sums = refs[:split], refs[split:]
    rows = lhs.shape[1] // 2
    lag_dev = keep.shape[-1]
    cores = 2
    at_once = span == lag_dev
    first = scal[CORE] == 0
    for start in range(0, span, chunk):
        values = []
        for r in range(classes):
            whole_turns = all(
                r * (span * k - origin) * 2 % period == 0 for k in range(outputs)
            )
            left = lhs[r, :rows] if whole_turns else lhs[r]
            y = jnp.dot(left, table[r, :, start : start + chunk], preferred_element_type=F32)
            values.append((y[:rows], None if whole_turns else y[rows:]))
        corr = combine(values, classes, outputs, origin, span, period)
        lags = slice(start, start + chunk)
        for column in range(keep.shape[0]) if at_once else ():
            even, odd = corr[2 * column], corr[2 * column + 1]
            keep[column, :, lags] = jnp.where(first, even, odd)
            other = jnp.where(first, odd, even).astype(BF16)
            for i, out in enumerate(sends):
                out[column, :, lags] = other[i * out.shape[1] : (i + 1) * out.shape[1]]
        for k, value in enumerate(corr) if not at_once else ():
            lag = span * k + start
            sums[0][lag // lag_dev, :, lag % lag_dev : lag % lag_dev + chunk] = value
    if at_once:
        return
    for column in range(keep.shape[0]):
        keep[column] = sums[0][cores * column + scal[CORE]]
        for i, out in enumerate(sends):
            at = slice(i * out.shape[1], (i + 1) * out.shape[1])
            out[column] = sums[0][cores * column + 1 - scal[CORE], at].astype(BF16)


def lag_parts(scal, after, lhs, table, geometry, columns, lag_dev, split, effort):
    rows = lhs.shape[1] // 2
    shape = lambda count: (columns, count, lag_dev)
    return pl.pallas_call(
        functools.partial(lags_kernel, geometry, split, len(after)),
        out_shape=[jax.ShapeDtypeStruct(shape(rows), F32)]
        + [jax.ShapeDtypeStruct(shape(rows // split), BF16)] * split,
        in_specs=[SMEM] + [ANY] * len(after) + [VMEM] * 2,
        out_specs=[VMEM] * (split + 1),
        scratch_shapes=[pltpu.VMEM((2 * columns, rows, lag_dev), F32)] * (geometry[1] != lag_dev),
        compiler_params=params(16),
        cost_estimate=effort,
        name="lags",
    )(scal, *after, lhs, table)


def cross_lags_kernel(geometry, split, skip, pieces, scal, weight, *refs):
    count = len(pieces) + 1
    rows, table, refs = refs[skip : skip + count], refs[skip + count], refs[skip + count + 1 :]
    outs, lhs, sums = refs[: split + 1], refs[split + 1], refs[split + 2 :]
    cross_kernel(pieces, 0, weight, *rows, lhs)
    lags_kernel(geometry, split, 0, scal, lhs, table, *outs, *sums)


def cross_lag_parts(
    scal, weight, after, rows, own, pieces, table, geometry, columns, lag_dev, split, effort
):
    classes, span = geometry[:2]
    count = sum(p[2] for p in pieces)
    shape = lambda rows: (columns, rows, lag_dev)
    return pl.pallas_call(
        functools.partial(cross_lags_kernel, geometry, split, len(after), pieces),
        out_shape=[jax.ShapeDtypeStruct(shape(count), F32)]
        + [jax.ShapeDtypeStruct(shape(count // split), BF16)] * split,
        in_specs=[SMEM] * 2 + [ANY] * len(after) + [VMEM] * (len(rows) + 2),
        out_specs=[VMEM] * (split + 1),
        scratch_shapes=[pltpu.VMEM((classes, 2 * count, 2 * LANES), BF16)]
        + [pltpu.VMEM((2 * columns, count, lag_dev), F32)] * (span != lag_dev),
        compiler_params=params(16),
        cost_estimate=effort,
        name="cross_lags",
    )(scal, weight, *after, *rows, own, table)


def cores_kernel(skip, split, scal, *refs):
    keep, *refs = refs[skip:]
    more, own, sends = refs[:split], refs[split], refs[split + 1 :]
    columns = keep.shape[0]
    for i, m in enumerate(more):
        at = slice(i * m.shape[1], (i + 1) * m.shape[1])
        for column in range(columns):
            value = keep[column, at] + m[column].astype(F32)

            @pl.when(scal[COLUMN] == column)
            def _():
                own[at] = value

            for s, out in enumerate(sends):

                @pl.when(scal[COLUMN] ^ (s + 1) == column)
                def _():
                    out[at] = value.astype(BF16)


def add_cores(scal, after, keep, more):
    columns, rows, lag_dev = keep.shape
    return pl.pallas_call(
        functools.partial(cores_kernel, len(after), len(more)),
        out_shape=[jax.ShapeDtypeStruct((rows, lag_dev), F32)]
        + [jax.ShapeDtypeStruct((rows, lag_dev), BF16)] * (columns - 1),
        in_specs=[SMEM] + [ANY] * len(after) + [VMEM] * (1 + len(more)),
        out_specs=[VMEM] * columns,
        compiler_params=params(8),
        cost_estimate=SMALL,
        name="cores",
    )(scal, *after, keep, *more)


def stats_kernel(scale, q, pieces, others, scal, *refs):
    count = min(q, 1)
    earlier, (own, *refs) = refs[:count], refs[count:]
    more, refs = refs[:others], refs[others:]
    targets, (corr, sums) = refs[: len(pieces)], refs[len(pieces) :]
    columns = []
    for target, (unit, first, count, at) in zip(targets, placed(pieces)):
        value = own[at]
        for m in more:
            value = value + m[at].astype(F32)
        slot = first + lax.broadcasted_iota(jnp.int32, (count, 1), 0)
        value = value * jnp.where(slot < scal[COUNT + unit], scale, 0.0)
        corr[at] = value
        square = jnp.sum(value * value, axis=1, keepdims=True)
        product = jnp.sum(value * target[0], axis=1, keepdims=True)
        lane = lax.broadcasted_iota(jnp.int32, (count, LANES), 1)
        columns.append(jnp.where(lane == 2 * q, square, jnp.where(lane == 2 * q + 1, product, 0.0)))
    spare = sums.shape[1] - own.shape[0]
    if spare:
        columns.append(jnp.zeros((spare, LANES), F32))
    total = jnp.concatenate(columns, axis=0).T[:8]
    for e in earlier:
        total = total + e[...]
    sums[...] = total


def target_specs(pieces, lag_dev):
    return [
        pl.BlockSpec(
            (1, count, lag_dev),
            lambda i, scal, unit=unit, block=first // count: (scal[BLOCK + unit], block, 0),
        )
        for unit, first, count in pieces
    ]


def whole(shape):
    return pl.BlockSpec(shape, lambda i, scal: (0,) * len(shape))


def lag_stats(scal, scale, q, pieces, earlier, own, more, observed):
    rows, lag_dev = own.shape
    outs = [jax.ShapeDtypeStruct((rows, lag_dev), F32), jax.ShapeDtypeStruct((8, -(-rows // LANES) * LANES), F32)]
    return pl.pallas_call(
        functools.partial(stats_kernel, scale, q, pieces, len(more)),
        grid_spec=pltpu.PrefetchScalarGridSpec(
            num_scalar_prefetch=1,
            grid=(1,),
            in_specs=[whole(e.shape) for e in earlier]
            + [whole(own.shape)] * (1 + len(more))
            + target_specs(pieces, lag_dev),
            out_specs=[whole(o.shape) for o in outs],
        ),
        out_shape=outs,
        compiler_params=params(16),
        cost_estimate=SMALL,
        name="stats",
    )(scal, *earlier, own, *more, *[observed] * len(pieces))


def slot_scales(sums, lag_total, q):
    total = sums[0][...]
    for s in sums[1:]:
        total = total + s[...]
    rows = total.shape[1]
    square, product = total[2 * q : 2 * q + 1], total[2 * q + 1 : 2 * q + 2]
    inverse = 1.0 / jnp.sqrt(square / lag_total + EPSILON)
    bending = (square * inverse * inverse - product * inverse) / lag_total
    sub = lax.broadcasted_iota(jnp.int32, (LANES, rows), 0)
    both = jnp.where(sub == 0, inverse, jnp.where(sub == 1, bending, 0.0)).T
    return both[:, 0:1], both[:, 1:2]


def gradient_kernel(lag_total, chunks, parts, skip, scal, *refs):
    sums, refs = refs[skip : skip + parts], refs[skip + parts :]
    corrs, refs = refs[: len(chunks)], refs[len(chunks) :]
    targets, outs = refs[: len(refs) // 2], refs[len(refs) // 2 :]
    i = 0
    for corr, (q, pieces) in zip(corrs, chunks):
        inverse, bending = slot_scales(sums, lag_total, q)
        for unit, first, count, at in placed(pieces):
            slot = first + lax.broadcasted_iota(jnp.int32, (count, 1), 0)
            valid = jnp.where(slot < scal[COUNT + unit], inverse[at], 0.0)
            normed = corr[at] * inverse[at]
            outs[i][...] = ((normed - targets[i][0] - normed * bending[at]) * valid).astype(BF16)
            i += 1


def gradients(scal, lag_total, chunks, after, sums, corrs, observed):
    lag_dev = observed.shape[2]
    pieces = [p for _, some in chunks for p in some]
    outs = [jax.ShapeDtypeStruct((p[2], lag_dev), BF16) for p in pieces]
    return pl.pallas_call(
        functools.partial(gradient_kernel, lag_total, chunks, len(sums), len(after)),
        grid_spec=pltpu.PrefetchScalarGridSpec(
            num_scalar_prefetch=1,
            grid=(1,),
            in_specs=[ANY] * len(after)
            + [whole(x.shape) for x in (*sums, *corrs)]
            + target_specs(pieces, lag_dev),
            out_specs=[whole(o.shape) for o in outs],
        ),
        out_shape=outs,
        compiler_params=params(16),
        cost_estimate=SMALL,
        name="gradient",
    )(scal, *after, *sums, *corrs, *[observed] * len(pieces))


def normed_kernel(lag_total, chunks, parts, scal, *refs):
    sums, corrs, out = refs[:parts], refs[parts:-1], refs[-1]
    for q, (pieces, corr) in enumerate(zip(chunks, corrs)):
        inverse, _ = slot_scales(sums, lag_total, q)
        for unit, first, count, at in placed(pieces):

            @pl.when(pl.program_id(0) == unit)
            def _():
                out[0, first : first + count] = corr[at] * inverse[at]


def normed_rows(scal, lag_total, chunks, sums, corrs, observed):
    blocks, slots, lag_dev = observed.shape
    ins = [*sums, *corrs]
    return pl.pallas_call(
        functools.partial(normed_kernel, lag_total, chunks, len(sums)),
        grid_spec=pltpu.PrefetchScalarGridSpec(
            num_scalar_prefetch=1,
            grid=(blocks,),
            in_specs=[whole(x.shape) for x in ins],
            out_specs=pl.BlockSpec((1, slots, lag_dev), lambda i, scal: (scal[BLOCK + i], 0, 0)),
        ),
        out_shape=jax.ShapeDtypeStruct(observed.shape, F32),
        compiler_params=params(16),
        cost_estimate=SMALL,
        name="normed",
    )(scal, *ins)


def adjoint_kernel(pieces, *refs):
    ids, parts, out = refs[: len(pieces)], refs[len(pieces) : -1], refs[-1]
    pick = picks([i.at[:, p[1] : p[1] + p[2]] for i, p in zip(ids, pieces)], out.shape[0])
    rows = jnp.concatenate([p[...] for p in parts], axis=0)
    out[...] = jnp.dot(pick, rows, preferred_element_type=F32)


def adjoint_rows(src_ids, pieces, parts, channels):
    lag_dev = parts[0].shape[1]
    return pl.pallas_call(
        functools.partial(adjoint_kernel, pieces),
        out_shape=jax.ShapeDtypeStruct((channels, lag_dev), F32),
        in_specs=[VMEM] * (2 * len(parts)),
        out_specs=VMEM,
        compiler_params=params(16),
        cost_estimate=SMALL,
        name="adjoint",
    )(*[src_ids[p[0]] for p in pieces], *parts)


def shards(spectra, window_keep, owners, pair_src, pair_rec, pair_count, observed):
    columns, cores, places = lax.axis_size("win"), lax.axis_size("freq"), lax.axis_size("recv")
    column, core, place = lax.axis_index("win"), lax.axis_index("freq"), lax.axis_index("recv")
    assert spectra.shape[0] == 1 and cores == 2
    channels, bins_dev = spectra.shape[2:]
    blocks, slots, lag_dev = observed.shape
    lag_total = lag_dev * columns * cores
    bin_total = bins_dev * cores
    period = 2 * bin_total
    part = bins_dev // columns
    classes = part // LANES
    span = period // classes
    geometry = (classes, span, lag_total // span, lag_total // 2, period, 256)
    lag_scale = 1.0 / math.sqrt(bin_total * columns)
    peers = columns * cores
    some = slots // 2
    shifts = range(places)

    def cut(values, s):
        return lax.dynamic_slice(values, (0, 0, 0, (column ^ s) * part), (1, 2, channels, part))

    here, *held = [swapped(cut(spectra, s), "win", columns, s) for s in range(columns)]
    scal, wanted, rec_ids = index(
        window_keep, owners, pair_count, pair_src, pair_rec, places
    )
    if columns == 2:
        weight = jnp.ones((1,), F32)
    else:
        keeps = jnp.stack([swapped(window_keep[0], "win", columns, s) for s in range(columns)])
        ranked = jnp.argsort(-keeps)[: columns - 1].astype(jnp.int32)
        weight = keeps[ranked].astype(F32)
        scal = lax.dynamic_update_slice(scal, ranked, (ORDER,))

    direct = places == blocks
    src_ids = [swapped(wanted[d], "recv", places, d) for d in reversed(shifts)][::-1]
    trig = tables(classes, span, period, bins_dev, columns, cores)
    if direct and blocks == 4:
        chunks = [
            [(0, 0, slots), (1, 0, slots)],
            [(2, 0, slots)],
            [(3, 0, slots)],
        ]
    else:
        chunks = [[(d, first, some) for d in range(blocks)] for first in (0, some)]
    if direct:
        messages = [piece for pieces in chunks for piece in pieces]
    else:
        messages = [(d, 0, slots) for d in shifts]
    sent, kept = gather_rows(scal, here, held, make_perm(part), src_ids, messages)
    own_rows, table = gather_own(scal, kept, rec_ids, trig, classes, span, peers)
    arrived = [swapped(x, "recv", places, m[0]) for m, x in reversed(list(zip(messages, sent)))][::-1]
    if not direct:
        stacked = jnp.stack(arrived)
        whole_rows = [
            lax.dynamic_index_in_dim(stacked, place ^ owners[b], 0, False) for b in range(blocks)
        ]
        arrived = [whole_rows[piece[0]] for pieces in chunks for piece in pieces]
    corrs, all_sums, returned, returned_pieces = [], [], [], []
    after = []
    for q, pieces in enumerate(chunks):
        rows, arrived = arrived[: len(pieces)], arrived[len(pieces) :]
        groups = sum(p[2] for p in pieces) // (32 if q else 16)
        if q:
            keep, *sends = cross_lag_parts(
                scal,
                weight,
                after[:1],
                rows,
                own_rows,
                pieces,
                table,
                geometry,
                columns,
                lag_dev,
                groups,
                SMALL if q == 1 else LARGE,
            )
        else:
            lhs = cross_rows(weight, [], rows, own_rows, pieces, classes, LARGE)
            keep, *sends = lag_parts(
                scal, [], lhs, table, geometry, columns, lag_dev, groups, LARGE
            )
        sends = [swapped(x, "freq", cores, 1) for x in sends]
        own, *sends = add_cores(scal, after[1:], keep, sends)
        more = [swapped(x, "win", columns, s + 1) for s, x in enumerate(sends)]
        after = [own, *more] if q == 0 else []
        corr, sums = lag_stats(scal, lag_scale, q, pieces, all_sums, own, more, observed)
        corrs.append(corr)
        all_sums = [sums]
    sums = [swapped(sums, ("win", "freq"), peers, s) for s in reversed(range(peers))]
    after = []
    numbered = list(enumerate(chunks))
    for group in (numbered[:0:-1], numbered[:1]):
        grads = gradients(scal, lag_total, group, after, sums, [corrs[q] for q, _ in group], observed)
        pieces = [p for _, some_pieces in group for p in some_pieces]
        after = [grads[0]]
        if not direct:
            stacked = jnp.stack(list(grads) + [jnp.zeros_like(grads[0])])
            grads = []
            for d in shifts:
                block = jnp.int32(blocks)
                for b in range(blocks):
                    block = jnp.where(owners[b] == place ^ d, b, block)
                grads.append(lax.dynamic_index_in_dim(stacked, block, 0, False))
            pieces = [(d, pieces[0][1], some) for d in shifts]
        sent = [swapped(g, "recv", places, p[0]) for p, g in reversed(list(zip(pieces, grads)))]
        returned += sent[::-1]
        returned_pieces += pieces
    normed = normed_rows(scal, lag_total, chunks, sums, corrs, observed)
    adjoint = adjoint_rows(src_ids, returned_pieces, returned, channels)
    return (normed, adjoint)


def solution(mesh):
    return jax.shard_map(
        shards,
        mesh=mesh,
        in_specs=(
            P("win", None, ("groups", "recv"), "freq"),
            P(("groups", "win")),
            P("groups"),
            P(None, ("groups", "recv")),
            P(None, ("groups", "recv")),
            P(None, ("groups", "recv")),
            P(None, ("groups", "recv"), ("win", "freq")),
        ),
        out_specs=(
            P(None, ("groups", "recv"), ("win", "freq")),
            P(("groups", "recv"), ("win", "freq")),
        ),
        check_vma=False,
    )
```

```python
import functools
import math

import jax
import jax.numpy as jnp
import ml_dtypes
import numpy as np
from jax import lax
from jax.experimental import pallas as pl
from jax.experimental.pallas import tpu as pltpu
from jax.sharding import PartitionSpec as P

EPSILON = 1e-06
MIB = 1 << 20
LANES = 128
CORE, COLUMN, ORDER, BLOCK, COUNT = 0, 1, 2, 8, 16
BF16 = jnp.bfloat16
F32 = jnp.float32
VMEM = pl.BlockSpec(memory_space=pltpu.VMEM)
SMEM = pl.BlockSpec(memory_space=pltpu.SMEM)
HBM = pl.BlockSpec(memory_space=pltpu.HBM)
ANY = pl.BlockSpec(memory_space=pl.ANY)


def swapped(value, axis, size, step):
    assert size & (size - 1) == 0
    if step == 0:
        return value
    return lax.ppermute(value, axis, [(i, i ^ step) for i in range(size)])


def params(mib):
    return pltpu.CompilerParams(vmem_limit_bytes=mib * MIB)


SMALL = pl.CostEstimate(flops=1, bytes_accessed=1, transcendentals=0)
LARGE = pl.CostEstimate(flops=2 * 10**10, bytes_accessed=MIB, transcendentals=0)


def tables(classes, span, period, bins_dev, columns, cores):
    u = np.arange(span, dtype=np.int64)[None, :]
    piece = np.arange(columns * cores, dtype=np.int64)[:, None]
    first = piece % cores * bins_dev + piece // cores * (bins_dev // columns)
    rows = (first + np.arange(classes)).reshape(-1)
    high = 16 * classes * np.arange(LANES // 16, dtype=np.int64)
    low = classes * np.arange(16, dtype=np.int64)
    angle = (np.concatenate([rows, high, low])[:, None] * u % period) * (2.0 * math.pi / period)
    return np.stack([np.cos(angle), np.sin(angle)]).astype(np.float32)


def fetch(pairs, sems):
    copies = [pltpu.make_async_copy(a, b, sems.at[i]) for i, (a, b) in enumerate(pairs)]
    for c in copies:
        c.start()
    for c in copies:
        c.wait()


def index_kernel(blocks, direct, *refs):
    given, refs = refs[:5], refs[5:]
    scal, wanted, rec_ids, held, sems = refs[0], refs[1:-7], refs[-7], refs[-6:-1], refs[-1]
    fetch(zip(given, held), sems)
    window_keep, owners, pair_count, src, rec = held
    place = lax.axis_index("recv")
    column, columns = lax.axis_index("win"), lax.axis_size("win")
    core = lax.axis_index("freq")
    scal[CORE] = core
    scal[COLUMN] = column
    scal[ORDER] = 1 - window_keep[0]
    for b in range(blocks):
        unit = place ^ owners[b] if direct else b
        scal[BLOCK + unit] = b
        scal[COUNT + unit] = pair_count[b]
    for d, out in enumerate(wanted):
        chosen = jnp.full(out.shape, -1, jnp.int32)
        received = jnp.zeros(out.shape, jnp.int32)
        for b in range(blocks):
            mine = jnp.full(out.shape, owners[b], jnp.int32) == (place ^ d)
            chosen = jnp.where(mine, src[b : b + 1], chosen)
            received = jnp.where(mine, rec[b : b + 1], received)
        out[...] = chosen
        if direct:
            rec_ids[d : d + 1] = received
    if not direct:
        rec_ids[...] = rec[...]


def index(window_keep, owners, pair_count, pair_src, pair_rec, places):
    blocks, slots = pair_src.shape
    ids = jax.ShapeDtypeStruct((1, slots), jnp.int32)
    given = [window_keep, owners, pair_count[:, 0], pair_src, pair_rec]
    scal, *wanted, rec_ids = pl.pallas_call(
        functools.partial(index_kernel, blocks, places == blocks),
        out_shape=[jax.ShapeDtypeStruct((LANES,), jnp.int32)]
        + [ids] * places
        + [jax.ShapeDtypeStruct(pair_rec.shape, jnp.int32)],
        in_specs=[HBM] * 5,
        out_specs=[SMEM] + [VMEM] * (places + 1),
        scratch_shapes=[pltpu.SMEM(g.shape, g.dtype) for g in given[:3]]
        + [pltpu.VMEM(g.shape, g.dtype) for g in given[3:]]
        + [pltpu.SemaphoreType.DMA((5,))],
        compiler_params=params(16),
        cost_estimate=SMALL,
        name="index",
    )(*given)
    return scal, wanted, rec_ids


def table_kernel(classes, parts, scal, trig, table, base):
    rows = parts * classes
    low = slice(rows + LANES // 16, rows + LANES // 16 + 16)
    cl, sl = trig[0, low], trig[1, low]
    for h in range(LANES // 16):
        ch, sh = trig[0, rows + h : rows + h + 1], trig[1, rows + h : rows + h + 1]
        base[0, 16 * h : 16 * h + 16] = ch * cl - sh * sl
        base[1, 16 * h : 16 * h + 16] = sh * cl + ch * sl
    first = (scal[CORE] + 2 * scal[COLUMN]) * classes
    cb, sb = base[0], base[1]
    for r in range(classes):
        ca, sa = trig[0, pl.ds(first + r, 1)], trig[1, pl.ds(first + r, 1)]
        table[r, :LANES] = (ca * cb - sa * sb).astype(BF16)
        table[r, LANES:] = (-(sa * cb + ca * sb)).astype(BF16)


def perm_kernel(perm):
    part = perm.shape[0]
    classes = part // LANES
    source = lax.broadcasted_iota(jnp.int32, (part, LANES), 0)
    target = classes * lax.broadcasted_iota(jnp.int32, (part, LANES), 1)
    for r in range(classes):
        perm[:, r * LANES : (r + 1) * LANES] = (source == target + r).astype(BF16)


def make_perm(part):
    return pl.pallas_call(
        perm_kernel,
        out_shape=jax.ShapeDtypeStruct((part, part), BF16),
        out_specs=VMEM,
        compiler_params=params(8),
        cost_estimate=SMALL,
        name="perm",
    )()


def picks(ids, channels):
    row = jnp.concatenate([i[...] for i in ids], axis=1)
    return (lax.broadcasted_iota(jnp.int32, (channels, row.shape[1]), 0) == row).astype(BF16)


def rows_kernel(used, sends, messages, scal, here, *refs):
    held, perm, src_ids, refs = refs[:used], refs[used], refs[used + 1 : used + 1 + sends], refs[used + 1 + sends :]
    outs, kept = refs[:-1], refs[-1]
    _, _, channels, part = kept.shape
    slots = src_ids[0].shape[1]
    pick = picks(src_ids[::-1], channels)
    for u in range(used):
        x = here[0].reshape(2 * channels, part)
        for s in range(used):
            x = jnp.where(scal[ORDER + u] == s + 1, held[s][0].reshape(2 * channels, part), x)
        x = jnp.dot(x, perm[...], preferred_element_type=F32).astype(BF16)
        for half in range(2):
            z = x[half * channels : (half + 1) * channels]
            kept[u, half] = z
            y = lax.dot_general(
                pick, z, (((0,), (0,)), ((), ())), preferred_element_type=F32
            ).astype(BF16)
            for (d, first, count), out in zip(messages, outs):
                at = d * slots + first
                out[u, half] = y[at : at + count]


def gather_rows(scal, here, held, perm, src_ids, messages):
    used = len(held)
    channels, part = held[0].shape[-2:]
    *sent, kept = pl.pallas_call(
        functools.partial(rows_kernel, used, len(src_ids), messages),
        out_shape=[jax.ShapeDtypeStruct((used, 2, m[2], part), BF16) for m in messages]
        + [jax.ShapeDtypeStruct((used, 2, channels, part), BF16)],
        in_specs=[SMEM] + [VMEM] * (used + 2 + len(src_ids)),
        out_specs=[VMEM] * (len(messages) + 1),
        compiler_params=params(16),
        cost_estimate=SMALL,
        name="rows",
    )(scal, here, *held, perm, *src_ids[::-1])
    return sent, kept


def own_kernel(classes, parts, scal, kept, rec_ids, trig, own, table, base):
    units, used, _, slots, _ = own.shape
    pick = picks([rec_ids.at[d : d + 1] for d in range(units)], kept.shape[2])
    for u in range(used):
        for half in range(2):
            y = lax.dot_general(
                pick, kept[u, half], (((0,), (0,)), ((), ())), preferred_element_type=F32
            ).astype(BF16)
            for d in range(units):
                own[d, u, half] = y[d * slots : (d + 1) * slots]
    table_kernel(classes, parts, scal, trig, table, base)


def gather_own(scal, kept, rec_ids, trig, classes, span, parts):
    used, _, _, part = kept.shape
    units, slots = rec_ids.shape
    return pl.pallas_call(
        functools.partial(own_kernel, classes, parts),
        out_shape=[
            jax.ShapeDtypeStruct((units, used, 2, slots, part), BF16),
            jax.ShapeDtypeStruct((classes, 2 * LANES, span), BF16),
        ],
        in_specs=[SMEM] + [VMEM] * 3,
        out_specs=[VMEM] * 2,
        scratch_shapes=[pltpu.VMEM((2, LANES, span), F32)],
        compiler_params=params(16),
        cost_estimate=SMALL,
        name="own",
    )(scal, kept, rec_ids, jnp.asarray(trig))


def combine(values, classes, outputs, origin, span, period):
    plain, scaled = [None] * outputs, [None] * outputs

    def add(into, k, value, sign):
        if into[k] is None:
            into[k] = value if sign > 0 else -value
        else:
            into[k] = into[k] + value if sign > 0 else into[k] - value

    for r, (real, imag) in enumerate(values):
        both = None
        for k in range(outputs):
            eighths = r * (span * k - origin) * 8 // period % 8
            assert r * (span * k - origin) * 8 % period == 0
            if eighths % 2 == 0:
                value, sign = ((real, 1), (imag, -1), (real, -1), (imag, 1))[eighths // 2]
                add(plain, k, value, sign)
            else:
                if both is None:
                    both = real + imag, real - imag
                value, sign = ((both[1], 1), (both[0], -1), (both[1], -1), (both[0], 1))[eighths // 2]
                add(scaled, k, value, sign)
    root = math.sqrt(0.5)
    return [a if b is None else a + root * b for a, b in zip(plain, scaled)]


def placed(pieces):
    at = 0
    for unit, first, count in pieces:
        yield unit, first, count, slice(at, at + count)
        at += count


def cross_kernel(pieces, skip, weight, *refs):
    refs = refs[skip:]
    s_refs, own, lhs = refs[:-2], refs[-2], refs[-1]
    used = own.shape[1]
    rows = lhs.shape[1] // 2
    for s_ref, (unit, first, count, at) in zip(s_refs, placed(pieces)):
        turned = slice(rows + at.start, rows + at.stop)
        mine = slice(first, first + count)
        sent = mine if s_ref.shape[2] > count else slice(0, count)
        for r in range(lhs.shape[0]):
            bins = slice(r * LANES, (r + 1) * LANES)
            real = imag = None
            for u in range(used):
                sr, si = (s_ref[u, half, sent, bins].astype(F32) for half in range(2))
                rr, ri = (own[unit, u, half, mine, bins].astype(F32) for half in range(2))
                re, im = sr * rr + si * ri, si * rr - sr * ri
                if u:
                    re, im = real + weight[u] * re, imag + weight[u] * im
                real, imag = re, im
            lhs[r, at, :LANES] = real.astype(BF16)
            lhs[r, at, LANES:] = imag.astype(BF16)
            lhs[r, turned, :LANES] = imag.astype(BF16)
            lhs[r, turned, LANES:] = (-real).astype(BF16)


def cross_rows(weight, after, rows, own, pieces, classes, effort):
    count = sum(p[2] for p in pieces)
    return pl.pallas_call(
        functools.partial(cross_kernel, pieces, len(after)),
        out_shape=jax.ShapeDtypeStruct((classes, 2 * count, 2 * LANES), BF16),
        in_specs=[SMEM] + [ANY] * len(after) + [VMEM] * (len(rows) + 1),
        out_specs=VMEM,
        compiler_params=params(8),
        cost_estimate=effort,
        name="cross",
    )(weight, *after, *rows, own)


def lags_kernel(geometry, split, skip, scal, *refs):
    classes, span, outputs, origin, period, chunk = geometry
    lhs, table, keep, *refs = refs[skip:]
    sends, sums = refs[:split], refs[split:]
    rows = lhs.shape[1] // 2
    lag_dev = keep.shape[-1]
    cores = 2
    at_once = span == lag_dev
    first = scal[CORE] == 0
    for start in range(0, span, chunk):
        values = []
        for r in range(classes):
            whole_turns = all(
                r * (span * k - origin) * 2 % period == 0 for k in range(outputs)
            )
            left = lhs[r, :rows] if whole_turns else lhs[r]
            y = jnp.dot(left, table[r, :, start : start + chunk], preferred_element_type=F32)
            values.append((y[:rows], None if whole_turns else y[rows:]))
        corr = combine(values, classes, outputs, origin, span, period)
        lags = slice(start, start + chunk)
        for column in range(keep.shape[0]) if at_once else ():
            even, odd = corr[2 * column], corr[2 * column + 1]
            keep[column, :, lags] = jnp.where(first, even, odd)
            other = jnp.where(first, odd, even).astype(BF16)
            for i, out in enumerate(sends):
                out[column, :, lags] = other[i * out.shape[1] : (i + 1) * out.shape[1]]
        for k, value in enumerate(corr) if not at_once else ():
            lag = span * k + start
            sums[0][lag // lag_dev, :, lag % lag_dev : lag % lag_dev + chunk] = value
    if at_once:
        return
    for column in range(keep.shape[0]):
        keep[column] = sums[0][cores * column + scal[CORE]]
        for i, out in enumerate(sends):
            at = slice(i * out.shape[1], (i + 1) * out.shape[1])
            out[column] = sums[0][cores * column + 1 - scal[CORE], at].astype(BF16)


def lag_parts(scal, after, lhs, table, geometry, columns, lag_dev, split, effort):
    rows = lhs.shape[1] // 2
    shape = lambda count: (columns, count, lag_dev)
    return pl.pallas_call(
        functools.partial(lags_kernel, geometry, split, len(after)),
        out_shape=[jax.ShapeDtypeStruct(shape(rows), F32)]
        + [jax.ShapeDtypeStruct(shape(rows // split), BF16)] * split,
        in_specs=[SMEM] + [ANY] * len(after) + [VMEM] * 2,
        out_specs=[VMEM] * (split + 1),
        scratch_shapes=[pltpu.VMEM((2 * columns, rows, lag_dev), F32)] * (geometry[1] != lag_dev),
        compiler_params=params(16),
        cost_estimate=effort,
        name="lags",
    )(scal, *after, lhs, table)


def cross_lags_kernel(geometry, split, skip, pieces, scal, weight, *refs):
    count = len(pieces) + 1
    rows, table, refs = refs[skip : skip + count], refs[skip + count], refs[skip + count + 1 :]
    outs, lhs, sums = refs[: split + 1], refs[split + 1], refs[split + 2 :]
    cross_kernel(pieces, 0, weight, *rows, lhs)
    lags_kernel(geometry, split, 0, scal, lhs, table, *outs, *sums)


def cross_lag_parts(
    scal, weight, after, rows, own, pieces, table, geometry, columns, lag_dev, split, effort
):
    classes, span = geometry[:2]
    count = sum(p[2] for p in pieces)
    shape = lambda rows: (columns, rows, lag_dev)
    return pl.pallas_call(
        functools.partial(cross_lags_kernel, geometry, split, len(after), pieces),
        out_shape=[jax.ShapeDtypeStruct(shape(count), F32)]
        + [jax.ShapeDtypeStruct(shape(count // split), BF16)] * split,
        in_specs=[SMEM] * 2 + [ANY] * len(after) + [VMEM] * (len(rows) + 2),
        out_specs=[VMEM] * (split + 1),
        scratch_shapes=[pltpu.VMEM((classes, 2 * count, 2 * LANES), BF16)]
        + [pltpu.VMEM((2 * columns, count, lag_dev), F32)] * (span != lag_dev),
        compiler_params=params(16),
        cost_estimate=effort,
        name="cross_lags",
    )(scal, weight, *after, *rows, own, table)


def cores_kernel(skip, split, scal, *refs):
    keep, *refs = refs[skip:]
    more, own, sends = refs[:split], refs[split], refs[split + 1 :]
    columns = keep.shape[0]
    for i, m in enumerate(more):
        at = slice(i * m.shape[1], (i + 1) * m.shape[1])
        for column in range(columns):
            value = keep[column, at] + m[column].astype(F32)

            @pl.when(scal[COLUMN] == column)
            def _():
                own[at] = value

            for s, out in enumerate(sends):

                @pl.when(scal[COLUMN] ^ (s + 1) == column)
                def _():
                    out[at] = value.astype(BF16)


def add_cores(scal, after, keep, more):
    columns, rows, lag_dev = keep.shape
    return pl.pallas_call(
        functools.partial(cores_kernel, len(after), len(more)),
        out_shape=[jax.ShapeDtypeStruct((rows, lag_dev), F32)]
        + [jax.ShapeDtypeStruct((rows, lag_dev), BF16)] * (columns - 1),
        in_specs=[SMEM] + [ANY] * len(after) + [VMEM] * (1 + len(more)),
        out_specs=[VMEM] * columns,
        compiler_params=params(8),
        cost_estimate=SMALL,
        name="cores",
    )(scal, *after, keep, *more)


def stats_kernel(scale, q, pieces, others, scal, *refs):
    count = min(q, 1)
    earlier, (own, *refs) = refs[:count], refs[count:]
    more, refs = refs[:others], refs[others:]
    targets, (corr, sums) = refs[: len(pieces)], refs[len(pieces) :]
    columns = []
    for target, (unit, first, count, at) in zip(targets, placed(pieces)):
        value = own[at]
        for m in more:
            value = value + m[at].astype(F32)
        slot = first + lax.broadcasted_iota(jnp.int32, (count, 1), 0)
        value = value * jnp.where(slot < scal[COUNT + unit], scale, 0.0)
        corr[at] = value
        square = jnp.sum(value * value, axis=1, keepdims=True)
        product = jnp.sum(value * target[0], axis=1, keepdims=True)
        lane = lax.broadcasted_iota(jnp.int32, (count, LANES), 1)
        columns.append(jnp.where(lane == 2 * q, square, jnp.where(lane == 2 * q + 1, product, 0.0)))
    spare = sums.shape[1] - own.shape[0]
    if spare:
        columns.append(jnp.zeros((spare, LANES), F32))
    total = jnp.concatenate(columns, axis=0).T[:8]
    for e in earlier:
        total = total + e[...]
    sums[...] = total


def target_specs(pieces, lag_dev):
    return [
        pl.BlockSpec(
            (1, count, lag_dev),
            lambda i, scal, unit=unit, block=first // count: (scal[BLOCK + unit], block, 0),
        )
        for unit, first, count in pieces
    ]


def whole(shape):
    return pl.BlockSpec(shape, lambda i, scal: (0,) * len(shape))


def lag_stats(scal, scale, q, pieces, earlier, own, more, observed):
    rows, lag_dev = own.shape
    outs = [jax.ShapeDtypeStruct((rows, lag_dev), F32), jax.ShapeDtypeStruct((8, -(-rows // LANES) * LANES), F32)]
    return pl.pallas_call(
        functools.partial(stats_kernel, scale, q, pieces, len(more)),
        grid_spec=pltpu.PrefetchScalarGridSpec(
            num_scalar_prefetch=1,
            grid=(1,),
            in_specs=[whole(e.shape) for e in earlier]
            + [whole(own.shape)] * (1 + len(more))
            + target_specs(pieces, lag_dev),
            out_specs=[whole(o.shape) for o in outs],
        ),
        out_shape=outs,
        compiler_params=params(16),
        cost_estimate=SMALL,
        name="stats",
    )(scal, *earlier, own, *more, *[observed] * len(pieces))


def slot_scales(sums, lag_total, q):
    total = sums[0][...]
    for s in sums[1:]:
        total = total + s[...]
    rows = total.shape[1]
    square, product = total[2 * q : 2 * q + 1], total[2 * q + 1 : 2 * q + 2]
    inverse = 1.0 / jnp.sqrt(square / lag_total + EPSILON)
    bending = (square * inverse * inverse - product * inverse) / lag_total
    sub = lax.broadcasted_iota(jnp.int32, (LANES, rows), 0)
    both = jnp.where(sub == 0, inverse, jnp.where(sub == 1, bending, 0.0)).T
    return both[:, 0:1], both[:, 1:2]


def gradient_kernel(lag_total, chunks, parts, skip, scal, *refs):
    sums, refs = refs[skip : skip + parts], refs[skip + parts :]
    corrs, refs = refs[: len(chunks)], refs[len(chunks) :]
    targets, outs = refs[: len(refs) // 2], refs[len(refs) // 2 :]
    i = 0
    for corr, (q, pieces) in zip(corrs, chunks):
        inverse, bending = slot_scales(sums, lag_total, q)
        for unit, first, count, at in placed(pieces):
            slot = first + lax.broadcasted_iota(jnp.int32, (count, 1), 0)
            valid = jnp.where(slot < scal[COUNT + unit], inverse[at], 0.0)
            normed = corr[at] * inverse[at]
            outs[i][...] = ((normed - targets[i][0] - normed * bending[at]) * valid).astype(BF16)
            i += 1


def gradients(scal, lag_total, chunks, after, sums, corrs, observed):
    lag_dev = observed.shape[2]
    pieces = [p for _, some in chunks for p in some]
    outs = [jax.ShapeDtypeStruct((p[2], lag_dev), BF16) for p in pieces]
    return pl.pallas_call(
        functools.partial(gradient_kernel, lag_total, chunks, len(sums), len(after)),
        grid_spec=pltpu.PrefetchScalarGridSpec(
            num_scalar_prefetch=1,
            grid=(1,),
            in_specs=[ANY] * len(after)
            + [whole(x.shape) for x in (*sums, *corrs)]
            + target_specs(pieces, lag_dev),
            out_specs=[whole(o.shape) for o in outs],
        ),
        out_shape=outs,
        compiler_params=params(16),
        cost_estimate=SMALL,
        name="gradient",
    )(scal, *after, *sums, *corrs, *[observed] * len(pieces))


def normed_kernel(lag_total, chunks, parts, scal, *refs):
    sums, corrs, out = refs[:parts], refs[parts:-1], refs[-1]
    for q, (pieces, corr) in enumerate(zip(chunks, corrs)):
        inverse, _ = slot_scales(sums, lag_total, q)
        for unit, first, count, at in placed(pieces):

            @pl.when(pl.program_id(0) == unit)
            def _():
                out[0, first : first + count] = corr[at] * inverse[at]


def normed_rows(scal, lag_total, chunks, sums, corrs, observed):
    blocks, slots, lag_dev = observed.shape
    ins = [*sums, *corrs]
    return pl.pallas_call(
        functools.partial(normed_kernel, lag_total, chunks, len(sums)),
        grid_spec=pltpu.PrefetchScalarGridSpec(
            num_scalar_prefetch=1,
            grid=(blocks,),
            in_specs=[whole(x.shape) for x in ins],
            out_specs=pl.BlockSpec((1, slots, lag_dev), lambda i, scal: (scal[BLOCK + i], 0, 0)),
        ),
        out_shape=jax.ShapeDtypeStruct(observed.shape, F32),
        compiler_params=params(16),
        cost_estimate=SMALL,
        name="normed",
    )(scal, *ins)


def adjoint_kernel(pieces, *refs):
    ids, parts, out = refs[: len(pieces)], refs[len(pieces) : -1], refs[-1]
    pick = picks([i.at[:, p[1] : p[1] + p[2]] for i, p in zip(ids, pieces)], out.shape[0])
    rows = jnp.concatenate([p[...] for p in parts], axis=0)
    out[...] = jnp.dot(pick, rows, preferred_element_type=F32)


def adjoint_rows(src_ids, pieces, parts, channels):
    lag_dev = parts[0].shape[1]
    return pl.pallas_call(
        functools.partial(adjoint_kernel, pieces),
        out_shape=jax.ShapeDtypeStruct((channels, lag_dev), F32),
        in_specs=[VMEM] * (2 * len(parts)),
        out_specs=VMEM,
        compiler_params=params(16),
        cost_estimate=SMALL,
        name="adjoint",
    )(*[src_ids[p[0]] for p in pieces], *parts)


def shards(spectra, window_keep, owners, pair_src, pair_rec, pair_count, observed):
    columns, cores, places = lax.axis_size("win"), lax.axis_size("freq"), lax.axis_size("recv")
    column, core, place = lax.axis_index("win"), lax.axis_index("freq"), lax.axis_index("recv")
    assert spectra.shape[0] == 1 and cores == 2
    channels, bins_dev = spectra.shape[2:]
    blocks, slots, lag_dev = observed.shape
    lag_total = lag_dev * columns * cores
    bin_total = bins_dev * cores
    period = 2 * bin_total
    part = bins_dev // columns
    classes = part // LANES
    span = period // classes
    geometry = (classes, span, lag_total // span, lag_total // 2, period, 256)
    lag_scale = 1.0 / math.sqrt(bin_total * columns)
    peers = columns * cores
    some = slots // 2
    shifts = range(places)

    def cut(values, s):
        return lax.dynamic_slice(values, (0, 0, 0, (column ^ s) * part), (1, 2, channels, part))

    here, *held = [swapped(cut(spectra, s), "win", columns, s) for s in range(columns)]
    scal, wanted, rec_ids = index(
        window_keep, owners, pair_count, pair_src, pair_rec, places
    )
    if columns == 2:
        weight = jnp.ones((1,), F32)
    else:
        keeps = jnp.stack([swapped(window_keep[0], "win", columns, s) for s in range(columns)])
        ranked = jnp.argsort(-keeps)[: columns - 1].astype(jnp.int32)
        weight = keeps[ranked].astype(F32)
        scal = lax.dynamic_update_slice(scal, ranked, (ORDER,))

    direct = places == blocks
    src_ids = [swapped(wanted[d], "recv", places, d) for d in reversed(shifts)][::-1]
    trig = tables(classes, span, period, bins_dev, columns, cores)
    if direct and blocks == 4:
        chunks = [
            [(0, 0, slots), (1, 0, slots)],
            [(3, 0, slots)],
            [(2, 0, slots)],
        ]
    else:
        chunks = [[(d, first, some) for d in range(blocks)] for first in (0, some)]
    if direct:
        messages = [piece for pieces in chunks for piece in pieces]
    else:
        messages = [(d, 0, slots) for d in shifts]
    sent, kept = gather_rows(scal, here, held, make_perm(part), src_ids, messages)
    own_rows, table = gather_own(scal, kept, rec_ids, trig, classes, span, peers)
    arrived = [swapped(x, "recv", places, m[0]) for m, x in reversed(list(zip(messages, sent)))][::-1]
    if not direct:
        stacked = jnp.stack(arrived)
        whole_rows = [
            lax.dynamic_index_in_dim(stacked, place ^ owners[b], 0, False) for b in range(blocks)
        ]
        arrived = [whole_rows[piece[0]] for pieces in chunks for piece in pieces]
    corrs, all_sums, returned, returned_pieces = [], [], [], []
    after = []
    for q, pieces in enumerate(chunks):
        rows, arrived = arrived[: len(pieces)], arrived[len(pieces) :]
        groups = sum(p[2] for p in pieces) // (32 if q else 16)
        if q:
            keep, *sends = cross_lag_parts(
                scal,
                weight,
                after[:1],
                rows,
                own_rows,
                pieces,
                table,
                geometry,
                columns,
                lag_dev,
                groups,
                SMALL if q == 1 else LARGE,
            )
        else:
            lhs = cross_rows(weight, [], rows, own_rows, pieces, classes, LARGE)
            keep, *sends = lag_parts(
                scal, [], lhs, table, geometry, columns, lag_dev, groups, LARGE
            )
        sends = [swapped(x, "freq", cores, 1) for x in sends]
        own, *sends = add_cores(scal, after[1:], keep, sends)
        more = [swapped(x, "win", columns, s + 1) for s, x in enumerate(sends)]
        after = [own, *more] if q == 0 else []
        corr, sums = lag_stats(scal, lag_scale, q, pieces, all_sums, own, more, observed)
        corrs.append(corr)
        all_sums = [sums]
    sums = [swapped(sums, ("win", "freq"), peers, s) for s in reversed(range(peers))]
    after = []
    numbered = list(enumerate(chunks))
    for group in (numbered[1:], numbered[:1]):
        grads = gradients(scal, lag_total, group, after, sums, [corrs[q] for q, _ in group], observed)
        pieces = [p for _, some_pieces in group for p in some_pieces]
        after = [grads[0]]
        if not direct:
            stacked = jnp.stack(list(grads) + [jnp.zeros_like(grads[0])])
            grads = []
            for d in shifts:
                block = jnp.int32(blocks)
                for b in range(blocks):
                    block = jnp.where(owners[b] == place ^ d, b, block)
                grads.append(lax.dynamic_index_in_dim(stacked, block, 0, False))
            pieces = [(d, pieces[0][1], some) for d in shifts]
        sent = [swapped(g, "recv", places, p[0]) for p, g in reversed(list(zip(pieces, grads)))]
        returned += sent[::-1]
        returned_pieces += pieces
    normed = normed_rows(scal, lag_total, chunks, sums, corrs, observed)
    adjoint = adjoint_rows(src_ids, returned_pieces, returned, channels)
    return (normed, adjoint)


def solution(mesh):
    return jax.shard_map(
        shards,
        mesh=mesh,
        in_specs=(
            P("win", None, ("groups", "recv"), "freq"),
            P(("groups", "win")),
            P("groups"),
            P(None, ("groups", "recv")),
            P(None, ("groups", "recv")),
            P(None, ("groups", "recv")),
            P(None, ("groups", "recv"), ("win", "freq")),
        ),
        out_specs=(
            P(None, ("groups", "recv"), ("win", "freq")),
            P(("groups", "recv"), ("win", "freq")),
        ),
        check_vma=False,
    )
```

```python
import functools
import math

import jax
import jax.numpy as jnp
import ml_dtypes
import numpy as np
from jax import lax
from jax.experimental import pallas as pl
from jax.experimental.pallas import tpu as pltpu
from jax.sharding import PartitionSpec as P

EPSILON = 1e-06
MIB = 1 << 20
LANES = 128
CORE, COLUMN, ORDER, BLOCK, COUNT = 0, 1, 2, 8, 16
BF16 = jnp.bfloat16
F32 = jnp.float32
VMEM = pl.BlockSpec(memory_space=pltpu.VMEM)
SMEM = pl.BlockSpec(memory_space=pltpu.SMEM)
HBM = pl.BlockSpec(memory_space=pltpu.HBM)
ANY = pl.BlockSpec(memory_space=pl.ANY)


def swapped(value, axis, size, step):
    assert size & (size - 1) == 0
    if step == 0:
        return value
    return lax.ppermute(value, axis, [(i, i ^ step) for i in range(size)])


def params(mib):
    return pltpu.CompilerParams(vmem_limit_bytes=mib * MIB)


SMALL = pl.CostEstimate(flops=1, bytes_accessed=1, transcendentals=0)
LARGE = pl.CostEstimate(flops=2 * 10**10, bytes_accessed=MIB, transcendentals=0)


def tables(classes, span, period, bins_dev, columns, cores):
    u = np.arange(span, dtype=np.int64)[None, :]
    piece = np.arange(columns * cores, dtype=np.int64)[:, None]
    first = piece % cores * bins_dev + piece // cores * (bins_dev // columns)
    rows = (first + np.arange(classes)).reshape(-1)
    high = 16 * classes * np.arange(LANES // 16, dtype=np.int64)
    low = classes * np.arange(16, dtype=np.int64)
    angle = (np.concatenate([rows, high, low])[:, None] * u % period) * (2.0 * math.pi / period)
    return np.stack([np.cos(angle), np.sin(angle)]).astype(np.float32)


def fetch(pairs, sems):
    copies = [pltpu.make_async_copy(a, b, sems.at[i]) for i, (a, b) in enumerate(pairs)]
    for c in copies:
        c.start()
    for c in copies:
        c.wait()


def index_kernel(blocks, direct, *refs):
    given, refs = refs[:5], refs[5:]
    scal, wanted, rec_ids, held, sems = refs[0], refs[1:-7], refs[-7], refs[-6:-1], refs[-1]
    fetch(zip(given, held), sems)
    window_keep, owners, pair_count, src, rec = held
    place = lax.axis_index("recv")
    column, columns = lax.axis_index("win"), lax.axis_size("win")
    core = lax.axis_index("freq")
    scal[CORE] = core
    scal[COLUMN] = column
    scal[ORDER] = 1 - window_keep[0]
    for b in range(blocks):
        unit = place ^ owners[b] if direct else b
        scal[BLOCK + unit] = b
        scal[COUNT + unit] = pair_count[b]
    for d, out in enumerate(wanted):
        chosen = jnp.full(out.shape, -1, jnp.int32)
        received = jnp.zeros(out.shape, jnp.int32)
        for b in range(blocks):
            mine = jnp.full(out.shape, owners[b], jnp.int32) == (place ^ d)
            chosen = jnp.where(mine, src[b : b + 1], chosen)
            received = jnp.where(mine, rec[b : b + 1], received)
        out[...] = chosen
        if direct:
            rec_ids[d : d + 1] = received
    if not direct:
        rec_ids[...] = rec[...]


def index(window_keep, owners, pair_count, pair_src, pair_rec, places):
    blocks, slots = pair_src.shape
    ids = jax.ShapeDtypeStruct((1, slots), jnp.int32)
    given = [window_keep, owners, pair_count[:, 0], pair_src, pair_rec]
    scal, *wanted, rec_ids = pl.pallas_call(
        functools.partial(index_kernel, blocks, places == blocks),
        out_shape=[jax.ShapeDtypeStruct((LANES,), jnp.int32)]
        + [ids] * places
        + [jax.ShapeDtypeStruct(pair_rec.shape, jnp.int32)],
        in_specs=[HBM] * 5,
        out_specs=[SMEM] + [VMEM] * (places + 1),
        scratch_shapes=[pltpu.SMEM(g.shape, g.dtype) for g in given[:3]]
        + [pltpu.VMEM(g.shape, g.dtype) for g in given[3:]]
        + [pltpu.SemaphoreType.DMA((5,))],
        compiler_params=params(16),
        cost_estimate=SMALL,
        name="index",
    )(*given)
    return scal, wanted, rec_ids


def table_kernel(classes, parts, scal, trig, table, base):
    rows = parts * classes
    low = slice(rows + LANES // 16, rows + LANES // 16 + 16)
    cl, sl = trig[0, low], trig[1, low]
    for h in range(LANES // 16):
        ch, sh = trig[0, rows + h : rows + h + 1], trig[1, rows + h : rows + h + 1]
        base[0, 16 * h : 16 * h + 16] = ch * cl - sh * sl
        base[1, 16 * h : 16 * h + 16] = sh * cl + ch * sl
    first = (scal[CORE] + 2 * scal[COLUMN]) * classes
    cb, sb = base[0], base[1]
    for r in range(classes):
        ca, sa = trig[0, pl.ds(first + r, 1)], trig[1, pl.ds(first + r, 1)]
        table[r, :LANES] = (ca * cb - sa * sb).astype(BF16)
        table[r, LANES:] = (-(sa * cb + ca * sb)).astype(BF16)


def perm_kernel(perm):
    part = perm.shape[0]
    classes = part // LANES
    source = lax.broadcasted_iota(jnp.int32, (part, LANES), 0)
    target = classes * lax.broadcasted_iota(jnp.int32, (part, LANES), 1)
    for r in range(classes):
        perm[:, r * LANES : (r + 1) * LANES] = (source == target + r).astype(BF16)


def make_perm(part):
    return pl.pallas_call(
        perm_kernel,
        out_shape=jax.ShapeDtypeStruct((part, part), BF16),
        out_specs=VMEM,
        compiler_params=params(8),
        cost_estimate=SMALL,
        name="perm",
    )()


def picks(ids, channels):
    row = jnp.concatenate([i[...] for i in ids], axis=1)
    return (lax.broadcasted_iota(jnp.int32, (channels, row.shape[1]), 0) == row).astype(BF16)


def rows_kernel(used, sends, messages, scal, here, *refs):
    held, perm, src_ids, refs = refs[:used], refs[used], refs[used + 1 : used + 1 + sends], refs[used + 1 + sends :]
    outs, kept = refs[:-1], refs[-1]
    _, _, channels, part = kept.shape
    slots = src_ids[0].shape[1]
    pick = picks(src_ids[::-1], channels)
    for u in range(used):
        x = here[0].reshape(2 * channels, part)
        for s in range(used):
            x = jnp.where(scal[ORDER + u] == s + 1, held[s][0].reshape(2 * channels, part), x)
        x = jnp.dot(x, perm[...], preferred_element_type=F32).astype(BF16)
        for half in range(2):
            z = x[half * channels : (half + 1) * channels]
            kept[u, half] = z
            y = lax.dot_general(
                pick, z, (((0,), (0,)), ((), ())), preferred_element_type=F32
            ).astype(BF16)
            for (d, first, count), out in zip(messages, outs):
                at = d * slots + first
                out[u, half] = y[at : at + count]


def gather_rows(scal, here, held, perm, src_ids, messages):
    used = len(held)
    channels, part = held[0].shape[-2:]
    *sent, kept = pl.pallas_call(
        functools.partial(rows_kernel, used, len(src_ids), messages),
        out_shape=[jax.ShapeDtypeStruct((used, 2, m[2], part), BF16) for m in messages]
        + [jax.ShapeDtypeStruct((used, 2, channels, part), BF16)],
        in_specs=[SMEM] + [VMEM] * (used + 2 + len(src_ids)),
        out_specs=[VMEM] * (len(messages) + 1),
        compiler_params=params(16),
        cost_estimate=SMALL,
        name="rows",
    )(scal, here, *held, perm, *src_ids[::-1])
    return sent, kept


def own_kernel(classes, parts, scal, kept, rec_ids, trig, own, table, base):
    units, used, _, slots, _ = own.shape
    pick = picks([rec_ids.at[d : d + 1] for d in range(units)], kept.shape[2])
    for u in range(used):
        for half in range(2):
            y = lax.dot_general(
                pick, kept[u, half], (((0,), (0,)), ((), ())), preferred_element_type=F32
            ).astype(BF16)
            for d in range(units):
                own[d, u, half] = y[d * slots : (d + 1) * slots]
    table_kernel(classes, parts, scal, trig, table, base)


def gather_own(scal, kept, rec_ids, trig, classes, span, parts):
    used, _, _, part = kept.shape
    units, slots = rec_ids.shape
    return pl.pallas_call(
        functools.partial(own_kernel, classes, parts),
        out_shape=[
            jax.ShapeDtypeStruct((units, used, 2, slots, part), BF16),
            jax.ShapeDtypeStruct((classes, 2 * LANES, span), BF16),
        ],
        in_specs=[SMEM] + [VMEM] * 3,
        out_specs=[VMEM] * 2,
        scratch_shapes=[pltpu.VMEM((2, LANES, span), F32)],
        compiler_params=params(16),
        cost_estimate=SMALL,
        name="own",
    )(scal, kept, rec_ids, jnp.asarray(trig))


def combine(values, classes, outputs, origin, span, period):
    plain, scaled = [None] * outputs, [None] * outputs

    def add(into, k, value, sign):
        if into[k] is None:
            into[k] = value if sign > 0 else -value
        else:
            into[k] = into[k] + value if sign > 0 else into[k] - value

    for r, (real, imag) in enumerate(values):
        both = None
        for k in range(outputs):
            eighths = r * (span * k - origin) * 8 // period % 8
            assert r * (span * k - origin) * 8 % period == 0
            if eighths % 2 == 0:
                value, sign = ((real, 1), (imag, -1), (real, -1), (imag, 1))[eighths // 2]
                add(plain, k, value, sign)
            else:
                if both is None:
                    both = real + imag, real - imag
                value, sign = ((both[1], 1), (both[0], -1), (both[1], -1), (both[0], 1))[eighths // 2]
                add(scaled, k, value, sign)
    root = math.sqrt(0.5)
    return [a if b is None else a + root * b for a, b in zip(plain, scaled)]


def placed(pieces):
    at = 0
    for unit, first, count in pieces:
        yield unit, first, count, slice(at, at + count)
        at += count


def cross_kernel(pieces, skip, weight, *refs):
    refs = refs[skip:]
    s_refs, own, lhs = refs[:-2], refs[-2], refs[-1]
    used = own.shape[1]
    rows = lhs.shape[1] // 2
    for s_ref, (unit, first, count, at) in zip(s_refs, placed(pieces)):
        turned = slice(rows + at.start, rows + at.stop)
        mine = slice(first, first + count)
        sent = mine if s_ref.shape[2] > count else slice(0, count)
        for r in range(lhs.shape[0]):
            bins = slice(r * LANES, (r + 1) * LANES)
            real = imag = None
            for u in range(used):
                sr, si = (s_ref[u, half, sent, bins].astype(F32) for half in range(2))
                rr, ri = (own[unit, u, half, mine, bins].astype(F32) for half in range(2))
                re, im = sr * rr + si * ri, si * rr - sr * ri
                if u:
                    re, im = real + weight[u] * re, imag + weight[u] * im
                real, imag = re, im
            lhs[r, at, :LANES] = real.astype(BF16)
            lhs[r, at, LANES:] = imag.astype(BF16)
            lhs[r, turned, :LANES] = imag.astype(BF16)
            lhs[r, turned, LANES:] = (-real).astype(BF16)


def cross_rows(weight, after, rows, own, pieces, classes, effort):
    count = sum(p[2] for p in pieces)
    return pl.pallas_call(
        functools.partial(cross_kernel, pieces, len(after)),
        out_shape=jax.ShapeDtypeStruct((classes, 2 * count, 2 * LANES), BF16),
        in_specs=[SMEM] + [ANY] * len(after) + [VMEM] * (len(rows) + 1),
        out_specs=VMEM,
        compiler_params=params(8),
        cost_estimate=effort,
        name="cross",
    )(weight, *after, *rows, own)


def lags_kernel(geometry, split, skip, scal, *refs):
    classes, span, outputs, origin, period, chunk = geometry
    lhs, table, keep, *refs = refs[skip:]
    sends, sums = refs[:split], refs[split:]
    rows = lhs.shape[1] // 2
    lag_dev = keep.shape[-1]
    cores = 2
    at_once = span == lag_dev
    first = scal[CORE] == 0
    for start in range(0, span, chunk):
        values = []
        for r in range(classes):
            whole_turns = all(
                r * (span * k - origin) * 2 % period == 0 for k in range(outputs)
            )
            left = lhs[r, :rows] if whole_turns else lhs[r]
            y = jnp.dot(left, table[r, :, start : start + chunk], preferred_element_type=F32)
            values.append((y[:rows], None if whole_turns else y[rows:]))
        corr = combine(values, classes, outputs, origin, span, period)
        lags = slice(start, start + chunk)
        for column in range(keep.shape[0]) if at_once else ():
            even, odd = corr[2 * column], corr[2 * column + 1]
            keep[column, :, lags] = jnp.where(first, even, odd)
            other = jnp.where(first, odd, even).astype(BF16)
            for i, out in enumerate(sends):
                out[column, :, lags] = other[i * out.shape[1] : (i + 1) * out.shape[1]]
        for k, value in enumerate(corr) if not at_once else ():
            lag = span * k + start
            sums[0][lag // lag_dev, :, lag % lag_dev : lag % lag_dev + chunk] = value
    if at_once:
        return
    for column in range(keep.shape[0]):
        keep[column] = sums[0][cores * column + scal[CORE]]
        for i, out in enumerate(sends):
            at = slice(i * out.shape[1], (i + 1) * out.shape[1])
            out[column] = sums[0][cores * column + 1 - scal[CORE], at].astype(BF16)


def lag_parts(scal, after, lhs, table, geometry, columns, lag_dev, split, effort):
    rows = lhs.shape[1] // 2
    shape = lambda count: (columns, count, lag_dev)
    return pl.pallas_call(
        functools.partial(lags_kernel, geometry, split, len(after)),
        out_shape=[jax.ShapeDtypeStruct(shape(rows), F32)]
        + [jax.ShapeDtypeStruct(shape(rows // split), BF16)] * split,
        in_specs=[SMEM] + [ANY] * len(after) + [VMEM] * 2,
        out_specs=[VMEM] * (split + 1),
        scratch_shapes=[pltpu.VMEM((2 * columns, rows, lag_dev), F32)] * (geometry[1] != lag_dev),
        compiler_params=params(16),
        cost_estimate=effort,
        name="lags",
    )(scal, *after, lhs, table)


def cross_lags_kernel(geometry, split, skip, pieces, scal, weight, *refs):
    count = len(pieces) + 1
    rows, table, refs = refs[skip : skip + count], refs[skip + count], refs[skip + count + 1 :]
    outs, lhs, sums = refs[: split + 1], refs[split + 1], refs[split + 2 :]
    cross_kernel(pieces, 0, weight, *rows, lhs)
    lags_kernel(geometry, split, 0, scal, lhs, table, *outs, *sums)


def cross_lag_parts(
    scal, weight, after, rows, own, pieces, table, geometry, columns, lag_dev, split, effort
):
    classes, span = geometry[:2]
    count = sum(p[2] for p in pieces)
    shape = lambda rows: (columns, rows, lag_dev)
    return pl.pallas_call(
        functools.partial(cross_lags_kernel, geometry, split, len(after), pieces),
        out_shape=[jax.ShapeDtypeStruct(shape(count), F32)]
        + [jax.ShapeDtypeStruct(shape(count // split), BF16)] * split,
        in_specs=[SMEM] * 2 + [ANY] * len(after) + [VMEM] * (len(rows) + 2),
        out_specs=[VMEM] * (split + 1),
        scratch_shapes=[pltpu.VMEM((classes, 2 * count, 2 * LANES), BF16)]
        + [pltpu.VMEM((2 * columns, count, lag_dev), F32)] * (span != lag_dev),
        compiler_params=params(16),
        cost_estimate=effort,
        name="cross_lags",
    )(scal, weight, *after, *rows, own, table)


def cores_kernel(skip, split, scal, *refs):
    keep, *refs = refs[skip:]
    more, own, sends = refs[:split], refs[split], refs[split + 1 :]
    columns = keep.shape[0]
    for i, m in enumerate(more):
        at = slice(i * m.shape[1], (i + 1) * m.shape[1])
        for column in range(columns):
            value = keep[column, at] + m[column].astype(F32)

            @pl.when(scal[COLUMN] == column)
            def _():
                own[at] = value

            for s, out in enumerate(sends):

                @pl.when(scal[COLUMN] ^ (s + 1) == column)
                def _():
                    out[at] = value.astype(BF16)


def add_cores(scal, after, keep, more):
    columns, rows, lag_dev = keep.shape
    return pl.pallas_call(
        functools.partial(cores_kernel, len(after), len(more)),
        out_shape=[jax.ShapeDtypeStruct((rows, lag_dev), F32)]
        + [jax.ShapeDtypeStruct((rows, lag_dev), BF16)] * (columns - 1),
        in_specs=[SMEM] + [ANY] * len(after) + [VMEM] * (1 + len(more)),
        out_specs=[VMEM] * columns,
        compiler_params=params(8),
        cost_estimate=SMALL,
        name="cores",
    )(scal, *after, keep, *more)


def stats_kernel(scale, q, pieces, others, scal, *refs):
    count = min(q, 1)
    earlier, (own, *refs) = refs[:count], refs[count:]
    more, refs = refs[:others], refs[others:]
    targets, (corr, sums) = refs[: len(pieces)], refs[len(pieces) :]
    columns = []
    for target, (unit, first, count, at) in zip(targets, placed(pieces)):
        value = own[at]
        for m in more:
            value = value + m[at].astype(F32)
        slot = first + lax.broadcasted_iota(jnp.int32, (count, 1), 0)
        value = value * jnp.where(slot < scal[COUNT + unit], scale, 0.0)
        corr[at] = value
        square = jnp.sum(value * value, axis=1, keepdims=True)
        product = jnp.sum(value * target[0], axis=1, keepdims=True)
        lane = lax.broadcasted_iota(jnp.int32, (count, LANES), 1)
        columns.append(jnp.where(lane == 2 * q, square, jnp.where(lane == 2 * q + 1, product, 0.0)))
    spare = sums.shape[1] - own.shape[0]
    if spare:
        columns.append(jnp.zeros((spare, LANES), F32))
    total = jnp.concatenate(columns, axis=0).T[:8]
    for e in earlier:
        total = total + e[...]
    sums[...] = total


def target_specs(pieces, lag_dev):
    return [
        pl.BlockSpec(
            (1, count, lag_dev),
            lambda i, scal, unit=unit, block=first // count: (scal[BLOCK + unit], block, 0),
        )
        for unit, first, count in pieces
    ]


def whole(shape):
    return pl.BlockSpec(shape, lambda i, scal: (0,) * len(shape))


def lag_stats(scal, scale, q, pieces, earlier, own, more, observed):
    rows, lag_dev = own.shape
    outs = [jax.ShapeDtypeStruct((rows, lag_dev), F32), jax.ShapeDtypeStruct((8, -(-rows // LANES) * LANES), F32)]
    return pl.pallas_call(
        functools.partial(stats_kernel, scale, q, pieces, len(more)),
        grid_spec=pltpu.PrefetchScalarGridSpec(
            num_scalar_prefetch=1,
            grid=(1,),
            in_specs=[whole(e.shape) for e in earlier]
            + [whole(own.shape)] * (1 + len(more))
            + target_specs(pieces, lag_dev),
            out_specs=[whole(o.shape) for o in outs],
        ),
        out_shape=outs,
        compiler_params=params(16),
        cost_estimate=SMALL,
        name="stats",
    )(scal, *earlier, own, *more, *[observed] * len(pieces))


def slot_scales(sums, lag_total, q):
    total = sums[0][...]
    for s in sums[1:]:
        total = total + s[...]
    rows = total.shape[1]
    square, product = total[2 * q : 2 * q + 1], total[2 * q + 1 : 2 * q + 2]
    inverse = 1.0 / jnp.sqrt(square / lag_total + EPSILON)
    bending = (square * inverse * inverse - product * inverse) / lag_total
    sub = lax.broadcasted_iota(jnp.int32, (LANES, rows), 0)
    both = jnp.where(sub == 0, inverse, jnp.where(sub == 1, bending, 0.0)).T
    return both[:, 0:1], both[:, 1:2]


def gradient_kernel(lag_total, chunks, parts, skip, scal, *refs):
    sums, refs = refs[skip : skip + parts], refs[skip + parts :]
    corrs, refs = refs[: len(chunks)], refs[len(chunks) :]
    targets, outs = refs[: len(refs) // 2], refs[len(refs) // 2 :]
    i = 0
    for corr, (q, pieces) in zip(corrs, chunks):
        inverse, bending = slot_scales(sums, lag_total, q)
        for unit, first, count, at in placed(pieces):
            slot = first + lax.broadcasted_iota(jnp.int32, (count, 1), 0)
            valid = jnp.where(slot < scal[COUNT + unit], inverse[at], 0.0)
            normed = corr[at] * inverse[at]
            outs[i][...] = ((normed - targets[i][0] - normed * bending[at]) * valid).astype(BF16)
            i += 1


def gradients(scal, lag_total, chunks, after, sums, corrs, observed):
    lag_dev = observed.shape[2]
    pieces = [p for _, some in chunks for p in some]
    outs = [jax.ShapeDtypeStruct((p[2], lag_dev), BF16) for p in pieces]
    return pl.pallas_call(
        functools.partial(gradient_kernel, lag_total, chunks, len(sums), len(after)),
        grid_spec=pltpu.PrefetchScalarGridSpec(
            num_scalar_prefetch=1,
            grid=(1,),
            in_specs=[ANY] * len(after)
            + [whole(x.shape) for x in (*sums, *corrs)]
            + target_specs(pieces, lag_dev),
            out_specs=[whole(o.shape) for o in outs],
        ),
        out_shape=outs,
        compiler_params=params(16),
        cost_estimate=SMALL,
        name="gradient",
    )(scal, *after, *sums, *corrs, *[observed] * len(pieces))


def normed_kernel(lag_total, chunks, parts, scal, *refs):
    sums, corrs, out = refs[:parts], refs[parts:-1], refs[-1]
    for q, (pieces, corr) in enumerate(zip(chunks, corrs)):
        inverse, _ = slot_scales(sums, lag_total, q)
        for unit, first, count, at in placed(pieces):

            @pl.when(pl.program_id(0) == unit)
            def _():
                out[0, first : first + count] = corr[at] * inverse[at]


def normed_rows(scal, lag_total, chunks, sums, corrs, observed):
    blocks, slots, lag_dev = observed.shape
    ins = [*sums, *corrs]
    return pl.pallas_call(
        functools.partial(normed_kernel, lag_total, chunks, len(sums)),
        grid_spec=pltpu.PrefetchScalarGridSpec(
            num_scalar_prefetch=1,
            grid=(blocks,),
            in_specs=[whole(x.shape) for x in ins],
            out_specs=pl.BlockSpec((1, slots, lag_dev), lambda i, scal: (scal[BLOCK + i], 0, 0)),
        ),
        out_shape=jax.ShapeDtypeStruct(observed.shape, F32),
        compiler_params=params(16),
        cost_estimate=SMALL,
        name="normed",
    )(scal, *ins)


def adjoint_kernel(pieces, *refs):
    ids, parts, out = refs[: len(pieces)], refs[len(pieces) : -1], refs[-1]
    pick = picks([i.at[:, p[1] : p[1] + p[2]] for i, p in zip(ids, pieces)], out.shape[0])
    rows = jnp.concatenate([p[...] for p in parts], axis=0)
    out[...] = jnp.dot(pick, rows, preferred_element_type=F32)


def adjoint_rows(src_ids, pieces, parts, channels):
    lag_dev = parts[0].shape[1]
    return pl.pallas_call(
        functools.partial(adjoint_kernel, pieces),
        out_shape=jax.ShapeDtypeStruct((channels, lag_dev), F32),
        in_specs=[VMEM] * (2 * len(parts)),
        out_specs=VMEM,
        compiler_params=params(16),
        cost_estimate=SMALL,
        name="adjoint",
    )(*[src_ids[p[0]] for p in pieces], *parts)


def shards(spectra, window_keep, owners, pair_src, pair_rec, pair_count, observed):
    columns, cores, places = lax.axis_size("win"), lax.axis_size("freq"), lax.axis_size("recv")
    column, core, place = lax.axis_index("win"), lax.axis_index("freq"), lax.axis_index("recv")
    assert spectra.shape[0] == 1 and cores == 2
    channels, bins_dev = spectra.shape[2:]
    blocks, slots, lag_dev = observed.shape
    lag_total = lag_dev * columns * cores
    bin_total = bins_dev * cores
    period = 2 * bin_total
    part = bins_dev // columns
    classes = part // LANES
    span = period // classes
    geometry = (classes, span, lag_total // span, lag_total // 2, period, 256)
    lag_scale = 1.0 / math.sqrt(bin_total * columns)
    peers = columns * cores
    some = slots // 2
    shifts = range(places)

    def cut(values, s):
        return lax.dynamic_slice(values, (0, 0, 0, (column ^ s) * part), (1, 2, channels, part))

    here, *held = [swapped(cut(spectra, s), "win", columns, s) for s in range(columns)]
    scal, wanted, rec_ids = index(
        window_keep, owners, pair_count, pair_src, pair_rec, places
    )
    if columns == 2:
        weight = jnp.ones((1,), F32)
    else:
        keeps = jnp.stack([swapped(window_keep[0], "win", columns, s) for s in range(columns)])
        ranked = jnp.argsort(-keeps)[: columns - 1].astype(jnp.int32)
        weight = keeps[ranked].astype(F32)
        scal = lax.dynamic_update_slice(scal, ranked, (ORDER,))

    direct = places == blocks
    src_ids = [swapped(wanted[d], "recv", places, d) for d in reversed(shifts)][::-1]
    trig = tables(classes, span, period, bins_dev, columns, cores)
    if direct and blocks == 4:
        chunks = [
            [(0, 0, slots), (1, 0, slots)],
            [(3, 0, slots)],
            [(2, 0, slots)],
        ]
    else:
        chunks = [[(d, first, some) for d in range(blocks)] for first in (0, some)]
    if direct:
        messages = [piece for pieces in chunks for piece in pieces]
    else:
        messages = [(d, 0, slots) for d in shifts]
    sent, kept = gather_rows(scal, here, held, make_perm(part), src_ids, messages)
    own_rows, table = gather_own(scal, kept, rec_ids, trig, classes, span, peers)
    arrived = [swapped(x, "recv", places, m[0]) for m, x in reversed(list(zip(messages, sent)))][::-1]
    if not direct:
        stacked = jnp.stack(arrived)
        whole_rows = [
            lax.dynamic_index_in_dim(stacked, place ^ owners[b], 0, False) for b in range(blocks)
        ]
        arrived = [whole_rows[piece[0]] for pieces in chunks for piece in pieces]
    corrs, all_sums, returned, returned_pieces = [], [], [], []
    after = []
    for q, pieces in enumerate(chunks):
        rows, arrived = arrived[: len(pieces)], arrived[len(pieces) :]
        groups = sum(p[2] for p in pieces) // (32 if q else 16)
        if q:
            keep, *sends = cross_lag_parts(
                scal,
                weight,
                after[:1],
                rows,
                own_rows,
                pieces,
                table,
                geometry,
                columns,
                lag_dev,
                groups,
                SMALL if q == 1 else LARGE,
            )
        else:
            lhs = cross_rows(weight, [], rows, own_rows, pieces, classes, LARGE)
            keep, *sends = lag_parts(
                scal, [], lhs, table, geometry, columns, lag_dev, groups, LARGE
            )
        sends = [swapped(x, "freq", cores, 1) for x in sends]
        own, *sends = add_cores(scal, after[1:], keep, sends)
        more = [swapped(x, "win", columns, s + 1) for s, x in enumerate(sends)]
        after = [own, *more] if q == 0 else []
        corr, sums = lag_stats(scal, lag_scale, q, pieces, all_sums, own, more, observed)
        corrs.append(corr)
        all_sums = [sums]
    sums = [swapped(sums, ("win", "freq"), peers, s) for s in reversed(range(peers))]
    after = []
    numbered = list(enumerate(chunks))
    for group in (numbered[:0:-1], numbered[:1]):
        grads = gradients(scal, lag_total, group, after, sums, [corrs[q] for q, _ in group], observed)
        pieces = [p for _, some_pieces in group for p in some_pieces]
        after = [grads[0]]
        if not direct:
            stacked = jnp.stack(list(grads) + [jnp.zeros_like(grads[0])])
            grads = []
            for d in shifts:
                block = jnp.int32(blocks)
                for b in range(blocks):
                    block = jnp.where(owners[b] == place ^ d, b, block)
                grads.append(lax.dynamic_index_in_dim(stacked, block, 0, False))
            pieces = [(d, pieces[0][1], some) for d in shifts]
        sent = [swapped(g, "recv", places, p[0]) for p, g in reversed(list(zip(pieces, grads)))]
        returned += sent[::-1]
        returned_pieces += pieces
    normed = normed_rows(scal, lag_total, chunks, sums, corrs, observed)
    adjoint = adjoint_rows(src_ids, returned_pieces, returned, channels)
    return (normed, adjoint)


def solution(mesh):
    return jax.shard_map(
        shards,
        mesh=mesh,
        in_specs=(
            P("win", None, ("groups", "recv"), "freq"),
            P(("groups", "win")),
            P("groups"),
            P(None, ("groups", "recv")),
            P(None, ("groups", "recv")),
            P(None, ("groups", "recv")),
            P(None, ("groups", "recv"), ("win", "freq")),
        ),
        out_specs=(
            P(None, ("groups", "recv"), ("win", "freq")),
            P(("groups", "recv"), ("win", "freq")),
        ),
        check_vma=False,
    )
```

```python
import functools
import math

import jax
import jax.numpy as jnp
import ml_dtypes
import numpy as np
from jax import lax
from jax.experimental import pallas as pl
from jax.experimental.pallas import tpu as pltpu
from jax.sharding import PartitionSpec as P

EPSILON = 1e-06
MIB = 1 << 20
LANES = 128
CORE, COLUMN, ORDER, BLOCK, COUNT = 0, 1, 2, 8, 16
BF16 = jnp.bfloat16
F32 = jnp.float32
VMEM = pl.BlockSpec(memory_space=pltpu.VMEM)
SMEM = pl.BlockSpec(memory_space=pltpu.SMEM)
HBM = pl.BlockSpec(memory_space=pltpu.HBM)
ANY = pl.BlockSpec(memory_space=pl.ANY)


def swapped(value, axis, size, step):
    assert size & (size - 1) == 0
    if step == 0:
        return value
    return lax.ppermute(value, axis, [(i, i ^ step) for i in range(size)])


def params(mib):
    return pltpu.CompilerParams(vmem_limit_bytes=mib * MIB)


SMALL = pl.CostEstimate(flops=1, bytes_accessed=1, transcendentals=0)
LARGE = pl.CostEstimate(flops=2 * 10**10, bytes_accessed=MIB, transcendentals=0)


def tables(classes, span, period, bins_dev, columns, cores):
    u = np.arange(span, dtype=np.int64)[None, :]
    piece = np.arange(columns * cores, dtype=np.int64)[:, None]
    first = piece % cores * bins_dev + piece // cores * (bins_dev // columns)
    rows = (first + np.arange(classes)).reshape(-1)
    high = 16 * classes * np.arange(LANES // 16, dtype=np.int64)
    low = classes * np.arange(16, dtype=np.int64)
    angle = (np.concatenate([rows, high, low])[:, None] * u % period) * (2.0 * math.pi / period)
    return np.stack([np.cos(angle), np.sin(angle)]).astype(np.float32)


def fetch(pairs, sems):
    copies = [pltpu.make_async_copy(a, b, sems.at[i]) for i, (a, b) in enumerate(pairs)]
    for c in copies:
        c.start()
    for c in copies:
        c.wait()


def index_kernel(blocks, direct, *refs):
    given, refs = refs[:5], refs[5:]
    scal, wanted, rec_ids, held, sems = refs[0], refs[1:-7], refs[-7], refs[-6:-1], refs[-1]
    fetch(zip(given, held), sems)
    window_keep, owners, pair_count, src, rec = held
    place = lax.axis_index("recv")
    column, columns = lax.axis_index("win"), lax.axis_size("win")
    core = lax.axis_index("freq")
    scal[CORE] = core
    scal[COLUMN] = column
    scal[ORDER] = 1 - window_keep[0]
    for b in range(blocks):
        unit = place ^ owners[b] if direct else b
        scal[BLOCK + unit] = b
        scal[COUNT + unit] = pair_count[b]
    for d, out in enumerate(wanted):
        chosen = jnp.full(out.shape, -1, jnp.int32)
        received = jnp.zeros(out.shape, jnp.int32)
        for b in range(blocks):
            mine = jnp.full(out.shape, owners[b], jnp.int32) == (place ^ d)
            chosen = jnp.where(mine, src[b : b + 1], chosen)
            received = jnp.where(mine, rec[b : b + 1], received)
        out[...] = chosen
        if direct:
            rec_ids[d : d + 1] = received
    if not direct:
        rec_ids[...] = rec[...]


def index(window_keep, owners, pair_count, pair_src, pair_rec, places):
    blocks, slots = pair_src.shape
    ids = jax.ShapeDtypeStruct((1, slots), jnp.int32)
    given = [window_keep, owners, pair_count[:, 0], pair_src, pair_rec]
    scal, *wanted, rec_ids = pl.pallas_call(
        functools.partial(index_kernel, blocks, places == blocks),
        out_shape=[jax.ShapeDtypeStruct((LANES,), jnp.int32)]
        + [ids] * places
        + [jax.ShapeDtypeStruct(pair_rec.shape, jnp.int32)],
        in_specs=[HBM] * 5,
        out_specs=[SMEM] + [VMEM] * (places + 1),
        scratch_shapes=[pltpu.SMEM(g.shape, g.dtype) for g in given[:3]]
        + [pltpu.VMEM(g.shape, g.dtype) for g in given[3:]]
        + [pltpu.SemaphoreType.DMA((5,))],
        compiler_params=params(16),
        cost_estimate=SMALL,
        name="index",
    )(*given)
    return scal, wanted, rec_ids


def table_kernel(classes, parts, scal, trig, table, base):
    rows = parts * classes
    low = slice(rows + LANES // 16, rows + LANES // 16 + 16)
    cl, sl = trig[0, low], trig[1, low]
    for h in range(LANES // 16):
        ch, sh = trig[0, rows + h : rows + h + 1], trig[1, rows + h : rows + h + 1]
        base[0, 16 * h : 16 * h + 16] = ch * cl - sh * sl
        base[1, 16 * h : 16 * h + 16] = sh * cl + ch * sl
    first = (scal[CORE] + 2 * scal[COLUMN]) * classes
    cb, sb = base[0], base[1]
    for r in range(classes):
        ca, sa = trig[0, pl.ds(first + r, 1)], trig[1, pl.ds(first + r, 1)]
        table[r, :LANES] = (ca * cb - sa * sb).astype(BF16)
        table[r, LANES:] = (-(sa * cb + ca * sb)).astype(BF16)


def perm_kernel(perm):
    part = perm.shape[0]
    classes = part // LANES
    source = lax.broadcasted_iota(jnp.int32, (part, LANES), 0)
    target = classes * lax.broadcasted_iota(jnp.int32, (part, LANES), 1)
    for r in range(classes):
        perm[:, r * LANES : (r + 1) * LANES] = (source == target + r).astype(BF16)


def make_perm(part):
    return pl.pallas_call(
        perm_kernel,
        out_shape=jax.ShapeDtypeStruct((part, part), BF16),
        out_specs=VMEM,
        compiler_params=params(8),
        cost_estimate=SMALL,
        name="perm",
    )()


def picks(ids, channels):
    row = jnp.concatenate([i[...] for i in ids], axis=1)
    return (lax.broadcasted_iota(jnp.int32, (channels, row.shape[1]), 0) == row).astype(BF16)


def rows_kernel(used, sends, messages, scal, here, *refs):
    held, perm, src_ids, refs = refs[:used], refs[used], refs[used + 1 : used + 1 + sends], refs[used + 1 + sends :]
    outs, kept = refs[:-1], refs[-1]
    _, _, channels, part = kept.shape
    slots = src_ids[0].shape[1]
    pick = picks(src_ids[: sends - 1][::-1], channels)
    for u in range(used):
        x = here[0].reshape(2 * channels, part)
        for s in range(used):
            x = jnp.where(scal[ORDER + u] == s + 1, held[s][0].reshape(2 * channels, part), x)
        x = jnp.dot(x, perm[...], preferred_element_type=F32).astype(BF16)
        for half in range(2):
            z = x[half * channels : (half + 1) * channels]
            kept[u, half] = z
            y = lax.dot_general(
                pick, z, (((0,), (0,)), ((), ())), preferred_element_type=F32
            ).astype(BF16)
            for (d, first, count), out in zip(messages, outs):
                at = (d - 1) * slots + first
                out[u, half] = y[at : at + count]


def gather_rows(scal, here, held, perm, src_ids, messages):
    used = len(held)
    channels, part = held[0].shape[-2:]
    *sent, kept = pl.pallas_call(
        functools.partial(rows_kernel, used, len(src_ids), messages),
        out_shape=[jax.ShapeDtypeStruct((used, 2, m[2], part), BF16) for m in messages]
        + [jax.ShapeDtypeStruct((used, 2, channels, part), BF16)],
        in_specs=[SMEM] + [VMEM] * (used + 2 + len(src_ids)),
        out_specs=[VMEM] * (len(messages) + 1),
        compiler_params=params(16),
        cost_estimate=SMALL,
        name="rows",
    )(scal, here, *held, perm, *src_ids[::-1])
    return sent, kept


def own_kernel(classes, parts, scal, kept, src_ids, rec_ids, trig, here, own, table, base):
    units, used, _, slots, _ = own.shape
    ids = [rec_ids.at[d : d + 1] for d in range(units)] + [src_ids]
    pick = picks(ids, kept.shape[2])
    for u in range(used):
        for half in range(2):
            y = lax.dot_general(
                pick, kept[u, half], (((0,), (0,)), ((), ())), preferred_element_type=F32
            ).astype(BF16)
            for d in range(units):
                own[d, u, half] = y[d * slots : (d + 1) * slots]
            here[u, half] = y[units * slots :]
    table_kernel(classes, parts, scal, trig, table, base)


def gather_own(scal, kept, src_ids, rec_ids, trig, classes, span, parts):
    used, _, _, part = kept.shape
    units, slots = rec_ids.shape
    return pl.pallas_call(
        functools.partial(own_kernel, classes, parts),
        out_shape=[
            jax.ShapeDtypeStruct((used, 2, slots, part), BF16),
            jax.ShapeDtypeStruct((units, used, 2, slots, part), BF16),
            jax.ShapeDtypeStruct((classes, 2 * LANES, span), BF16),
        ],
        in_specs=[SMEM] + [VMEM] * 4,
        out_specs=[VMEM] * 3,
        scratch_shapes=[pltpu.VMEM((2, LANES, span), F32)],
        compiler_params=params(16),
        cost_estimate=SMALL,
        name="own",
    )(scal, kept, src_ids, rec_ids, jnp.asarray(trig))


def combine(values, classes, outputs, origin, span, period):
    plain, scaled = [None] * outputs, [None] * outputs

    def add(into, k, value, sign):
        if into[k] is None:
            into[k] = value if sign > 0 else -value
        else:
            into[k] = into[k] + value if sign > 0 else into[k] - value

    for r, (real, imag) in enumerate(values):
        both = None
        for k in range(outputs):
            eighths = r * (span * k - origin) * 8 // period % 8
            assert r * (span * k - origin) * 8 % period == 0
            if eighths % 2 == 0:
                value, sign = ((real, 1), (imag, -1), (real, -1), (imag, 1))[eighths // 2]
                add(plain, k, value, sign)
            else:
                if both is None:
                    both = real + imag, real - imag
                value, sign = ((both[1], 1), (both[0], -1), (both[1], -1), (both[0], 1))[eighths // 2]
                add(scaled, k, value, sign)
    root = math.sqrt(0.5)
    return [a if b is None else a + root * b for a, b in zip(plain, scaled)]


def placed(pieces):
    at = 0
    for unit, first, count in pieces:
        yield unit, first, count, slice(at, at + count)
        at += count


def cross_kernel(pieces, skip, weight, *refs):
    refs = refs[skip:]
    s_refs, own, lhs = refs[:-2], refs[-2], refs[-1]
    used = own.shape[1]
    rows = lhs.shape[1] // 2
    for s_ref, (unit, first, count, at) in zip(s_refs, placed(pieces)):
        turned = slice(rows + at.start, rows + at.stop)
        mine = slice(first, first + count)
        sent = mine if s_ref.shape[2] > count else slice(0, count)
        for r in range(lhs.shape[0]):
            bins = slice(r * LANES, (r + 1) * LANES)
            real = imag = None
            for u in range(used):
                sr, si = (s_ref[u, half, sent, bins].astype(F32) for half in range(2))
                rr, ri = (own[unit, u, half, mine, bins].astype(F32) for half in range(2))
                re, im = sr * rr + si * ri, si * rr - sr * ri
                if u:
                    re, im = real + weight[u] * re, imag + weight[u] * im
                real, imag = re, im
            lhs[r, at, :LANES] = real.astype(BF16)
            lhs[r, at, LANES:] = imag.astype(BF16)
            lhs[r, turned, :LANES] = imag.astype(BF16)
            lhs[r, turned, LANES:] = (-real).astype(BF16)


def cross_rows(weight, after, rows, own, pieces, classes, effort):
    count = sum(p[2] for p in pieces)
    return pl.pallas_call(
        functools.partial(cross_kernel, pieces, len(after)),
        out_shape=jax.ShapeDtypeStruct((classes, 2 * count, 2 * LANES), BF16),
        in_specs=[SMEM] + [ANY] * len(after) + [VMEM] * (len(rows) + 1),
        out_specs=VMEM,
        compiler_params=params(8),
        cost_estimate=effort,
        name="cross",
    )(weight, *after, *rows, own)


def lags_kernel(geometry, split, skip, scal, *refs):
    classes, span, outputs, origin, period, chunk = geometry
    lhs, table, keep, *refs = refs[skip:]
    sends, sums = refs[:split], refs[split:]
    rows = lhs.shape[1] // 2
    lag_dev = keep.shape[-1]
    cores = 2
    at_once = span == lag_dev
    first = scal[CORE] == 0
    for start in range(0, span, chunk):
        values = []
        for r in range(classes):
            whole_turns = all(
                r * (span * k - origin) * 2 % period == 0 for k in range(outputs)
            )
            left = lhs[r, :rows] if whole_turns else lhs[r]
            y = jnp.dot(left, table[r, :, start : start + chunk], preferred_element_type=F32)
            values.append((y[:rows], None if whole_turns else y[rows:]))
        corr = combine(values, classes, outputs, origin, span, period)
        lags = slice(start, start + chunk)
        for column in range(keep.shape[0]) if at_once else ():
            even, odd = corr[2 * column], corr[2 * column + 1]
            keep[column, :, lags] = jnp.where(first, even, odd)
            other = jnp.where(first, odd, even).astype(BF16)
            for i, out in enumerate(sends):
                out[column, :, lags] = other[i * out.shape[1] : (i + 1) * out.shape[1]]
        for k, value in enumerate(corr) if not at_once else ():
            lag = span * k + start
            sums[0][lag // lag_dev, :, lag % lag_dev : lag % lag_dev + chunk] = value
    if at_once:
        return
    for column in range(keep.shape[0]):
        keep[column] = sums[0][cores * column + scal[CORE]]
        for i, out in enumerate(sends):
            at = slice(i * out.shape[1], (i + 1) * out.shape[1])
            out[column] = sums[0][cores * column + 1 - scal[CORE], at].astype(BF16)


def lag_parts(scal, after, lhs, table, geometry, columns, lag_dev, split, effort):
    rows = lhs.shape[1] // 2
    shape = lambda count: (columns, count, lag_dev)
    return pl.pallas_call(
        functools.partial(lags_kernel, geometry, split, len(after)),
        out_shape=[jax.ShapeDtypeStruct(shape(rows), F32)]
        + [jax.ShapeDtypeStruct(shape(rows // split), BF16)] * split,
        in_specs=[SMEM] + [ANY] * len(after) + [VMEM] * 2,
        out_specs=[VMEM] * (split + 1),
        scratch_shapes=[pltpu.VMEM((2 * columns, rows, lag_dev), F32)] * (geometry[1] != lag_dev),
        compiler_params=params(16),
        cost_estimate=effort,
        name="lags",
    )(scal, *after, lhs, table)


def cross_lags_kernel(geometry, split, skip, pieces, scal, weight, *refs):
    count = len(pieces) + 1
    rows, table, refs = refs[skip : skip + count], refs[skip + count], refs[skip + count + 1 :]
    outs, lhs, sums = refs[: split + 1], refs[split + 1], refs[split + 2 :]
    cross_kernel(pieces, 0, weight, *rows, lhs)
    lags_kernel(geometry, split, 0, scal, lhs, table, *outs, *sums)


def cross_lag_parts(
    scal, weight, after, rows, own, pieces, table, geometry, columns, lag_dev, split, effort
):
    classes, span = geometry[:2]
    count = sum(p[2] for p in pieces)
    shape = lambda rows: (columns, rows, lag_dev)
    return pl.pallas_call(
        functools.partial(cross_lags_kernel, geometry, split, len(after), pieces),
        out_shape=[jax.ShapeDtypeStruct(shape(count), F32)]
        + [jax.ShapeDtypeStruct(shape(count // split), BF16)] * split,
        in_specs=[SMEM] * 2 + [ANY] * len(after) + [VMEM] * (len(rows) + 2),
        out_specs=[VMEM] * (split + 1),
        scratch_shapes=[pltpu.VMEM((classes, 2 * count, 2 * LANES), BF16)]
        + [pltpu.VMEM((2 * columns, count, lag_dev), F32)] * (span != lag_dev),
        compiler_params=params(16),
        cost_estimate=effort,
        name="cross_lags",
    )(scal, weight, *after, *rows, own, table)


def cores_kernel(skip, split, scal, *refs):
    keep, *refs = refs[skip:]
    more, own, sends = refs[:split], refs[split], refs[split + 1 :]
    columns = keep.shape[0]
    for i, m in enumerate(more):
        at = slice(i * m.shape[1], (i + 1) * m.shape[1])
        for column in range(columns):
            value = keep[column, at] + m[column].astype(F32)

            @pl.when(scal[COLUMN] == column)
            def _():
                own[at] = value

            for s, out in enumerate(sends):

                @pl.when(scal[COLUMN] ^ (s + 1) == column)
                def _():
                    out[at] = value.astype(BF16)


def add_cores(scal, after, keep, more):
    columns, rows, lag_dev = keep.shape
    return pl.pallas_call(
        functools.partial(cores_kernel, len(after), len(more)),
        out_shape=[jax.ShapeDtypeStruct((rows, lag_dev), F32)]
        + [jax.ShapeDtypeStruct((rows, lag_dev), BF16)] * (columns - 1),
        in_specs=[SMEM] + [ANY] * len(after) + [VMEM] * (1 + len(more)),
        out_specs=[VMEM] * columns,
        compiler_params=params(8),
        cost_estimate=SMALL,
        name="cores",
    )(scal, *after, keep, *more)


def stats_kernel(scale, q, pieces, others, scal, *refs):
    count = min(q, 1)
    earlier, (own, *refs) = refs[:count], refs[count:]
    more, refs = refs[:others], refs[others:]
    targets, (corr, sums) = refs[: len(pieces)], refs[len(pieces) :]
    columns = []
    for target, (unit, first, count, at) in zip(targets, placed(pieces)):
        value = own[at]
        for m in more:
            value = value + m[at].astype(F32)
        slot = first + lax.broadcasted_iota(jnp.int32, (count, 1), 0)
        value = value * jnp.where(slot < scal[COUNT + unit], scale, 0.0)
        corr[at] = value
        square = jnp.sum(value * value, axis=1, keepdims=True)
        product = jnp.sum(value * target[0], axis=1, keepdims=True)
        lane = lax.broadcasted_iota(jnp.int32, (count, LANES), 1)
        columns.append(jnp.where(lane == 2 * q, square, jnp.where(lane == 2 * q + 1, product, 0.0)))
    spare = sums.shape[1] - own.shape[0]
    if spare:
        columns.append(jnp.zeros((spare, LANES), F32))
    total = jnp.concatenate(columns, axis=0).T[:8]
    for e in earlier:
        total = total + e[...]
    sums[...] = total


def target_specs(pieces, lag_dev):
    return [
        pl.BlockSpec(
            (1, count, lag_dev),
            lambda i, scal, unit=unit, block=first // count: (scal[BLOCK + unit], block, 0),
        )
        for unit, first, count in pieces
    ]


def whole(shape):
    return pl.BlockSpec(shape, lambda i, scal: (0,) * len(shape))


def lag_stats(scal, scale, q, pieces, earlier, own, more, observed):
    rows, lag_dev = own.shape
    outs = [jax.ShapeDtypeStruct((rows, lag_dev), F32), jax.ShapeDtypeStruct((8, -(-rows // LANES) * LANES), F32)]
    return pl.pallas_call(
        functools.partial(stats_kernel, scale, q, pieces, len(more)),
        grid_spec=pltpu.PrefetchScalarGridSpec(
            num_scalar_prefetch=1,
            grid=(1,),
            in_specs=[whole(e.shape) for e in earlier]
            + [whole(own.shape)] * (1 + len(more))
            + target_specs(pieces, lag_dev),
            out_specs=[whole(o.shape) for o in outs],
        ),
        out_shape=outs,
        compiler_params=params(16),
        cost_estimate=SMALL,
        name="stats",
    )(scal, *earlier, own, *more, *[observed] * len(pieces))


def slot_scales(sums, lag_total, q):
    total = sums[0][...]
    for s in sums[1:]:
        total = total + s[...]
    rows = total.shape[1]
    square, product = total[2 * q : 2 * q + 1], total[2 * q + 1 : 2 * q + 2]
    inverse = 1.0 / jnp.sqrt(square / lag_total + EPSILON)
    bending = (square * inverse * inverse - product * inverse) / lag_total
    sub = lax.broadcasted_iota(jnp.int32, (LANES, rows), 0)
    both = jnp.where(sub == 0, inverse, jnp.where(sub == 1, bending, 0.0)).T
    return both[:, 0:1], both[:, 1:2]


def gradient_kernel(lag_total, chunks, parts, skip, scal, *refs):
    sums, refs = refs[skip : skip + parts], refs[skip + parts :]
    corrs, refs = refs[: len(chunks)], refs[len(chunks) :]
    targets, outs = refs[: len(refs) // 2], refs[len(refs) // 2 :]
    i = 0
    for corr, (q, pieces) in zip(corrs, chunks):
        inverse, bending = slot_scales(sums, lag_total, q)
        for unit, first, count, at in placed(pieces):
            slot = first + lax.broadcasted_iota(jnp.int32, (count, 1), 0)
            valid = jnp.where(slot < scal[COUNT + unit], inverse[at], 0.0)
            normed = corr[at] * inverse[at]
            outs[i][...] = ((normed - targets[i][0] - normed * bending[at]) * valid).astype(BF16)
            i += 1


def gradients(scal, lag_total, chunks, after, sums, corrs, observed):
    lag_dev = observed.shape[2]
    pieces = [p for _, some in chunks for p in some]
    outs = [jax.ShapeDtypeStruct((p[2], lag_dev), BF16) for p in pieces]
    return pl.pallas_call(
        functools.partial(gradient_kernel, lag_total, chunks, len(sums), len(after)),
        grid_spec=pltpu.PrefetchScalarGridSpec(
            num_scalar_prefetch=1,
            grid=(1,),
            in_specs=[ANY] * len(after)
            + [whole(x.shape) for x in (*sums, *corrs)]
            + target_specs(pieces, lag_dev),
            out_specs=[whole(o.shape) for o in outs],
        ),
        out_shape=outs,
        compiler_params=params(16),
        cost_estimate=SMALL,
        name="gradient",
    )(scal, *after, *sums, *corrs, *[observed] * len(pieces))


def normed_kernel(lag_total, chunks, parts, scal, *refs):
    sums, corrs, out = refs[:parts], refs[parts:-1], refs[-1]
    for q, (pieces, corr) in enumerate(zip(chunks, corrs)):
        inverse, _ = slot_scales(sums, lag_total, q)
        for unit, first, count, at in placed(pieces):

            @pl.when(pl.program_id(0) == unit)
            def _():
                out[0, first : first + count] = corr[at] * inverse[at]


def normed_rows(scal, lag_total, chunks, sums, corrs, observed):
    blocks, slots, lag_dev = observed.shape
    ins = [*sums, *corrs]
    return pl.pallas_call(
        functools.partial(normed_kernel, lag_total, chunks, len(sums)),
        grid_spec=pltpu.PrefetchScalarGridSpec(
            num_scalar_prefetch=1,
            grid=(blocks,),
            in_specs=[whole(x.shape) for x in ins],
            out_specs=pl.BlockSpec((1, slots, lag_dev), lambda i, scal: (scal[BLOCK + i], 0, 0)),
        ),
        out_shape=jax.ShapeDtypeStruct(observed.shape, F32),
        compiler_params=params(16),
        cost_estimate=SMALL,
        name="normed",
    )(scal, *ins)


def adjoint_kernel(pieces, *refs):
    ids, parts, out = refs[: len(pieces)], refs[len(pieces) : -1], refs[-1]
    pick = picks([i.at[:, p[1] : p[1] + p[2]] for i, p in zip(ids, pieces)], out.shape[0])
    rows = jnp.concatenate([p[...] for p in parts], axis=0)
    out[...] = jnp.dot(pick, rows, preferred_element_type=F32)


def adjoint_rows(src_ids, pieces, parts, channels):
    lag_dev = parts[0].shape[1]
    return pl.pallas_call(
        functools.partial(adjoint_kernel, pieces),
        out_shape=jax.ShapeDtypeStruct((channels, lag_dev), F32),
        in_specs=[VMEM] * (2 * len(parts)),
        out_specs=VMEM,
        compiler_params=params(16),
        cost_estimate=SMALL,
        name="adjoint",
    )(*[src_ids[p[0]] for p in pieces], *parts)


def shards(spectra, window_keep, owners, pair_src, pair_rec, pair_count, observed):
    columns, cores, places = lax.axis_size("win"), lax.axis_size("freq"), lax.axis_size("recv")
    column, core, place = lax.axis_index("win"), lax.axis_index("freq"), lax.axis_index("recv")
    assert spectra.shape[0] == 1 and cores == 2
    channels, bins_dev = spectra.shape[2:]
    blocks, slots, lag_dev = observed.shape
    lag_total = lag_dev * columns * cores
    bin_total = bins_dev * cores
    period = 2 * bin_total
    part = bins_dev // columns
    classes = part // LANES
    span = period // classes
    geometry = (classes, span, lag_total // span, lag_total // 2, period, 256)
    lag_scale = 1.0 / math.sqrt(bin_total * columns)
    peers = columns * cores
    some = slots // 2
    shifts = range(places)

    def cut(values, s):
        return lax.dynamic_slice(values, (0, 0, 0, (column ^ s) * part), (1, 2, channels, part))

    here, *held = [swapped(cut(spectra, s), "win", columns, s) for s in range(columns)]
    scal, wanted, rec_ids = index(
        window_keep, owners, pair_count, pair_src, pair_rec, places
    )
    if columns == 2:
        weight = jnp.ones((1,), F32)
    else:
        keeps = jnp.stack([swapped(window_keep[0], "win", columns, s) for s in range(columns)])
        ranked = jnp.argsort(-keeps)[: columns - 1].astype(jnp.int32)
        weight = keeps[ranked].astype(F32)
        scal = lax.dynamic_update_slice(scal, ranked, (ORDER,))

    direct = places == blocks
    src_ids = [swapped(wanted[d], "recv", places, d) for d in reversed(shifts)][::-1]
    trig = tables(classes, span, period, bins_dev, columns, cores)
    if direct and blocks == 4:
        chunks = [
            [(0, 0, slots), (1, 0, slots)],
            [(3, 0, slots)],
            [(2, 0, slots)],
        ]
    else:
        chunks = [[(d, first, some) for d in range(blocks)] for first in (0, some)]
    if direct:
        messages = [piece for pieces in chunks for piece in pieces]
    else:
        messages = [(d, 0, slots) for d in shifts]
    sent, kept = gather_rows(scal, here, held, make_perm(part), src_ids, [m for m in messages if m[0]])
    own_sent, own_rows, table = gather_own(scal, kept, src_ids[0], rec_ids, trig, classes, span, peers)
    sent = list(sent)
    sent = [sent.pop(0) if m[0] else own_sent for m in messages]
    arrived = [swapped(x, "recv", places, m[0]) for m, x in reversed(list(zip(messages, sent)))][::-1]
    if not direct:
        stacked = jnp.stack(arrived)
        whole_rows = [
            lax.dynamic_index_in_dim(stacked, place ^ owners[b], 0, False) for b in range(blocks)
        ]
        arrived = [whole_rows[piece[0]] for pieces in chunks for piece in pieces]
    corrs, all_sums, returned, returned_pieces = [], [], [], []
    after = []
    for q, pieces in enumerate(chunks):
        rows, arrived = arrived[: len(pieces)], arrived[len(pieces) :]
        groups = sum(p[2] for p in pieces) // (32 if q else 16)
        if q:
            keep, *sends = cross_lag_parts(
                scal,
                weight,
                after[:1],
                rows,
                own_rows,
                pieces,
                table,
                geometry,
                columns,
                lag_dev,
                groups,
                SMALL if q == 1 else LARGE,
            )
        else:
            lhs = cross_rows(weight, [], rows, own_rows, pieces, classes, LARGE)
            keep, *sends = lag_parts(
                scal, [], lhs, table, geometry, columns, lag_dev, groups, LARGE
            )
        sends = [swapped(x, "freq", cores, 1) for x in sends]
        own, *sends = add_cores(scal, after[1:], keep, sends)
        more = [swapped(x, "win", columns, s + 1) for s, x in enumerate(sends)]
        after = [own, *more] if q == 0 else []
        corr, sums = lag_stats(scal, lag_scale, q, pieces, all_sums, own, more, observed)
        corrs.append(corr)
        all_sums = [sums]
    sums = [swapped(sums, ("win", "freq"), peers, s) for s in reversed(range(peers))]
    after = []
    numbered = list(enumerate(chunks))
    for group in (numbered[1:], numbered[:1]):
        grads = gradients(scal, lag_total, group, after, sums, [corrs[q] for q, _ in group], observed)
        pieces = [p for _, some_pieces in group for p in some_pieces]
        after = [grads[0]]
        if not direct:
            stacked = jnp.stack(list(grads) + [jnp.zeros_like(grads[0])])
            grads = []
            for d in shifts:
                block = jnp.int32(blocks)
                for b in range(blocks):
                    block = jnp.where(owners[b] == place ^ d, b, block)
                grads.append(lax.dynamic_index_in_dim(stacked, block, 0, False))
            pieces = [(d, pieces[0][1], some) for d in shifts]
        sent = [swapped(g, "recv", places, p[0]) for p, g in reversed(list(zip(pieces, grads)))]
        returned += sent[::-1]
        returned_pieces += pieces
    normed = normed_rows(scal, lag_total, chunks, sums, corrs, observed)
    adjoint = adjoint_rows(src_ids, returned_pieces, returned, channels)
    return (normed, adjoint)


def solution(mesh):
    return jax.shard_map(
        shards,
        mesh=mesh,
        in_specs=(
            P("win", None, ("groups", "recv"), "freq"),
            P(("groups", "win")),
            P("groups"),
            P(None, ("groups", "recv")),
            P(None, ("groups", "recv")),
            P(None, ("groups", "recv")),
            P(None, ("groups", "recv"), ("win", "freq")),
        ),
        out_specs=(
            P(None, ("groups", "recv"), ("win", "freq")),
            P(("groups", "recv"), ("win", "freq")),
        ),
        check_vma=False,
    )
```

```python
import functools
import math

import jax
import jax.numpy as jnp
import ml_dtypes
import numpy as np
from jax import lax
from jax.experimental import pallas as pl
from jax.experimental.pallas import tpu as pltpu
from jax.sharding import PartitionSpec as P

EPSILON = 1e-06
MIB = 1 << 20
LANES = 128
CORE, COLUMN, ORDER, BLOCK, COUNT = 0, 1, 2, 8, 16
BF16 = jnp.bfloat16
F32 = jnp.float32
VMEM = pl.BlockSpec(memory_space=pltpu.VMEM)
SMEM = pl.BlockSpec(memory_space=pltpu.SMEM)
HBM = pl.BlockSpec(memory_space=pltpu.HBM)
ANY = pl.BlockSpec(memory_space=pl.ANY)


def swapped(value, axis, size, step):
    assert size & (size - 1) == 0
    if step == 0:
        return value
    return lax.ppermute(value, axis, [(i, i ^ step) for i in range(size)])


def params(mib):
    return pltpu.CompilerParams(vmem_limit_bytes=mib * MIB)


SMALL = pl.CostEstimate(flops=1, bytes_accessed=1, transcendentals=0)
LARGE = pl.CostEstimate(flops=2 * 10**10, bytes_accessed=MIB, transcendentals=0)


def tables(classes, span, period, bins_dev, columns, cores):
    u = np.arange(span, dtype=np.int64)[None, :]
    piece = np.arange(columns * cores, dtype=np.int64)[:, None]
    first = piece % cores * bins_dev + piece // cores * (bins_dev // columns)
    rows = (first + np.arange(classes)).reshape(-1)
    high = 16 * classes * np.arange(LANES // 16, dtype=np.int64)
    low = classes * np.arange(16, dtype=np.int64)
    angle = (np.concatenate([rows, high, low])[:, None] * u % period) * (2.0 * math.pi / period)
    return np.stack([np.cos(angle), np.sin(angle)]).astype(np.float32)


def fetch(pairs, sems):
    copies = [pltpu.make_async_copy(a, b, sems.at[i]) for i, (a, b) in enumerate(pairs)]
    for c in copies:
        c.start()
    for c in copies:
        c.wait()


def index_kernel(blocks, direct, *refs):
    given, refs = refs[:5], refs[5:]
    scal, wanted, rec_ids, held, sems = refs[0], refs[1:-7], refs[-7], refs[-6:-1], refs[-1]
    fetch(zip(given, held), sems)
    window_keep, owners, pair_count, src, rec = held
    place = lax.axis_index("recv")
    column, columns = lax.axis_index("win"), lax.axis_size("win")
    core = lax.axis_index("freq")
    scal[CORE] = core
    scal[COLUMN] = column
    scal[ORDER] = 1 - window_keep[0]
    for b in range(blocks):
        unit = place ^ owners[b] if direct else b
        scal[BLOCK + unit] = b
        scal[COUNT + unit] = pair_count[b]
    for d, out in enumerate(wanted):
        chosen = jnp.full(out.shape, -1, jnp.int32)
        received = jnp.zeros(out.shape, jnp.int32)
        for b in range(blocks):
            mine = jnp.full(out.shape, owners[b], jnp.int32) == (place ^ d)
            chosen = jnp.where(mine, src[b : b + 1], chosen)
            received = jnp.where(mine, rec[b : b + 1], received)
        out[...] = chosen
        if direct:
            rec_ids[d : d + 1] = received
    if not direct:
        rec_ids[...] = rec[...]


def index(window_keep, owners, pair_count, pair_src, pair_rec, places):
    blocks, slots = pair_src.shape
    ids = jax.ShapeDtypeStruct((1, slots), jnp.int32)
    given = [window_keep, owners, pair_count[:, 0], pair_src, pair_rec]
    scal, *wanted, rec_ids = pl.pallas_call(
        functools.partial(index_kernel, blocks, places == blocks),
        out_shape=[jax.ShapeDtypeStruct((LANES,), jnp.int32)]
        + [ids] * places
        + [jax.ShapeDtypeStruct(pair_rec.shape, jnp.int32)],
        in_specs=[HBM] * 5,
        out_specs=[SMEM] + [VMEM] * (places + 1),
        scratch_shapes=[pltpu.SMEM(g.shape, g.dtype) for g in given[:3]]
        + [pltpu.VMEM(g.shape, g.dtype) for g in given[3:]]
        + [pltpu.SemaphoreType.DMA((5,))],
        compiler_params=params(16),
        cost_estimate=SMALL,
        name="index",
    )(*given)
    return scal, wanted, rec_ids


def table_kernel(classes, parts, scal, trig, table, base):
    rows = parts * classes
    low = slice(rows + LANES // 16, rows + LANES // 16 + 16)
    cl, sl = trig[0, low], trig[1, low]
    for h in range(LANES // 16):
        ch, sh = trig[0, rows + h : rows + h + 1], trig[1, rows + h : rows + h + 1]
        base[0, 16 * h : 16 * h + 16] = ch * cl - sh * sl
        base[1, 16 * h : 16 * h + 16] = sh * cl + ch * sl
    first = (scal[CORE] + 2 * scal[COLUMN]) * classes
    cb, sb = base[0], base[1]
    for r in range(classes):
        ca, sa = trig[0, pl.ds(first + r, 1)], trig[1, pl.ds(first + r, 1)]
        table[r, :LANES] = (ca * cb - sa * sb).astype(BF16)
        table[r, LANES:] = (-(sa * cb + ca * sb)).astype(BF16)


def perm_kernel(perm):
    part = perm.shape[0]
    classes = part // LANES
    source = lax.broadcasted_iota(jnp.int32, (part, LANES), 0)
    target = classes * lax.broadcasted_iota(jnp.int32, (part, LANES), 1)
    for r in range(classes):
        perm[:, r * LANES : (r + 1) * LANES] = (source == target + r).astype(BF16)


def make_perm(part):
    return pl.pallas_call(
        perm_kernel,
        out_shape=jax.ShapeDtypeStruct((part, part), BF16),
        out_specs=VMEM,
        compiler_params=params(8),
        cost_estimate=SMALL,
        name="perm",
    )()


def picks(ids, channels):
    row = jnp.concatenate([i[...] for i in ids], axis=1)
    return (lax.broadcasted_iota(jnp.int32, (channels, row.shape[1]), 0) == row).astype(BF16)


def rows_kernel(used, sends, messages, scal, here, *refs):
    held, perm, src_ids, refs = refs[:used], refs[used], refs[used + 1 : used + 1 + sends], refs[used + 1 + sends :]
    outs, kept = refs[:-1], refs[-1]
    _, _, channels, part = kept.shape
    slots = src_ids[0].shape[1]
    pick = picks(src_ids[: sends - 1][::-1], channels)
    for u in range(used):
        x = here[0].reshape(2 * channels, part)
        for s in range(used):
            x = jnp.where(scal[ORDER + u] == s + 1, held[s][0].reshape(2 * channels, part), x)
        x = jnp.dot(x, perm[...], preferred_element_type=F32).astype(BF16)
        for half in range(2):
            z = x[half * channels : (half + 1) * channels]
            kept[u, half] = z
            y = lax.dot_general(
                pick, z, (((0,), (0,)), ((), ())), preferred_element_type=F32
            ).astype(BF16)
            for (d, first, count), out in zip(messages, outs):
                at = (d - 1) * slots + first
                out[u, half] = y[at : at + count]


def gather_rows(scal, here, held, perm, src_ids, messages):
    used = len(held)
    channels, part = held[0].shape[-2:]
    *sent, kept = pl.pallas_call(
        functools.partial(rows_kernel, used, len(src_ids), messages),
        out_shape=[jax.ShapeDtypeStruct((used, 2, m[2], part), BF16) for m in messages]
        + [jax.ShapeDtypeStruct((used, 2, channels, part), BF16)],
        in_specs=[SMEM] + [VMEM] * (used + 2 + len(src_ids)),
        out_specs=[VMEM] * (len(messages) + 1),
        compiler_params=params(16),
        cost_estimate=SMALL,
        name="rows",
    )(scal, here, *held, perm, *src_ids[::-1])
    return sent, kept


def own_kernel(classes, parts, scal, kept, src_ids, rec_ids, trig, here, own, table, base):
    units, used, _, slots, _ = own.shape
    ids = [rec_ids.at[d : d + 1] for d in range(units)] + [src_ids]
    pick = picks(ids, kept.shape[2])
    for u in range(used):
        for half in range(2):
            y = lax.dot_general(
                pick, kept[u, half], (((0,), (0,)), ((), ())), preferred_element_type=F32
            ).astype(BF16)
            for d in range(units):
                own[d, u, half] = y[d * slots : (d + 1) * slots]
            here[u, half] = y[units * slots :]
    table_kernel(classes, parts, scal, trig, table, base)


def gather_own(scal, kept, src_ids, rec_ids, trig, classes, span, parts):
    used, _, _, part = kept.shape
    units, slots = rec_ids.shape
    return pl.pallas_call(
        functools.partial(own_kernel, classes, parts),
        out_shape=[
            jax.ShapeDtypeStruct((used, 2, slots, part), BF16),
            jax.ShapeDtypeStruct((units, used, 2, slots, part), BF16),
            jax.ShapeDtypeStruct((classes, 2 * LANES, span), BF16),
        ],
        in_specs=[SMEM] + [VMEM] * 4,
        out_specs=[VMEM] * 3,
        scratch_shapes=[pltpu.VMEM((2, LANES, span), F32)],
        compiler_params=params(16),
        cost_estimate=SMALL,
        name="own",
    )(scal, kept, src_ids, rec_ids, jnp.asarray(trig))


def combine(values, classes, outputs, origin, span, period):
    plain, scaled = [None] * outputs, [None] * outputs

    def add(into, k, value, sign):
        if into[k] is None:
            into[k] = value if sign > 0 else -value
        else:
            into[k] = into[k] + value if sign > 0 else into[k] - value

    for r, (real, imag) in enumerate(values):
        both = None
        for k in range(outputs):
            eighths = r * (span * k - origin) * 8 // period % 8
            assert r * (span * k - origin) * 8 % period == 0
            if eighths % 2 == 0:
                value, sign = ((real, 1), (imag, -1), (real, -1), (imag, 1))[eighths // 2]
                add(plain, k, value, sign)
            else:
                if both is None:
                    both = real + imag, real - imag
                value, sign = ((both[1], 1), (both[0], -1), (both[1], -1), (both[0], 1))[eighths // 2]
                add(scaled, k, value, sign)
    root = math.sqrt(0.5)
    return [a if b is None else a + root * b for a, b in zip(plain, scaled)]


def placed(pieces):
    at = 0
    for unit, first, count in pieces:
        yield unit, first, count, slice(at, at + count)
        at += count


def cross_kernel(pieces, skip, weight, *refs):
    refs = refs[skip:]
    s_refs, own, lhs = refs[:-2], refs[-2], refs[-1]
    used = own.shape[1]
    rows = lhs.shape[1] // 2
    for s_ref, (unit, first, count, at) in zip(s_refs, placed(pieces)):
        turned = slice(rows + at.start, rows + at.stop)
        mine = slice(first, first + count)
        sent = mine if s_ref.shape[2] > count else slice(0, count)
        for r in range(lhs.shape[0]):
            bins = slice(r * LANES, (r + 1) * LANES)
            real = imag = None
            for u in range(used):
                sr, si = (s_ref[u, half, sent, bins].astype(F32) for half in range(2))
                rr, ri = (own[unit, u, half, mine, bins].astype(F32) for half in range(2))
                re, im = sr * rr + si * ri, si * rr - sr * ri
                if u:
                    re, im = real + weight[u] * re, imag + weight[u] * im
                real, imag = re, im
            lhs[r, at, :LANES] = real.astype(BF16)
            lhs[r, at, LANES:] = imag.astype(BF16)
            lhs[r, turned, :LANES] = imag.astype(BF16)
            lhs[r, turned, LANES:] = (-real).astype(BF16)


def cross_rows(weight, after, rows, own, pieces, classes, effort):
    count = sum(p[2] for p in pieces)
    return pl.pallas_call(
        functools.partial(cross_kernel, pieces, len(after)),
        out_shape=jax.ShapeDtypeStruct((classes, 2 * count, 2 * LANES), BF16),
        in_specs=[SMEM] + [ANY] * len(after) + [VMEM] * (len(rows) + 1),
        out_specs=VMEM,
        compiler_params=params(8),
        cost_estimate=effort,
        name="cross",
    )(weight, *after, *rows, own)


def lags_kernel(geometry, split, skip, scal, *refs):
    classes, span, outputs, origin, period, chunk = geometry
    lhs, table, keep, *refs = refs[skip:]
    sends, sums = refs[:split], refs[split:]
    rows = lhs.shape[1] // 2
    lag_dev = keep.shape[-1]
    cores = 2
    at_once = span == lag_dev
    first = scal[CORE] == 0
    for start in range(0, span, chunk):
        values = []
        for r in range(classes):
            whole_turns = all(
                r * (span * k - origin) * 2 % period == 0 for k in range(outputs)
            )
            left = lhs[r, :rows] if whole_turns else lhs[r]
            y = jnp.dot(left, table[r, :, start : start + chunk], preferred_element_type=F32)
            values.append((y[:rows], None if whole_turns else y[rows:]))
        corr = combine(values, classes, outputs, origin, span, period)
        lags = slice(start, start + chunk)
        for column in range(keep.shape[0]) if at_once else ():
            even, odd = corr[2 * column], corr[2 * column + 1]
            keep[column, :, lags] = jnp.where(first, even, odd)
            other = jnp.where(first, odd, even).astype(BF16)
            for i, out in enumerate(sends):
                out[column, :, lags] = other[i * out.shape[1] : (i + 1) * out.shape[1]]
        for k, value in enumerate(corr) if not at_once else ():
            lag = span * k + start
            sums[0][lag // lag_dev, :, lag % lag_dev : lag % lag_dev + chunk] = value
    if at_once:
        return
    for column in range(keep.shape[0]):
        keep[column] = sums[0][cores * column + scal[CORE]]
        for i, out in enumerate(sends):
            at = slice(i * out.shape[1], (i + 1) * out.shape[1])
            out[column] = sums[0][cores * column + 1 - scal[CORE], at].astype(BF16)


def lag_parts(scal, after, lhs, table, geometry, columns, lag_dev, split, effort):
    rows = lhs.shape[1] // 2
    shape = lambda count: (columns, count, lag_dev)
    return pl.pallas_call(
        functools.partial(lags_kernel, geometry, split, len(after)),
        out_shape=[jax.ShapeDtypeStruct(shape(rows), F32)]
        + [jax.ShapeDtypeStruct(shape(rows // split), BF16)] * split,
        in_specs=[SMEM] + [ANY] * len(after) + [VMEM] * 2,
        out_specs=[VMEM] * (split + 1),
        scratch_shapes=[pltpu.VMEM((2 * columns, rows, lag_dev), F32)] * (geometry[1] != lag_dev),
        compiler_params=params(16),
        cost_estimate=effort,
        name="lags",
    )(scal, *after, lhs, table)


def cross_lags_kernel(geometry, split, skip, pieces, scal, weight, *refs):
    count = len(pieces) + 1
    rows, table, refs = refs[skip : skip + count], refs[skip + count], refs[skip + count + 1 :]
    outs, lhs, sums = refs[: split + 1], refs[split + 1], refs[split + 2 :]
    cross_kernel(pieces, 0, weight, *rows, lhs)
    lags_kernel(geometry, split, 0, scal, lhs, table, *outs, *sums)


def cross_lag_parts(
    scal, weight, after, rows, own, pieces, table, geometry, columns, lag_dev, split, effort
):
    classes, span = geometry[:2]
    count = sum(p[2] for p in pieces)
    shape = lambda rows: (columns, rows, lag_dev)
    return pl.pallas_call(
        functools.partial(cross_lags_kernel, geometry, split, len(after), pieces),
        out_shape=[jax.ShapeDtypeStruct(shape(count), F32)]
        + [jax.ShapeDtypeStruct(shape(count // split), BF16)] * split,
        in_specs=[SMEM] * 2 + [ANY] * len(after) + [VMEM] * (len(rows) + 2),
        out_specs=[VMEM] * (split + 1),
        scratch_shapes=[pltpu.VMEM((classes, 2 * count, 2 * LANES), BF16)]
        + [pltpu.VMEM((2 * columns, count, lag_dev), F32)] * (span != lag_dev),
        compiler_params=params(16),
        cost_estimate=effort,
        name="cross_lags",
    )(scal, weight, *after, *rows, own, table)


def cores_kernel(skip, split, scal, *refs):
    keep, *refs = refs[skip:]
    more, own, sends = refs[:split], refs[split], refs[split + 1 :]
    columns = keep.shape[0]
    for i, m in enumerate(more):
        at = slice(i * m.shape[1], (i + 1) * m.shape[1])
        for column in range(columns):
            value = keep[column, at] + m[column].astype(F32)

            @pl.when(scal[COLUMN] == column)
            def _():
                own[at] = value

            for s, out in enumerate(sends):

                @pl.when(scal[COLUMN] ^ (s + 1) == column)
                def _():
                    out[at] = value.astype(BF16)


def add_cores(scal, after, keep, more):
    columns, rows, lag_dev = keep.shape
    return pl.pallas_call(
        functools.partial(cores_kernel, len(after), len(more)),
        out_shape=[jax.ShapeDtypeStruct((rows, lag_dev), F32)]
        + [jax.ShapeDtypeStruct((rows, lag_dev), BF16)] * (columns - 1),
        in_specs=[SMEM] + [ANY] * len(after) + [VMEM] * (1 + len(more)),
        out_specs=[VMEM] * columns,
        compiler_params=params(8),
        cost_estimate=SMALL,
        name="cores",
    )(scal, *after, keep, *more)


def stats_kernel(scale, q, pieces, others, scal, *refs):
    count = min(q, 1)
    earlier, (own, *refs) = refs[:count], refs[count:]
    more, refs = refs[:others], refs[others:]
    targets, (corr, sums) = refs[: len(pieces)], refs[len(pieces) :]
    columns = []
    for target, (unit, first, count, at) in zip(targets, placed(pieces)):
        value = own[at]
        for m in more:
            value = value + m[at].astype(F32)
        slot = first + lax.broadcasted_iota(jnp.int32, (count, 1), 0)
        value = value * jnp.where(slot < scal[COUNT + unit], scale, 0.0)
        corr[at] = value
        square = jnp.sum(value * value, axis=1, keepdims=True)
        product = jnp.sum(value * target[0], axis=1, keepdims=True)
        lane = lax.broadcasted_iota(jnp.int32, (count, LANES), 1)
        columns.append(jnp.where(lane == 2 * q, square, jnp.where(lane == 2 * q + 1, product, 0.0)))
    spare = sums.shape[1] - own.shape[0]
    if spare:
        columns.append(jnp.zeros((spare, LANES), F32))
    total = jnp.concatenate(columns, axis=0).T[:8]
    for e in earlier:
        total = total + e[...]
    sums[...] = total


def target_specs(pieces, lag_dev):
    return [
        pl.BlockSpec(
            (1, count, lag_dev),
            lambda i, scal, unit=unit, block=first // count: (scal[BLOCK + unit], block, 0),
        )
        for unit, first, count in pieces
    ]


def whole(shape):
    return pl.BlockSpec(shape, lambda i, scal: (0,) * len(shape))


def lag_stats(scal, scale, q, pieces, earlier, own, more, observed):
    rows, lag_dev = own.shape
    outs = [jax.ShapeDtypeStruct((rows, lag_dev), F32), jax.ShapeDtypeStruct((8, -(-rows // LANES) * LANES), F32)]
    return pl.pallas_call(
        functools.partial(stats_kernel, scale, q, pieces, len(more)),
        grid_spec=pltpu.PrefetchScalarGridSpec(
            num_scalar_prefetch=1,
            grid=(1,),
            in_specs=[whole(e.shape) for e in earlier]
            + [whole(own.shape)] * (1 + len(more))
            + target_specs(pieces, lag_dev),
            out_specs=[whole(o.shape) for o in outs],
        ),
        out_shape=outs,
        compiler_params=params(16),
        cost_estimate=SMALL,
        name="stats",
    )(scal, *earlier, own, *more, *[observed] * len(pieces))


def slot_scales(sums, lag_total, q):
    total = sums[0][...]
    for s in sums[1:]:
        total = total + s[...]
    rows = total.shape[1]
    square, product = total[2 * q : 2 * q + 1], total[2 * q + 1 : 2 * q + 2]
    inverse = 1.0 / jnp.sqrt(square / lag_total + EPSILON)
    bending = (square * inverse * inverse - product * inverse) / lag_total
    sub = lax.broadcasted_iota(jnp.int32, (LANES, rows), 0)
    both = jnp.where(sub == 0, inverse, jnp.where(sub == 1, bending, 0.0)).T
    return both[:, 0:1], both[:, 1:2]


def gradient_kernel(lag_total, chunks, parts, skip, scal, *refs):
    sums, refs = refs[skip : skip + parts], refs[skip + parts :]
    corrs, refs = refs[: len(chunks)], refs[len(chunks) :]
    targets, outs = refs[: len(refs) // 2], refs[len(refs) // 2 :]
    i = 0
    for corr, (q, pieces) in zip(corrs, chunks):
        inverse, bending = slot_scales(sums, lag_total, q)
        for unit, first, count, at in placed(pieces):
            slot = first + lax.broadcasted_iota(jnp.int32, (count, 1), 0)
            valid = jnp.where(slot < scal[COUNT + unit], inverse[at], 0.0)
            normed = corr[at] * inverse[at]
            outs[i][...] = ((normed - targets[i][0] - normed * bending[at]) * valid).astype(BF16)
            i += 1


def gradients(scal, lag_total, chunks, after, sums, corrs, observed):
    lag_dev = observed.shape[2]
    pieces = [p for _, some in chunks for p in some]
    outs = [jax.ShapeDtypeStruct((p[2], lag_dev), BF16) for p in pieces]
    return pl.pallas_call(
        functools.partial(gradient_kernel, lag_total, chunks, len(sums), len(after)),
        grid_spec=pltpu.PrefetchScalarGridSpec(
            num_scalar_prefetch=1,
            grid=(1,),
            in_specs=[ANY] * len(after)
            + [whole(x.shape) for x in (*sums, *corrs)]
            + target_specs(pieces, lag_dev),
            out_specs=[whole(o.shape) for o in outs],
        ),
        out_shape=outs,
        compiler_params=params(16),
        cost_estimate=SMALL,
        name="gradient",
    )(scal, *after, *sums, *corrs, *[observed] * len(pieces))


def normed_kernel(lag_total, chunks, parts, scal, *refs):
    sums, corrs, out = refs[:parts], refs[parts:-1], refs[-1]
    for q, (pieces, corr) in enumerate(zip(chunks, corrs)):
        inverse, _ = slot_scales(sums, lag_total, q)
        for unit, first, count, at in placed(pieces):

            @pl.when(pl.program_id(0) == unit)
            def _():
                out[0, first : first + count] = corr[at] * inverse[at]


def normed_rows(scal, lag_total, chunks, sums, corrs, observed):
    blocks, slots, lag_dev = observed.shape
    ins = [*sums, *corrs]
    return pl.pallas_call(
        functools.partial(normed_kernel, lag_total, chunks, len(sums)),
        grid_spec=pltpu.PrefetchScalarGridSpec(
            num_scalar_prefetch=1,
            grid=(blocks,),
            in_specs=[whole(x.shape) for x in ins],
            out_specs=pl.BlockSpec((1, slots, lag_dev), lambda i, scal: (scal[BLOCK + i], 0, 0)),
        ),
        out_shape=jax.ShapeDtypeStruct(observed.shape, F32),
        compiler_params=params(16),
        cost_estimate=SMALL,
        name="normed",
    )(scal, *ins)


def adjoint_kernel(pieces, *refs):
    ids, parts, out = refs[: len(pieces)], refs[len(pieces) : -1], refs[-1]
    pick = picks([i.at[:, p[1] : p[1] + p[2]] for i, p in zip(ids, pieces)], out.shape[0])
    rows = jnp.concatenate([p[...] for p in parts], axis=0)
    out[...] = jnp.dot(pick, rows, preferred_element_type=F32)


def adjoint_rows(src_ids, pieces, parts, channels):
    lag_dev = parts[0].shape[1]
    return pl.pallas_call(
        functools.partial(adjoint_kernel, pieces),
        out_shape=jax.ShapeDtypeStruct((channels, lag_dev), F32),
        in_specs=[VMEM] * (2 * len(parts)),
        out_specs=VMEM,
        compiler_params=params(16),
        cost_estimate=SMALL,
        name="adjoint",
    )(*[src_ids[p[0]] for p in pieces], *parts)


def shards(spectra, window_keep, owners, pair_src, pair_rec, pair_count, observed):
    columns, cores, places = lax.axis_size("win"), lax.axis_size("freq"), lax.axis_size("recv")
    column, core, place = lax.axis_index("win"), lax.axis_index("freq"), lax.axis_index("recv")
    assert spectra.shape[0] == 1 and cores == 2
    channels, bins_dev = spectra.shape[2:]
    blocks, slots, lag_dev = observed.shape
    lag_total = lag_dev * columns * cores
    bin_total = bins_dev * cores
    period = 2 * bin_total
    part = bins_dev // columns
    classes = part // LANES
    span = period // classes
    geometry = (classes, span, lag_total // span, lag_total // 2, period, 256)
    lag_scale = 1.0 / math.sqrt(bin_total * columns)
    peers = columns * cores
    some = slots // 2
    shifts = range(places)

    def cut(values, s):
        return lax.dynamic_slice(values, (0, 0, 0, (column ^ s) * part), (1, 2, channels, part))

    here, *held = [swapped(cut(spectra, s), "win", columns, s) for s in range(columns)]
    scal, wanted, rec_ids = index(
        window_keep, owners, pair_count, pair_src, pair_rec, places
    )
    if columns == 2:
        weight = jnp.ones((1,), F32)
    else:
        keeps = jnp.stack([swapped(window_keep[0], "win", columns, s) for s in range(columns)])
        ranked = jnp.argsort(-keeps)[: columns - 1].astype(jnp.int32)
        weight = keeps[ranked].astype(F32)
        scal = lax.dynamic_update_slice(scal, ranked, (ORDER,))

    direct = places == blocks
    src_ids = [swapped(wanted[d], "recv", places, d) for d in reversed(shifts)][::-1]
    trig = tables(classes, span, period, bins_dev, columns, cores)
    if direct and blocks == 4:
        chunks = [
            [(0, 0, slots), (1, 0, slots)],
            [(3, 0, slots)],
            [(2, 0, slots)],
        ]
    else:
        chunks = [[(d, first, some) for d in range(blocks)] for first in (0, some)]
    if direct:
        messages = [piece for pieces in chunks for piece in pieces]
    else:
        messages = [(d, 0, slots) for d in shifts]
    sent, kept = gather_rows(scal, here, held, make_perm(part), src_ids, [m for m in messages if m[0]])
    own_sent, own_rows, table = gather_own(scal, kept, src_ids[0], rec_ids, trig, classes, span, peers)
    sent = list(sent)
    sent = [sent.pop(0) if m[0] else own_sent for m in messages]
    arrived = [swapped(x, "recv", places, m[0]) for m, x in reversed(list(zip(messages, sent)))][::-1]
    if not direct:
        stacked = jnp.stack(arrived)
        whole_rows = [
            lax.dynamic_index_in_dim(stacked, place ^ owners[b], 0, False) for b in range(blocks)
        ]
        arrived = [whole_rows[piece[0]] for pieces in chunks for piece in pieces]
    corrs, all_sums, returned, returned_pieces = [], [], [], []
    after = []
    for q, pieces in enumerate(chunks):
        rows, arrived = arrived[: len(pieces)], arrived[len(pieces) :]
        groups = sum(p[2] for p in pieces) // (64 if q else 16)
        if q:
            keep, *sends = cross_lag_parts(
                scal,
                weight,
                after[:1],
                rows,
                own_rows,
                pieces,
                table,
                geometry,
                columns,
                lag_dev,
                groups,
                SMALL if q == 1 else LARGE,
            )
        else:
            lhs = cross_rows(weight, [], rows, own_rows, pieces, classes, LARGE)
            keep, *sends = lag_parts(
                scal, [], lhs, table, geometry, columns, lag_dev, groups, LARGE
            )
        sends = [swapped(x, "freq", cores, 1) for x in sends]
        own, *sends = add_cores(scal, after[1:], keep, sends)
        more = [swapped(x, "win", columns, s + 1) for s, x in enumerate(sends)]
        after = [own, *more] if q == 0 else []
        corr, sums = lag_stats(scal, lag_scale, q, pieces, all_sums, own, more, observed)
        corrs.append(corr)
        all_sums = [sums]
    sums = [swapped(sums, ("win", "freq"), peers, s) for s in reversed(range(peers))]
    after = []
    numbered = list(enumerate(chunks))
    for group in (numbered[1:], numbered[:1]):
        grads = gradients(scal, lag_total, group, after, sums, [corrs[q] for q, _ in group], observed)
        pieces = [p for _, some_pieces in group for p in some_pieces]
        after = [grads[0]]
        if not direct:
            stacked = jnp.stack(list(grads) + [jnp.zeros_like(grads[0])])
            grads = []
            for d in shifts:
                block = jnp.int32(blocks)
                for b in range(blocks):
                    block = jnp.where(owners[b] == place ^ d, b, block)
                grads.append(lax.dynamic_index_in_dim(stacked, block, 0, False))
            pieces = [(d, pieces[0][1], some) for d in shifts]
        sent = [swapped(g, "recv", places, p[0]) for p, g in reversed(list(zip(pieces, grads)))]
        returned += sent[::-1]
        returned_pieces += pieces
    normed = normed_rows(scal, lag_total, chunks, sums, corrs, observed)
    adjoint = adjoint_rows(src_ids, returned_pieces, returned, channels)
    return (normed, adjoint)


def solution(mesh):
    return jax.shard_map(
        shards,
        mesh=mesh,
        in_specs=(
            P("win", None, ("groups", "recv"), "freq"),
            P(("groups", "win")),
            P("groups"),
            P(None, ("groups", "recv")),
            P(None, ("groups", "recv")),
            P(None, ("groups", "recv")),
            P(None, ("groups", "recv"), ("win", "freq")),
        ),
        out_specs=(
            P(None, ("groups", "recv"), ("win", "freq")),
            P(("groups", "recv"), ("win", "freq")),
        ),
        check_vma=False,
    )
```
